32 devices in a mesh: row: 8 (over z, x), col: 4 (over y, core).
Axes of the slice: x: 2, y: 2, z: 4, core: 2. Of those that a mesh axis runs over, the one named last changes fastest.
Arguments:
- charges: bfloat16 [262144], P(('row', 'col')), may hold values from -6 to 6
- panel_order: int32 [262144], P(('row', 'col')), may hold values from 0 to 8191, as said below
- patch_anchor: int32 [3, 4096], P(None, ('row', 'col')), may hold values from 0 to 252, as said below
- project: bfloat16 [4096, 4096], P(('row', 'col')), may hold values from -0.75 to 0.75
- interpolate: bfloat16 [4096, 4096], P(('row', 'col')), may hold values from -0.75 to 0.75
- kernel_spectrum: float32 [512, 512, 512], P('row', 'col'), may hold values from 0.5 to 8
- near_pairs: int32 [2, 16384], P(None, ('row', 'col')), may hold values from 0 to 4095, as said below
- near_blocks: bfloat16 [16384, 4096], P(('row', 'col')), may hold values from -0.75 to 0.75
Outputs:
- potential: float32 [262144], P(('row', 'col'))
The draws below stay inside these ranges and needn't reach their ends.
Inputs may be any that keep to these rules, and one draw needn't show every extreme that they name: `panel_order`: the entries of each aligned run of 8192 slots (one device's slots) are a permutation of 0 to 8191. `patch_anchor`: block b lies on device d = b // 128 at row index r = d // 4 and col index c = d % 4; its first coordinate lies in r * 32 to (r + 1) * 32 - 1, its second in c * 64 to (c + 1) * 64 - 1, and all three coordinates are at most 252. `near_pairs`: the pairs on a device have that device's blocks as targets, each block exactly 4 times; each source block lies on the same device or on one whose row and col indices each differ by at most one.
All inputs are finite; a program needn't handle non-finite values.
Results may differ from the reference program's by a relative error of at most 0.0025.
Values may be sent and summed in bfloat16 or wider, within the bound.
No kernel may reach another device: no remote copies, remote signals or barrier semaphores. Data moves between devices by JAX's collectives and lax.ppermute only.
A program may use at most 128 MiB of HBM per device.

```python
import math
import jax
import jax.numpy as jnp
from jax import lax

G = 256
P_SIZE = 512
BLK = 64
PTS = 64
NB = 128
NEAR = 4
CX = 32
CY = 64
BLOCKS = 4096
PANELS = 262144
PAIRS = 16384
DEVICES = 32


def draw_panel_order(key, part):
    keys = jax.random.split(jax.random.fold_in(key, 11), DEVICES)
    orders = jax.vmap(lambda one: jax.random.permutation(one, NB * BLK))(keys).astype(jnp.int32)
    return orders.reshape(PANELS)


def draw_patch_anchor(key, part):
    mesh_cols = G // CY
    index = jnp.arange(BLOCKS, dtype=jnp.int32)
    device = index // NB
    local = index % NB
    row_at = device // mesh_cols
    col_at = device % mesh_cols

    def along(salt, start, cells):
        upper = jnp.minimum(start + cells, G - 3)
        raw = jax.random.randint(jax.random.fold_in(key, salt), (BLOCKS,), 0, 1 << 20)
        picked = start + raw % (upper - start)
        return jnp.where(local == 0, start, jnp.where(local == 1, upper - 1, picked))
    first = along(21, row_at * CX, CX)
    second = along(22, col_at * CY, CY)
    third = along(23, jnp.zeros_like(index), G)
    return jnp.stack([first, second, third]).astype(jnp.int32)


def draw_near_pairs(key, part):
    mesh_rows = G // CX
    mesh_cols = G // CY
    index = jnp.arange(PAIRS, dtype=jnp.int32)
    device = index // (NEAR * NB)
    target = device * NB + index % (NEAR * NB) % NB
    row_at = device // mesh_cols
    col_at = device % mesh_cols
    step_row = jax.random.randint(jax.random.fold_in(key, 31), (PAIRS,), -1, 2)
    step_col = jax.random.randint(jax.random.fold_in(key, 32), (PAIRS,), -1, 2)
    local = jax.random.randint(jax.random.fold_in(key, 33), (PAIRS,), 0, NB)
    source_row = jnp.clip(row_at + step_row, 0, mesh_rows - 1)
    source_col = jnp.clip(col_at + step_col, 0, mesh_cols - 1)
    source = (source_row * mesh_cols + source_col) * NB + local
    return jnp.stack([target, source]).astype(jnp.int32)


def block_levels(own_key, dims, shards, least, top_value):
    gain, own = 1.0, jax.random.fold_in(own_key, 6)
    for position, shards_of in shards:
        heights = jnp.exp(jax.random.uniform(jax.random.fold_in(own, position), (shards_of,), jnp.float32, least / len(shards), top_value / len(shards)))
        gain = gain * jnp.repeat(heights, dims[position] // shards_of).reshape([-1 if axis == position else 1 for axis in range(len(dims))])
    return gain


def scatter_about(key, extent, scale, reach, pieces=(), held_as=jnp.bfloat16):
    loudness = block_levels(key, extent, pieces, -0.22, 0.18) if pieces else 1.0
    values = jax.random.normal(key, extent, jnp.float32) * scale * loudness
    return jnp.minimum(jnp.maximum(values, -reach), reach).astype(held_as)


def setup_inputs(seed: int = 0) -> dict:
    seeds = jax.random.split(jax.random.key(seed), 9)
    charges = scatter_about(seeds[0], (PANELS,), 1.0, 6.0, ((0, 32),))
    panel_order = draw_panel_order(jax.random.fold_in(seeds[8], 71), 0)
    patch_anchor = draw_patch_anchor(jax.random.fold_in(seeds[8], 71), 0)
    project = scatter_about(seeds[3], (BLOCKS, PTS * BLK), BLK ** -0.5, 0.75, ((0, 32),))
    interpolate = scatter_about(seeds[4], (BLOCKS, BLK * PTS), PTS ** -0.5, 0.75, ((0, 32),))
    kernel_spectrum = jnp.clip(jnp.exp(math.log(8.0) - 2.7725887 * jax.random.uniform(seeds[5], (P_SIZE, P_SIZE, P_SIZE), jnp.float32) ** block_levels(seeds[5], (P_SIZE, P_SIZE, P_SIZE), ((0, 8), (1, 4)), -0.2, 0.2)), 0.5, 8.0)
    near_pairs = draw_near_pairs(jax.random.fold_in(seeds[8], 71), 0)
    near_blocks = scatter_about(seeds[7], (PAIRS, BLK * BLK), BLK ** -0.5, 0.75, ((0, 32),))
    return dict(charges=charges, panel_order=panel_order, patch_anchor=patch_anchor, project=project, interpolate=interpolate, kernel_spectrum=kernel_spectrum, near_pairs=near_pairs, near_blocks=near_blocks)


def cas_table(rows, cols):
    first = jnp.arange(rows, dtype=jnp.int32)[:, None]
    second = jnp.arange(cols, dtype=jnp.int32)[None, :]
    phase = (first * second % P_SIZE).astype(jnp.float32) * (2.0 * math.pi / P_SIZE)
    return (jnp.cos(phase) + jnp.sin(phase)) / math.sqrt(P_SIZE)

def block_products(mats, vecs, rows_out):
    count = mats.shape[0] // NB
    cols_in = vecs.shape[1]

    def single(pair):
        shaped = pair[0].reshape(NB, rows_out, cols_in).astype(jnp.float32)
        return jnp.einsum('bij,bj->bi', shaped, pair[1].astype(jnp.float32))
    stacked = lax.map(single, (mats.reshape(count, NB, mats.shape[1]), vecs.reshape(count, NB, cols_in)))
    return stacked.reshape(mats.shape[0], rows_out)

def reference(charges, panel_order, patch_anchor, project, interpolate, kernel_spectrum, near_pairs, near_blocks):
    slots = jnp.arange(PANELS, dtype=jnp.int32)
    global_order = slots // (NB * BLK) * (NB * BLK) + panel_order
    block_charges = charges[global_order].reshape(BLOCKS, BLK)
    patch = block_products(project, block_charges, PTS)
    points = jnp.arange(PTS, dtype=jnp.int32)
    xs = patch_anchor[0][:, None] + (points // 16)[None, :]
    ys = patch_anchor[1][:, None] + (points // 4 % 4)[None, :]
    zs = patch_anchor[2][:, None] + (points % 4)[None, :]
    grid = jnp.zeros((G, G, G), jnp.float32).at[xs, ys, zs].add(patch)
    forward = cas_table(G, P_SIZE)
    backward = cas_table(P_SIZE, G)
    highest = lax.Precision.HIGHEST
    spec = jnp.einsum('xyz,zf->xyf', grid, forward, precision=highest)
    spec = jnp.einsum('xyf,yg->xgf', spec, forward, precision=highest)
    spec = jnp.einsum('xgf,xh->hgf', spec, forward, precision=highest)
    spec = spec * jnp.transpose(kernel_spectrum, (2, 0, 1))
    field = jnp.einsum('hgf,hx->xgf', spec, backward, precision=highest)
    field = jnp.einsum('xgf,gy->xyf', field, backward, precision=highest)
    field = jnp.einsum('xyf,fz->xyz', field, backward, precision=highest)
    values = field[xs, ys, zs].astype(jnp.bfloat16)
    far = block_products(interpolate, values, BLK)
    near_terms = block_products(near_blocks, block_charges[near_pairs[1]], BLK)
    near = jnp.zeros((BLOCKS, BLK), jnp.float32).at[near_pairs[0]].add(near_terms)
    return jnp.zeros((PANELS,), jnp.float32).at[global_order].set((far + near).reshape(PANELS))
```

```python
import functools

import jax
import jax.numpy as jnp
import ml_dtypes
import numpy as np
from jax import lax
from jax.experimental import pallas as pl
from jax.experimental.pallas import tpu as pltpu
from jax.sharding import PartitionSpec as P

G = 256
P_SIZE = 512
BLK = 64
PTS = 64
LANES = 128
GROUP = LANES // 4
HALVES = G // LANES
SLABS = 4
PIECE = G // SLABS
SLAB = PIECE + 8
ZC = 16
MB = 1 << 20
NT = (((1,), (1,)), ((), ()))


def cas_table():
    index = np.arange(P_SIZE, dtype=np.int64)
    phase = (index[:, None] * index[None, :] % P_SIZE).astype(np.float64) * (2.0 * np.pi / P_SIZE)
    return ((np.cos(phase) + np.sin(phase)) / np.sqrt(P_SIZE)).astype(ml_dtypes.bfloat16)


CAS = cas_table()


def dot(a, b):
    return jnp.dot(a, b, preferred_element_type=jnp.float32)


def dot_nt(a, b):
    return lax.dot_general(a, b, NT, preferred_element_type=jnp.float32)


def iota(shape, dim):
    return lax.broadcasted_iota(jnp.int32, shape, dim)


def split(value):
    high = value.astype(jnp.bfloat16)
    return high, (value - high.astype(jnp.float32)).astype(jnp.bfloat16)


def lane_gather(table, index):
    return jnp.take_along_axis(table, index, axis=1, mode="promise_in_bounds")


def block_sums(mats, vecs):
    rows = vecs.shape[0]
    pair = jnp.concatenate([vecs, vecs], axis=1)
    total = jnp.zeros((2 * rows, LANES), jnp.float32)
    for t in range(mats.shape[1] // 256):
        high, low = split(mats[:, 256 * t : 256 * t + 256].astype(jnp.float32) * pair)
        owner = iota((256, LANES), 0) // BLK + 4 * t
        table = (owner == iota((256, LANES), 1) % BLK).astype(jnp.bfloat16)
        total = total + dot(jnp.concatenate([high, low], axis=0), table)
    return total[:rows] + total[rows:]


def patch_places(blocks):
    lanes = [
        (iota((blocks, 4 * blocks), 1) == 4 * iota((blocks, 4 * blocks), 0) + i).astype(
            jnp.bfloat16
        )
        for i in range(4)
    ]
    row = iota((16, LANES), 0)
    rows = [
        (iota((16, LANES), 1) % PTS == 16 * i + 4 * (row % 4) + row // 4).astype(jnp.bfloat16)
        for i in range(4)
    ]
    return rows, lanes


def project_kernel(charges, order, project, out, table):
    blocks = order.shape[0]
    table[...] = charges[...].astype(jnp.float32)
    upper = order[...] // LANES
    lower = order[...] % LANES

    def step(u, acc):
        row = jnp.broadcast_to(table[pl.ds(u, 1), :], lower.shape)
        return jnp.where(upper == u, lane_gather(row, lower), acc)

    twice = lax.fori_loop(0, table.shape[0], step, jnp.zeros(lower.shape, jnp.float32), unroll=4)
    out[:blocks] = twice.astype(jnp.bfloat16)
    patch = block_sums(project, twice)
    patch = jnp.where(iota(patch.shape, 1) < PTS, patch, 0.0)
    rows, lanes = patch_places(blocks)
    start = blocks
    for part in split(patch):
        spread = jnp.zeros((16, 4 * blocks), jnp.float32)
        for i in range(4):
            turned = dot_nt(rows[i], part).astype(jnp.bfloat16)
            spread = spread + dot(turned, lanes[i])
        for t in range(blocks // GROUP):
            out[start : start + 16] = spread[:, LANES * t : LANES * t + LANES].astype(jnp.bfloat16)
            start += 16


def inverse_kernel(order, out):
    rows = order.shape[0]

    def step(r, acc):
        here = order[pl.ds(r, 1), :]
        upper = iota((rows, LANES), 0) == here // LANES
        lower = iota((LANES, LANES), 0) == here % LANES
        values = jnp.concatenate(
            [
                jnp.where(upper, r.astype(jnp.float32), 0.0),
                jnp.where(upper, iota((rows, LANES), 1).astype(jnp.float32), 0.0),
            ],
            axis=0,
        )
        return acc + dot_nt(
            values.astype(jnp.bfloat16), lower.astype(jnp.float32).astype(jnp.bfloat16)
        )

    out[...] = lax.fori_loop(
        0, rows, step, jnp.zeros((2 * rows, LANES), jnp.float32), unroll=4
    ).astype(jnp.int32)


def near_kernel(source, near_blocks, target, charges, out, table, picked):
    step = pl.program_id(0)
    pairs = picked.shape[0]
    blocks = out.shape[0]

    @pl.when(step == 0)
    def _():
        for d in range(charges.shape[0]):
            table[d * blocks : (d + 1) * blocks] = charges[d].astype(jnp.float32)
        out[...] = jnp.zeros_like(out)

    def pick(p, carry):
        picked[pl.ds(p, 1), :] = table[pl.ds(source[step * pairs + p], 1), :]
        return carry

    lax.fori_loop(0, pairs, pick, 0, unroll=8)
    terms = block_sums(near_blocks, picked[...])
    owner = (iota((blocks, pairs), 0) == target[...]).astype(jnp.float32).astype(jnp.bfloat16)
    high, low = split(terms)
    out[...] += dot(owner, high) + dot(owner, low)


def lane_spot(first, half, lane):
    return ((lane - (first - half * LANES)) & -4) == 0


def tile_loop(half, rows, cols, groups, body):
    per_slab = cols // SLABS
    low = jnp.maximum(half * (rows // HALVES) - 1, 0)
    high = (half + 1) * (rows // HALVES)
    per_row = per_slab * groups

    def step(n, carry):
        row = low + n // per_row
        left = n % per_row
        devices = [row * cols + s * per_slab + left // groups for s in range(SLABS)]
        body(devices, left % groups)
        return carry

    lax.fori_loop(0, (high - low) * per_row, step, 0)


def scatter_kernel(cols, first, place, patches, table, out, columns, *slabs):
    half = pl.program_id(0)
    chunk = pl.program_id(1)
    devices, held, _ = patches.shape
    groups = held // (GROUP + 32)
    blocks = groups * GROUP
    freqs = table.shape[0]
    lane = iota((8, LANES), 1)
    sub = iota((8, LANES), 0)

    @pl.when((half == 0) & (chunk == 0))
    def _():
        def clear(n, carry):
            for slab in slabs:
                slab[pl.ds(pl.multiple_of(n * SLAB, 8), SLAB), :] = jnp.zeros(
                    (SLAB, LANES), jnp.float32
                )
            return carry

        lax.fori_loop(0, G, clear, 0)

    @pl.when(chunk == 0)
    def _():
        def tile(numbers, t):
            values = []
            for d in numbers:
                at = pl.multiple_of(blocks + 16 * t, 16)
                high = patches[d, pl.ds(at, 16), :].astype(jnp.float32)
                at = pl.multiple_of(blocks + 16 * groups + 16 * t, 16)
                both = high + patches[d, pl.ds(at, 16), :].astype(jnp.float32)
                values.append((both[:8], both[8:]))

            def one(k, carry):
                sums = []
                for s in range(SLABS):
                    b = numbers[s] * blocks + t * GROUP + k
                    spot = lane_spot(first[b], half, lane)
                    spots = (spot & (sub < 4), spot & (sub >= 4))
                    shift = (first[b] - 4 * k) & (LANES - 1)
                    for l in range(4):
                        if l % 2 == 0:
                            moved = pltpu.roll(values[s][l // 2], shift, 1)
                        at = place[b] + (l * SLAB - 4 * (l % 2))
                        new = jnp.where(spots[l % 2], moved, 0.0)
                        sums.append((s, at, slabs[s][pl.ds(at, 8), :] + new))
                for s, at, new in sums:
                    slabs[s][pl.ds(at, 8), :] = new
                return carry

            lax.fori_loop(0, GROUP, one, 0, unroll=4)

        tile_loop(half, devices // cols, cols, groups, tile)

    for z in range(0, ZC, 2):
        pair = []
        for plane in (z, z + 1):
            at = pl.multiple_of((chunk * ZC + plane) * SLAB, 8)
            parts = []
            for s in range(SLABS):
                part = slabs[s][pl.ds(at, PIECE), :]
                if s > 0:
                    over = slabs[s - 1][pl.ds(at + PIECE, 8), :]
                    part = jnp.concatenate([part[:8] + over, part[8:]], axis=0)
                parts.append(part.astype(jnp.bfloat16))
            for slab in slabs:
                slab[pl.ds(at, SLAB), :] = jnp.zeros((SLAB, LANES), jnp.float32)
            pair.append(jnp.concatenate(parts, axis=0))
        lines = dot(table[...], jnp.concatenate(pair, axis=1))
        columns[pl.ds(z, freqs, stride=ZC), :] = lines[:, :LANES]
        columns[pl.ds(z + 1, freqs, stride=ZC), :] = lines[:, LANES:]
    out[...] = columns[...].reshape(freqs, ZC, LANES).astype(jnp.bfloat16)


def spectrum_kernel(lines, weights, third, third_back, first, first_back, out):
    for g in range(lines.shape[0]):
        v = dot(third[...], lines[g]).astype(jnp.bfloat16)
        s = (dot(v, first[...]) * weights[g]).astype(jnp.bfloat16)
        v = dot(s, first_back[...]).astype(jnp.bfloat16)
        out[g] = dot(third_back[...], v).astype(jnp.bfloat16)


def sample_kernel(cols, first, place, lines, table, out, columns, cells):
    half = pl.program_id(0)
    chunk = pl.program_id(1)
    devices, held, _ = out.shape
    groups = held // 16
    blocks = groups * GROUP
    freqs = table.shape[1]
    lane = iota((8, LANES), 1)
    sub = iota((8, LANES), 0)
    columns[...] = lines[...].astype(jnp.float32).reshape(freqs * ZC, LANES)
    for z in range(0, ZC, 2):
        pair = [
            columns[pl.ds(plane, freqs, stride=ZC), :].astype(jnp.bfloat16) for plane in (z, z + 1)
        ]
        field = dot(table[...], jnp.concatenate(pair, axis=1))
        at = pl.multiple_of((chunk * ZC + z) * G, 8)
        cells[pl.ds(at, G), :] = field[:, :LANES]
        cells[pl.ds(at + G, G), :] = field[:, LANES:]

    @pl.when((half == 0) & (chunk == 0))
    def _():
        out[...] = jnp.zeros_like(out)

    @pl.when(chunk == pl.num_programs(1) - 1)
    def _():
        def tile(numbers, t):
            def one(k, sums):
                sums = list(sums)
                for s in range(SLABS):
                    b = numbers[s] * blocks + t * GROUP + k
                    spot = lane_spot(first[b], half, lane)
                    spots = (spot & (sub < 4), spot & (sub >= 4))
                    shift = (4 * k - first[b]) & (LANES - 1)
                    for v in range(2):
                        even = cells[pl.ds(place[b] + 2 * v * G, 8), :]
                        odd = cells[pl.ds(place[b] + ((2 * v + 1) * G - 4), 8), :]
                        here = jnp.where(spots[0], even, jnp.where(spots[1], odd, 0.0))
                        sums[2 * s + v] = sums[2 * s + v] + pltpu.roll(here, shift, 1)
                return tuple(sums)

            zero = jnp.zeros((8, LANES), jnp.float32)
            sums = lax.fori_loop(0, GROUP, one, (zero,) * (2 * SLABS), unroll=4)
            at = pl.multiple_of(16 * t, 16)
            for s in range(SLABS):
                out[numbers[s], pl.ds(at, 16), :] += jnp.concatenate(
                    [sums[2 * s], sums[2 * s + 1]], axis=0
                )

        tile_loop(half, devices // cols, cols, groups, tile)


def finish_kernel(values, interpolate, near, inverse, out, total):
    blocks = near.shape[0]
    groups = values.shape[0] // 16
    rows, lanes = patch_places(blocks)
    spread = jnp.concatenate([values[16 * t : 16 * t + 16] for t in range(groups)], axis=1)
    patch = jnp.zeros((blocks, LANES), jnp.float32)
    for part in split(spread):
        for i in range(4):
            turned = dot_nt(lanes[i], part).astype(jnp.bfloat16)
            patch = patch + dot(turned, rows[i])
    total[...] = block_sums(interpolate, patch) + near[...]
    count = out.shape[0]
    even = total[pl.ds(0, count, stride=2), :]
    odd = total[pl.ds(1, count, stride=2), :]
    total[:count] = jnp.where(iota(even.shape, 1) < BLK, even, odd)
    upper = inverse[:count]
    lower = inverse[count:]

    def step(u, acc):
        row = jnp.broadcast_to(total[pl.ds(u, 1), :], lower.shape)
        return jnp.where(upper == u, lane_gather(row, lower), acc)

    out[...] = lax.fori_loop(0, count, step, jnp.zeros(out.shape, jnp.float32), unroll=4)


def struct(shape, dtype):
    return jax.ShapeDtypeStruct(shape, dtype)


def whole(shape):
    return pl.BlockSpec(shape, lambda *_: (0,) * len(shape))


def params(mib):
    return pltpu.CompilerParams(vmem_limit_bytes=mib * MB)


def body(
    charges,
    panel_order,
    patch_anchor,
    project,
    interpolate,
    kernel_spectrum,
    near_pairs,
    near_blocks,
):
    axes = ("row", "col")
    rows = lax.axis_size("row")
    cols = lax.axis_size("col")
    devices = rows * cols
    row_at = lax.axis_index("row")
    col_at = lax.axis_index("col")
    blocks = project.shape[0]
    groups = blocks // GROUP
    panels = charges.shape[0]
    strips = panels // LANES
    gs, fs, _ = kernel_spectrum.shape

    anchors = lax.all_gather(patch_anchor, axes)
    order = panel_order.reshape(blocks, BLK)
    sent = pl.pallas_call(
        project_kernel,
        out_shape=struct((blocks + 32 * groups, LANES), jnp.bfloat16),
        scratch_shapes=[pltpu.VMEM((strips, LANES), jnp.float32)],
        compiler_params=params(32),
        name="project",
    )(charges.reshape(strips, LANES), jnp.concatenate([order, order], axis=1), project)
    gathered = lax.all_gather(sent, axes)
    inverse = pl.pallas_call(
        inverse_kernel,
        out_shape=struct((2 * strips, LANES), jnp.int32),
        compiler_params=params(32),
        name="inverse",
    )(panel_order.reshape(strips, LANES))

    first = anchors[:, 0].reshape(devices * blocks)
    piece = (jnp.arange(devices, dtype=jnp.int32) % cols * SLABS // cols * PIECE)[:, None]
    slab_place = (anchors[:, 2] * SLAB + anchors[:, 1] - piece).reshape(devices * blocks)
    cell_place = (anchors[:, 2] * G + anchors[:, 1]).reshape(devices * blocks)

    table = jnp.asarray(CAS)
    second = lax.dynamic_slice_in_dim(table[:, :G], row_at * gs, gs, axis=0)
    third = lax.dynamic_slice_in_dim(table[:, :G], col_at * fs, fs, axis=0)
    chunks = G // ZC
    smem = pl.BlockSpec(memory_space=pltpu.SMEM)
    line_block = pl.BlockSpec((gs, ZC, LANES), lambda h, z: (0, z, h))
    lines = pl.pallas_call(
        functools.partial(scatter_kernel, cols),
        grid=(HALVES, chunks),
        in_specs=[smem, smem, whole(gathered.shape), whole(second.shape)],
        out_specs=line_block,
        out_shape=struct((gs, G, G), jnp.bfloat16),
        scratch_shapes=[pltpu.VMEM((gs * ZC, LANES), jnp.float32)]
        + [pltpu.VMEM((G * SLAB, LANES), jnp.float32)] * SLABS,
        compiler_params=params(56),
        name="scatter",
    )(first, slab_place, gathered, second)

    batch = 4
    part = lambda shape: pl.BlockSpec((batch,) + shape, lambda n: (n, 0, 0))
    lines = pl.pallas_call(
        spectrum_kernel,
        grid=(gs // batch,),
        in_specs=[
            part((G, G)),
            part((fs, P_SIZE)),
            whole((fs, G)),
            whole((G, fs)),
            whole((G, P_SIZE)),
            whole((P_SIZE, G)),
        ],
        out_specs=part((G, G)),
        out_shape=struct((gs, G, G), jnp.bfloat16),
        compiler_params=params(48),
        name="spectrum",
    )(lines, kernel_spectrum, third, third.T, table[:G], table[:, :G])

    values = pl.pallas_call(
        functools.partial(sample_kernel, cols),
        grid=(HALVES, chunks),
        in_specs=[smem, smem, line_block, whole((G, gs))],
        out_specs=whole((devices, 16 * groups, LANES)),
        out_shape=struct((devices, 16 * groups, LANES), jnp.float32),
        scratch_shapes=[
            pltpu.VMEM((gs * ZC, LANES), jnp.float32),
            pltpu.VMEM((G * G + 8, LANES), jnp.float32),
        ],
        compiler_params=params(56),
        name="sample",
    )(first, cell_place, lines, second.T)
    values = lax.psum_scatter(
        values.reshape(devices * 16 * groups, LANES), axes, scatter_dimension=0, tiled=True
    )

    pairs = near_blocks.shape[0]
    target = near_pairs[0] - (row_at * cols + col_at) * blocks
    near = pl.pallas_call(
        near_kernel,
        grid=(pairs // blocks,),
        in_specs=[
            smem,
            pl.BlockSpec((blocks, BLK * BLK), lambda n: (n, 0)),
            pl.BlockSpec((1, blocks), lambda n: (0, n)),
            whole((devices, blocks, LANES)),
        ],
        out_specs=whole((blocks, LANES)),
        out_shape=struct((blocks, LANES), jnp.float32),
        scratch_shapes=[
            pltpu.VMEM((devices * blocks, LANES), jnp.float32),
            pltpu.VMEM((blocks, LANES), jnp.float32),
        ],
        compiler_params=params(48),
        name="near",
    )(near_pairs[1], near_blocks, target.reshape(1, pairs), gathered)

    result = pl.pallas_call(
        finish_kernel,
        out_shape=struct((strips, LANES), jnp.float32),
        scratch_shapes=[pltpu.VMEM((blocks, LANES), jnp.float32)],
        compiler_params=params(32),
        name="finish",
    )(values, interpolate, near, inverse)
    return result.reshape(panels)


def solution(mesh):
    placed = (
        P(("row", "col")),
        P(("row", "col")),
        P(None, ("row", "col")),
        P(("row", "col"), None),
        P(("row", "col"), None),
        P("row", "col", None),
        P(None, ("row", "col")),
        P(("row", "col"), None),
    )
    return jax.shard_map(
        body, mesh=mesh, in_specs=placed, out_specs=P(("row", "col")), check_vma=False
    )
```

```python
import functools

import jax
import jax.numpy as jnp
import ml_dtypes
import numpy as np
from jax import lax
from jax.experimental import pallas as pl
from jax.experimental.pallas import tpu as pltpu
from jax.sharding import PartitionSpec as P

G = 256
P_SIZE = 512
BLK = 64
PTS = 64
LANES = 128
GROUP = LANES // 4
HALVES = G // LANES
SLABS = 4
PIECE = G // SLABS
SLAB = PIECE + 8
ZC = 16
MB = 1 << 20
NT = (((1,), (1,)), ((), ()))


def cas_table():
    index = np.arange(P_SIZE, dtype=np.int64)
    phase = (index[:, None] * index[None, :] % P_SIZE).astype(np.float64) * (2.0 * np.pi / P_SIZE)
    return ((np.cos(phase) + np.sin(phase)) / np.sqrt(P_SIZE)).astype(ml_dtypes.bfloat16)


CAS = cas_table()


def dot(a, b):
    return jnp.dot(a, b, preferred_element_type=jnp.float32)


def dot_nt(a, b):
    return lax.dot_general(a, b, NT, preferred_element_type=jnp.float32)


def iota(shape, dim):
    return lax.broadcasted_iota(jnp.int32, shape, dim)


def split(value):
    high = value.astype(jnp.bfloat16)
    return high, (value - high.astype(jnp.float32)).astype(jnp.bfloat16)


def lane_gather(table, index):
    return jnp.take_along_axis(table, index, axis=1, mode="promise_in_bounds")


def block_sums(mats, vecs):
    rows = vecs.shape[0]
    pair = jnp.concatenate([vecs, vecs], axis=1)
    total = jnp.zeros((2 * rows, LANES), jnp.float32)
    for t in range(mats.shape[1] // 256):
        high, low = split(mats[:, 256 * t : 256 * t + 256].astype(jnp.float32) * pair)
        owner = iota((256, LANES), 0) // BLK + 4 * t
        table = (owner == iota((256, LANES), 1) % BLK).astype(jnp.bfloat16)
        total = total + dot(jnp.concatenate([high, low], axis=0), table)
    return total[:rows] + total[rows:]


def patch_places(blocks):
    lanes = [
        (iota((blocks, 4 * blocks), 1) == 4 * iota((blocks, 4 * blocks), 0) + i).astype(
            jnp.bfloat16
        )
        for i in range(4)
    ]
    row = iota((16, LANES), 0)
    rows = [
        (iota((16, LANES), 1) % PTS == 16 * i + 4 * (row % 4) + row // 4).astype(jnp.bfloat16)
        for i in range(4)
    ]
    return rows, lanes


def project_kernel(charges, order, project, anchors, charge_out, patch_out, table):
    blocks = order.shape[0]
    groups = blocks // GROUP
    table[...] = charges[...].astype(jnp.float32)
    upper = order[...] // LANES
    lower = order[...] % LANES

    def step(u, acc):
        row = jnp.broadcast_to(table[pl.ds(u, 1), :], lower.shape)
        return jnp.where(upper == u, lane_gather(row, lower), acc)

    twice = lax.fori_loop(0, table.shape[0], step, jnp.zeros(lower.shape, jnp.float32), unroll=4)
    charge_out[...] = twice.astype(jnp.bfloat16)
    patch = block_sums(project, twice)
    patch = jnp.where(iota(patch.shape, 1) < PTS, patch, 0.0).astype(jnp.bfloat16)
    rows, lanes = patch_places(blocks)
    corner = anchors[...].astype(jnp.float32)
    spread = jnp.zeros((16, 4 * blocks), jnp.float32)
    cells = (iota((8, 4 * blocks), 1) % 4).astype(jnp.float32)
    start = jnp.broadcast_to(corner[:1], (8, blocks)).astype(jnp.bfloat16)
    for i in range(4):
        spread = spread + dot(dot_nt(rows[i], patch).astype(jnp.bfloat16), lanes[i])
        cells = cells + dot(start, lanes[i])
    tiles = [slice(LANES * t, LANES * t + LANES) for t in range(groups)]
    for t in range(groups):
        patch_out[16 * t : 16 * t + 16] = spread[:, tiles[t]].astype(jnp.bfloat16)
    extra = [cells[:1, tile] for tile in tiles] + [corner]
    extra.append(jnp.zeros((16 - groups - corner.shape[0], LANES), jnp.float32))
    patch_out[16 * groups :] = jnp.concatenate(extra, axis=0).astype(jnp.bfloat16)


def inverse_kernel(order, out):
    rows = order.shape[0]

    def step(r, acc):
        here = order[pl.ds(r, 1), :]
        upper = iota((rows, LANES), 0) == here // LANES
        lower = iota((LANES, LANES), 0) == here % LANES
        values = jnp.concatenate(
            [
                jnp.where(upper, r.astype(jnp.float32), 0.0),
                jnp.where(upper, iota((rows, LANES), 1).astype(jnp.float32), 0.0),
            ],
            axis=0,
        )
        return acc + dot_nt(
            values.astype(jnp.bfloat16), lower.astype(jnp.float32).astype(jnp.bfloat16)
        )

    out[...] = lax.fori_loop(
        0, rows, step, jnp.zeros((2 * rows, LANES), jnp.float32), unroll=4
    ).astype(jnp.int32)


def near_kernel(source, near_blocks, target, charges, out, table, picked):
    step = pl.program_id(0)
    pairs = picked.shape[0]
    blocks = out.shape[0]

    @pl.when(step == 0)
    def _():
        for d in range(charges.shape[0]):
            table[d * blocks : (d + 1) * blocks] = charges[d].astype(jnp.float32)
        out[...] = jnp.zeros_like(out)

    def pick(p, carry):
        picked[pl.ds(p, 1), :] = table[pl.ds(source[step * pairs + p], 1), :]
        return carry

    lax.fori_loop(0, pairs, pick, 0, unroll=8)
    terms = block_sums(near_blocks, picked[...])
    owner = (iota((blocks, pairs), 0) == target[...]).astype(jnp.float32).astype(jnp.bfloat16)
    high, low = split(terms)
    out[...] += dot(owner, high) + dot(owner, low)


def tile_loop(half, rows, cols, groups, body):
    per_slab = cols // SLABS
    low = jnp.maximum(half * (rows // HALVES) - 1, 0)
    high = (half + 1) * (rows // HALVES)
    per_row = per_slab * groups

    def step(n, carry):
        row = low + n // per_row
        left = n % per_row
        devices = [row * cols + s * per_slab + left // groups for s in range(SLABS)]
        body(devices, left % groups)
        return carry

    lax.fori_loop(0, (high - low) * per_row, step, 0)


def tile_cells(patches, d, t, groups):
    extra = patches[d, 16 * groups :, :].astype(jnp.float32)
    picked = jnp.where(iota(extra.shape, 0) == t, extra, 0.0)
    return jnp.broadcast_to(jnp.sum(picked, axis=0, keepdims=True), (8, LANES))


def scatter_kernel(cols, place, shift, second, third, patches, table, out, columns, *slabs):
    half = place[0]
    chunk = pl.program_id(0)
    devices, held, _ = patches.shape
    groups = (held - 16) // 16
    blocks = groups * GROUP
    freqs = table.shape[0]
    quad = iota((8, LANES), 1) // 4

    @pl.when(chunk == 0)
    def _():
        def clear(n, carry):
            for slab in slabs:
                slab[n] = jnp.zeros((SLAB, LANES), jnp.float32)
            return carry

        lax.fori_loop(0, G, clear, 0)

        def tile(numbers, t):
            values = []
            for d in numbers:
                both = patches[d, pl.ds(pl.multiple_of(16 * t, 16), 16), :].astype(jnp.float32)
                cells = tile_cells(patches, d, t, groups) - (half * LANES).astype(jnp.float32)
                inside = (cells >= 0.0) & (cells < LANES) & (iota((8, LANES), 0) < 4)
                planes = [jnp.concatenate([both[4 * l : 4 * l + 4]] * 2, axis=0) for l in range(4)]
                values.append([jnp.where(inside, plane, 0.0) for plane in planes])

            def one(k, carry):
                spot = quad == k
                sums = []
                for s in range(SLABS):
                    b = numbers[s] * blocks + t * GROUP + k
                    amount = shift[b]
                    at = (pl.ds(third[b], 4), pl.ds(second[b], 8))
                    new = [
                        pltpu.roll(jnp.where(spot, plane, 0.0), amount, 1) for plane in values[s]
                    ]
                    sums.append((at, slabs[s][at[0], at[1], :] + jnp.stack(new)))
                for s, (at, new) in enumerate(sums):
                    slabs[s][at[0], at[1], :] = new
                return carry

            lax.fori_loop(0, GROUP, one, 0, unroll=4)

        tile_loop(half, devices // cols, cols, groups, tile)

    for z in range(0, ZC, 2):
        pair = []
        for plane in (z, z + 1):
            at = chunk * ZC + plane
            parts = []
            for s in range(SLABS):
                part = slabs[s][at, :PIECE, :]
                if s > 0:
                    over = slabs[s - 1][at, PIECE:, :]
                    part = jnp.concatenate([part[:8] + over, part[8:]], axis=0)
                parts.append(part.astype(jnp.bfloat16))
            pair.append(jnp.concatenate(parts, axis=0))
        lines = dot(table[...], jnp.concatenate(pair, axis=1))
        columns[pl.ds(z, freqs, stride=ZC), :] = lines[:, :LANES]
        columns[pl.ds(z + 1, freqs, stride=ZC), :] = lines[:, LANES:]
    out[...] = columns[...].reshape(freqs, ZC, LANES).astype(jnp.bfloat16)


def spectrum_kernel(
    own, other, weights, third, third_back, first, first_back, own_out, other_out, held
):
    count, freqs, _ = weights.shape
    for g in range(count):
        line = jnp.concatenate([own[g], other[g]], axis=1)
        held[g * freqs : (g + 1) * freqs] = dot(third[...], line).astype(jnp.bfloat16)
    s = dot(held[...], first[...]) * weights[...].reshape(count * freqs, P_SIZE)
    held[...] = dot(s.astype(jnp.bfloat16), first_back[...]).astype(jnp.bfloat16)
    for g in range(count):
        line = dot(third_back[...], held[g * freqs : (g + 1) * freqs]).astype(jnp.bfloat16)
        own_out[g] = line[:, :LANES]
        other_out[g] = line[:, LANES:]


def sample_kernel(
    cols, place, shift, second, third, patches, own, other, table, out, columns, cells
):
    half = place[0]
    chunk = pl.program_id(0)
    devices, held, _ = out.shape
    groups = held // 16
    blocks = groups * GROUP
    freqs = table.shape[1]
    quad = iota((8, LANES), 1) // 4
    both = own[...].astype(jnp.float32) + other[...].astype(jnp.float32)
    columns[...] = both.reshape(freqs * ZC, LANES)
    for z in range(0, ZC, 2):
        pair = [
            columns[pl.ds(plane, freqs, stride=ZC), :].astype(jnp.bfloat16) for plane in (z, z + 1)
        ]
        field = dot(table[...], jnp.concatenate(pair, axis=1))
        cells[chunk * ZC + z, :G, :] = field[:, :LANES]
        cells[chunk * ZC + z + 1, :G, :] = field[:, LANES:]

    @pl.when(chunk == pl.num_programs(0) - 1)
    def _():
        out[...] = jnp.zeros_like(out)

        def tile(numbers, t):
            def one(k, sums):
                spot = quad == k
                sums = list(sums)
                for s in range(SLABS):
                    b = numbers[s] * blocks + t * GROUP + k
                    amount = shift[b]
                    here = cells[pl.ds(third[b], 4), pl.ds(second[b], 8), :]
                    for l in range(4):
                        moved = pltpu.roll(here[l], amount, 1)
                        sums[4 * s + l] = jnp.where(spot, moved, sums[4 * s + l])
                return tuple(sums)

            zero = jnp.zeros((8, LANES), jnp.float32)
            sums = lax.fori_loop(0, GROUP, one, (zero,) * (4 * SLABS), unroll=4)
            at = pl.multiple_of(16 * t, 16)
            for s in range(SLABS):
                first = tile_cells(patches, numbers[s], t, groups)
                first = first - (half * LANES).astype(jnp.float32)
                inside = (first >= 0.0) & (first < LANES)
                planes = [jnp.where(inside, sums[4 * s + l], 0.0)[:4] for l in range(4)]
                out[numbers[s], pl.ds(at, 16), :] = jnp.concatenate(planes, axis=0).astype(
                    jnp.bfloat16
                )

        tile_loop(half, devices // cols, cols, groups, tile)


def finish_kernel(values, interpolate, near, inverse, out, total):
    blocks = near.shape[0]
    groups = values.shape[1] // 16
    rows, lanes = patch_places(blocks)
    summed = values[0].astype(jnp.float32)
    for d in range(1, values.shape[0]):
        summed = summed + values[d].astype(jnp.float32)
    spread = jnp.concatenate([summed[16 * t : 16 * t + 16] for t in range(groups)], axis=1)
    patch = jnp.zeros((blocks, LANES), jnp.float32)
    for part in split(spread):
        for i in range(4):
            turned = dot_nt(lanes[i], part).astype(jnp.bfloat16)
            patch = patch + dot(turned, rows[i])
    total[...] = block_sums(interpolate, patch) + near[...]
    count = out.shape[0]
    even = total[pl.ds(0, count, stride=2), :]
    odd = total[pl.ds(1, count, stride=2), :]
    total[:count] = jnp.where(iota(even.shape, 1) < BLK, even, odd)
    upper = inverse[:count]
    lower = inverse[count:]

    def step(u, acc):
        row = jnp.broadcast_to(total[pl.ds(u, 1), :], lower.shape)
        return jnp.where(upper == u, lane_gather(row, lower), acc)

    out[...] = lax.fori_loop(0, count, step, jnp.zeros(out.shape, jnp.float32), unroll=4)


def struct(shape, dtype):
    return jax.ShapeDtypeStruct(shape, dtype)


def whole(shape):
    return pl.BlockSpec(shape, lambda *_: (0,) * len(shape))


def params(mib):
    return pltpu.CompilerParams(vmem_limit_bytes=mib * MB)


def neighbourhood(array):
    array = array[None, None]
    for axis, dim in (("row", 0), ("col", 1)):
        count = lax.axis_size(axis)
        up = [(i, i + 1) for i in range(count - 1)]
        down = [(j, i) for i, j in up]
        before = lax.ppermute(array, axis, up)
        after = lax.ppermute(array, axis, down)
        array = jnp.concatenate([before, array, after], axis=dim)
    return array


def body(
    charges,
    panel_order,
    patch_anchor,
    project,
    interpolate,
    kernel_spectrum,
    near_pairs,
    near_blocks,
):
    axes = ("row", "col")
    rows = lax.axis_size("row")
    cols = lax.axis_size("col")
    devices = rows * cols
    row_at = lax.axis_index("row")
    col_at = lax.axis_index("col")
    half = col_at % HALVES
    mates = [(c, c ^ 1) for c in range(cols)]
    blocks = project.shape[0]
    groups = blocks // GROUP
    panels = charges.shape[0]
    strips = panels // LANES
    gs, fs, _ = kernel_spectrum.shape
    held = 16 * groups + 16

    order = panel_order.reshape(blocks, BLK)
    block_charges, sent = pl.pallas_call(
        project_kernel,
        out_shape=(
            struct((blocks, LANES), jnp.bfloat16),
            struct((held, LANES), jnp.bfloat16),
        ),
        scratch_shapes=[pltpu.VMEM((strips, LANES), jnp.float32)],
        compiler_params=params(32),
        name="project",
    )(
        charges.reshape(strips, LANES),
        jnp.concatenate([order, order], axis=1),
        project,
        patch_anchor,
    )
    copies = jnp.broadcast_to(sent[None], (devices, held, LANES))
    gathered = lax.all_to_all(copies, axes, split_axis=0, concat_axis=0, tiled=True)
    inverse = pl.pallas_call(
        inverse_kernel,
        out_shape=struct((2 * strips, LANES), jnp.int32),
        compiler_params=params(32),
        name="inverse",
    )(panel_order.reshape(strips, LANES))

    anchors = gathered[:, 17 * groups : 17 * groups + 3].astype(jnp.int32)
    lane = 4 * (jnp.arange(blocks, dtype=jnp.int32) % GROUP)
    forth = ((anchors[:, 0] - lane) & (LANES - 1)).reshape(devices * blocks)
    back = ((lane - anchors[:, 0]) & (LANES - 1)).reshape(devices * blocks)
    second_at = anchors[:, 1].reshape(devices * blocks)
    piece = (jnp.arange(devices, dtype=jnp.int32) % cols * SLABS // cols * PIECE)[:, None]
    slab_at = (anchors[:, 1] - piece).reshape(devices * blocks)
    third_at = anchors[:, 2].reshape(devices * blocks)
    place = half.astype(jnp.int32).reshape(1)

    table = jnp.asarray(CAS)
    second = lax.dynamic_slice_in_dim(table[:, :G], row_at * gs, gs, axis=0)
    third = lax.dynamic_slice_in_dim(table[:, :G], col_at * fs, fs, axis=0)
    mine = lax.dynamic_slice_in_dim(table, half * LANES, LANES, axis=0)
    yours = lax.dynamic_slice_in_dim(table, (1 - half) * LANES, LANES, axis=0)
    first = jnp.concatenate([mine, yours], axis=0)
    chunks = G // ZC
    smem = pl.BlockSpec(memory_space=pltpu.SMEM)
    line_block = pl.BlockSpec((gs, ZC, LANES), lambda z: (0, z, 0))
    lines_type = struct((gs, G, LANES), jnp.bfloat16)
    own = pl.pallas_call(
        functools.partial(scatter_kernel, cols),
        grid=(chunks,),
        in_specs=[smem] * 4 + [whole(gathered.shape), whole(second.shape)],
        out_specs=line_block,
        out_shape=lines_type,
        scratch_shapes=[pltpu.VMEM((gs * ZC, LANES), jnp.float32)]
        + [pltpu.VMEM((G, SLAB, LANES), jnp.float32)] * SLABS,
        compiler_params=params(56),
        name="scatter",
    )(place, forth, slab_at, third_at, gathered, second)
    other = lax.ppermute(own, "col", mates)

    batch = 8
    part = lambda shape: pl.BlockSpec((batch,) + shape, lambda n: (n, 0, 0))
    own, other = pl.pallas_call(
        spectrum_kernel,
        grid=(gs // batch,),
        in_specs=[
            part((G, LANES)),
            part((G, LANES)),
            part((fs, P_SIZE)),
            whole((fs, G)),
            whole((G, fs)),
            whole((G, P_SIZE)),
            whole((P_SIZE, G)),
        ],
        out_specs=(part((G, LANES)), part((G, LANES))),
        out_shape=(lines_type, lines_type),
        scratch_shapes=[pltpu.VMEM((batch * fs, G), jnp.bfloat16)],
        compiler_params=params(56),
        name="spectrum",
    )(own, other, kernel_spectrum, third, third.T, first, first.T)
    other = lax.ppermute(other, "col", mates)

    source = near_pairs[1]
    source_device = source // blocks
    code = (source_device // cols - row_at + 1) * 3 + (source_device % cols - col_at + 1)
    wanted = code * blocks + source % blocks
    target = near_pairs[0] - (row_at * cols + col_at) * blocks
    around = neighbourhood(block_charges).reshape(9, blocks, LANES)
    pairs = near_blocks.shape[0]
    near = pl.pallas_call(
        near_kernel,
        grid=(pairs // blocks,),
        in_specs=[
            smem,
            pl.BlockSpec((blocks, BLK * BLK), lambda n: (n, 0)),
            pl.BlockSpec((1, blocks), lambda n: (0, n)),
            whole((9, blocks, LANES)),
        ],
        out_specs=whole((blocks, LANES)),
        out_shape=struct((blocks, LANES), jnp.float32),
        scratch_shapes=[
            pltpu.VMEM((9 * blocks, LANES), jnp.float32),
            pltpu.VMEM((blocks, LANES), jnp.float32),
        ],
        compiler_params=params(48),
        name="near",
    )(wanted, near_blocks, target.reshape(1, pairs), around)

    values = pl.pallas_call(
        functools.partial(sample_kernel, cols),
        grid=(chunks,),
        in_specs=[smem] * 4 + [whole(gathered.shape), line_block, line_block, whole((G, gs))],
        out_specs=whole((devices, 16 * groups, LANES)),
        out_shape=struct((devices, 16 * groups, LANES), jnp.bfloat16),
        scratch_shapes=[
            pltpu.VMEM((gs * ZC, LANES), jnp.float32),
            pltpu.VMEM((G, G + 8, LANES), jnp.float32),
        ],
        compiler_params=params(56),
        name="sample",
    )(place, back, second_at, third_at, gathered, own, other, second.T)
    values = lax.all_to_all(values, axes, split_axis=0, concat_axis=0, tiled=True)

    result = pl.pallas_call(
        finish_kernel,
        out_shape=struct((strips, LANES), jnp.float32),
        scratch_shapes=[pltpu.VMEM((blocks, LANES), jnp.float32)],
        compiler_params=params(32),
        name="finish",
    )(values, interpolate, near, inverse)
    return result.reshape(panels)


def solution(mesh):
    placed = (
        P(("row", "col")),
        P(("row", "col")),
        P(None, ("row", "col")),
        P(("row", "col"), None),
        P(("row", "col"), None),
        P("row", "col", None),
        P(None, ("row", "col")),
        P(("row", "col"), None),
    )
    return jax.shard_map(
        body, mesh=mesh, in_specs=placed, out_specs=P(("row", "col")), check_vma=False
    )
```

```python
import functools

import jax
import jax.numpy as jnp
import ml_dtypes
import numpy as np
from jax import lax
from jax.experimental import pallas as pl
from jax.experimental.pallas import tpu as pltpu
from jax.sharding import PartitionSpec as P

G = 256
P_SIZE = 512
BLK = 64
PTS = 64
LANES = 128
GROUP = LANES // 4
HALVES = G // LANES
SLABS = 4
PIECE = G // SLABS
PAD = 8
SLAB = PIECE + 2 * PAD
ZC = 32
MB = 1 << 20
NT = (((1,), (1,)), ((), ()))


def cas_table():
    index = np.arange(P_SIZE, dtype=np.int64)
    phase = (index[:, None] * index[None, :] % P_SIZE).astype(np.float64) * (2.0 * np.pi / P_SIZE)
    return ((np.cos(phase) + np.sin(phase)) / np.sqrt(P_SIZE)).astype(ml_dtypes.bfloat16)


CAS = cas_table()


def dot(a, b):
    return jnp.dot(a, b, preferred_element_type=jnp.float32)


def dot_nt(a, b):
    return lax.dot_general(a, b, NT, preferred_element_type=jnp.float32)


def iota(shape, dim):
    return lax.broadcasted_iota(jnp.int32, shape, dim)


def split(value):
    high = value.astype(jnp.bfloat16)
    return high, (value - high.astype(jnp.float32)).astype(jnp.bfloat16)


def lane_gather(table, index):
    return jnp.take_along_axis(table, index, axis=1, mode="promise_in_bounds")


def block_sums(mats, vecs):
    rows = vecs.shape[0]
    pair = jnp.concatenate([vecs, vecs], axis=1)
    total = jnp.zeros((2 * rows, LANES), jnp.float32)
    for t in range(mats.shape[1] // 256):
        high, low = split(mats[:, 256 * t : 256 * t + 256].astype(jnp.float32) * pair)
        owner = iota((256, LANES), 0) // BLK + 4 * t
        table = (owner == iota((256, LANES), 1) % BLK).astype(jnp.bfloat16)
        total = total + dot(jnp.concatenate([high, low], axis=0), table)
    return total[:rows] + total[rows:]


def patch_places(blocks):
    lanes = [
        (iota((blocks, 4 * blocks), 1) == 4 * iota((blocks, 4 * blocks), 0) + i).astype(
            jnp.bfloat16
        )
        for i in range(4)
    ]
    row = iota((16, LANES), 0)
    rows = [
        (iota((16, LANES), 1) % PTS == 16 * i + 4 * (row % 4) + row // 4).astype(jnp.bfloat16)
        for i in range(4)
    ]
    return rows, lanes


def project_kernel(charges, order, project, anchors, charge_out, patch_out, table, doubled):
    blocks = charge_out.shape[0]
    groups = blocks // GROUP
    table[...] = charges[...].astype(jnp.float32)
    strips = table.shape[0]
    upper = order[...] // LANES
    lower = order[...] % LANES

    def step(u, acc):
        row = jnp.broadcast_to(table[pl.ds(u, 1), :], lower.shape)
        return jnp.where(upper == u, lane_gather(row, lower), acc)

    slots = lax.fori_loop(0, strips, step, jnp.zeros(lower.shape, jnp.float32), unroll=4)
    turned = pltpu.roll(slots, BLK, 1)
    left = iota(slots.shape, 1) < BLK
    doubled[pl.ds(0, strips, stride=2), :] = jnp.where(left, slots, turned)
    doubled[pl.ds(1, strips, stride=2), :] = jnp.where(left, turned, slots)
    twice = doubled[...]
    charge_out[...] = twice.astype(jnp.bfloat16)
    patch = block_sums(project, twice)
    patch = jnp.where(iota(patch.shape, 1) < PTS, patch, 0.0).astype(jnp.bfloat16)
    rows, lanes = patch_places(blocks)
    corner = anchors[...].astype(jnp.float32)
    spread = jnp.zeros((16, 4 * blocks), jnp.float32)
    cells = (iota((8, 4 * blocks), 1) % 4).astype(jnp.float32)
    start = jnp.broadcast_to(corner[:1], (8, blocks)).astype(jnp.bfloat16)
    for i in range(4):
        spread = spread + dot(dot_nt(rows[i], patch).astype(jnp.bfloat16), lanes[i])
        cells = cells + dot(start, lanes[i])
    tiles = [slice(LANES * t, LANES * t + LANES) for t in range(groups)]
    for t in range(groups):
        patch_out[16 * t : 16 * t + 16] = spread[:, tiles[t]].astype(jnp.bfloat16)
    extra = [cells[:1, tile] for tile in tiles] + [corner]
    extra.append(jnp.zeros((16 - groups - corner.shape[0], LANES), jnp.float32))
    patch_out[16 * groups :] = jnp.concatenate(extra, axis=0).astype(jnp.bfloat16)


def inverse_kernel(order, out):
    rows = order.shape[0]

    def step(r, acc):
        here = order[pl.ds(r, 1), :]
        upper = iota((rows, LANES), 0) == here // LANES
        lower = iota((LANES, LANES), 0) == here % LANES
        values = jnp.concatenate(
            [
                jnp.where(upper, r.astype(jnp.float32), 0.0),
                jnp.where(upper, iota((rows, LANES), 1).astype(jnp.float32), 0.0),
            ],
            axis=0,
        )
        return acc + dot_nt(
            values.astype(jnp.bfloat16), lower.astype(jnp.float32).astype(jnp.bfloat16)
        )

    out[...] = lax.fori_loop(
        0, rows, step, jnp.zeros((2 * rows, LANES), jnp.float32), unroll=4
    ).astype(jnp.int32)


def near_kernel(source, near_blocks, target, charges, out, table, picked):
    step = pl.program_id(0)
    pairs = picked.shape[0]
    blocks = out.shape[0]

    @pl.when(step == 0)
    def _():
        for d in range(charges.shape[0]):
            table[d * blocks : (d + 1) * blocks] = charges[d].astype(jnp.float32)
        out[...] = jnp.zeros_like(out)

    def pick(p, carry):
        picked[pl.ds(p, 1), :] = table[pl.ds(source[step * pairs + p], 1), :]
        return carry

    lax.fori_loop(0, pairs, pick, 0, unroll=8)
    terms = block_sums(near_blocks, picked[...])
    owner = (iota((blocks, pairs), 0) == target[...]).astype(jnp.float32).astype(jnp.bfloat16)
    high, low = split(terms)
    out[...] += dot(owner, high) + dot(owner, low)


def tile_loop(half, rows, cols, groups, body):
    per_slab = cols // SLABS
    low = jnp.maximum(half * (rows // HALVES) - 1, 0)
    high = (half + 1) * (rows // HALVES)
    per_row = per_slab * groups

    def step(n, carry):
        row = low + n // per_row
        left = n % per_row
        devices = [row * cols + s * per_slab + left // groups for s in range(SLABS)]
        body(devices, left % groups, row < half * (rows // HALVES))
        return carry

    lax.fori_loop(0, (high - low) * per_row, step, 0)


def tile_cells(patches, d, t, groups):
    extra = patches[d, 16 * groups :, :].astype(jnp.float32)
    picked = jnp.where(iota(extra.shape, 0) == t, extra, 0.0)
    return jnp.broadcast_to(jnp.sum(picked, axis=0, keepdims=True), (8, LANES))


def crosses(shift, numbers, k):
    found = [((shift[b] + 4 * k) & (LANES - 1)) > LANES - 4 for b in numbers]
    return functools.reduce(jnp.logical_or, found)


def scatter_kernel(cols, place, shift, second, third, patches, table, out, columns, *slabs):
    half = place[0]
    chunk = pl.program_id(0)
    devices, held, _ = patches.shape
    groups = (held - 16) // 16
    blocks = groups * GROUP
    freqs = table.shape[0]
    quad = iota((8, LANES), 1) // 4
    upper = iota((8, LANES), 0) < 4

    @pl.when(chunk == 0)
    def _():
        def clear(n, carry):
            for slab in slabs:
                slab[n] = jnp.zeros((SLAB, LANES), jnp.float32)
            return carry

        lax.fori_loop(0, G, clear, 0)

        def tile(numbers, t, crossing):
            values = []
            for d in numbers:
                both = patches[d, pl.ds(pl.multiple_of(16 * t, 16), 16), :].astype(jnp.float32)
                cells = tile_cells(patches, d, t, groups) - (half * LANES).astype(jnp.float32)
                inside = (cells >= 0.0) & (cells < LANES)
                values.append([jnp.where(inside, part, 0.0) for part in (both[:8], both[8:])])

            def add(k):
                spot = quad == k
                sums = []
                for s in range(SLABS):
                    b = numbers[s] * blocks + t * GROUP + k
                    amount = shift[b]
                    planes = slabs[s].at[pl.ds(third[b], 4)]
                    rows = (pl.ds(second[b] + PAD, 8), pl.ds(second[b] + (PAD - 4), 8))
                    for v in range(2):
                        moved = pltpu.roll(jnp.where(spot, values[s][v], 0.0), amount, 1)
                        parts = (jnp.where(upper, moved, 0.0), jnp.where(upper, 0.0, moved))
                        for odd in range(2):
                            l = 2 * v + odd
                            sums.append((planes, l, rows[odd], planes[l, rows[odd], :] + parts[odd]))
                for planes, l, at, new in sums:
                    planes[l, at, :] = new

            def one(k, carry):
                add(k)
                return carry

            def one_crossing(k, carry):
                pl.when(crosses(shift, [d * blocks + t * GROUP + k for d in numbers], k))(
                    lambda: add(k)
                )
                return carry

            @pl.when(crossing)
            def _():
                lax.fori_loop(0, GROUP, one_crossing, 0)

            @pl.when(jnp.logical_not(crossing))
            def _():
                lax.fori_loop(0, GROUP, one, 0, unroll=4)

        tile_loop(half, devices // cols, cols, groups, tile)

    for z in range(0, ZC, 2):
        pair = []
        for plane in (z, z + 1):
            at = chunk * ZC + plane
            parts = []
            for s in range(SLABS):
                part = slabs[s][at, PAD : PAD + PIECE, :]
                if s > 0:
                    over = slabs[s - 1][at, PAD + PIECE :, :]
                    part = jnp.concatenate([part[:8] + over, part[8:]], axis=0)
                parts.append(part.astype(jnp.bfloat16))
            pair.append(jnp.concatenate(parts, axis=0))
        lines = dot(table[...], jnp.concatenate(pair, axis=1))
        columns[pl.ds(z, freqs, stride=ZC), :] = lines[:, :LANES]
        columns[pl.ds(z + 1, freqs, stride=ZC), :] = lines[:, LANES:]
    out[...] = columns[...].reshape(freqs, ZC, LANES).astype(jnp.bfloat16)


def spectrum_kernel(
    own, other, weights, third, third_back, first, first_back, own_out, other_out, held
):
    count, freqs, _ = weights.shape
    for g in range(count):
        line = jnp.concatenate([own[g], other[g]], axis=1)
        held[g * freqs : (g + 1) * freqs] = dot(third[...], line).astype(jnp.bfloat16)
    step = max(1, G // freqs)
    for g in range(0, count, step):
        rows = slice(g * freqs, (g + step) * freqs)
        s = dot(held[rows], first[...]) * weights[g : g + step].reshape(step * freqs, P_SIZE)
        held[rows] = dot(s.astype(jnp.bfloat16), first_back[...]).astype(jnp.bfloat16)
    for g in range(count):
        line = dot(third_back[...], held[g * freqs : (g + 1) * freqs]).astype(jnp.bfloat16)
        own_out[g] = line[:, :LANES]
        other_out[g] = line[:, LANES:]


def sample_kernel(
    cols, place, shift, back, second, third, patches, own, other, table, out, columns, cells
):
    half = place[0]
    chunk = pl.program_id(0)
    devices, held, _ = out.shape
    groups = held // 16
    blocks = groups * GROUP
    freqs = table.shape[1]
    quad = iota((8, LANES), 1) // 4
    upper = iota((8, LANES), 0) < 4
    both = own[...].astype(jnp.float32) + other[...].astype(jnp.float32)
    columns[...] = both.reshape(freqs * ZC, LANES)
    for z in range(0, ZC, 2):
        pair = [
            columns[pl.ds(plane, freqs, stride=ZC), :].astype(jnp.bfloat16) for plane in (z, z + 1)
        ]
        field = dot(table[...], jnp.concatenate(pair, axis=1))
        cells[chunk * ZC + z, PAD : PAD + G, :] = field[:, :LANES]
        cells[chunk * ZC + z + 1, PAD : PAD + G, :] = field[:, LANES:]

    @pl.when(chunk == pl.num_programs(0) - 1)
    def _():
        out[...] = jnp.zeros_like(out)

        def tile(numbers, t, crossing):
            def one(k, sums):
                spot = quad == k
                sums = list(sums)
                for s in range(SLABS):
                    b = numbers[s] * blocks + t * GROUP + k
                    amount = shift[b]
                    planes = cells.at[pl.ds(third[b], 4)]
                    for v in range(2):
                        even = planes[2 * v, pl.ds(second[b] + PAD, 8), :]
                        odd = planes[2 * v + 1, pl.ds(second[b] + (PAD - 4), 8), :]
                        moved = pltpu.roll(jnp.where(upper, even, odd), amount, 1)
                        sums[2 * s + v] = jnp.where(spot, moved, sums[2 * s + v])
                return tuple(sums)

            def one_crossing(k, sums):
                found = crosses(back, [d * blocks + t * GROUP + k for d in numbers], k)
                return lax.cond(found, lambda old: one(k, old), lambda old: old, sums)

            zero = (jnp.zeros((8, LANES), jnp.float32),) * (2 * SLABS)

            def store(sums):
                for s in range(SLABS):
                    first = tile_cells(patches, numbers[s], t, groups)
                    first = first - (half * LANES).astype(jnp.float32)
                    inside = (first >= 0.0) & (first < LANES)
                    parts = [jnp.where(inside, part, 0.0) for part in sums[2 * s : 2 * s + 2]]
                    out[numbers[s], pl.ds(pl.multiple_of(16 * t, 16), 16), :] = jnp.concatenate(
                        parts, axis=0
                    ).astype(jnp.bfloat16)

            @pl.when(crossing)
            def _():
                store(lax.fori_loop(0, GROUP, one_crossing, zero))

            @pl.when(jnp.logical_not(crossing))
            def _():
                store(lax.fori_loop(0, GROUP, one, zero, unroll=4))

        tile_loop(half, devices // cols, cols, groups, tile)


def finish_kernel(values, interpolate, near, inverse, out, total):
    blocks = near.shape[0]
    groups = values.shape[1] // 16
    rows, lanes = patch_places(blocks)
    summed = values[0].astype(jnp.float32)
    for d in range(1, values.shape[0]):
        summed = summed + values[d].astype(jnp.float32)
    spread = jnp.concatenate([summed[16 * t : 16 * t + 16] for t in range(groups)], axis=1)
    patch = jnp.zeros((blocks, LANES), jnp.float32)
    for part in split(spread):
        for i in range(4):
            turned = dot_nt(lanes[i], part).astype(jnp.bfloat16)
            patch = patch + dot(turned, rows[i])
    total[...] = block_sums(interpolate, patch) + near[...]
    count = out.shape[0]
    even = total[pl.ds(0, count, stride=2), :]
    odd = total[pl.ds(1, count, stride=2), :]
    total[:count] = jnp.where(iota(even.shape, 1) < BLK, even, odd)
    upper = inverse[:count]
    lower = inverse[count:]

    def step(u, acc):
        row = jnp.broadcast_to(total[pl.ds(u, 1), :], lower.shape)
        return jnp.where(upper == u, lane_gather(row, lower), acc)

    out[...] = lax.fori_loop(0, count, step, jnp.zeros(out.shape, jnp.float32), unroll=4)


def struct(shape, dtype):
    return jax.ShapeDtypeStruct(shape, dtype)


def whole(shape):
    return pl.BlockSpec(shape, lambda *_: (0,) * len(shape))


def params(mib):
    return pltpu.CompilerParams(vmem_limit_bytes=mib * MB)


def neighbourhood(array):
    array = array[None, None]
    for axis, dim in (("row", 0), ("col", 1)):
        count = lax.axis_size(axis)
        up = [(i, i + 1) for i in range(count - 1)]
        down = [(j, i) for i, j in up]
        before = lax.ppermute(array, axis, up)
        after = lax.ppermute(array, axis, down)
        array = jnp.concatenate([before, array, after], axis=dim)
    return array


def body(
    charges,
    panel_order,
    patch_anchor,
    project,
    interpolate,
    kernel_spectrum,
    near_pairs,
    near_blocks,
):
    axes = ("row", "col")
    rows = lax.axis_size("row")
    cols = lax.axis_size("col")
    devices = rows * cols
    row_at = lax.axis_index("row")
    col_at = lax.axis_index("col")
    half = col_at % HALVES
    mates = [(c, c ^ 1) for c in range(cols)]
    blocks = project.shape[0]
    groups = blocks // GROUP
    panels = charges.shape[0]
    strips = panels // LANES
    gs, fs, _ = kernel_spectrum.shape
    held = 16 * groups + 16

    order = panel_order.reshape(strips, LANES)
    block_charges, sent = pl.pallas_call(
        project_kernel,
        out_shape=(
            struct((blocks, LANES), jnp.bfloat16),
            struct((held, LANES), jnp.bfloat16),
        ),
        scratch_shapes=[
            pltpu.VMEM((strips, LANES), jnp.float32),
            pltpu.VMEM((blocks, LANES), jnp.float32),
        ],
        compiler_params=params(32),
        name="project",
    )(
        charges.reshape(strips, LANES),
        order,
        project,
        patch_anchor,
    )
    copies = jnp.broadcast_to(sent[None], (devices, held, LANES))
    gathered = lax.all_to_all(copies, axes, split_axis=0, concat_axis=0, tiled=True)
    inverse = pl.pallas_call(
        inverse_kernel,
        out_shape=struct((2 * strips, LANES), jnp.int32),
        compiler_params=params(32),
        name="inverse",
    )(order)

    around = neighbourhood(block_charges).reshape(9, blocks, LANES)
    gathered, around = lax.optimization_barrier((gathered, around))
    anchors = gathered[:, 17 * groups : 17 * groups + 3].astype(jnp.int32)
    lane = 4 * (jnp.arange(blocks, dtype=jnp.int32) % GROUP)
    forth = ((anchors[:, 0] - lane) & (LANES - 1)).reshape(devices * blocks)
    back = ((lane - anchors[:, 0]) & (LANES - 1)).reshape(devices * blocks)
    second_at = anchors[:, 1].reshape(devices * blocks)
    piece = (jnp.arange(devices, dtype=jnp.int32) % cols * SLABS // cols * PIECE)[:, None]
    slab_at = (anchors[:, 1] - piece).reshape(devices * blocks)
    third_at = anchors[:, 2].reshape(devices * blocks)
    place = half.astype(jnp.int32).reshape(1)

    table = jnp.asarray(CAS)
    second = lax.dynamic_slice_in_dim(table[:, :G], row_at * gs, gs, axis=0)
    third = lax.dynamic_slice_in_dim(table[:, :G], col_at * fs, fs, axis=0)
    mine = lax.dynamic_slice_in_dim(table, half * LANES, LANES, axis=0)
    yours = lax.dynamic_slice_in_dim(table, (1 - half) * LANES, LANES, axis=0)
    first = jnp.concatenate([mine, yours], axis=0)
    chunks = G // ZC
    smem = pl.BlockSpec(memory_space=pltpu.SMEM)
    line_block = pl.BlockSpec((gs, ZC, LANES), lambda z: (0, z, 0))
    lines_type = struct((gs, G, LANES), jnp.bfloat16)
    own = pl.pallas_call(
        functools.partial(scatter_kernel, cols),
        grid=(chunks,),
        in_specs=[smem] * 4 + [whole(gathered.shape), whole(second.shape)],
        out_specs=line_block,
        out_shape=lines_type,
        scratch_shapes=[pltpu.VMEM((gs * ZC, LANES), jnp.float32)]
        + [pltpu.VMEM((G, SLAB, LANES), jnp.float32)] * SLABS,
        compiler_params=params(56),
        name="scatter",
    )(place, forth, slab_at, third_at, gathered, second)
    other = lax.ppermute(own, "col", mates)

    source = near_pairs[1]
    source_device = source // blocks
    code = (source_device // cols - row_at + 1) * 3 + (source_device % cols - col_at + 1)
    wanted = code * blocks + source % blocks
    target = near_pairs[0] - (row_at * cols + col_at) * blocks
    pairs = near_blocks.shape[0]
    near = pl.pallas_call(
        near_kernel,
        grid=(pairs // blocks,),
        in_specs=[
            smem,
            pl.BlockSpec((blocks, BLK * BLK), lambda n: (n, 0)),
            pl.BlockSpec((1, blocks), lambda n: (0, n)),
            whole((9, blocks, LANES)),
        ],
        out_specs=whole((blocks, LANES)),
        out_shape=struct((blocks, LANES), jnp.float32),
        scratch_shapes=[
            pltpu.VMEM((9 * blocks, LANES), jnp.float32),
            pltpu.VMEM((blocks, LANES), jnp.float32),
        ],
        compiler_params=params(48),
        name="near",
    )(wanted, near_blocks, target.reshape(1, pairs), around)
    other, near = lax.optimization_barrier((other, near))

    batch = 8
    part = lambda shape: pl.BlockSpec((batch,) + shape, lambda n: (n, 0, 0))
    own, other = pl.pallas_call(
        spectrum_kernel,
        grid=(gs // batch,),
        in_specs=[
            part((G, LANES)),
            part((G, LANES)),
            part((fs, P_SIZE)),
            whole((fs, G)),
            whole((G, fs)),
            whole((G, P_SIZE)),
            whole((P_SIZE, G)),
        ],
        out_specs=(part((G, LANES)), part((G, LANES))),
        out_shape=(lines_type, lines_type),
        scratch_shapes=[pltpu.VMEM((batch * fs, G), jnp.bfloat16)],
        compiler_params=params(56),
        name="spectrum",
    )(own, other, kernel_spectrum, third, third.T, first, first.T)
    other = lax.ppermute(other, "col", mates)

    other, inverse = lax.optimization_barrier((other, inverse))
    values = pl.pallas_call(
        functools.partial(sample_kernel, cols),
        grid=(chunks,),
        in_specs=[smem] * 5 + [whole(gathered.shape), line_block, line_block, whole((G, gs))],
        out_specs=whole((devices, 16 * groups, LANES)),
        out_shape=struct((devices, 16 * groups, LANES), jnp.bfloat16),
        scratch_shapes=[
            pltpu.VMEM((gs * ZC, LANES), jnp.float32),
            pltpu.VMEM((G, G + 2 * PAD, LANES), jnp.float32),
        ],
        compiler_params=params(56),
        name="sample",
    )(place, back, forth, second_at, third_at, gathered, own, other, second.T)
    values = lax.all_to_all(values, axes, split_axis=0, concat_axis=0, tiled=True)

    result = pl.pallas_call(
        finish_kernel,
        out_shape=struct((strips, LANES), jnp.float32),
        scratch_shapes=[pltpu.VMEM((blocks, LANES), jnp.float32)],
        compiler_params=params(32),
        name="finish",
    )(values, interpolate, near, inverse)
    return result.reshape(panels)


def solution(mesh):
    placed = (
        P(("row", "col")),
        P(("row", "col")),
        P(None, ("row", "col")),
        P(("row", "col"), None),
        P(("row", "col"), None),
        P("row", "col", None),
        P(None, ("row", "col")),
        P(("row", "col"), None),
    )
    return jax.shard_map(
        body, mesh=mesh, in_specs=placed, out_specs=P(("row", "col")), check_vma=False
    )
```

```python
import functools

import jax
import jax.numpy as jnp
import ml_dtypes
import numpy as np
from jax import lax
from jax.experimental import pallas as pl
from jax.experimental.pallas import tpu as pltpu
from jax.sharding import PartitionSpec as P

G = 256
P_SIZE = 512
BLK = 64
PTS = 64
LANES = 128
GROUP = LANES // 4
HALVES = G // LANES
SLABS = 4
PIECE = G // SLABS
QUAD = 4
PAD = 8
SLAB = PAD + QUAD * PIECE + 32
CELLS = PAD + QUAD * G + 16
ZC = 32
MB = 1 << 20
NT = (((1,), (1,)), ((), ()))


def cas_table():
    index = np.arange(P_SIZE, dtype=np.int64)
    phase = (index[:, None] * index[None, :] % P_SIZE).astype(np.float64) * (2.0 * np.pi / P_SIZE)
    return ((np.cos(phase) + np.sin(phase)) / np.sqrt(P_SIZE)).astype(ml_dtypes.bfloat16)


CAS = cas_table()


def dot(a, b):
    return jnp.dot(a, b, preferred_element_type=jnp.float32)


def dot_nt(a, b):
    return lax.dot_general(a, b, NT, preferred_element_type=jnp.float32)


def iota(shape, dim):
    return lax.broadcasted_iota(jnp.int32, shape, dim)


def split(value):
    high = value.astype(jnp.bfloat16)
    return high, (value - high.astype(jnp.float32)).astype(jnp.bfloat16)


def lane_gather(table, index):
    return jnp.take_along_axis(table, index, axis=1, mode="promise_in_bounds")


def block_sums(mats, vecs):
    rows = vecs.shape[0]
    pair = jnp.concatenate([vecs, vecs], axis=1)
    total = jnp.zeros((2 * rows, LANES), jnp.float32)
    for t in range(mats.shape[1] // 256):
        high, low = split(mats[:, 256 * t : 256 * t + 256].astype(jnp.float32) * pair)
        owner = iota((256, LANES), 0) // BLK + 4 * t
        table = (owner == iota((256, LANES), 1) % BLK).astype(jnp.bfloat16)
        total = total + dot(jnp.concatenate([high, low], axis=0), table)
    return total[:rows] + total[rows:]


def patch_places(blocks):
    lanes = [
        (iota((blocks, 4 * blocks), 1) == 4 * iota((blocks, 4 * blocks), 0) + i).astype(
            jnp.bfloat16
        )
        for i in range(4)
    ]
    row = iota((16, LANES), 0)
    rows = [
        (iota((16, LANES), 1) % PTS == 16 * i + row).astype(jnp.bfloat16)
        for i in range(4)
    ]
    return rows, lanes


def project_kernel(charges, order, project, anchors, charge_out, patch_out, table, doubled):
    blocks = charge_out.shape[0]
    groups = blocks // GROUP
    table[...] = charges[...].astype(jnp.float32)
    strips = table.shape[0]
    upper = order[...] // LANES
    lower = order[...] % LANES

    def step(u, acc):
        row = jnp.broadcast_to(table[pl.ds(u, 1), :], lower.shape)
        return jnp.where(upper == u, lane_gather(row, lower), acc)

    slots = lax.fori_loop(0, strips, step, jnp.zeros(lower.shape, jnp.float32), unroll=4)
    turned = pltpu.roll(slots, BLK, 1)
    left = iota(slots.shape, 1) < BLK
    doubled[pl.ds(0, strips, stride=2), :] = jnp.where(left, slots, turned)
    doubled[pl.ds(1, strips, stride=2), :] = jnp.where(left, turned, slots)
    twice = doubled[...]
    charge_out[...] = twice.astype(jnp.bfloat16)
    patch = block_sums(project, twice)
    patch = jnp.where(iota(patch.shape, 1) < PTS, patch, 0.0).astype(jnp.bfloat16)
    rows, lanes = patch_places(blocks)
    corner = anchors[...].astype(jnp.float32)
    spread = jnp.zeros((16, 4 * blocks), jnp.float32)
    cells = (iota((8, 4 * blocks), 1) % 4).astype(jnp.float32)
    start = jnp.broadcast_to(corner[:1], (8, blocks)).astype(jnp.bfloat16)
    for i in range(4):
        spread = spread + dot(dot_nt(rows[i], patch).astype(jnp.bfloat16), lanes[i])
        cells = cells + dot(start, lanes[i])
    tiles = [slice(LANES * t, LANES * t + LANES) for t in range(groups)]
    for t in range(groups):
        patch_out[16 * t : 16 * t + 16] = spread[:, tiles[t]].astype(jnp.bfloat16)
    extra = [cells[:1, tile] for tile in tiles] + [corner]
    extra.append(jnp.zeros((16 - groups - corner.shape[0], LANES), jnp.float32))
    patch_out[16 * groups :] = jnp.concatenate(extra, axis=0).astype(jnp.bfloat16)


def inverse_kernel(order, out):
    rows = order.shape[0]

    def step(r, acc):
        here = order[pl.ds(r, 1), :]
        upper = iota((rows, LANES), 0) == here // LANES
        lower = iota((LANES, LANES), 0) == here % LANES
        values = jnp.concatenate(
            [
                jnp.where(upper, r.astype(jnp.float32), 0.0),
                jnp.where(upper, iota((rows, LANES), 1).astype(jnp.float32), 0.0),
            ],
            axis=0,
        )
        return acc + dot_nt(
            values.astype(jnp.bfloat16), lower.astype(jnp.float32).astype(jnp.bfloat16)
        )

    out[...] = lax.fori_loop(
        0, rows, step, jnp.zeros((2 * rows, LANES), jnp.float32), unroll=4
    ).astype(jnp.int32)


def near_kernel(source, near_blocks, target, charges, out, table, picked):
    step = pl.program_id(0)
    pairs = picked.shape[0]
    blocks = out.shape[0]

    @pl.when(step == 0)
    def _():
        for d in range(charges.shape[0]):
            table[d * blocks : (d + 1) * blocks] = charges[d].astype(jnp.float32)
        out[...] = jnp.zeros_like(out)

    def pick(p, carry):
        picked[pl.ds(p, 1), :] = table[pl.ds(source[step * pairs + p], 1), :]
        return carry

    lax.fori_loop(0, pairs, pick, 0, unroll=8)
    terms = block_sums(near_blocks, picked[...])
    owner = (iota((blocks, pairs), 0) == target[...]).astype(jnp.float32).astype(jnp.bfloat16)
    high, low = split(terms)
    out[...] += dot(owner, high) + dot(owner, low)


def tile_loop(half, rows, cols, groups, body):
    per_slab = cols // SLABS
    low = jnp.maximum(half * (rows // HALVES) - 1, 0)
    high = (half + 1) * (rows // HALVES)
    per_row = per_slab * groups

    def step(n, carry):
        row = low + n // per_row
        left = n % per_row
        body([row * cols + s * per_slab + left // groups for s in range(SLABS)], left % groups)
        return carry

    lax.fori_loop(0, (high - low) * per_row, step, 0)


def lanes_inside(patches, d, t, groups, half):
    extra = patches[d, 16 * groups :, :].astype(jnp.float32)
    picked = jnp.where(iota(extra.shape, 0) == t, extra, 0.0)
    cells = jnp.sum(picked, axis=0, keepdims=True) - (half * LANES).astype(jnp.float32)
    return jnp.broadcast_to((cells >= 0.0) & (cells < LANES), (16, LANES))


def scatter_kernel(cols, place, shift, start, patches, table, out, columns, *slabs):
    half = place[0]
    chunk = pl.program_id(0)
    devices, held, _ = patches.shape
    groups = (held - 16) // 16
    blocks = groups * GROUP
    freqs = table.shape[0]
    owner = iota((16, LANES), 1) // 4
    plane = iota((16, LANES), 0) % QUAD

    @pl.when(chunk == 0)
    def _():
        def clear(n, carry):
            for slab in slabs:
                slab[pl.ds(pl.multiple_of(n * SLAB, 8), SLAB), :] = jnp.zeros(
                    (SLAB, LANES), jnp.float32
                )
            return carry

        lax.fori_loop(0, slabs[0].shape[0] // SLAB, clear, 0)

        def tile(numbers, t):
            values = []
            for d in numbers:
                part = patches[d, pl.ds(pl.multiple_of(16 * t, 16), 16), :].astype(jnp.float32)
                values.append(jnp.where(lanes_inside(patches, d, t, groups, half), part, 0.0))

            def one(k, carry):
                spot = owner == k
                sums = []
                for s in range(SLABS):
                    b = numbers[s] * blocks + t * GROUP + k
                    at = start[b]
                    moved = pltpu.roll(jnp.where(spot, values[s], 0.0), shift[b], 1)
                    here = plane < QUAD - (at & (QUAD - 1))
                    near = slabs[s][pl.ds(at, 16), :] + jnp.where(here, moved, 0.0)
                    at_next = at + (SLAB - QUAD)
                    far = slabs[s][pl.ds(at_next, 16), :] + jnp.where(here, 0.0, moved)
                    sums.append((at, near, at_next, far))
                for s, (at, near, at_next, far) in enumerate(sums):
                    slabs[s][pl.ds(at, 16), :] = near
                    slabs[s][pl.ds(at_next, 16), :] = far
                return carry

            lax.fori_loop(0, GROUP, one, 0, unroll=4)

        tile_loop(half, devices // cols, cols, groups, tile)

    for z in range(0, ZC, QUAD):
        base = pl.multiple_of((chunk * (ZC // QUAD) + z // QUAD) * SLAB, 8)
        planes = []
        for q in range(QUAD):
            parts = []
            for s in range(SLABS):
                part = slabs[s][pl.ds(base + (PAD + q), PIECE, stride=QUAD), :]
                if s > 0:
                    at = base + (PAD + QUAD * PIECE + q)
                    over = slabs[s - 1][pl.ds(at, 8, stride=QUAD), :]
                    part = jnp.concatenate([part[:8] + over, part[8:]], axis=0)
                parts.append(part.astype(jnp.bfloat16))
            planes.append(jnp.concatenate(parts, axis=0))
        lines = dot(table[...], jnp.concatenate(planes, axis=1))
        for q in range(QUAD):
            columns[pl.ds(z + q, freqs, stride=ZC), :] = lines[:, LANES * q : LANES * q + LANES]
    out[...] = columns[...].reshape(freqs, ZC, LANES).astype(jnp.bfloat16)


def spectrum_kernel(
    own, other, weights, third, third_back, first, first_back, own_out, other_out, held
):
    count, freqs, _ = weights.shape
    for g in range(count):
        line = jnp.concatenate([own[g], other[g]], axis=1)
        held[g * freqs : (g + 1) * freqs] = dot(third[...], line).astype(jnp.bfloat16)
    step = max(1, G // freqs)
    for g in range(0, count, step):
        rows = slice(g * freqs, (g + step) * freqs)
        s = dot(held[rows], first[...]) * weights[g : g + step].reshape(step * freqs, P_SIZE)
        held[rows] = dot(s.astype(jnp.bfloat16), first_back[...]).astype(jnp.bfloat16)
    for g in range(count):
        line = dot(third_back[...], held[g * freqs : (g + 1) * freqs]).astype(jnp.bfloat16)
        own_out[g] = line[:, :LANES]
        other_out[g] = line[:, LANES:]


def sample_kernel(cols, place, shift, start, patches, own, other, table, out, columns, cells):
    half = place[0]
    chunk = pl.program_id(0)
    devices, held, _ = out.shape
    groups = held // 16
    blocks = groups * GROUP
    freqs = table.shape[1]
    owner = iota((16, LANES), 1) // 4
    plane = iota((16, LANES), 0) % QUAD
    both = own[...].astype(jnp.float32) + other[...].astype(jnp.float32)
    columns[...] = both.reshape(freqs * ZC, LANES)
    for z in range(0, ZC, QUAD):
        planes = [
            columns[pl.ds(z + q, freqs, stride=ZC), :].astype(jnp.bfloat16) for q in range(QUAD)
        ]
        field = dot(table[...], jnp.concatenate(planes, axis=1))
        base = pl.multiple_of((chunk * (ZC // QUAD) + z // QUAD) * CELLS, 8)
        for q in range(QUAD):
            part = field[:, LANES * q : LANES * q + LANES]
            cells[pl.ds(base + (PAD + q), G, stride=QUAD), :] = part

    @pl.when(chunk == pl.num_programs(0) - 1)
    def _():
        out[...] = jnp.zeros_like(out)

        def tile(numbers, t):
            def one(k, sums):
                spot = owner == k
                new = []
                for s in range(SLABS):
                    b = numbers[s] * blocks + t * GROUP + k
                    at = start[b]
                    here = plane < QUAD - (at & (QUAD - 1))
                    near = cells[pl.ds(at, 16), :]
                    far = cells[pl.ds(at + (CELLS - QUAD), 16), :]
                    moved = pltpu.roll(jnp.where(here, near, far), shift[b], 1)
                    new.append(jnp.where(spot, moved, sums[s]))
                return tuple(new)

            zero = (jnp.zeros((16, LANES), jnp.float32),) * SLABS
            sums = lax.fori_loop(0, GROUP, one, zero, unroll=4)
            for s, d in enumerate(numbers):
                inside = lanes_inside(patches, d, t, groups, half)
                out[d, pl.ds(pl.multiple_of(16 * t, 16), 16), :] = jnp.where(
                    inside, sums[s], 0.0
                ).astype(jnp.bfloat16)

        tile_loop(half, devices // cols, cols, groups, tile)


def finish_kernel(values, interpolate, near, inverse, out, total):
    blocks = near.shape[0]
    groups = values.shape[1] // 16
    rows, lanes = patch_places(blocks)
    summed = values[0].astype(jnp.float32)
    for d in range(1, values.shape[0]):
        summed = summed + values[d].astype(jnp.float32)
    spread = jnp.concatenate([summed[16 * t : 16 * t + 16] for t in range(groups)], axis=1)
    patch = jnp.zeros((blocks, LANES), jnp.float32)
    for part in split(spread):
        for i in range(4):
            turned = dot_nt(lanes[i], part).astype(jnp.bfloat16)
            patch = patch + dot(turned, rows[i])
    total[...] = block_sums(interpolate, patch) + near[...]
    count = out.shape[0]
    even = total[pl.ds(0, count, stride=2), :]
    odd = total[pl.ds(1, count, stride=2), :]
    total[:count] = jnp.where(iota(even.shape, 1) < BLK, even, odd)
    upper = inverse[:count]
    lower = inverse[count:]

    def step(u, acc):
        row = jnp.broadcast_to(total[pl.ds(u, 1), :], lower.shape)
        return jnp.where(upper == u, lane_gather(row, lower), acc)

    out[...] = lax.fori_loop(0, count, step, jnp.zeros(out.shape, jnp.float32), unroll=4)


def struct(shape, dtype):
    return jax.ShapeDtypeStruct(shape, dtype)


def whole(shape):
    return pl.BlockSpec(shape, lambda *_: (0,) * len(shape))


def params(mib):
    return pltpu.CompilerParams(vmem_limit_bytes=mib * MB)


def beside(array, axis, dim):
    count = lax.axis_size(axis)
    up = [(i, i + 1) for i in range(count - 1)]
    before = lax.ppermute(array, axis, up)
    after = lax.ppermute(array, axis, [(j, i) for i, j in up])
    return jnp.concatenate([before, array, after], axis=dim)


def body(
    charges,
    panel_order,
    patch_anchor,
    project,
    interpolate,
    kernel_spectrum,
    near_pairs,
    near_blocks,
):
    axes = ("row", "col")
    rows = lax.axis_size("row")
    cols = lax.axis_size("col")
    devices = rows * cols
    row_at = lax.axis_index("row")
    col_at = lax.axis_index("col")
    half = col_at % HALVES
    mates = [(c, c ^ 1) for c in range(cols)]
    blocks = project.shape[0]
    groups = blocks // GROUP
    panels = charges.shape[0]
    strips = panels // LANES
    gs, fs, _ = kernel_spectrum.shape
    held = 16 * groups + 16

    order = panel_order.reshape(strips, LANES)
    block_charges, sent = pl.pallas_call(
        project_kernel,
        out_shape=(
            struct((blocks, LANES), jnp.bfloat16),
            struct((held, LANES), jnp.bfloat16),
        ),
        scratch_shapes=[
            pltpu.VMEM((strips, LANES), jnp.float32),
            pltpu.VMEM((blocks, LANES), jnp.float32),
        ],
        compiler_params=params(32),
        name="project",
    )(
        charges.reshape(strips, LANES),
        order,
        project,
        patch_anchor,
    )
    copies = jnp.broadcast_to(sent[None], (devices, held, LANES))
    gathered = lax.all_to_all(copies, axes, split_axis=0, concat_axis=0, tiled=True)
    inverse = pl.pallas_call(
        inverse_kernel,
        out_shape=struct((2 * strips, LANES), jnp.int32),
        compiler_params=params(32),
        name="inverse",
    )(order)

    around = beside(block_charges[None, None], "row", 0)
    gathered, around = lax.optimization_barrier((gathered, around))
    around = beside(around, "col", 1).reshape(9, blocks, LANES)
    anchors = gathered[:, 17 * groups : 17 * groups + 3].astype(jnp.int32)
    lane = 4 * (jnp.arange(blocks, dtype=jnp.int32) % GROUP)
    forth = ((anchors[:, 0] - lane) & (LANES - 1)).reshape(devices * blocks)
    back = ((lane - anchors[:, 0]) & (LANES - 1)).reshape(devices * blocks)
    group = anchors[:, 2] // QUAD
    inner = PAD + QUAD * anchors[:, 1] + anchors[:, 2] % QUAD
    piece = (jnp.arange(devices, dtype=jnp.int32) % cols * SLABS // cols * PIECE)[:, None]
    slab_at = (group * SLAB + inner - QUAD * piece).reshape(devices * blocks)
    cell_at = (group * CELLS + inner).reshape(devices * blocks)
    place = half.astype(jnp.int32).reshape(1)

    table = jnp.asarray(CAS)
    second = lax.dynamic_slice_in_dim(table[:, :G], row_at * gs, gs, axis=0)
    third = lax.dynamic_slice_in_dim(table[:, :G], col_at * fs, fs, axis=0)
    mine = lax.dynamic_slice_in_dim(table, half * LANES, LANES, axis=0)
    yours = lax.dynamic_slice_in_dim(table, (1 - half) * LANES, LANES, axis=0)
    first = jnp.concatenate([mine, yours], axis=0)
    chunks = G // ZC
    smem = pl.BlockSpec(memory_space=pltpu.SMEM)
    line_block = pl.BlockSpec((gs, ZC, LANES), lambda z: (0, z, 0))
    lines_type = struct((gs, G, LANES), jnp.bfloat16)
    own = pl.pallas_call(
        functools.partial(scatter_kernel, cols),
        grid=(chunks,),
        in_specs=[smem] * 3 + [whole(gathered.shape), whole(second.shape)],
        out_specs=line_block,
        out_shape=lines_type,
        scratch_shapes=[pltpu.VMEM((gs * ZC, LANES), jnp.float32)]
        + [pltpu.VMEM(((G // QUAD + 1) * SLAB, LANES), jnp.float32)] * SLABS,
        compiler_params=params(56),
        name="scatter",
    )(place, forth, slab_at, gathered, second)
    other = lax.ppermute(own, "col", mates)

    other, around, inverse = lax.optimization_barrier((other, around, inverse))

    batch = 8
    part = lambda shape: pl.BlockSpec((batch,) + shape, lambda n: (n, 0, 0))
    own, other = pl.pallas_call(
        spectrum_kernel,
        grid=(gs // batch,),
        in_specs=[
            part((G, LANES)),
            part((G, LANES)),
            part((fs, P_SIZE)),
            whole((fs, G)),
            whole((G, fs)),
            whole((G, P_SIZE)),
            whole((P_SIZE, G)),
        ],
        out_specs=(part((G, LANES)), part((G, LANES))),
        out_shape=(lines_type, lines_type),
        scratch_shapes=[pltpu.VMEM((batch * fs, G), jnp.bfloat16)],
        compiler_params=params(56),
        name="spectrum",
    )(own, other, kernel_spectrum, third, third.T, first, first.T)
    other = lax.ppermute(other, "col", mates)

    source = near_pairs[1]
    source_device = source // blocks
    code = (source_device // cols - row_at + 1) * 3 + (source_device % cols - col_at + 1)
    wanted = code * blocks + source % blocks
    target = near_pairs[0] - (row_at * cols + col_at) * blocks
    pairs = near_blocks.shape[0]
    near = pl.pallas_call(
        near_kernel,
        grid=(pairs // blocks,),
        in_specs=[
            smem,
            pl.BlockSpec((blocks, BLK * BLK), lambda n: (n, 0)),
            pl.BlockSpec((1, blocks), lambda n: (0, n)),
            whole((9, blocks, LANES)),
        ],
        out_specs=whole((blocks, LANES)),
        out_shape=struct((blocks, LANES), jnp.float32),
        scratch_shapes=[
            pltpu.VMEM((9 * blocks, LANES), jnp.float32),
            pltpu.VMEM((blocks, LANES), jnp.float32),
        ],
        compiler_params=params(48),
        name="near",
    )(wanted, near_blocks, target.reshape(1, pairs), around)
    other, near = lax.optimization_barrier((other, near))
    values = pl.pallas_call(
        functools.partial(sample_kernel, cols),
        grid=(chunks,),
        in_specs=[smem] * 3 + [whole(gathered.shape), line_block, line_block, whole((G, gs))],
        out_specs=whole((devices, 16 * groups, LANES)),
        out_shape=struct((devices, 16 * groups, LANES), jnp.bfloat16),
        scratch_shapes=[
            pltpu.VMEM((gs * ZC, LANES), jnp.float32),
            pltpu.VMEM(((G // QUAD + 1) * CELLS, LANES), jnp.float32),
        ],
        compiler_params=params(56),
        name="sample",
    )(place, back, cell_at, gathered, own, other, second.T)
    values = lax.all_to_all(values, axes, split_axis=0, concat_axis=0, tiled=True)

    result = pl.pallas_call(
        finish_kernel,
        out_shape=struct((strips, LANES), jnp.float32),
        scratch_shapes=[pltpu.VMEM((blocks, LANES), jnp.float32)],
        compiler_params=params(32),
        name="finish",
    )(values, interpolate, near, inverse)
    return result.reshape(panels)


def solution(mesh):
    placed = (
        P(("row", "col")),
        P(("row", "col")),
        P(None, ("row", "col")),
        P(("row", "col"), None),
        P(("row", "col"), None),
        P("row", "col", None),
        P(None, ("row", "col")),
        P(("row", "col"), None),
    )
    return jax.shard_map(
        body, mesh=mesh, in_specs=placed, out_specs=P(("row", "col")), check_vma=False
    )
```

```python
import functools

import jax
import jax.numpy as jnp
import ml_dtypes
import numpy as np
from jax import lax
from jax.experimental import pallas as pl
from jax.experimental.pallas import tpu as pltpu
from jax.sharding import PartitionSpec as P

G = 256
P_SIZE = 512
BLK = 64
PTS = 64
LANES = 128
GROUP = LANES // 4
HALVES = G // LANES
SLABS = 4
PIECE = G // SLABS
QUAD = 4
PAD = 8
SLAB = PAD + QUAD * PIECE + 32
CELLS = PAD + QUAD * G + 16
ZC = 32
STRIDE = G + 1
BATCH = 8
UNROLL = 16
MB = 1 << 20
NT = (((1,), (1,)), ((), ()))


def cas_table():
    index = np.arange(P_SIZE, dtype=np.int64)
    phase = (index[:, None] * index[None, :] % P_SIZE).astype(np.float64) * (2.0 * np.pi / P_SIZE)
    return ((np.cos(phase) + np.sin(phase)) / np.sqrt(P_SIZE)).astype(ml_dtypes.bfloat16)


CAS = cas_table()


def dot(a, b):
    return jnp.dot(a, b, preferred_element_type=jnp.float32)


def dot_nt(a, b):
    return lax.dot_general(a, b, NT, preferred_element_type=jnp.float32)


def iota(shape, dim):
    return lax.broadcasted_iota(jnp.int32, shape, dim)


def split(value):
    high = value.astype(jnp.bfloat16)
    return high, (value - high.astype(jnp.float32)).astype(jnp.bfloat16)


def lane_gather(table, index):
    return jnp.take_along_axis(table, index, axis=1, mode="promise_in_bounds")


def block_sums(mats, vecs):
    rows = vecs.shape[0]
    pair = jnp.concatenate([vecs, vecs], axis=1)
    total = jnp.zeros((2 * rows, LANES), jnp.float32)
    for t in range(mats.shape[1] // 256):
        high, low = split(mats[:, 256 * t : 256 * t + 256].astype(jnp.float32) * pair)
        owner = iota((256, LANES), 0) // BLK + 4 * t
        table = (owner == iota((256, LANES), 1) % BLK).astype(jnp.bfloat16)
        total = total + dot(jnp.concatenate([high, low], axis=0), table)
    return total[:rows] + total[rows:]


def patch_places(blocks):
    lanes = [
        (iota((blocks, 4 * blocks), 1) == 4 * iota((blocks, 4 * blocks), 0) + i).astype(
            jnp.bfloat16
        )
        for i in range(4)
    ]
    row = iota((16, LANES), 0)
    rows = [
        (iota((16, LANES), 1) % PTS == 16 * i + row).astype(jnp.bfloat16)
        for i in range(4)
    ]
    return rows, lanes


def project_kernel(
    charges_in,
    order_in,
    project_in,
    anchors_in,
    charge_out,
    patch_out,
    charges,
    order,
    project,
    anchors,
    table,
    doubled,
    sems,
):
    blocks = charge_out.shape[0]
    groups = blocks // GROUP
    pairs = ((charges_in, charges), (order_in, order), (project_in, project), (anchors_in, anchors))
    copies = [pltpu.make_async_copy(a, b, sems.at[n]) for n, (a, b) in enumerate(pairs)]
    for copy in copies:
        copy.start()
    copies[0].wait()
    copies[1].wait()
    table[...] = charges[...].astype(jnp.float32)
    strips = table.shape[0]
    upper = order[...] // LANES
    lower = order[...] % LANES

    def step(u, acc):
        row = jnp.broadcast_to(table[pl.ds(u, 1), :], lower.shape)
        return jnp.where(upper == u, lane_gather(row, lower), acc)

    slots = lax.fori_loop(0, strips, step, jnp.zeros(lower.shape, jnp.float32), unroll=4)
    turned = pltpu.roll(slots, BLK, 1)
    left = iota(slots.shape, 1) < BLK
    doubled[pl.ds(0, strips, stride=2), :] = jnp.where(left, slots, turned)
    doubled[pl.ds(1, strips, stride=2), :] = jnp.where(left, turned, slots)
    twice = doubled[...]
    charge_out[...] = twice.astype(jnp.bfloat16)
    copies[2].wait()
    copies[3].wait()
    patch = block_sums(project, twice)
    patch = jnp.where(iota(patch.shape, 1) < PTS, patch, 0.0).astype(jnp.bfloat16)
    rows, lanes = patch_places(blocks)
    corner = anchors[...].astype(jnp.float32)
    spread = jnp.zeros((16, 4 * blocks), jnp.float32)
    cells = (iota((8, 4 * blocks), 1) % 4).astype(jnp.float32)
    start = jnp.broadcast_to(corner[:1], (8, blocks)).astype(jnp.bfloat16)
    for i in range(4):
        spread = spread + dot(dot_nt(rows[i], patch).astype(jnp.bfloat16), lanes[i])
        cells = cells + dot(start, lanes[i])
    tiles = [slice(LANES * t, LANES * t + LANES) for t in range(groups)]
    for t in range(groups):
        patch_out[16 * t : 16 * t + 16] = spread[:, tiles[t]].astype(jnp.bfloat16)
    extra = [cells[:1, tile] for tile in tiles] + [corner]
    extra.append(jnp.zeros((16 - groups - corner.shape[0], LANES), jnp.float32))
    patch_out[16 * groups :] = jnp.concatenate(extra, axis=0).astype(jnp.bfloat16)


def inverse_kernel(order, out):
    rows = order.shape[0]

    def step(r, acc):
        here = order[pl.ds(r, 1), :]
        upper = iota((rows, LANES), 0) == here // LANES
        lower = iota((LANES, LANES), 0) == here % LANES
        values = jnp.concatenate(
            [
                jnp.where(upper, r.astype(jnp.float32), 0.0),
                jnp.where(upper, iota((rows, LANES), 1).astype(jnp.float32), 0.0),
            ],
            axis=0,
        )
        return acc + dot_nt(
            values.astype(jnp.bfloat16), lower.astype(jnp.float32).astype(jnp.bfloat16)
        )

    out[...] = lax.fori_loop(
        0, rows, step, jnp.zeros((2 * rows, LANES), jnp.float32), unroll=4
    ).astype(jnp.int32)


def near_kernel(source, near_blocks, target, charges, out, table, picked):
    step = pl.program_id(0)
    pairs = picked.shape[0]
    blocks = out.shape[0]

    @pl.when(step == 0)
    def _():
        for d in range(charges.shape[0]):
            table[d * blocks : (d + 1) * blocks] = charges[d].astype(jnp.float32)
        out[...] = jnp.zeros_like(out)

    def pick(p, carry):
        picked[pl.ds(p, 1), :] = table[pl.ds(source[step * pairs + p], 1), :]
        return carry

    lax.fori_loop(0, pairs, pick, 0, unroll=8)
    terms = block_sums(near_blocks, picked[...])
    owner = (iota((blocks, pairs), 0) == target[...]).astype(jnp.float32).astype(jnp.bfloat16)
    high, low = split(terms)
    out[...] += dot(owner, high) + dot(owner, low)


def tile_loop(half, rows, cols, groups, body):
    per_slab = cols // SLABS
    low = jnp.maximum(half * (rows // HALVES) - 1, 0)
    high = (half + 1) * (rows // HALVES)
    per_row = per_slab * groups

    def step(n, carry):
        row = low + n // per_row
        left = n % per_row
        body([row * cols + s * per_slab + left // groups for s in range(SLABS)], left % groups)
        return carry

    lax.fori_loop(0, (high - low) * per_row, step, 0)


def lanes_inside(patches, d, t, groups, half):
    extra = patches[d, 16 * groups :, :].astype(jnp.float32)
    picked = jnp.where(iota(extra.shape, 0) == t, extra, 0.0)
    cells = jnp.sum(picked, axis=0, keepdims=True) - (half * LANES).astype(jnp.float32)
    return jnp.broadcast_to((cells >= 0.0) & (cells < LANES), (16, LANES))


def scatter_kernel(
    cols, place, shift, start, patches, table, third, own_out, other_out, lines, *slabs
):
    half = place[0]
    chunk = pl.program_id(0)
    devices, held, _ = patches.shape
    groups = (held - 16) // 16
    blocks = groups * GROUP
    freqs = table.shape[0]
    owner = iota((16, LANES), 1) // 4
    plane = iota((16, LANES), 0) % QUAD

    @pl.when(chunk == 0)
    def _():
        def clear(n, carry):
            for slab in slabs:
                slab[pl.ds(pl.multiple_of(n * SLAB, 8), SLAB), :] = jnp.zeros(
                    (SLAB, LANES), jnp.float32
                )
            return carry

        lax.fori_loop(0, slabs[0].shape[0] // SLAB, clear, 0)

        def tile(numbers, t):
            values = []
            for d in numbers:
                part = patches[d, pl.ds(pl.multiple_of(16 * t, 16), 16), :].astype(jnp.float32)
                values.append(jnp.where(lanes_inside(patches, d, t, groups, half), part, 0.0))

            def one(k, carry):
                spot = owner == k
                sums = []
                for s in range(SLABS):
                    b = numbers[s] * blocks + t * GROUP + k
                    at = start[b]
                    moved = pltpu.roll(jnp.where(spot, values[s], 0.0), shift[b], 1)
                    here = plane < QUAD - (at & (QUAD - 1))
                    near = slabs[s][pl.ds(at, 16), :] + jnp.where(here, moved, 0.0)
                    at_next = at + (SLAB - QUAD)
                    far = slabs[s][pl.ds(at_next, 16), :] + jnp.where(here, 0.0, moved)
                    sums.append((at, near, at_next, far))
                for s, (at, near, at_next, far) in enumerate(sums):
                    slabs[s][pl.ds(at, 16), :] = near
                    slabs[s][pl.ds(at_next, 16), :] = far
                return carry

            lax.fori_loop(0, GROUP, one, 0, unroll=UNROLL)

        tile_loop(half, devices // cols, cols, groups, tile)

    @pl.when(chunk < G // ZC)
    def _():
        for z in range(0, ZC, QUAD):
            base = pl.multiple_of((chunk * (ZC // QUAD) + z // QUAD) * SLAB, 8)
            planes = []
            for q in range(QUAD):
                parts = []
                for s in range(SLABS):
                    part = slabs[s][pl.ds(base + (PAD + q), PIECE, stride=QUAD), :]
                    if s > 0:
                        at = base + (PAD + QUAD * PIECE + q)
                        over = slabs[s - 1][pl.ds(at, 8, stride=QUAD), :]
                        part = jnp.concatenate([part[:8] + over, part[8:]], axis=0)
                    parts.append(part.astype(jnp.bfloat16))
                planes.append(jnp.concatenate(parts, axis=0))
            field = dot(table[...], jnp.concatenate(planes, axis=1))
            for q in range(QUAD):
                part = field[:, LANES * q : LANES * q + LANES]
                lines[pl.ds(chunk * ZC + z + q, freqs, stride=STRIDE), :] = part

    @pl.when(chunk >= G // ZC)
    def _():
        fs = third.shape[0] // 2
        for g in range(0, BATCH, 2):
            pair = []
            for n in (g, g + 1):
                at = ((chunk - G // ZC) * BATCH + n) * STRIDE
                pair.append(lines[pl.ds(at, G), :].astype(jnp.bfloat16))
            field = dot(third[...], jnp.concatenate(pair, axis=1)).astype(jnp.bfloat16)
            for n in range(2):
                own_out[g + n] = field[:fs, LANES * n : LANES * n + LANES]
                other_out[g + n] = field[fs:, LANES * n : LANES * n + LANES]


def spectrum_kernel(own, other, weights, first, first_back, own_out, other_out):
    count, freqs, _ = weights.shape
    step = max(1, G // freqs)
    rows = step * freqs
    for g in range(0, count, step):
        part = slice(g, g + step)
        line = jnp.concatenate(
            [own[part].reshape(rows, LANES), other[part].reshape(rows, LANES)], axis=1
        )
        s = dot(line, first[...]) * weights[part].reshape(rows, P_SIZE)
        line = dot(s.astype(jnp.bfloat16), first_back[...]).astype(jnp.bfloat16)
        own_out[part] = line[:, :LANES].reshape(step, freqs, LANES)
        other_out[part] = line[:, LANES:].reshape(step, freqs, LANES)


def sample_kernel(
    cols, place, shift, start, patches, own, other, table, third, out, lines, cells
):
    half = place[0]
    step = pl.program_id(0)
    devices, held, _ = out.shape
    groups = held // 16
    blocks = groups * GROUP
    freqs = table.shape[1]
    batches = freqs // BATCH
    chunk = step - batches
    owner = iota((16, LANES), 1) // 4
    plane = iota((16, LANES), 0) % QUAD

    @pl.when(step < batches)
    def _():
        for g in range(0, BATCH, 2):
            pair = [jnp.concatenate([own[n], other[n]], axis=0) for n in (g, g + 1)]
            field = dot(third[...], jnp.concatenate(pair, axis=1))
            for n in range(2):
                at = (step * BATCH + g + n) * STRIDE
                lines[pl.ds(at, G), :] = field[:, LANES * n : LANES * n + LANES]

    @pl.when(step >= batches)
    def _():
        for z in range(0, ZC, QUAD):
            planes = [
                lines[pl.ds(chunk * ZC + z + q, freqs, stride=STRIDE), :].astype(jnp.bfloat16)
                for q in range(QUAD)
            ]
            field = dot(table[...], jnp.concatenate(planes, axis=1))
            base = pl.multiple_of((chunk * (ZC // QUAD) + z // QUAD) * CELLS, 8)
            for q in range(QUAD):
                part = field[:, LANES * q : LANES * q + LANES]
                cells[pl.ds(base + (PAD + q), G, stride=QUAD), :] = part

    @pl.when(step == pl.num_programs(0) - 1)
    def _():
        out[...] = jnp.zeros_like(out)

        def tile(numbers, t):
            def one(k, sums):
                spot = owner == k
                new = []
                for s in range(SLABS):
                    b = numbers[s] * blocks + t * GROUP + k
                    at = start[b]
                    here = plane < QUAD - (at & (QUAD - 1))
                    near = cells[pl.ds(at, 16), :]
                    far = cells[pl.ds(at + (CELLS - QUAD), 16), :]
                    moved = pltpu.roll(jnp.where(here, near, far), shift[b], 1)
                    new.append(jnp.where(spot, moved, sums[s]))
                return tuple(new)

            zero = (jnp.zeros((16, LANES), jnp.float32),) * SLABS
            sums = lax.fori_loop(0, GROUP, one, zero, unroll=UNROLL)
            for s, d in enumerate(numbers):
                inside = lanes_inside(patches, d, t, groups, half)
                out[d, pl.ds(pl.multiple_of(16 * t, 16), 16), :] = jnp.where(
                    inside, sums[s], 0.0
                ).astype(jnp.bfloat16)

        tile_loop(half, devices // cols, cols, groups, tile)


def finish_kernel(values, interpolate, near, inverse, out, total):
    blocks = near.shape[0]
    groups = values.shape[1] // 16
    rows, lanes = patch_places(blocks)
    summed = values[0].astype(jnp.float32)
    for d in range(1, values.shape[0]):
        summed = summed + values[d].astype(jnp.float32)
    spread = jnp.concatenate([summed[16 * t : 16 * t + 16] for t in range(groups)], axis=1)
    patch = jnp.zeros((blocks, LANES), jnp.float32)
    for part in split(spread):
        for i in range(4):
            turned = dot_nt(lanes[i], part).astype(jnp.bfloat16)
            patch = patch + dot(turned, rows[i])
    total[...] = block_sums(interpolate, patch) + near[...]
    count = out.shape[0]
    even = total[pl.ds(0, count, stride=2), :]
    odd = total[pl.ds(1, count, stride=2), :]
    total[:count] = jnp.where(iota(even.shape, 1) < BLK, even, odd)
    upper = inverse[:count]
    lower = inverse[count:]

    def step(u, acc):
        row = jnp.broadcast_to(total[pl.ds(u, 1), :], lower.shape)
        return jnp.where(upper == u, lane_gather(row, lower), acc)

    out[...] = lax.fori_loop(0, count, step, jnp.zeros(out.shape, jnp.float32), unroll=4)


def struct(shape, dtype):
    return jax.ShapeDtypeStruct(shape, dtype)


def whole(shape):
    return pl.BlockSpec(shape, lambda *_: (0,) * len(shape))


def params(mib):
    return pltpu.CompilerParams(vmem_limit_bytes=mib * MB)


def beside(array, axis, dim):
    count = lax.axis_size(axis)
    up = [(i, i + 1) for i in range(count - 1)]
    before = lax.ppermute(array, axis, up)
    after = lax.ppermute(array, axis, [(j, i) for i, j in up])
    return jnp.concatenate([before, array, after], axis=dim)


def body(
    charges,
    panel_order,
    patch_anchor,
    project,
    interpolate,
    kernel_spectrum,
    near_pairs,
    near_blocks,
):
    axes = ("row", "col")
    rows = lax.axis_size("row")
    cols = lax.axis_size("col")
    devices = rows * cols
    row_at = lax.axis_index("row")
    col_at = lax.axis_index("col")
    half = col_at % HALVES
    mates = [(c, c ^ 1) for c in range(cols)]
    blocks = project.shape[0]
    groups = blocks // GROUP
    panels = charges.shape[0]
    strips = panels // LANES
    gs, fs, _ = kernel_spectrum.shape
    held = 16 * groups + 16

    order = panel_order.reshape(strips, LANES)
    block_charges, sent = pl.pallas_call(
        project_kernel,
        out_shape=(
            struct((blocks, LANES), jnp.bfloat16),
            struct((held, LANES), jnp.bfloat16),
        ),
        in_specs=[pl.BlockSpec(memory_space=pltpu.HBM)] * 4,
        scratch_shapes=[
            pltpu.VMEM((strips, LANES), jnp.bfloat16),
            pltpu.VMEM((strips, LANES), jnp.int32),
            pltpu.VMEM(project.shape, jnp.bfloat16),
            pltpu.VMEM(patch_anchor.shape, jnp.int32),
            pltpu.VMEM((strips, LANES), jnp.float32),
            pltpu.VMEM((blocks, LANES), jnp.float32),
            pltpu.SemaphoreType.DMA((4,)),
        ],
        compiler_params=params(32),
        name="project",
    )(
        charges.reshape(strips, LANES),
        order,
        project,
        patch_anchor,
    )
    copies = jnp.broadcast_to(sent[None], (devices, held, LANES))
    gathered = lax.all_to_all(copies, axes, split_axis=0, concat_axis=0, tiled=True)
    inverse = pl.pallas_call(
        inverse_kernel,
        out_shape=struct((2 * strips, LANES), jnp.int32),
        compiler_params=params(32),
        name="inverse",
    )(order)

    around = beside(block_charges[None, None], "row", 0)
    cas = jnp.asarray(CAS)
    second = lax.dynamic_slice_in_dim(cas[:, :G], row_at * gs, gs, axis=0)
    third = jnp.concatenate(
        [lax.dynamic_slice_in_dim(cas[:, :G], c * fs, fs, axis=0) for c in (col_at, col_at ^ 1)],
        axis=0,
    )
    first = jnp.concatenate(
        [lax.dynamic_slice_in_dim(cas, h * LANES, LANES, axis=0) for h in (half, 1 - half)],
        axis=0,
    )
    (gathered, around, inverse, second, second_back, third, third_back, first, first_back) = (
        lax.optimization_barrier(
            (gathered, around, inverse, second, second.T, third, third.T, first, first.T)
        )
    )
    around = beside(around, "col", 1).reshape(9, blocks, LANES)
    anchors = gathered[:, 17 * groups : 17 * groups + 3].astype(jnp.int32)
    lane = 4 * (jnp.arange(blocks, dtype=jnp.int32) % GROUP)
    forth = ((anchors[:, 0] - lane) & (LANES - 1)).reshape(devices * blocks)
    back = ((lane - anchors[:, 0]) & (LANES - 1)).reshape(devices * blocks)
    group = anchors[:, 2] // QUAD
    inner = PAD + QUAD * anchors[:, 1] + anchors[:, 2] % QUAD
    piece = (jnp.arange(devices, dtype=jnp.int32) % cols * SLABS // cols * PIECE)[:, None]
    slab_at = (group * SLAB + inner - QUAD * piece).reshape(devices * blocks)
    cell_at = (group * CELLS + inner).reshape(devices * blocks)
    place = half.astype(jnp.int32).reshape(1)

    smem = pl.BlockSpec(memory_space=pltpu.SMEM)
    chunks = G // ZC
    batches = gs // BATCH
    lines_type = struct((gs, fs, LANES), jnp.bfloat16)
    late = pl.BlockSpec((BATCH, fs, LANES), lambda n: (jnp.maximum(n - chunks, 0), 0, 0))
    own, other = pl.pallas_call(
        functools.partial(scatter_kernel, cols),
        grid=(chunks + batches,),
        in_specs=[smem] * 3 + [whole(gathered.shape), whole(second.shape), whole(third.shape)],
        out_specs=(late, late),
        out_shape=(lines_type, lines_type),
        scratch_shapes=[pltpu.VMEM((gs * STRIDE, LANES), jnp.float32)]
        + [pltpu.VMEM(((G // QUAD + 1) * SLAB, LANES), jnp.float32)] * SLABS,
        compiler_params=params(58),
        name="scatter",
    )(place, forth, slab_at, gathered, second, third)
    other = lax.ppermute(other, "col", mates)
    other, around = lax.optimization_barrier((other, around))

    part = lambda shape: pl.BlockSpec((BATCH,) + shape, lambda n: (n, 0, 0))
    own, other = pl.pallas_call(
        spectrum_kernel,
        grid=(batches,),
        in_specs=[
            part((fs, LANES)),
            part((fs, LANES)),
            part((fs, P_SIZE)),
            whole((G, P_SIZE)),
            whole((P_SIZE, G)),
        ],
        out_specs=(part((fs, LANES)), part((fs, LANES))),
        out_shape=(lines_type, lines_type),
        compiler_params=params(56),
        name="spectrum",
    )(own, other, kernel_spectrum, first, first_back)
    other = lax.ppermute(other, "col", mates)

    source = near_pairs[1]
    source_device = source // blocks
    code = (source_device // cols - row_at + 1) * 3 + (source_device % cols - col_at + 1)
    wanted = code * blocks + source % blocks
    target = near_pairs[0] - (row_at * cols + col_at) * blocks
    pairs = near_blocks.shape[0]
    near = pl.pallas_call(
        near_kernel,
        grid=(pairs // blocks,),
        in_specs=[
            smem,
            pl.BlockSpec((blocks, BLK * BLK), lambda n: (n, 0)),
            pl.BlockSpec((1, blocks), lambda n: (0, n)),
            whole((9, blocks, LANES)),
        ],
        out_specs=whole((blocks, LANES)),
        out_shape=struct((blocks, LANES), jnp.float32),
        scratch_shapes=[
            pltpu.VMEM((9 * blocks, LANES), jnp.float32),
            pltpu.VMEM((blocks, LANES), jnp.float32),
        ],
        compiler_params=params(48),
        name="near",
    )(wanted, near_blocks, target.reshape(1, pairs), around)
    other, near = lax.optimization_barrier((other, near))
    early = pl.BlockSpec((BATCH, fs, LANES), lambda n: (jnp.minimum(n, batches - 1), 0, 0))
    values = pl.pallas_call(
        functools.partial(sample_kernel, cols),
        grid=(batches + chunks,),
        in_specs=[smem] * 3
        + [whole(gathered.shape), early, early, whole((G, gs)), whole((G, 2 * fs))],
        out_specs=whole((devices, 16 * groups, LANES)),
        out_shape=struct((devices, 16 * groups, LANES), jnp.bfloat16),
        scratch_shapes=[
            pltpu.VMEM((gs * STRIDE, LANES), jnp.float32),
            pltpu.VMEM(((G // QUAD + 1) * CELLS, LANES), jnp.float32),
        ],
        compiler_params=params(58),
        name="sample",
    )(place, back, cell_at, gathered, own, other, second_back, third_back)
    values = lax.all_to_all(values, axes, split_axis=0, concat_axis=0, tiled=True)

    result = pl.pallas_call(
        finish_kernel,
        out_shape=struct((strips, LANES), jnp.float32),
        scratch_shapes=[pltpu.VMEM((blocks, LANES), jnp.float32)],
        compiler_params=params(32),
        name="finish",
    )(values, interpolate, near, inverse)
    return result.reshape(panels)


def solution(mesh):
    placed = (
        P(("row", "col")),
        P(("row", "col")),
        P(None, ("row", "col")),
        P(("row", "col"), None),
        P(("row", "col"), None),
        P("row", "col", None),
        P(None, ("row", "col")),
        P(("row", "col"), None),
    )
    return jax.shard_map(
        body, mesh=mesh, in_specs=placed, out_specs=P(("row", "col")), check_vma=False
    )
```

```python
import functools

import jax
import jax.numpy as jnp
import ml_dtypes
import numpy as np
from jax import lax
from jax.experimental import pallas as pl
from jax.experimental.pallas import tpu as pltpu
from jax.sharding import PartitionSpec as P

G = 256
P_SIZE = 512
BLK = 64
PTS = 64
LANES = 128
GROUP = LANES // 4
HALVES = G // LANES
SLABS = 4
PIECE = G // SLABS
QUAD = 4
PAD = 8
SLAB = PAD + QUAD * PIECE + 32
CELLS = PAD + QUAD * G + 16
STRIDE = G + 1
BATCH = 8
LINES = 16
UNROLL = 16
UNROLL_PLANES = 8
MB = 1 << 20
NT = (((1,), (1,)), ((), ()))


def cas_table():
    index = np.arange(P_SIZE, dtype=np.int64)
    phase = (index[:, None] * index[None, :] % P_SIZE).astype(np.float64) * (2.0 * np.pi / P_SIZE)
    return ((np.cos(phase) + np.sin(phase)) / np.sqrt(P_SIZE)).astype(ml_dtypes.bfloat16)


CAS = cas_table()


def dot(a, b):
    return jnp.dot(a, b, preferred_element_type=jnp.float32)


def dot_nt(a, b):
    return lax.dot_general(a, b, NT, preferred_element_type=jnp.float32)


def iota(shape, dim):
    return lax.broadcasted_iota(jnp.int32, shape, dim)


def split(value):
    high = value.astype(jnp.bfloat16)
    return high, (value - high.astype(jnp.float32)).astype(jnp.bfloat16)


def lane_gather(table, index):
    return jnp.take_along_axis(table, index, axis=1, mode="promise_in_bounds")


def block_sums(mats, vecs):
    rows = vecs.shape[0]
    pair = jnp.concatenate([vecs, vecs], axis=1)
    total = jnp.zeros((2 * rows, LANES), jnp.float32)
    for t in range(mats.shape[1] // 256):
        high, low = split(mats[:, 256 * t : 256 * t + 256].astype(jnp.float32) * pair)
        owner = iota((256, LANES), 0) // BLK + 4 * t
        table = (owner == iota((256, LANES), 1) % BLK).astype(jnp.bfloat16)
        total = total + dot(jnp.concatenate([high, low], axis=0), table)
    return total[:rows] + total[rows:]


def patch_places(blocks):
    lanes = [
        (iota((blocks, 4 * blocks), 1) == 4 * iota((blocks, 4 * blocks), 0) + i).astype(
            jnp.bfloat16
        )
        for i in range(4)
    ]
    row = iota((16, LANES), 0)
    rows = [
        (iota((16, LANES), 1) % PTS == 16 * i + row).astype(jnp.bfloat16)
        for i in range(4)
    ]
    return rows, lanes


def project_kernel(
    charges_in,
    order_in,
    project_in,
    anchors_in,
    charge_out,
    patch_out,
    charges,
    order,
    project,
    anchors,
    table,
    doubled,
    sems,
):
    blocks = charge_out.shape[0]
    groups = blocks // GROUP
    pairs = ((charges_in, charges), (order_in, order), (project_in, project), (anchors_in, anchors))
    copies = [pltpu.make_async_copy(a, b, sems.at[n]) for n, (a, b) in enumerate(pairs)]
    for copy in copies:
        copy.start()
    copies[0].wait()
    copies[1].wait()
    table[...] = charges[...].astype(jnp.float32)
    strips = table.shape[0]
    upper = order[...] // LANES
    lower = order[...] % LANES

    def step(u, acc):
        row = jnp.broadcast_to(table[pl.ds(u, 1), :], lower.shape)
        return jnp.where(upper == u, lane_gather(row, lower), acc)

    slots = lax.fori_loop(0, strips, step, jnp.zeros(lower.shape, jnp.float32), unroll=4)
    swapped = pltpu.roll(slots, BLK, 1)
    left = iota(slots.shape, 1) < BLK
    doubled[pl.ds(0, strips, stride=2), :] = jnp.where(left, slots, swapped)
    doubled[pl.ds(1, strips, stride=2), :] = jnp.where(left, swapped, slots)
    twice = doubled[...]
    charge_out[...] = twice.astype(jnp.bfloat16)
    copies[2].wait()
    copies[3].wait()
    patch = block_sums(project, twice)
    patch = jnp.where(iota(patch.shape, 1) < PTS, patch, 0.0).astype(jnp.bfloat16)
    rows, lanes = patch_places(blocks)
    corner = anchors[...].astype(jnp.float32)
    spread = jnp.zeros((16, 4 * blocks), jnp.float32)
    cells = (iota((8, 4 * blocks), 1) % 4).astype(jnp.float32)
    start = jnp.broadcast_to(corner[:1], (8, blocks)).astype(jnp.bfloat16)
    for i in range(4):
        spread = spread + dot(dot_nt(rows[i], patch).astype(jnp.bfloat16), lanes[i])
        cells = cells + dot(start, lanes[i])
    tiles = [slice(LANES * t, LANES * t + LANES) for t in range(groups)]
    for t in range(groups):
        patch_out[16 * t : 16 * t + 16] = spread[:, tiles[t]].astype(jnp.bfloat16)
    extra = [cells[:1, tile] for tile in tiles] + [corner]
    extra.append(jnp.zeros((16 - groups - corner.shape[0], LANES), jnp.float32))
    patch_out[16 * groups :] = jnp.concatenate(extra, axis=0).astype(jnp.bfloat16)


def inverse_kernel(order, out):
    rows = order.shape[0]

    def step(r, acc):
        here = order[pl.ds(r, 1), :]
        upper = iota((rows, LANES), 0) == here // LANES
        lower = iota((LANES, LANES), 0) == here % LANES
        values = jnp.concatenate(
            [
                jnp.where(upper, r.astype(jnp.float32), 0.0),
                jnp.where(upper, iota((rows, LANES), 1).astype(jnp.float32), 0.0),
            ],
            axis=0,
        )
        return acc + dot_nt(
            values.astype(jnp.bfloat16), lower.astype(jnp.float32).astype(jnp.bfloat16)
        )

    out[...] = lax.fori_loop(
        0, rows, step, jnp.zeros((2 * rows, LANES), jnp.float32), unroll=4
    ).astype(jnp.int32)


def near_kernel(source, near_blocks, target, charges, out, table, picked):
    step = pl.program_id(0)
    pairs = picked.shape[0]
    blocks = out.shape[0]

    @pl.when(step == 0)
    def _():
        for d in range(charges.shape[0]):
            table[d * blocks : (d + 1) * blocks] = charges[d].astype(jnp.float32)
        out[...] = jnp.zeros_like(out)

    def pick(p, carry):
        picked[pl.ds(p, 1), :] = table[pl.ds(source[step * pairs + p], 1), :]
        return carry

    lax.fori_loop(0, pairs, pick, 0, unroll=8)
    terms = block_sums(near_blocks, picked[...])
    owner = (iota((blocks, pairs), 0) == target[...]).astype(jnp.float32).astype(jnp.bfloat16)
    high, low = split(terms)
    out[...] += dot(owner, high) + dot(owner, low)


def table_rows(cas, numbers, count):
    parts = [cas[pl.ds(pl.multiple_of(n * count, 16), count), :G] for n in numbers]
    return jnp.concatenate(parts, axis=0) if len(parts) > 1 else parts[0]


def turned(rows):
    unit = (iota((G, G), 0) == iota((G, G), 1)).astype(jnp.float32).astype(jnp.bfloat16)
    return dot_nt(unit, rows).astype(jnp.bfloat16)


def tile_loop(half, rows, cols, groups, body):
    per_slab = cols // SLABS
    low = jnp.maximum(half * (rows // HALVES) - 1, 0)
    high = (half + 1) * (rows // HALVES)
    per_row = per_slab * groups

    def step(n, carry):
        row = low + n // per_row
        left = n % per_row
        body([row * cols + s * per_slab + left // groups for s in range(SLABS)], left % groups)
        return carry

    lax.fori_loop(0, (high - low) * per_row, step, 0)


def lanes_inside(patches, d, t, groups, half):
    extra = patches[d, 16 * groups :, :].astype(jnp.float32)
    picked = jnp.where(iota(extra.shape, 0) == t, extra, 0.0)
    cells = jnp.sum(picked, axis=0, keepdims=True) - (half * LANES).astype(jnp.float32)
    return jnp.broadcast_to((cells >= 0.0) & (cells < LANES), (16, LANES))


def scatter_kernel(
    cols, gs, fs, place, shift, start, patches, cas, own_out, other_out, lines, *slabs
):
    half = place[0]
    step = pl.program_id(0)
    devices, held, _ = patches.shape
    groups = (held - 16) // 16
    blocks = groups * GROUP
    owner = iota((16, LANES), 1) // 4
    plane = iota((16, LANES), 0) % QUAD

    @pl.when(step == 0)
    def _():
        def clear(n, carry):
            for slab in slabs:
                slab[pl.ds(pl.multiple_of(n * SLAB, 8), SLAB), :] = jnp.zeros(
                    (SLAB, LANES), jnp.float32
                )
            return carry

        lax.fori_loop(0, slabs[0].shape[0] // SLAB, clear, 0)

        def tile(numbers, t):
            values = []
            for d in numbers:
                part = patches[d, pl.ds(pl.multiple_of(16 * t, 16), 16), :].astype(jnp.float32)
                values.append(jnp.where(lanes_inside(patches, d, t, groups, half), part, 0.0))

            def one(k, carry):
                spot = owner == k
                sums = []
                for s in range(SLABS):
                    b = numbers[s] * blocks + t * GROUP + k
                    at = start[b]
                    moved = pltpu.roll(jnp.where(spot, values[s], 0.0), shift[b], 1)
                    here = plane < QUAD - (at & (QUAD - 1))
                    near = slabs[s][pl.ds(at, 16), :] + jnp.where(here, moved, 0.0)
                    at_next = at + (SLAB - QUAD)
                    far = slabs[s][pl.ds(at_next, 16), :] + jnp.where(here, 0.0, moved)
                    sums.append((at, near, at_next, far))
                for s, (at, near, at_next, far) in enumerate(sums):
                    slabs[s][pl.ds(at, 16), :] = near
                    slabs[s][pl.ds(at_next, 16), :] = far
                return carry

            lax.fori_loop(0, GROUP, one, 0, unroll=UNROLL)

        tile_loop(half, devices // cols, cols, groups, tile)

        table = table_rows(cas, [place[1]], gs)

        def planes(n, carry):
            base = pl.multiple_of(n * SLAB, 8)
            sheets = []
            for q in range(QUAD):
                parts = []
                for s in range(SLABS):
                    part = slabs[s][pl.ds(base + (PAD + q), PIECE, stride=QUAD), :]
                    if s > 0:
                        at = base + (PAD + QUAD * PIECE + q)
                        over = slabs[s - 1][pl.ds(at, 8, stride=QUAD), :]
                        part = jnp.concatenate([part[:8] + over, part[8:]], axis=0)
                    parts.append(part.astype(jnp.bfloat16))
                sheets.append(jnp.concatenate(parts, axis=0))
            field = dot(table, jnp.concatenate(sheets, axis=1))
            for q in range(QUAD):
                part = field[:, LANES * q : LANES * q + LANES]
                lines[pl.ds(n * QUAD + q, gs, stride=STRIDE), :] = part
            return carry

        lax.fori_loop(0, G // QUAD, planes, 0, unroll=UNROLL_PLANES)

    @pl.when(step > 0)
    def _():
        third = table_rows(cas, [place[2], place[2] ^ 1], fs)
        for g in range(0, LINES, 2):
            pair = []
            for n in (g, g + 1):
                at = ((step - 1) * LINES + n) * STRIDE
                pair.append(lines[pl.ds(at, G), :].astype(jnp.bfloat16))
            field = dot(third, jnp.concatenate(pair, axis=1)).astype(jnp.bfloat16)
            for n in range(2):
                own_out[g + n] = field[:fs, LANES * n : LANES * n + LANES]
                other_out[g + n] = field[fs:, LANES * n : LANES * n + LANES]


def spectrum_kernel(place, own, other, weights, cas, own_out, other_out):
    tiles = [pl.ds(pl.multiple_of(h * LANES, LANES), LANES) for h in (place[0], 1 - place[0])]
    first = jnp.concatenate([cas[tile, :] for tile in tiles], axis=0)
    first_back = jnp.concatenate([cas[:, tile] for tile in tiles], axis=1)
    count, freqs, _ = weights.shape
    step = max(1, G // freqs)
    rows = step * freqs
    for g in range(0, count, step):
        part = slice(g, g + step)
        line = jnp.concatenate(
            [own[part].reshape(rows, LANES), other[part].reshape(rows, LANES)], axis=1
        )
        s = dot(line, first) * weights[part].reshape(rows, P_SIZE)
        line = dot(s.astype(jnp.bfloat16), first_back).astype(jnp.bfloat16)
        own_out[part] = line[:, :LANES].reshape(step, freqs, LANES)
        other_out[part] = line[:, LANES:].reshape(step, freqs, LANES)


def sample_kernel(
    cols, place, shift, start, patches, own, other, cas, out, second, third, lines, cells
):
    half = place[0]
    step = pl.program_id(0)
    devices, held, _ = out.shape
    groups = held // 16
    blocks = groups * GROUP
    gs = second.shape[1]
    owner = iota((16, LANES), 1) // 4
    plane = iota((16, LANES), 0) % QUAD

    @pl.when(step == 0)
    def _():
        second[...] = turned(table_rows(cas, [place[1]], gs))
        third[...] = turned(table_rows(cas, [place[2], place[2] ^ 1], own.shape[1]))

    for g in range(0, LINES, 2):
        pair = [jnp.concatenate([own[n], other[n]], axis=0) for n in (g, g + 1)]
        field = dot(third[...], jnp.concatenate(pair, axis=1))
        for n in range(2):
            at = (step * LINES + g + n) * STRIDE
            lines[pl.ds(at, G), :] = field[:, LANES * n : LANES * n + LANES]

    @pl.when(step == pl.num_programs(0) - 1)
    def _():
        def planes(n, carry):
            sheets = [
                lines[pl.ds(n * QUAD + q, gs, stride=STRIDE), :].astype(jnp.bfloat16)
                for q in range(QUAD)
            ]
            field = dot(second[...], jnp.concatenate(sheets, axis=1))
            base = pl.multiple_of(n * CELLS, 8)
            for q in range(QUAD):
                part = field[:, LANES * q : LANES * q + LANES]
                cells[pl.ds(base + (PAD + q), G, stride=QUAD), :] = part
            return carry

        lax.fori_loop(0, G // QUAD, planes, 0, unroll=UNROLL_PLANES)
        out[...] = jnp.zeros_like(out)

        def tile(numbers, t):
            def one(k, sums):
                spot = owner == k
                new = []
                for s in range(SLABS):
                    b = numbers[s] * blocks + t * GROUP + k
                    at = start[b]
                    here = plane < QUAD - (at & (QUAD - 1))
                    near = cells[pl.ds(at, 16), :]
                    far = cells[pl.ds(at + (CELLS - QUAD), 16), :]
                    moved = pltpu.roll(jnp.where(here, near, far), shift[b], 1)
                    new.append(jnp.where(spot, moved, sums[s]))
                return tuple(new)

            zero = (jnp.zeros((16, LANES), jnp.float32),) * SLABS
            sums = lax.fori_loop(0, GROUP, one, zero, unroll=UNROLL)
            for s, d in enumerate(numbers):
                inside = lanes_inside(patches, d, t, groups, half)
                out[d, pl.ds(pl.multiple_of(16 * t, 16), 16), :] = jnp.where(
                    inside, sums[s], 0.0
                ).astype(jnp.bfloat16)

        tile_loop(half, devices // cols, cols, groups, tile)


def finish_kernel(values, interpolate, near, inverse, out, total):
    blocks = near.shape[0]
    groups = values.shape[1] // 16
    rows, lanes = patch_places(blocks)
    summed = values[0].astype(jnp.float32)
    for d in range(1, values.shape[0]):
        summed = summed + values[d].astype(jnp.float32)
    spread = jnp.concatenate([summed[16 * t : 16 * t + 16] for t in range(groups)], axis=1)
    patch = jnp.zeros((blocks, LANES), jnp.float32)
    for part in split(spread):
        for i in range(4):
            column = dot_nt(lanes[i], part).astype(jnp.bfloat16)
            patch = patch + dot(column, rows[i])
    total[...] = block_sums(interpolate, patch) + near[...]
    count = out.shape[0]
    even = total[pl.ds(0, count, stride=2), :]
    odd = total[pl.ds(1, count, stride=2), :]
    total[:count] = jnp.where(iota(even.shape, 1) < BLK, even, odd)
    upper = inverse[:count]
    lower = inverse[count:]

    def step(u, acc):
        row = jnp.broadcast_to(total[pl.ds(u, 1), :], lower.shape)
        return jnp.where(upper == u, lane_gather(row, lower), acc)

    out[...] = lax.fori_loop(0, count, step, jnp.zeros(out.shape, jnp.float32), unroll=4)


def struct(shape, dtype):
    return jax.ShapeDtypeStruct(shape, dtype)


def whole(shape):
    return pl.BlockSpec(shape, lambda *_: (0,) * len(shape))


def params(mib):
    return pltpu.CompilerParams(vmem_limit_bytes=mib * MB)


def beside(array, axis, dim):
    count = lax.axis_size(axis)
    up = [(i, i + 1) for i in range(count - 1)]
    before = lax.ppermute(array, axis, up)
    after = lax.ppermute(array, axis, [(j, i) for i, j in up])
    return jnp.concatenate([before, array, after], axis=dim)


def body(
    charges,
    panel_order,
    patch_anchor,
    project,
    interpolate,
    kernel_spectrum,
    near_pairs,
    near_blocks,
):
    axes = ("row", "col")
    rows = lax.axis_size("row")
    cols = lax.axis_size("col")
    devices = rows * cols
    row_at = lax.axis_index("row")
    col_at = lax.axis_index("col")
    half = col_at % HALVES
    mates = [(c, c ^ 1) for c in range(cols)]
    blocks = project.shape[0]
    groups = blocks // GROUP
    panels = charges.shape[0]
    strips = panels // LANES
    gs, fs, _ = kernel_spectrum.shape
    held = 16 * groups + 16

    order = panel_order.reshape(strips, LANES)
    block_charges, sent = pl.pallas_call(
        project_kernel,
        out_shape=(
            struct((blocks, LANES), jnp.bfloat16),
            struct((held, LANES), jnp.bfloat16),
        ),
        in_specs=[pl.BlockSpec(memory_space=pltpu.HBM)] * 4,
        scratch_shapes=[
            pltpu.VMEM((strips, LANES), jnp.bfloat16),
            pltpu.VMEM((strips, LANES), jnp.int32),
            pltpu.VMEM(project.shape, jnp.bfloat16),
            pltpu.VMEM(patch_anchor.shape, jnp.int32),
            pltpu.VMEM((strips, LANES), jnp.float32),
            pltpu.VMEM((blocks, LANES), jnp.float32),
            pltpu.SemaphoreType.DMA((4,)),
        ],
        compiler_params=params(58),
        name="project",
    )(
        charges.reshape(strips, LANES),
        order,
        project,
        patch_anchor,
    )
    copies = jnp.broadcast_to(sent[None], (devices, held, LANES))
    gathered = lax.all_to_all(copies, axes, split_axis=0, concat_axis=0, tiled=True)
    inverse = pl.pallas_call(
        inverse_kernel,
        out_shape=struct((2 * strips, LANES), jnp.int32),
        compiler_params=params(32),
        name="inverse",
    )(order)

    around = beside(block_charges[None, None], "row", 0)
    gathered, around, inverse = lax.optimization_barrier((gathered, around, inverse))
    anchors = gathered[:, 17 * groups : 17 * groups + 3].astype(jnp.int32)
    lane = 4 * (jnp.arange(blocks, dtype=jnp.int32) % GROUP)
    forth = ((anchors[:, 0] - lane) & (LANES - 1)).reshape(devices * blocks)
    back = ((lane - anchors[:, 0]) & (LANES - 1)).reshape(devices * blocks)
    group = anchors[:, 2] // QUAD
    inner = PAD + QUAD * anchors[:, 1] + anchors[:, 2] % QUAD
    piece = (jnp.arange(devices, dtype=jnp.int32) % cols * SLABS // cols * PIECE)[:, None]
    slab_at = (group * SLAB + inner - QUAD * piece).reshape(devices * blocks)
    cell_at = (group * CELLS + inner).reshape(devices * blocks)
    place = jnp.stack([half, row_at, col_at]).astype(jnp.int32)
    cas = jnp.asarray(CAS)

    smem = pl.BlockSpec(memory_space=pltpu.SMEM)
    steps = gs // LINES
    lines_type = struct((gs, fs, LANES), jnp.bfloat16)
    late = pl.BlockSpec((LINES, fs, LANES), lambda n: (jnp.maximum(n - 1, 0), 0, 0))
    own, other = pl.pallas_call(
        functools.partial(scatter_kernel, cols, gs, fs),
        grid=(1 + steps,),
        in_specs=[smem] * 3 + [whole(gathered.shape), whole(cas.shape)],
        out_specs=(late, late),
        out_shape=(lines_type, lines_type),
        scratch_shapes=[pltpu.VMEM((gs * STRIDE, LANES), jnp.float32)]
        + [pltpu.VMEM(((G // QUAD + 1) * SLAB, LANES), jnp.float32)] * SLABS,
        compiler_params=params(53),
        name="scatter",
    )(place, forth, slab_at, gathered, cas)
    other = lax.ppermute(other, "col", mates)

    part = lambda shape: pl.BlockSpec((BATCH,) + shape, lambda n: (n, 0, 0))
    own, other = pl.pallas_call(
        spectrum_kernel,
        grid=(gs // BATCH,),
        in_specs=[
            smem,
            part((fs, LANES)),
            part((fs, LANES)),
            part((fs, P_SIZE)),
            whole(cas.shape),
        ],
        out_specs=(part((fs, LANES)), part((fs, LANES))),
        out_shape=(lines_type, lines_type),
        compiler_params=params(40),
        name="spectrum",
    )(place, own, other, kernel_spectrum, cas)
    other = lax.ppermute(other, "col", mates)

    early = pl.BlockSpec((LINES, fs, LANES), lambda n: (n, 0, 0))
    values = pl.pallas_call(
        functools.partial(sample_kernel, cols),
        grid=(steps,),
        in_specs=[smem] * 3 + [whole(gathered.shape), early, early, whole(cas.shape)],
        out_specs=whole((devices, 16 * groups, LANES)),
        out_shape=struct((devices, 16 * groups, LANES), jnp.bfloat16),
        scratch_shapes=[
            pltpu.VMEM((G, gs), jnp.bfloat16),
            pltpu.VMEM((G, 2 * fs), jnp.bfloat16),
            pltpu.VMEM((gs * STRIDE, LANES), jnp.float32),
            pltpu.VMEM(((G // QUAD + 1) * CELLS, LANES), jnp.float32),
        ],
        compiler_params=params(46),
        name="sample",
    )(place, back, cell_at, gathered, own, other, cas)
    values, around = lax.optimization_barrier((values, around))
    values = lax.all_to_all(values, axes, split_axis=0, concat_axis=0, tiled=True)

    around = beside(around, "col", 1).reshape(9, blocks, LANES)
    source = near_pairs[1]
    source_device = source // blocks
    code = (source_device // cols - row_at + 1) * 3 + (source_device % cols - col_at + 1)
    wanted = code * blocks + source % blocks
    target = near_pairs[0] - (row_at * cols + col_at) * blocks
    pairs = near_blocks.shape[0]
    near = pl.pallas_call(
        near_kernel,
        grid=(pairs // blocks,),
        in_specs=[
            smem,
            pl.BlockSpec((blocks, BLK * BLK), lambda n: (n, 0)),
            pl.BlockSpec((1, blocks), lambda n: (0, n)),
            whole((9, blocks, LANES)),
        ],
        out_specs=whole((blocks, LANES)),
        out_shape=struct((blocks, LANES), jnp.float32),
        scratch_shapes=[
            pltpu.VMEM((9 * blocks, LANES), jnp.float32),
            pltpu.VMEM((blocks, LANES), jnp.float32),
        ],
        compiler_params=params(56),
        name="near",
    )(wanted, near_blocks, target.reshape(1, pairs), around)

    result = pl.pallas_call(
        finish_kernel,
        out_shape=struct((strips, LANES), jnp.float32),
        scratch_shapes=[pltpu.VMEM((blocks, LANES), jnp.float32)],
        compiler_params=params(32),
        name="finish",
    )(values, interpolate, near, inverse)
    return result.reshape(panels)


def solution(mesh):
    placed = (
        P(("row", "col")),
        P(("row", "col")),
        P(None, ("row", "col")),
        P(("row", "col"), None),
        P(("row", "col"), None),
        P("row", "col", None),
        P(None, ("row", "col")),
        P(("row", "col"), None),
    )
    return jax.shard_map(
        body, mesh=mesh, in_specs=placed, out_specs=P(("row", "col")), check_vma=False
    )
```

```python
import functools

import jax
import jax.numpy as jnp
import ml_dtypes
import numpy as np
from jax import lax
from jax.experimental import pallas as pl
from jax.experimental.pallas import tpu as pltpu
from jax.sharding import PartitionSpec as P

G = 256
P_SIZE = 512
BLK = 64
PTS = 64
LANES = 128
GROUP = LANES // 4
HALVES = G // LANES
SLABS = 4
PIECE = G // SLABS
QUAD = 4
PAD = 8
SLAB = PAD + QUAD * PIECE + 32
CELLS = PAD + QUAD * G + 16
STRIDE = G + 1
BATCH = 8
LINES = 16
UNROLL = 16
UNROLL_PLANES = 8
MB = 1 << 20
NT = (((1,), (1,)), ((), ()))


def cas_table():
    index = np.arange(P_SIZE, dtype=np.int64)
    phase = (index[:, None] * index[None, :] % P_SIZE).astype(np.float64) * (2.0 * np.pi / P_SIZE)
    return ((np.cos(phase) + np.sin(phase)) / np.sqrt(P_SIZE)).astype(ml_dtypes.bfloat16)


CAS = cas_table()


def dot(a, b):
    return jnp.dot(a, b, preferred_element_type=jnp.float32)


def dot_nt(a, b):
    return lax.dot_general(a, b, NT, preferred_element_type=jnp.float32)


def iota(shape, dim):
    return lax.broadcasted_iota(jnp.int32, shape, dim)


def split(value):
    high = value.astype(jnp.bfloat16)
    return high, (value - high.astype(jnp.float32)).astype(jnp.bfloat16)


def lane_gather(table, index):
    return jnp.take_along_axis(table, index, axis=1, mode="promise_in_bounds")


def block_sums(mats, vecs):
    rows = vecs.shape[0]
    pair = jnp.concatenate([vecs, vecs], axis=1)
    total = jnp.zeros((2 * rows, LANES), jnp.float32)
    for t in range(mats.shape[1] // 256):
        high, low = split(mats[:, 256 * t : 256 * t + 256].astype(jnp.float32) * pair)
        owner = iota((256, LANES), 0) // BLK + 4 * t
        table = (owner == iota((256, LANES), 1) % BLK).astype(jnp.bfloat16)
        total = total + dot(jnp.concatenate([high, low], axis=0), table)
    return total[:rows] + total[rows:]


def patch_places(blocks):
    lanes = [
        (iota((blocks, 4 * blocks), 1) == 4 * iota((blocks, 4 * blocks), 0) + i).astype(
            jnp.bfloat16
        )
        for i in range(4)
    ]
    row = iota((16, LANES), 0)
    rows = [
        (iota((16, LANES), 1) % PTS == 16 * i + row).astype(jnp.bfloat16)
        for i in range(4)
    ]
    return rows, lanes


def project_kernel(
    charges_in,
    order_in,
    project_in,
    anchors_in,
    charge_out,
    patch_out,
    charges,
    order,
    project,
    anchors,
    table,
    doubled,
    sems,
):
    blocks = charge_out.shape[0]
    groups = blocks // GROUP
    pairs = ((charges_in, charges), (order_in, order), (project_in, project), (anchors_in, anchors))
    copies = [pltpu.make_async_copy(a, b, sems.at[n]) for n, (a, b) in enumerate(pairs)]
    for copy in copies:
        copy.start()
    copies[0].wait()
    copies[1].wait()
    table[...] = charges[...].astype(jnp.float32)
    strips = table.shape[0]
    upper = order[...] // LANES
    lower = order[...] % LANES

    def step(u, acc):
        row = jnp.broadcast_to(table[pl.ds(u, 1), :], lower.shape)
        return jnp.where(upper == u, lane_gather(row, lower), acc)

    slots = lax.fori_loop(0, strips, step, jnp.zeros(lower.shape, jnp.float32), unroll=4)
    swapped = pltpu.roll(slots, BLK, 1)
    left = iota(slots.shape, 1) < BLK
    doubled[pl.ds(0, strips, stride=2), :] = jnp.where(left, slots, swapped)
    doubled[pl.ds(1, strips, stride=2), :] = jnp.where(left, swapped, slots)
    twice = doubled[...]
    charge_out[...] = twice.astype(jnp.bfloat16)
    copies[2].wait()
    copies[3].wait()
    patch = block_sums(project, twice)
    patch = jnp.where(iota(patch.shape, 1) < PTS, patch, 0.0).astype(jnp.bfloat16)
    rows, lanes = patch_places(blocks)
    corner = anchors[...].astype(jnp.float32)
    spread = jnp.zeros((16, 4 * blocks), jnp.float32)
    cells = (iota((8, 4 * blocks), 1) % 4).astype(jnp.float32)
    start = jnp.broadcast_to(corner[:1], (8, blocks)).astype(jnp.bfloat16)
    for i in range(4):
        spread = spread + dot(dot_nt(rows[i], patch).astype(jnp.bfloat16), lanes[i])
        cells = cells + dot(start, lanes[i])
    tiles = [slice(LANES * t, LANES * t + LANES) for t in range(groups)]
    for t in range(groups):
        patch_out[16 * t : 16 * t + 16] = spread[:, tiles[t]].astype(jnp.bfloat16)
    extra = [cells[:1, tile] for tile in tiles] + [corner]
    extra.append(jnp.zeros((16 - groups - corner.shape[0], LANES), jnp.float32))
    patch_out[16 * groups :] = jnp.concatenate(extra, axis=0).astype(jnp.bfloat16)


def inverse_kernel(order, out):
    rows = order.shape[0]

    def step(r, acc):
        here = order[pl.ds(r, 1), :]
        upper = iota((rows, LANES), 0) == here // LANES
        lower = iota((LANES, LANES), 0) == here % LANES
        values = jnp.concatenate(
            [
                jnp.where(upper, r.astype(jnp.float32), 0.0),
                jnp.where(upper, iota((rows, LANES), 1).astype(jnp.float32), 0.0),
            ],
            axis=0,
        )
        return acc + dot_nt(
            values.astype(jnp.bfloat16), lower.astype(jnp.float32).astype(jnp.bfloat16)
        )

    out[...] = lax.fori_loop(
        0, rows, step, jnp.zeros((2 * rows, LANES), jnp.float32), unroll=4
    ).astype(jnp.int32)


def near_kernel(source, near_blocks, target, charges, out, table, picked):
    step = pl.program_id(0)
    pairs = picked.shape[0]
    blocks = out.shape[0]

    @pl.when(step == 0)
    def _():
        for d in range(charges.shape[0]):
            table[d * blocks : (d + 1) * blocks] = charges[d].astype(jnp.float32)
        out[...] = jnp.zeros_like(out)

    def pick(p, carry):
        picked[pl.ds(p, 1), :] = table[pl.ds(source[step * pairs + p], 1), :]
        return carry

    lax.fori_loop(0, pairs, pick, 0, unroll=8)
    terms = block_sums(near_blocks, picked[...])
    owner = (iota((blocks, pairs), 0) == target[...]).astype(jnp.float32).astype(jnp.bfloat16)
    high, low = split(terms)
    out[...] += dot(owner, high) + dot(owner, low)


def table_rows(cas, numbers, count):
    parts = [cas[pl.ds(pl.multiple_of(n * count, 16), count), :G] for n in numbers]
    return jnp.concatenate(parts, axis=0) if len(parts) > 1 else parts[0]


def turned(rows):
    unit = (iota((G, G), 0) == iota((G, G), 1)).astype(jnp.float32).astype(jnp.bfloat16)
    return dot_nt(unit, rows).astype(jnp.bfloat16)


def tile_loop(half, rows, cols, groups, body):
    per_slab = cols // SLABS
    low = jnp.maximum(half * (rows // HALVES) - 1, 0)
    high = (half + 1) * (rows // HALVES)
    per_row = per_slab * groups

    def place(row, col):
        side = (col % HALVES) ^ half
        return side * (rows * cols // HALVES) + row * (cols // HALVES) + col // HALVES

    def step(n, carry):
        row = low + n // per_row
        left = n % per_row
        body([place(row, s * per_slab + left // groups) for s in range(SLABS)], left % groups)
        return carry

    lax.fori_loop(0, (high - low) * per_row, step, 0)


def lanes_inside(extra, d, t, half):
    extra = extra[d].astype(jnp.float32)
    picked = jnp.where(iota(extra.shape, 0) == t, extra, 0.0)
    cells = jnp.sum(picked, axis=0, keepdims=True) - (half * LANES).astype(jnp.float32)
    return jnp.broadcast_to((cells >= 0.0) & (cells < LANES), (16, LANES))


def scatter_kernel(
    cols, gs, fs, place, shift, start, mine, theirs, cas, own_out, other_out, patches, extra, lines, *slabs
):
    half = place[0]
    step = pl.program_id(0)
    devices, held, _ = patches.shape
    groups = held // 16
    blocks = groups * GROUP
    owner = iota((16, LANES), 1) // 4
    plane = iota((16, LANES), 0) % QUAD

    @pl.when(step == 0)
    def _():
        def clear(n, carry):
            for slab in slabs:
                slab[pl.ds(pl.multiple_of(n * SLAB, 8), SLAB), :] = jnp.zeros(
                    (SLAB, LANES), jnp.float32
                )
            return carry

        lax.fori_loop(0, slabs[0].shape[0] // SLAB, clear, 0)
        for side, part in enumerate((mine, theirs)):
            at = slice(side * (devices // 2), (side + 1) * (devices // 2))
            patches[at] = part[:, :held]
            extra[at] = part[:, held:]

        def tile(numbers, t):
            values = []
            for d in numbers:
                part = patches[d, pl.ds(pl.multiple_of(16 * t, 16), 16), :].astype(jnp.float32)
                values.append(jnp.where(lanes_inside(extra, d, t, half), part, 0.0))

            def one(k, carry):
                spot = owner == k
                sums = []
                for s in range(SLABS):
                    b = numbers[s] * blocks + t * GROUP + k
                    at = start[b]
                    moved = pltpu.roll(jnp.where(spot, values[s], 0.0), shift[b], 1)
                    here = plane < QUAD - (at & (QUAD - 1))
                    near = slabs[s][pl.ds(at, 16), :] + jnp.where(here, moved, 0.0)
                    at_next = at + (SLAB - QUAD)
                    far = slabs[s][pl.ds(at_next, 16), :] + jnp.where(here, 0.0, moved)
                    sums.append((at, near, at_next, far))
                for s, (at, near, at_next, far) in enumerate(sums):
                    slabs[s][pl.ds(at, 16), :] = near
                    slabs[s][pl.ds(at_next, 16), :] = far
                return carry

            lax.fori_loop(0, GROUP, one, 0, unroll=UNROLL)

        tile_loop(half, devices // cols, cols, groups, tile)

        table = table_rows(cas, [place[1]], gs)

        def planes(n, carry):
            base = pl.multiple_of(n * SLAB, 8)
            sheets = []
            for q in range(QUAD):
                parts = []
                for s in range(SLABS):
                    part = slabs[s][pl.ds(base + (PAD + q), PIECE, stride=QUAD), :]
                    if s > 0:
                        at = base + (PAD + QUAD * PIECE + q)
                        over = slabs[s - 1][pl.ds(at, 8, stride=QUAD), :]
                        part = jnp.concatenate([part[:8] + over, part[8:]], axis=0)
                    parts.append(part.astype(jnp.bfloat16))
                sheets.append(jnp.concatenate(parts, axis=0))
            field = dot(table, jnp.concatenate(sheets, axis=1))
            for q in range(QUAD):
                part = field[:, LANES * q : LANES * q + LANES]
                lines[pl.ds(n * QUAD + q, gs, stride=STRIDE), :] = part
            return carry

        lax.fori_loop(0, G // QUAD, planes, 0, unroll=UNROLL_PLANES)

    @pl.when(step > 0)
    def _():
        third = table_rows(cas, [place[2], place[2] ^ 1], fs)
        for g in range(0, LINES, 2):
            pair = []
            for n in (g, g + 1):
                at = ((step - 1) * LINES + n) * STRIDE
                pair.append(lines[pl.ds(at, G), :].astype(jnp.bfloat16))
            field = dot(third, jnp.concatenate(pair, axis=1)).astype(jnp.bfloat16)
            for n in range(2):
                own_out[g + n] = field[:fs, LANES * n : LANES * n + LANES]
                other_out[g + n] = field[fs:, LANES * n : LANES * n + LANES]


def spectrum_kernel(place, own, other, weights, cas, own_out, other_out):
    tiles = [pl.ds(pl.multiple_of(h * LANES, LANES), LANES) for h in (place[0], 1 - place[0])]
    first = jnp.concatenate([cas[tile, :] for tile in tiles], axis=0)
    first_back = jnp.concatenate([cas[:, tile] for tile in tiles], axis=1)
    count, freqs, _ = weights.shape
    step = max(1, G // freqs)
    rows = step * freqs
    for g in range(0, count, step):
        part = slice(g, g + step)
        line = jnp.concatenate(
            [own[part].reshape(rows, LANES), other[part].reshape(rows, LANES)], axis=1
        )
        s = dot(line, first) * weights[part].reshape(rows, P_SIZE)
        line = dot(s.astype(jnp.bfloat16), first_back).astype(jnp.bfloat16)
        own_out[part] = line[:, :LANES].reshape(step, freqs, LANES)
        other_out[part] = line[:, LANES:].reshape(step, freqs, LANES)


def sample_kernel(
    cols, place, shift, start, mine, theirs, own, other, cas, out, extra, second, third, lines, cells
):
    half = place[0]
    step = pl.program_id(0)
    devices, held, _ = out.shape
    groups = held // 16
    blocks = groups * GROUP
    gs = second.shape[1]
    owner = iota((16, LANES), 1) // 4
    plane = iota((16, LANES), 0) % QUAD

    @pl.when(step == 0)
    def _():
        for side, part in enumerate((mine, theirs)):
            extra[side * (devices // 2) : (side + 1) * (devices // 2)] = part[:, held:]
        second[...] = turned(table_rows(cas, [place[1]], gs))
        third[...] = turned(table_rows(cas, [place[2], place[2] ^ 1], own.shape[1]))

    for g in range(0, LINES, 2):
        pair = [jnp.concatenate([own[n], other[n]], axis=0) for n in (g, g + 1)]
        field = dot(third[...], jnp.concatenate(pair, axis=1))
        for n in range(2):
            at = (step * LINES + g + n) * STRIDE
            lines[pl.ds(at, G), :] = field[:, LANES * n : LANES * n + LANES]

    @pl.when(step == pl.num_programs(0) - 1)
    def _():
        def planes(n, carry):
            sheets = [
                lines[pl.ds(n * QUAD + q, gs, stride=STRIDE), :].astype(jnp.bfloat16)
                for q in range(QUAD)
            ]
            field = dot(second[...], jnp.concatenate(sheets, axis=1))
            base = pl.multiple_of(n * CELLS, 8)
            for q in range(QUAD):
                part = field[:, LANES * q : LANES * q + LANES]
                cells[pl.ds(base + (PAD + q), G, stride=QUAD), :] = part
            return carry

        lax.fori_loop(0, G // QUAD, planes, 0, unroll=UNROLL_PLANES)
        out[...] = jnp.zeros_like(out)

        def tile(numbers, t):
            def one(k, sums):
                spot = owner == k
                new = []
                for s in range(SLABS):
                    b = numbers[s] * blocks + t * GROUP + k
                    at = start[b]
                    here = plane < QUAD - (at & (QUAD - 1))
                    near = cells[pl.ds(at, 16), :]
                    far = cells[pl.ds(at + (CELLS - QUAD), 16), :]
                    moved = pltpu.roll(jnp.where(here, near, far), shift[b], 1)
                    new.append(jnp.where(spot, moved, sums[s]))
                return tuple(new)

            zero = (jnp.zeros((16, LANES), jnp.float32),) * SLABS
            sums = lax.fori_loop(0, GROUP, one, zero, unroll=UNROLL)
            for s, d in enumerate(numbers):
                inside = lanes_inside(extra, d, t, half)
                out[d, pl.ds(pl.multiple_of(16 * t, 16), 16), :] = jnp.where(
                    inside, sums[s], 0.0
                ).astype(jnp.bfloat16)

        tile_loop(half, devices // cols, cols, groups, tile)


def finish_kernel(values, interpolate, near, inverse, out, total):
    blocks = near.shape[0]
    groups = values.shape[1] // 16
    rows, lanes = patch_places(blocks)
    summed = values[0].astype(jnp.float32)
    for d in range(1, values.shape[0]):
        summed = summed + values[d].astype(jnp.float32)
    spread = jnp.concatenate([summed[16 * t : 16 * t + 16] for t in range(groups)], axis=1)
    parts = jnp.concatenate(split(spread), axis=0)
    patch = jnp.zeros((blocks, LANES), jnp.float32)
    for i in range(4):
        column = dot_nt(lanes[i], parts).astype(jnp.bfloat16)
        patch = patch + dot(column, jnp.concatenate([rows[i], rows[i]], axis=0))
    total[...] = block_sums(interpolate, patch) + near[...]
    count = out.shape[0]
    even = total[pl.ds(0, count, stride=2), :]
    odd = total[pl.ds(1, count, stride=2), :]
    total[:count] = jnp.where(iota(even.shape, 1) < BLK, even, odd)
    upper = inverse[:count]
    lower = inverse[count:]

    def step(u, acc):
        row = jnp.broadcast_to(total[pl.ds(u, 1), :], lower.shape)
        return jnp.where(upper == u, lane_gather(row, lower), acc)

    out[...] = lax.fori_loop(0, count, step, jnp.zeros(out.shape, jnp.float32), unroll=4)


def struct(shape, dtype):
    return jax.ShapeDtypeStruct(shape, dtype)


def whole(shape):
    return pl.BlockSpec(shape, lambda *_: (0,) * len(shape))


def params(mib):
    return pltpu.CompilerParams(vmem_limit_bytes=mib * MB)


def beside(array, axis, dim):
    count = lax.axis_size(axis)
    up = [(i, i + 1) for i in range(count - 1)]
    before = lax.ppermute(array, axis, up)
    after = lax.ppermute(array, axis, [(j, i) for i, j in up])
    return jnp.concatenate([before, array, after], axis=dim)


def body(
    charges,
    panel_order,
    patch_anchor,
    project,
    interpolate,
    kernel_spectrum,
    near_pairs,
    near_blocks,
):
    axes = ("row", "col")
    rows = lax.axis_size("row")
    cols = lax.axis_size("col")
    devices = rows * cols
    row_at = lax.axis_index("row")
    col_at = lax.axis_index("col")
    half = col_at % HALVES
    mates = [(c, c ^ 1) for c in range(cols)]
    blocks = project.shape[0]
    groups = blocks // GROUP
    panels = charges.shape[0]
    strips = panels // LANES
    gs, fs, _ = kernel_spectrum.shape
    held = 16 * groups + 16

    order = panel_order.reshape(strips, LANES)
    block_charges, sent = pl.pallas_call(
        project_kernel,
        out_shape=(
            struct((blocks, LANES), jnp.bfloat16),
            struct((held, LANES), jnp.bfloat16),
        ),
        in_specs=[pl.BlockSpec(memory_space=pltpu.HBM)] * 4,
        scratch_shapes=[
            pltpu.VMEM((strips, LANES), jnp.bfloat16),
            pltpu.VMEM((strips, LANES), jnp.int32),
            pltpu.VMEM(project.shape, jnp.bfloat16),
            pltpu.VMEM(patch_anchor.shape, jnp.int32),
            pltpu.VMEM((strips, LANES), jnp.float32),
            pltpu.VMEM((blocks, LANES), jnp.float32),
            pltpu.SemaphoreType.DMA((4,)),
        ],
        compiler_params=params(58),
        name="project",
    )(
        charges.reshape(strips, LANES),
        order,
        project,
        patch_anchor,
    )
    members = devices // HALVES
    cores = [
        [r * cols + c for r in range(rows) for c in range(core, cols, HALVES)]
        for core in range(HALVES)
    ]

    def swap_members(array):
        return lax.all_to_all(
            array, axes, split_axis=0, concat_axis=0, axis_index_groups=cores, tiled=True
        )

    mine = swap_members(jnp.broadcast_to(sent[None], (members, held, LANES)))
    theirs = lax.ppermute(mine, "col", mates)
    inverse = pl.pallas_call(
        inverse_kernel,
        out_shape=struct((2 * strips, LANES), jnp.int32),
        compiler_params=params(32),
        name="inverse",
    )(order)

    around = beside(block_charges[None, None], "row", 0)
    mine, around, inverse = lax.optimization_barrier((mine, around, inverse))
    anchors = jnp.stack([part[:, 17 * groups : 17 * groups + 3] for part in (mine, theirs)])
    anchors = anchors.astype(jnp.int32)
    lane = 4 * (jnp.arange(blocks, dtype=jnp.int32) % GROUP)
    forth = ((anchors[:, :, 0] - lane) & (LANES - 1)).reshape(devices * blocks)
    back = ((lane - anchors[:, :, 0]) & (LANES - 1)).reshape(devices * blocks)
    group = anchors[:, :, 2] // QUAD
    inner = PAD + QUAD * anchors[:, :, 1] + anchors[:, :, 2] % QUAD
    side = jnp.arange(HALVES, dtype=jnp.int32)[:, None] ^ half
    col = jnp.arange(members, dtype=jnp.int32) % (cols // HALVES) * HALVES + side
    piece = (col * SLABS // cols * PIECE)[:, :, None]
    slab_at = (group * SLAB + inner - QUAD * piece).reshape(devices * blocks)
    cell_at = (group * CELLS + inner).reshape(devices * blocks)
    place = jnp.stack([half, row_at, col_at]).astype(jnp.int32)
    cas = jnp.asarray(CAS)

    smem = pl.BlockSpec(memory_space=pltpu.SMEM)
    steps = gs // LINES
    lines_type = struct((gs, fs, LANES), jnp.bfloat16)
    late = pl.BlockSpec((LINES, fs, LANES), lambda n: (jnp.maximum(n - 1, 0), 0, 0))
    own, other = pl.pallas_call(
        functools.partial(scatter_kernel, cols, gs, fs),
        grid=(1 + steps,),
        in_specs=[smem] * 3 + [whole(mine.shape)] * 2 + [whole(cas.shape)],
        out_specs=(late, late),
        out_shape=(lines_type, lines_type),
        scratch_shapes=[
            pltpu.VMEM((devices, 16 * groups, LANES), jnp.bfloat16),
            pltpu.VMEM((devices, 16, LANES), jnp.bfloat16),
            pltpu.VMEM((gs * STRIDE, LANES), jnp.float32),
        ]
        + [pltpu.VMEM(((G // QUAD + 1) * SLAB, LANES), jnp.float32)] * SLABS,
        compiler_params=params(53),
        name="scatter",
    )(place, forth, slab_at, mine, theirs, cas)
    other = lax.ppermute(other, "col", mates)
    around = beside(around, "col", 1).reshape(9, blocks, LANES)
    other, around = lax.optimization_barrier((other, around))

    part = lambda shape: pl.BlockSpec((BATCH,) + shape, lambda n: (n, 0, 0))
    own, other = pl.pallas_call(
        spectrum_kernel,
        grid=(gs // BATCH,),
        in_specs=[
            smem,
            part((fs, LANES)),
            part((fs, LANES)),
            part((fs, P_SIZE)),
            whole(cas.shape),
        ],
        out_specs=(part((fs, LANES)), part((fs, LANES))),
        out_shape=(lines_type, lines_type),
        compiler_params=params(40),
        name="spectrum",
    )(place, own, other, kernel_spectrum, cas)
    other = lax.ppermute(other, "col", mates)

    early = pl.BlockSpec((LINES, fs, LANES), lambda n: (n, 0, 0))
    values = pl.pallas_call(
        functools.partial(sample_kernel, cols),
        grid=(steps,),
        in_specs=[smem] * 3 + [whole(mine.shape)] * 2 + [early, early, whole(cas.shape)],
        out_specs=whole((devices, 16 * groups, LANES)),
        out_shape=struct((devices, 16 * groups, LANES), jnp.bfloat16),
        scratch_shapes=[
            pltpu.VMEM((devices, 16, LANES), jnp.bfloat16),
            pltpu.VMEM((G, gs), jnp.bfloat16),
            pltpu.VMEM((G, 2 * fs), jnp.bfloat16),
            pltpu.VMEM((gs * STRIDE, LANES), jnp.float32),
            pltpu.VMEM(((G // QUAD + 1) * CELLS, LANES), jnp.float32),
        ],
        compiler_params=params(46),
        name="sample",
    )(place, back, cell_at, mine, theirs, own, other, cas)
    values = values.reshape(HALVES, members, 16 * groups, LANES)
    received = lax.ppermute(values[1], "col", mates).astype(jnp.float32)
    values = (values[0].astype(jnp.float32) + received).astype(jnp.bfloat16)
    values, around = lax.optimization_barrier((values, around))
    values = swap_members(values)

    source = near_pairs[1]
    source_device = source // blocks
    code = (source_device // cols - row_at + 1) * 3 + (source_device % cols - col_at + 1)
    wanted = code * blocks + source % blocks
    target = near_pairs[0] - (row_at * cols + col_at) * blocks
    pairs = near_blocks.shape[0]
    near = pl.pallas_call(
        near_kernel,
        grid=(pairs // blocks,),
        in_specs=[
            smem,
            pl.BlockSpec((blocks, BLK * BLK), lambda n: (n, 0)),
            pl.BlockSpec((1, blocks), lambda n: (0, n)),
            whole((9, blocks, LANES)),
        ],
        out_specs=whole((blocks, LANES)),
        out_shape=struct((blocks, LANES), jnp.float32),
        scratch_shapes=[
            pltpu.VMEM((9 * blocks, LANES), jnp.float32),
            pltpu.VMEM((blocks, LANES), jnp.float32),
        ],
        compiler_params=params(56),
        name="near",
    )(wanted, near_blocks, target.reshape(1, pairs), around)

    result = pl.pallas_call(
        finish_kernel,
        out_shape=struct((strips, LANES), jnp.float32),
        scratch_shapes=[pltpu.VMEM((blocks, LANES), jnp.float32)],
        compiler_params=params(32),
        name="finish",
    )(values, interpolate, near, inverse)
    return result.reshape(panels)


def solution(mesh):
    placed = (
        P(("row", "col")),
        P(("row", "col")),
        P(None, ("row", "col")),
        P(("row", "col"), None),
        P(("row", "col"), None),
        P("row", "col", None),
        P(None, ("row", "col")),
        P(("row", "col"), None),
    )
    return jax.shard_map(
        body, mesh=mesh, in_specs=placed, out_specs=P(("row", "col")), check_vma=False
    )
```

```python
import functools

import jax
import jax.numpy as jnp
import ml_dtypes
import numpy as np
from jax import lax
from jax.experimental import pallas as pl
from jax.experimental.pallas import tpu as pltpu
from jax.sharding import PartitionSpec as P

G = 256
P_SIZE = 512
BLK = 64
PTS = 64
LANES = 128
GROUP = LANES // 4
HALVES = G // LANES
SLABS = 4
PIECE = G // SLABS
QUAD = 4
PAD = 8
SLAB = PAD + QUAD * PIECE + 32
CELLS = PAD + QUAD * G + 16
STRIDE = G + 1
BATCH = 8
LINES = 16
UNROLL = 32
UNROLL_PLANES = 16
MB = 1 << 20
NT = (((1,), (1,)), ((), ()))


def cas_table():
    index = np.arange(P_SIZE, dtype=np.int64)
    phase = (index[:, None] * index[None, :] % P_SIZE).astype(np.float64) * (2.0 * np.pi / P_SIZE)
    return ((np.cos(phase) + np.sin(phase)) / np.sqrt(P_SIZE)).astype(ml_dtypes.bfloat16)


CAS = cas_table()


def dot(a, b):
    return jnp.dot(a, b, preferred_element_type=jnp.float32)


def dot_nt(a, b):
    return lax.dot_general(a, b, NT, preferred_element_type=jnp.float32)


def iota(shape, dim):
    return lax.broadcasted_iota(jnp.int32, shape, dim)


def split(value):
    high = value.astype(jnp.bfloat16)
    return high, (value - high.astype(jnp.float32)).astype(jnp.bfloat16)


def lane_gather(table, index):
    return jnp.take_along_axis(table, index, axis=1, mode="promise_in_bounds")


def block_sums(mats, vecs):
    rows = vecs.shape[0]
    pair = jnp.concatenate([vecs, vecs], axis=1)
    total = jnp.zeros((2 * rows, LANES), jnp.float32)
    for t in range(mats.shape[1] // 256):
        high, low = split(mats[:, 256 * t : 256 * t + 256].astype(jnp.float32) * pair)
        owner = iota((256, LANES), 0) // BLK + 4 * t
        table = (owner == iota((256, LANES), 1) % BLK).astype(jnp.bfloat16)
        total = total + dot(jnp.concatenate([high, low], axis=0), table)
    return total[:rows] + total[rows:]


def patch_places(spots):
    blocks = spots.shape[0]
    spots = jnp.concatenate([spots] * (4 * blocks // LANES), axis=1)
    lane = iota(spots.shape, 1)
    lanes = [(lane == 4 * spots + i).astype(jnp.float32).astype(jnp.bfloat16) for i in range(4)]
    row = iota((16, LANES), 0)
    rows = [
        (iota((16, LANES), 1) % PTS == 16 * i + row).astype(jnp.float32).astype(jnp.bfloat16)
        for i in range(4)
    ]
    return rows, lanes


def block_spots(first):
    blocks = first.shape[1]
    shape = (blocks, blocks)
    crossing = ((first & (LANES - 1)) > LANES - 4).astype(jnp.float32)
    crossing = jnp.broadcast_to(crossing, (8, blocks))
    earlier = (iota(shape, 0) < iota(shape, 1)).astype(jnp.float32).astype(jnp.bfloat16)
    ahead = dot(crossing.astype(jnp.bfloat16), earlier)
    total = jnp.sum(crossing, axis=1, keepdims=True)
    block = iota((8, blocks), 1).astype(jnp.float32)
    spot = jnp.where(crossing > 0.0, ahead, total + block - ahead)
    spread = jnp.broadcast_to(spot[:1], (LANES, blocks)).astype(jnp.bfloat16)
    unit = (iota(shape, 0) == iota(shape, 1)).astype(jnp.float32).astype(jnp.bfloat16)
    return dot_nt(unit, spread).astype(jnp.int32)


def project_kernel(
    charges_in,
    order_in,
    project_in,
    anchors_in,
    charge_out,
    patch_out,
    spot_out,
    charges,
    order,
    project,
    anchors,
    table,
    doubled,
    sems,
):
    blocks = charge_out.shape[0]
    groups = blocks // GROUP
    pairs = ((charges_in, charges), (order_in, order), (project_in, project), (anchors_in, anchors))
    copies = [pltpu.make_async_copy(a, b, sems.at[n]) for n, (a, b) in enumerate(pairs)]
    for copy in copies:
        copy.start()
    copies[0].wait()
    copies[1].wait()
    table[...] = charges[...].astype(jnp.float32)
    strips = table.shape[0]
    upper = order[...] // LANES
    lower = order[...] % LANES

    def step(u, acc):
        row = jnp.broadcast_to(table[pl.ds(u, 1), :], lower.shape)
        return jnp.where(upper == u, lane_gather(row, lower), acc)

    slots = lax.fori_loop(0, strips, step, jnp.zeros(lower.shape, jnp.float32), unroll=4)
    swapped = pltpu.roll(slots, BLK, 1)
    left = iota(slots.shape, 1) < BLK
    doubled[pl.ds(0, strips, stride=2), :] = jnp.where(left, slots, swapped)
    doubled[pl.ds(1, strips, stride=2), :] = jnp.where(left, swapped, slots)
    twice = doubled[...]
    charge_out[...] = twice.astype(jnp.bfloat16)
    copies[2].wait()
    copies[3].wait()
    patch = block_sums(project, twice)
    patch = jnp.where(iota(patch.shape, 1) < PTS, patch, 0.0).astype(jnp.bfloat16)
    spots = block_spots(anchors[:1, :])
    spot_out[...] = spots
    rows, lanes = patch_places(spots)
    moved = (iota(spots.shape, 1) == spots).astype(jnp.float32).astype(jnp.bfloat16)
    corner = anchors[...].astype(jnp.float32).astype(jnp.bfloat16)
    corner = dot(jnp.concatenate([corner] * 3, axis=0)[:8], moved)
    spread = jnp.zeros((16, 4 * blocks), jnp.float32)
    cells = (iota((8, 4 * blocks), 1) % 4).astype(jnp.float32)
    start = jnp.broadcast_to(anchors[:1, :].astype(jnp.float32), (8, blocks)).astype(jnp.bfloat16)
    for i in range(4):
        spread = spread + dot(dot_nt(rows[i], patch).astype(jnp.bfloat16), lanes[i])
        cells = cells + dot(start, lanes[i])
    tiles = [slice(LANES * t, LANES * t + LANES) for t in range(groups)]
    sent = [spread[:, tile].astype(jnp.bfloat16) for tile in tiles]
    extra = [cells[:1, tile] for tile in tiles] + [corner[:3]]
    extra.append(jnp.zeros((13 - groups, LANES), jnp.float32))
    sent.append(jnp.concatenate(extra, axis=0).astype(jnp.bfloat16))
    for n in range(patch_out.shape[0]):
        for t, part in enumerate(sent):
            patch_out[n, 16 * t : 16 * t + 16] = part


def inverse_kernel(order, out):
    rows = order.shape[0]

    def step(r, acc):
        here = order[pl.ds(r, 1), :]
        upper = iota((rows, LANES), 0) == here // LANES
        lower = iota((LANES, LANES), 0) == here % LANES
        values = jnp.concatenate(
            [
                jnp.where(upper, r.astype(jnp.float32), 0.0),
                jnp.where(upper, iota((rows, LANES), 1).astype(jnp.float32), 0.0),
            ],
            axis=0,
        )
        return acc + dot_nt(
            values.astype(jnp.bfloat16), lower.astype(jnp.float32).astype(jnp.bfloat16)
        )

    out[...] = lax.fori_loop(
        0, rows, step, jnp.zeros((2 * rows, LANES), jnp.float32), unroll=4
    ).astype(jnp.int32)


def near_kernel(source, near_blocks, target, charges, out, table, picked):
    step = pl.program_id(0)
    pairs = picked.shape[0]
    blocks = out.shape[0]

    @pl.when(step == 0)
    def _():
        for d in range(charges.shape[0]):
            table[d * blocks : (d + 1) * blocks] = charges[d].astype(jnp.float32)
        out[...] = jnp.zeros_like(out)

    def pick(p, carry):
        picked[pl.ds(p, 1), :] = table[pl.ds(source[step * pairs + p], 1), :]
        return carry

    lax.fori_loop(0, pairs, pick, 0, unroll=8)
    terms = block_sums(near_blocks, picked[...])
    owner = (iota((blocks, pairs), 0) == target[...]).astype(jnp.float32).astype(jnp.bfloat16)
    high, low = split(terms)
    out[...] += dot(owner, high) + dot(owner, low)


def table_rows(cas, numbers, count):
    parts = [cas[pl.ds(pl.multiple_of(n * count, 16), count), :G] for n in numbers]
    return jnp.concatenate(parts, axis=0) if len(parts) > 1 else parts[0]


def turned(rows):
    unit = (iota((G, G), 0) == iota((G, G), 1)).astype(jnp.float32).astype(jnp.bfloat16)
    return dot_nt(unit, rows).astype(jnp.bfloat16)


def tile_loop(half, rows, cols, groups, crosses, body):
    per_slab = cols // SLABS
    low = jnp.maximum(half * (rows // HALVES) - 1, 0)
    high = (half + 1) * (rows // HALVES)
    per_row = per_slab * groups

    def place(row, col):
        side = (col % HALVES) ^ half
        return side * (rows * cols // HALVES) + row * (cols // HALVES) + col // HALVES

    def step(n, carry):
        row = low + n // per_row
        left = n % per_row
        t = left % groups
        devices = [place(row, s * per_slab + left // groups) for s in range(SLABS)]
        found = [crosses((d * groups + t) * GROUP) for d in devices]
        inside = row >= half * (rows // HALVES)
        pl.when(functools.reduce(jnp.logical_or, found, inside))(lambda: body(devices, t))
        return carry

    lax.fori_loop(0, (high - low) * per_row, step, 0)


def lanes_inside(extra, d, t, half):
    extra = extra[d].astype(jnp.float32)
    picked = jnp.where(iota(extra.shape, 0) == t, extra, 0.0)
    cells = jnp.sum(picked, axis=0, keepdims=True) - (half * LANES).astype(jnp.float32)
    return jnp.broadcast_to((cells >= 0.0) & (cells < LANES), (16, LANES))


def scatter_kernel(
    cols, gs, fs, place, shift, start, mine, theirs, cas, own_out, other_out, patches, extra, lines, *slabs
):
    half = place[0]
    step = pl.program_id(0)
    devices, held, _ = patches.shape
    groups = held // 16
    blocks = groups * GROUP
    owner = iota((16, LANES), 1) // 4
    plane = iota((16, LANES), 0) % QUAD

    @pl.when(step == 0)
    def _():
        def clear(n, carry):
            for slab in slabs:
                slab[pl.ds(pl.multiple_of(n * SLAB, 8), SLAB), :] = jnp.zeros(
                    (SLAB, LANES), jnp.float32
                )
            return carry

        lax.fori_loop(0, slabs[0].shape[0] // SLAB, clear, 0)
        for side, part in enumerate((mine, theirs)):
            at = slice(side * (devices // 2), (side + 1) * (devices // 2))
            patches[at] = part[:, :held]
            extra[at] = part[:, held:]

        def tile(numbers, t):
            values = []
            for d in numbers:
                part = patches[d, pl.ds(pl.multiple_of(16 * t, 16), 16), :].astype(jnp.float32)
                values.append(jnp.where(lanes_inside(extra, d, t, half), part, 0.0))

            def one(k, carry):
                spot = owner == k
                sums = []
                for s in range(SLABS):
                    b = numbers[s] * blocks + t * GROUP + k
                    at = start[b]
                    moved = pltpu.roll(jnp.where(spot, values[s], 0.0), shift[b], 1)
                    here = plane < QUAD - (at & (QUAD - 1))
                    near = slabs[s][pl.ds(at, 16), :] + jnp.where(here, moved, 0.0)
                    at_next = at + (SLAB - QUAD)
                    far = slabs[s][pl.ds(at_next, 16), :] + jnp.where(here, 0.0, moved)
                    sums.append((at, near, at_next, far))
                for s, (at, near, at_next, far) in enumerate(sums):
                    slabs[s][pl.ds(at, 16), :] = near
                    slabs[s][pl.ds(at_next, 16), :] = far
                return carry

            lax.fori_loop(0, GROUP, one, 0, unroll=UNROLL)

        def crosses(b):
            return shift[b] > LANES - 4

        tile_loop(half, devices // cols, cols, groups, crosses, tile)

        table = table_rows(cas, [place[1]], gs)

        def planes(n, carry):
            base = pl.multiple_of(n * SLAB, 8)
            sheets = []
            for q in range(QUAD):
                parts = []
                for s in range(SLABS):
                    part = slabs[s][pl.ds(base + (PAD + q), PIECE, stride=QUAD), :]
                    if s > 0:
                        at = base + (PAD + QUAD * PIECE + q)
                        over = slabs[s - 1][pl.ds(at, 8, stride=QUAD), :]
                        part = jnp.concatenate([part[:8] + over, part[8:]], axis=0)
                    parts.append(part.astype(jnp.bfloat16))
                sheets.append(jnp.concatenate(parts, axis=0))
            field = dot(table, jnp.concatenate(sheets, axis=1))
            for q in range(QUAD):
                part = field[:, LANES * q : LANES * q + LANES]
                lines[pl.ds(n * QUAD + q, gs, stride=STRIDE), :] = part
            return carry

        lax.fori_loop(0, G // QUAD, planes, 0, unroll=UNROLL_PLANES)

    @pl.when(step > 0)
    def _():
        third = table_rows(cas, [place[2], place[2] ^ 1], fs)
        for g in range(0, LINES, 2):
            pair = []
            for n in (g, g + 1):
                at = ((step - 1) * LINES + n) * STRIDE
                pair.append(lines[pl.ds(at, G), :].astype(jnp.bfloat16))
            field = dot(third, jnp.concatenate(pair, axis=1)).astype(jnp.bfloat16)
            for n in range(2):
                own_out[g + n] = field[:fs, LANES * n : LANES * n + LANES]
                other_out[g + n] = field[fs:, LANES * n : LANES * n + LANES]


def spectrum_kernel(place, own, other, weights, cas, own_out, other_out):
    tiles = [pl.ds(pl.multiple_of(h * LANES, LANES), LANES) for h in (place[0], 1 - place[0])]
    first = jnp.concatenate([cas[tile, :] for tile in tiles], axis=0)
    first_back = jnp.concatenate([cas[:, tile] for tile in tiles], axis=1)
    count, freqs, _ = weights.shape
    step = max(1, G // freqs)
    rows = step * freqs
    for g in range(0, count, step):
        part = slice(g, g + step)
        line = jnp.concatenate(
            [own[part].reshape(rows, LANES), other[part].reshape(rows, LANES)], axis=1
        )
        s = dot(line, first) * weights[part].reshape(rows, P_SIZE)
        line = dot(s.astype(jnp.bfloat16), first_back).astype(jnp.bfloat16)
        own_out[part] = line[:, :LANES].reshape(step, freqs, LANES)
        other_out[part] = line[:, LANES:].reshape(step, freqs, LANES)


def sample_kernel(
    cols, place, shift, start, mine, theirs, own, other, cas, out, extra, second, third, lines, cells
):
    half = place[0]
    step = pl.program_id(0)
    devices, held, _ = out.shape
    groups = held // 16
    blocks = groups * GROUP
    gs = second.shape[1]
    owner = iota((16, LANES), 1) // 4
    plane = iota((16, LANES), 0) % QUAD

    @pl.when(step == 0)
    def _():
        for side, part in enumerate((mine, theirs)):
            extra[side * (devices // 2) : (side + 1) * (devices // 2)] = part[:, held:]
        second[...] = turned(table_rows(cas, [place[1]], gs))
        third[...] = turned(table_rows(cas, [place[2], place[2] ^ 1], own.shape[1]))

    for g in range(0, LINES, 2):
        pair = [jnp.concatenate([own[n], other[n]], axis=0) for n in (g, g + 1)]
        field = dot(third[...], jnp.concatenate(pair, axis=1))
        for n in range(2):
            at = (step * LINES + g + n) * STRIDE
            lines[pl.ds(at, G), :] = field[:, LANES * n : LANES * n + LANES]

    @pl.when(step == pl.num_programs(0) - 1)
    def _():
        def planes(n, carry):
            sheets = [
                lines[pl.ds(n * QUAD + q, gs, stride=STRIDE), :].astype(jnp.bfloat16)
                for q in range(QUAD)
            ]
            field = dot(second[...], jnp.concatenate(sheets, axis=1))
            base = pl.multiple_of(n * CELLS, 8)
            for q in range(QUAD):
                part = field[:, LANES * q : LANES * q + LANES]
                cells[pl.ds(base + (PAD + q), G, stride=QUAD), :] = part
            return carry

        lax.fori_loop(0, G // QUAD, planes, 0, unroll=UNROLL_PLANES)
        out[...] = jnp.zeros_like(out)

        def tile(numbers, t):
            def one(k, sums):
                spot = owner == k
                new = []
                for s in range(SLABS):
                    b = numbers[s] * blocks + t * GROUP + k
                    at = start[b]
                    here = plane < QUAD - (at & (QUAD - 1))
                    near = cells[pl.ds(at, 16), :]
                    far = cells[pl.ds(at + (CELLS - QUAD), 16), :]
                    moved = pltpu.roll(jnp.where(here, near, far), shift[b], 1)
                    new.append(jnp.where(spot, moved, sums[s]))
                return tuple(new)

            zero = (jnp.zeros((16, LANES), jnp.float32),) * SLABS
            sums = lax.fori_loop(0, GROUP, one, zero, unroll=UNROLL)
            for s, d in enumerate(numbers):
                inside = lanes_inside(extra, d, t, half)
                out[d, pl.ds(pl.multiple_of(16 * t, 16), 16), :] = jnp.where(
                    inside, sums[s], 0.0
                ).astype(jnp.bfloat16)

        def crosses(b):
            return (shift[b] > 0) & (shift[b] < 4)

        tile_loop(half, devices // cols, cols, groups, crosses, tile)


def finish_kernel(values, interpolate, near, inverse, spots, out, total):
    blocks = near.shape[0]
    groups = values.shape[1] // 16
    rows, lanes = patch_places(spots[...])
    summed = values[0].astype(jnp.float32)
    for d in range(1, values.shape[0]):
        summed = summed + values[d].astype(jnp.float32)
    spread = jnp.concatenate([summed[16 * t : 16 * t + 16] for t in range(groups)], axis=1)
    parts = jnp.concatenate(split(spread), axis=0)
    patch = jnp.zeros((blocks, LANES), jnp.float32)
    for i in range(4):
        column = dot_nt(lanes[i], parts).astype(jnp.bfloat16)
        patch = patch + dot(column, jnp.concatenate([rows[i], rows[i]], axis=0))
    total[...] = block_sums(interpolate, patch) + near[...]
    count = out.shape[0]
    even = total[pl.ds(0, count, stride=2), :]
    odd = total[pl.ds(1, count, stride=2), :]
    total[:count] = jnp.where(iota(even.shape, 1) < BLK, even, odd)
    upper = inverse[:count]
    lower = inverse[count:]

    def step(u, acc):
        row = jnp.broadcast_to(total[pl.ds(u, 1), :], lower.shape)
        return jnp.where(upper == u, lane_gather(row, lower), acc)

    out[...] = lax.fori_loop(0, count, step, jnp.zeros(out.shape, jnp.float32), unroll=4)


def struct(shape, dtype):
    return jax.ShapeDtypeStruct(shape, dtype)


def whole(shape):
    return pl.BlockSpec(shape, lambda *_: (0,) * len(shape))


def params(mib):
    return pltpu.CompilerParams(vmem_limit_bytes=mib * MB)


def beside(array, axis, dim):
    count = lax.axis_size(axis)
    up = [(i, i + 1) for i in range(count - 1)]
    before = lax.ppermute(array, axis, up)
    after = lax.ppermute(array, axis, [(j, i) for i, j in up])
    return jnp.concatenate([before, array, after], axis=dim)


def body(
    charges,
    panel_order,
    patch_anchor,
    project,
    interpolate,
    kernel_spectrum,
    near_pairs,
    near_blocks,
):
    axes = ("row", "col")
    rows = lax.axis_size("row")
    cols = lax.axis_size("col")
    devices = rows * cols
    row_at = lax.axis_index("row")
    col_at = lax.axis_index("col")
    half = col_at % HALVES
    mates = [(c, c ^ 1) for c in range(cols)]
    blocks = project.shape[0]
    groups = blocks // GROUP
    panels = charges.shape[0]
    strips = panels // LANES
    gs, fs, _ = kernel_spectrum.shape
    held = 16 * groups + 16

    order = panel_order.reshape(strips, LANES)
    members = devices // HALVES
    block_charges, sent, spots = pl.pallas_call(
        project_kernel,
        out_shape=(
            struct((blocks, LANES), jnp.bfloat16),
            struct((members, held, LANES), jnp.bfloat16),
            struct((blocks, LANES), jnp.int32),
        ),
        in_specs=[pl.BlockSpec(memory_space=pltpu.HBM)] * 4,
        scratch_shapes=[
            pltpu.VMEM((strips, LANES), jnp.bfloat16),
            pltpu.VMEM((strips, LANES), jnp.int32),
            pltpu.VMEM(project.shape, jnp.bfloat16),
            pltpu.VMEM(patch_anchor.shape, jnp.int32),
            pltpu.VMEM((strips, LANES), jnp.float32),
            pltpu.VMEM((blocks, LANES), jnp.float32),
            pltpu.SemaphoreType.DMA((4,)),
        ],
        compiler_params=params(58),
        name="project",
    )(
        charges.reshape(strips, LANES),
        order,
        project,
        patch_anchor,
    )
    cores = [
        [r * cols + c for r in range(rows) for c in range(core, cols, HALVES)]
        for core in range(HALVES)
    ]

    def swap_members(array):
        return lax.all_to_all(
            array, axes, split_axis=0, concat_axis=0, axis_index_groups=cores, tiled=True
        )

    mine = swap_members(sent)
    theirs = lax.ppermute(mine, "col", mates)
    order, block_charges = lax.optimization_barrier((order, block_charges))
    inverse = pl.pallas_call(
        inverse_kernel,
        out_shape=struct((2 * strips, LANES), jnp.int32),
        compiler_params=params(32),
        name="inverse",
    )(order)

    block_charges, inverse = lax.optimization_barrier((block_charges, inverse))
    around = beside(block_charges[None, None], "row", 0)
    mine, around, inverse = lax.optimization_barrier((mine, around, inverse))
    anchors = jnp.stack([part[:, 17 * groups : 17 * groups + 3] for part in (mine, theirs)])
    anchors = anchors.astype(jnp.int32)
    lane = 4 * (jnp.arange(blocks, dtype=jnp.int32) % GROUP)
    forth = ((anchors[:, :, 0] - lane) & (LANES - 1)).reshape(devices * blocks)
    back = ((lane - anchors[:, :, 0]) & (LANES - 1)).reshape(devices * blocks)
    group = anchors[:, :, 2] // QUAD
    inner = PAD + QUAD * anchors[:, :, 1] + anchors[:, :, 2] % QUAD
    side = jnp.arange(HALVES, dtype=jnp.int32)[:, None] ^ half
    col = jnp.arange(members, dtype=jnp.int32) % (cols // HALVES) * HALVES + side
    piece = (col * SLABS // cols * PIECE)[:, :, None]
    slab_at = (group * SLAB + inner - QUAD * piece).reshape(devices * blocks)
    cell_at = (group * CELLS + inner).reshape(devices * blocks)
    place = jnp.stack([half, row_at, col_at]).astype(jnp.int32)
    cas = jnp.asarray(CAS)

    smem = pl.BlockSpec(memory_space=pltpu.SMEM)
    steps = gs // LINES
    lines_type = struct((gs, fs, LANES), jnp.bfloat16)
    late = pl.BlockSpec((LINES, fs, LANES), lambda n: (jnp.maximum(n - 1, 0), 0, 0))
    own, other = pl.pallas_call(
        functools.partial(scatter_kernel, cols, gs, fs),
        grid=(1 + steps,),
        in_specs=[smem] * 3 + [whole(mine.shape)] * 2 + [whole(cas.shape)],
        out_specs=(late, late),
        out_shape=(lines_type, lines_type),
        scratch_shapes=[
            pltpu.VMEM((devices, 16 * groups, LANES), jnp.bfloat16),
            pltpu.VMEM((devices, 16, LANES), jnp.bfloat16),
            pltpu.VMEM((gs * STRIDE, LANES), jnp.float32),
        ]
        + [pltpu.VMEM(((G // QUAD + 1) * SLAB, LANES), jnp.float32)] * SLABS,
        compiler_params=params(53),
        name="scatter",
    )(place, forth, slab_at, mine, theirs, cas)
    other = lax.ppermute(other, "col", mates)

    part = lambda shape: pl.BlockSpec((BATCH,) + shape, lambda n: (n, 0, 0))
    own, other = pl.pallas_call(
        spectrum_kernel,
        grid=(gs // BATCH,),
        in_specs=[
            smem,
            part((fs, LANES)),
            part((fs, LANES)),
            part((fs, P_SIZE)),
            whole(cas.shape),
        ],
        out_specs=(part((fs, LANES)), part((fs, LANES))),
        out_shape=(lines_type, lines_type),
        compiler_params=params(40),
        name="spectrum",
    )(place, own, other, kernel_spectrum, cas)
    other = lax.ppermute(other, "col", mates)
    own, around = lax.optimization_barrier((own, around))
    around = beside(around, "col", 1).reshape(9, blocks, LANES)
    other, around = lax.optimization_barrier((other, around))

    early = pl.BlockSpec((LINES, fs, LANES), lambda n: (n, 0, 0))
    values = pl.pallas_call(
        functools.partial(sample_kernel, cols),
        grid=(steps,),
        in_specs=[smem] * 3 + [whole(mine.shape)] * 2 + [early, early, whole(cas.shape)],
        out_specs=whole((devices, 16 * groups, LANES)),
        out_shape=struct((devices, 16 * groups, LANES), jnp.bfloat16),
        scratch_shapes=[
            pltpu.VMEM((devices, 16, LANES), jnp.bfloat16),
            pltpu.VMEM((G, gs), jnp.bfloat16),
            pltpu.VMEM((G, 2 * fs), jnp.bfloat16),
            pltpu.VMEM((gs * STRIDE, LANES), jnp.float32),
            pltpu.VMEM(((G // QUAD + 1) * CELLS, LANES), jnp.float32),
        ],
        compiler_params=params(46),
        name="sample",
    )(place, back, cell_at, mine, theirs, own, other, cas)
    values = values.reshape(HALVES, members, 16 * groups, LANES)
    received = lax.ppermute(values[1], "col", mates).astype(jnp.float32)
    values = (values[0].astype(jnp.float32) + received).astype(jnp.bfloat16)
    values, around = lax.optimization_barrier((values, around))
    values = swap_members(values)

    source = near_pairs[1]
    source_device = source // blocks
    code = (source_device // cols - row_at + 1) * 3 + (source_device % cols - col_at + 1)
    wanted = code * blocks + source % blocks
    target = near_pairs[0] - (row_at * cols + col_at) * blocks
    pairs = near_blocks.shape[0]
    near = pl.pallas_call(
        near_kernel,
        grid=(pairs // blocks,),
        in_specs=[
            smem,
            pl.BlockSpec((blocks, BLK * BLK), lambda n: (n, 0)),
            pl.BlockSpec((1, blocks), lambda n: (0, n)),
            whole((9, blocks, LANES)),
        ],
        out_specs=whole((blocks, LANES)),
        out_shape=struct((blocks, LANES), jnp.float32),
        scratch_shapes=[
            pltpu.VMEM((9 * blocks, LANES), jnp.float32),
            pltpu.VMEM((blocks, LANES), jnp.float32),
        ],
        compiler_params=params(56),
        name="near",
    )(wanted, near_blocks, target.reshape(1, pairs), around)

    result = pl.pallas_call(
        finish_kernel,
        out_shape=struct((strips, LANES), jnp.float32),
        scratch_shapes=[pltpu.VMEM((blocks, LANES), jnp.float32)],
        compiler_params=params(32),
        name="finish",
    )(values, interpolate, near, inverse, spots)
    return result.reshape(panels)


def solution(mesh):
    placed = (
        P(("row", "col")),
        P(("row", "col")),
        P(None, ("row", "col")),
        P(("row", "col"), None),
        P(("row", "col"), None),
        P("row", "col", None),
        P(None, ("row", "col")),
        P(("row", "col"), None),
    )
    return jax.shard_map(
        body, mesh=mesh, in_specs=placed, out_specs=P(("row", "col")), check_vma=False
    )
```

```python
import functools

import jax
import jax.numpy as jnp
import ml_dtypes
import numpy as np
from jax import lax
from jax.experimental import pallas as pl
from jax.experimental.pallas import tpu as pltpu
from jax.sharding import PartitionSpec as P

G = 256
P_SIZE = 512
BLK = 64
PTS = 64
LANES = 128
GROUP = LANES // 4
HALVES = G // LANES
SLABS = 4
PIECE = G // SLABS
QUAD = 4
PAD = 8
SLAB = PAD + QUAD * PIECE + 32
CELLS = PAD + QUAD * G + 16
STRIDE = G + 1
BATCH = 8
LINES = 16
UNROLL = 32
UNROLL_PLANES = 16
MB = 1 << 20
NT = (((1,), (1,)), ((), ()))


def cas_table():
    index = np.arange(P_SIZE, dtype=np.int64)
    phase = (index[:, None] * index[None, :] % P_SIZE).astype(np.float64) * (2.0 * np.pi / P_SIZE)
    return ((np.cos(phase) + np.sin(phase)) / np.sqrt(P_SIZE)).astype(ml_dtypes.bfloat16)


CAS = cas_table()


def dot(a, b):
    return jnp.dot(a, b, preferred_element_type=jnp.float32)


def dot_nt(a, b):
    return lax.dot_general(a, b, NT, preferred_element_type=jnp.float32)


def iota(shape, dim):
    return lax.broadcasted_iota(jnp.int32, shape, dim)


def split(value):
    high = value.astype(jnp.bfloat16)
    return high, (value - high.astype(jnp.float32)).astype(jnp.bfloat16)


def lane_gather(table, index):
    return jnp.take_along_axis(table, index, axis=1, mode="promise_in_bounds")


def block_sums(mats, vecs):
    rows = vecs.shape[0]
    pair = jnp.concatenate([vecs, vecs], axis=1)
    total = jnp.zeros((2 * rows, LANES), jnp.float32)
    for t in range(mats.shape[1] // 256):
        high, low = split(mats[:, 256 * t : 256 * t + 256].astype(jnp.float32) * pair)
        owner = iota((256, LANES), 0) // BLK + 4 * t
        table = (owner == iota((256, LANES), 1) % BLK).astype(jnp.bfloat16)
        total = total + dot(jnp.concatenate([high, low], axis=0), table)
    return total[:rows] + total[rows:]


def patch_places(spots):
    blocks = spots.shape[0]
    spots = jnp.concatenate([spots] * (4 * blocks // LANES), axis=1)
    lane = iota(spots.shape, 1)
    lanes = [(lane == 4 * spots + i).astype(jnp.float32).astype(jnp.bfloat16) for i in range(4)]
    row = iota((16, LANES), 0)
    rows = [
        (iota((16, LANES), 1) % PTS == 16 * i + row).astype(jnp.float32).astype(jnp.bfloat16)
        for i in range(4)
    ]
    return rows, lanes


def block_spots(first):
    blocks = first.shape[1]
    shape = (blocks, blocks)
    crossing = ((first & (LANES - 1)) > LANES - 4).astype(jnp.float32)
    crossing = jnp.broadcast_to(crossing, (8, blocks))
    earlier = (iota(shape, 0) < iota(shape, 1)).astype(jnp.float32).astype(jnp.bfloat16)
    ahead = dot(crossing.astype(jnp.bfloat16), earlier)
    total = jnp.sum(crossing, axis=1, keepdims=True)
    block = iota((8, blocks), 1).astype(jnp.float32)
    spot = jnp.where(crossing > 0.0, ahead, total + block - ahead)
    spread = jnp.broadcast_to(spot[:1], (LANES, blocks)).astype(jnp.bfloat16)
    unit = (iota(shape, 0) == iota(shape, 1)).astype(jnp.float32).astype(jnp.bfloat16)
    return dot_nt(unit, spread).astype(jnp.int32)


def project_kernel(
    charges_in,
    order_in,
    project_in,
    anchors_in,
    charge_out,
    patch_out,
    spot_out,
    charges,
    order,
    project,
    anchors,
    table,
    doubled,
    sems,
):
    blocks = charge_out.shape[0]
    groups = blocks // GROUP
    pairs = ((charges_in, charges), (order_in, order), (project_in, project), (anchors_in, anchors))
    copies = [pltpu.make_async_copy(a, b, sems.at[n]) for n, (a, b) in enumerate(pairs)]
    for copy in copies:
        copy.start()
    copies[3].wait()
    spots = block_spots(anchors[:1, :])
    spot_out[...] = spots
    rows, lanes = patch_places(spots)
    moved = (iota(spots.shape, 1) == spots).astype(jnp.float32).astype(jnp.bfloat16)
    corner = anchors[...].astype(jnp.float32).astype(jnp.bfloat16)
    corner = dot(jnp.concatenate([corner] * 3, axis=0)[:8], moved)
    cells = (iota((8, 4 * blocks), 1) % 4).astype(jnp.float32)
    start = jnp.broadcast_to(anchors[:1, :].astype(jnp.float32), (8, blocks)).astype(jnp.bfloat16)
    for i in range(4):
        cells = cells + dot(start, lanes[i])
    copies[0].wait()
    copies[1].wait()
    table[...] = charges[...].astype(jnp.float32)
    strips = table.shape[0]
    upper = order[...] // LANES
    lower = order[...] % LANES

    def step(u, acc):
        row = jnp.broadcast_to(table[pl.ds(u, 1), :], lower.shape)
        return jnp.where(upper == u, lane_gather(row, lower), acc)

    slots = lax.fori_loop(0, strips, step, jnp.zeros(lower.shape, jnp.float32), unroll=4)
    swapped = pltpu.roll(slots, BLK, 1)
    left = iota(slots.shape, 1) < BLK
    doubled[pl.ds(0, strips, stride=2), :] = jnp.where(left, slots, swapped)
    doubled[pl.ds(1, strips, stride=2), :] = jnp.where(left, swapped, slots)
    twice = doubled[...]
    charge_out[...] = twice.astype(jnp.bfloat16)
    copies[2].wait()
    patch = block_sums(project, twice)
    patch = jnp.where(iota(patch.shape, 1) < PTS, patch, 0.0).astype(jnp.bfloat16)
    spread = jnp.zeros((16, 4 * blocks), jnp.float32)
    for i in range(4):
        spread = spread + dot(dot_nt(rows[i], patch).astype(jnp.bfloat16), lanes[i])
    tiles = [slice(LANES * t, LANES * t + LANES) for t in range(groups)]
    sent = [spread[:, tile].astype(jnp.bfloat16) for tile in tiles]
    extra = [cells[:1, tile] for tile in tiles] + [corner[:3]]
    extra.append(jnp.zeros((13 - groups, LANES), jnp.float32))
    sent.append(jnp.concatenate(extra, axis=0).astype(jnp.bfloat16))
    for n in range(patch_out.shape[0]):
        for t, part in enumerate(sent):
            patch_out[n, 16 * t : 16 * t + 16] = part


def inverse_kernel(order, out):
    rows = order.shape[0]

    def step(r, acc):
        here = order[pl.ds(r, 1), :]
        upper = iota((rows, LANES), 0) == here // LANES
        lower = iota((LANES, LANES), 0) == here % LANES
        values = jnp.concatenate(
            [
                jnp.where(upper, r.astype(jnp.float32), 0.0),
                jnp.where(upper, iota((rows, LANES), 1).astype(jnp.float32), 0.0),
            ],
            axis=0,
        )
        return acc + dot_nt(
            values.astype(jnp.bfloat16), lower.astype(jnp.float32).astype(jnp.bfloat16)
        )

    out[...] = lax.fori_loop(
        0, rows, step, jnp.zeros((2 * rows, LANES), jnp.float32), unroll=4
    ).astype(jnp.int32)


def near_kernel(source, near_blocks, target, charges, out, table, picked):
    step = pl.program_id(0)
    pairs = picked.shape[0]
    blocks = out.shape[0]

    @pl.when(step == 0)
    def _():
        for d in range(charges.shape[0]):
            table[d * blocks : (d + 1) * blocks] = charges[d].astype(jnp.float32)
        out[...] = jnp.zeros_like(out)

    def pick(p, carry):
        picked[pl.ds(p, 1), :] = table[pl.ds(source[step * pairs + p], 1), :]
        return carry

    lax.fori_loop(0, pairs, pick, 0, unroll=8)
    terms = block_sums(near_blocks, picked[...])
    owner = (iota((blocks, pairs), 0) == target[...]).astype(jnp.float32).astype(jnp.bfloat16)
    high, low = split(terms)
    out[...] += dot(owner, high) + dot(owner, low)


def table_rows(cas, numbers, count):
    parts = [cas[pl.ds(pl.multiple_of(n * count, 16), count), :G] for n in numbers]
    return jnp.concatenate(parts, axis=0) if len(parts) > 1 else parts[0]


def turned(rows):
    unit = (iota((G, G), 0) == iota((G, G), 1)).astype(jnp.float32).astype(jnp.bfloat16)
    return dot_nt(unit, rows).astype(jnp.bfloat16)


def tile_loop(half, rows, cols, groups, crosses, body):
    per_slab = cols // SLABS
    low = jnp.maximum(half * (rows // HALVES) - 1, 0)
    high = (half + 1) * (rows // HALVES)
    per_row = per_slab * groups

    def place(row, col):
        side = (col % HALVES) ^ half
        return side * (rows * cols // HALVES) + row * (cols // HALVES) + col // HALVES

    def step(n, carry):
        row = low + n // per_row
        left = n % per_row
        t = left % groups
        devices = [place(row, s * per_slab + left // groups) for s in range(SLABS)]
        found = [crosses((d * groups + t) * GROUP) for d in devices]
        inside = row >= half * (rows // HALVES)
        pl.when(functools.reduce(jnp.logical_or, found, inside))(lambda: body(devices, t))
        return carry

    lax.fori_loop(0, (high - low) * per_row, step, 0)


def lanes_inside(extra, d, t, half):
    extra = extra[d].astype(jnp.float32)
    picked = jnp.where(iota(extra.shape, 0) == t, extra, 0.0)
    cells = jnp.sum(picked, axis=0, keepdims=True) - (half * LANES).astype(jnp.float32)
    return jnp.broadcast_to((cells >= 0.0) & (cells < LANES), (16, LANES))


def scatter_kernel(
    cols, gs, fs, place, shift, start, mine, theirs, cas, own_out, other_out, patches, extra, lines, *slabs
):
    half = place[0]
    step = pl.program_id(0)
    devices, held, _ = patches.shape
    groups = held // 16
    blocks = groups * GROUP
    owner = iota((16, LANES), 1) // 4
    plane = iota((16, LANES), 0) % QUAD

    @pl.when(step == 0)
    def _():
        def clear(n, carry):
            for slab in slabs:
                slab[pl.ds(pl.multiple_of(n * SLAB, 8), SLAB), :] = jnp.zeros(
                    (SLAB, LANES), jnp.float32
                )
            return carry

        lax.fori_loop(0, slabs[0].shape[0] // SLAB, clear, 0)
        for side, part in enumerate((mine, theirs)):
            at = slice(side * (devices // 2), (side + 1) * (devices // 2))
            patches[at] = part[:, :held]
            extra[at] = part[:, held:]

        def tile(numbers, t):
            values = []
            for d in numbers:
                part = patches[d, pl.ds(pl.multiple_of(16 * t, 16), 16), :].astype(jnp.float32)
                values.append(jnp.where(lanes_inside(extra, d, t, half), part, 0.0))

            def one(k, carry):
                spot = owner == k
                sums = []
                for s in range(SLABS):
                    b = numbers[s] * blocks + t * GROUP + k
                    at = start[b]
                    moved = pltpu.roll(jnp.where(spot, values[s], 0.0), shift[b], 1)
                    here = plane < QUAD - (at & (QUAD - 1))
                    near = slabs[s][pl.ds(at, 16), :] + jnp.where(here, moved, 0.0)
                    at_next = at + (SLAB - QUAD)
                    far = slabs[s][pl.ds(at_next, 16), :] + jnp.where(here, 0.0, moved)
                    sums.append((at, near, at_next, far))
                for s, (at, near, at_next, far) in enumerate(sums):
                    slabs[s][pl.ds(at, 16), :] = near
                    slabs[s][pl.ds(at_next, 16), :] = far
                return carry

            lax.fori_loop(0, GROUP, one, 0, unroll=UNROLL)

        def crosses(b):
            return shift[b] > LANES - 4

        tile_loop(half, devices // cols, cols, groups, crosses, tile)

        table = table_rows(cas, [place[1]], gs)

        def planes(n, carry):
            base = pl.multiple_of(n * SLAB, 8)
            sheets = []
            for q in range(QUAD):
                parts = []
                for s in range(SLABS):
                    part = slabs[s][pl.ds(base + (PAD + q), PIECE, stride=QUAD), :]
                    if s > 0:
                        at = base + (PAD + QUAD * PIECE + q)
                        over = slabs[s - 1][pl.ds(at, 8, stride=QUAD), :]
                        part = jnp.concatenate([part[:8] + over, part[8:]], axis=0)
                    parts.append(part.astype(jnp.bfloat16))
                sheets.append(jnp.concatenate(parts, axis=0))
            field = dot(table, jnp.concatenate(sheets, axis=1))
            for q in range(QUAD):
                part = field[:, LANES * q : LANES * q + LANES]
                lines[pl.ds(n * QUAD + q, gs, stride=STRIDE), :] = part
            return carry

        lax.fori_loop(0, G // QUAD, planes, 0, unroll=UNROLL_PLANES)

    @pl.when(step > 0)
    def _():
        third = table_rows(cas, [place[2], place[2] ^ 1], fs)
        for g in range(0, LINES, 2):
            pair = []
            for n in (g, g + 1):
                at = ((step - 1) * LINES + n) * STRIDE
                pair.append(lines[pl.ds(at, G), :].astype(jnp.bfloat16))
            field = dot(third, jnp.concatenate(pair, axis=1)).astype(jnp.bfloat16)
            for n in range(2):
                own_out[g + n] = field[:fs, LANES * n : LANES * n + LANES]
                other_out[g + n] = field[fs:, LANES * n : LANES * n + LANES]


def spectrum_kernel(place, own, other, weights, cas, own_out, other_out):
    tiles = [pl.ds(pl.multiple_of(h * LANES, LANES), LANES) for h in (place[0], 1 - place[0])]
    first = jnp.concatenate([cas[tile, :] for tile in tiles], axis=0)
    first_back = jnp.concatenate([cas[:, tile] for tile in tiles], axis=1)
    count, freqs, _ = weights.shape
    step = max(1, G // freqs)
    rows = step * freqs
    for g in range(0, count, step):
        part = slice(g, g + step)
        line = jnp.concatenate(
            [own[part].reshape(rows, LANES), other[part].reshape(rows, LANES)], axis=1
        )
        s = dot(line, first) * weights[part].reshape(rows, P_SIZE)
        line = dot(s.astype(jnp.bfloat16), first_back).astype(jnp.bfloat16)
        own_out[part] = line[:, :LANES].reshape(step, freqs, LANES)
        other_out[part] = line[:, LANES:].reshape(step, freqs, LANES)


def sample_kernel(
    cols, place, shift, start, mine, theirs, own, other, cas, out, extra, second, third, lines, cells
):
    half = place[0]
    step = pl.program_id(0)
    devices, held, _ = out.shape
    groups = held // 16
    blocks = groups * GROUP
    gs = second.shape[1]
    owner = iota((16, LANES), 1) // 4
    plane = iota((16, LANES), 0) % QUAD

    @pl.when(step == 0)
    def _():
        for side, part in enumerate((mine, theirs)):
            extra[side * (devices // 2) : (side + 1) * (devices // 2)] = part[:, held:]
        second[...] = turned(table_rows(cas, [place[1]], gs))
        third[...] = turned(table_rows(cas, [place[2], place[2] ^ 1], own.shape[1]))

    for g in range(0, LINES, 2):
        pair = [jnp.concatenate([own[n], other[n]], axis=0) for n in (g, g + 1)]
        field = dot(third[...], jnp.concatenate(pair, axis=1))
        for n in range(2):
            at = (step * LINES + g + n) * STRIDE
            lines[pl.ds(at, G), :] = field[:, LANES * n : LANES * n + LANES]

    @pl.when(step == pl.num_programs(0) - 1)
    def _():
        def planes(n, carry):
            sheets = [
                lines[pl.ds(n * QUAD + q, gs, stride=STRIDE), :].astype(jnp.bfloat16)
                for q in range(QUAD)
            ]
            field = dot(second[...], jnp.concatenate(sheets, axis=1))
            base = pl.multiple_of(n * CELLS, 8)
            for q in range(QUAD):
                part = field[:, LANES * q : LANES * q + LANES]
                cells[pl.ds(base + (PAD + q), G, stride=QUAD), :] = part
            return carry

        lax.fori_loop(0, G // QUAD, planes, 0, unroll=UNROLL_PLANES)
        out[...] = jnp.zeros_like(out)

        def tile(numbers, t):
            def one(k, sums):
                spot = owner == k
                new = []
                for s in range(SLABS):
                    b = numbers[s] * blocks + t * GROUP + k
                    at = start[b]
                    here = plane < QUAD - (at & (QUAD - 1))
                    near = cells[pl.ds(at, 16), :]
                    far = cells[pl.ds(at + (CELLS - QUAD), 16), :]
                    moved = pltpu.roll(jnp.where(here, near, far), shift[b], 1)
                    new.append(jnp.where(spot, moved, sums[s]))
                return tuple(new)

            zero = (jnp.zeros((16, LANES), jnp.float32),) * SLABS
            sums = lax.fori_loop(0, GROUP, one, zero, unroll=UNROLL)
            for s, d in enumerate(numbers):
                inside = lanes_inside(extra, d, t, half)
                out[d, pl.ds(pl.multiple_of(16 * t, 16), 16), :] = jnp.where(
                    inside, sums[s], 0.0
                ).astype(jnp.bfloat16)

        def crosses(b):
            return (shift[b] > 0) & (shift[b] < 4)

        tile_loop(half, devices // cols, cols, groups, crosses, tile)


def finish_kernel(values, interpolate, near, inverse, spots, out, total):
    blocks = near.shape[0]
    groups = values.shape[1] // 16
    rows, lanes = patch_places(spots[...])
    summed = values[0].astype(jnp.float32)
    for d in range(1, values.shape[0]):
        summed = summed + values[d].astype(jnp.float32)
    spread = jnp.concatenate([summed[16 * t : 16 * t + 16] for t in range(groups)], axis=1)
    parts = jnp.concatenate(split(spread), axis=0)
    patch = jnp.zeros((blocks, LANES), jnp.float32)
    for i in range(4):
        column = dot_nt(lanes[i], parts).astype(jnp.bfloat16)
        patch = patch + dot(column, jnp.concatenate([rows[i], rows[i]], axis=0))
    total[...] = block_sums(interpolate, patch) + near[...]
    count = out.shape[0]
    even = total[pl.ds(0, count, stride=2), :]
    odd = total[pl.ds(1, count, stride=2), :]
    total[:count] = jnp.where(iota(even.shape, 1) < BLK, even, odd)
    upper = inverse[:count]
    lower = inverse[count:]

    def step(u, acc):
        row = jnp.broadcast_to(total[pl.ds(u, 1), :], lower.shape)
        return jnp.where(upper == u, lane_gather(row, lower), acc)

    out[...] = lax.fori_loop(0, count, step, jnp.zeros(out.shape, jnp.float32), unroll=4)


def struct(shape, dtype):
    return jax.ShapeDtypeStruct(shape, dtype)


def whole(shape):
    return pl.BlockSpec(shape, lambda *_: (0,) * len(shape))


def params(mib):
    return pltpu.CompilerParams(vmem_limit_bytes=mib * MB)


def beside(array, axis, dim):
    count = lax.axis_size(axis)
    up = [(i, i + 1) for i in range(count - 1)]
    before = lax.ppermute(array, axis, up)
    after = lax.ppermute(array, axis, [(j, i) for i, j in up])
    return jnp.concatenate([before, array, after], axis=dim)


def body(
    charges,
    panel_order,
    patch_anchor,
    project,
    interpolate,
    kernel_spectrum,
    near_pairs,
    near_blocks,
):
    axes = ("row", "col")
    rows = lax.axis_size("row")
    cols = lax.axis_size("col")
    devices = rows * cols
    row_at = lax.axis_index("row")
    col_at = lax.axis_index("col")
    half = col_at % HALVES
    mates = [(c, c ^ 1) for c in range(cols)]
    blocks = project.shape[0]
    groups = blocks // GROUP
    panels = charges.shape[0]
    strips = panels // LANES
    gs, fs, _ = kernel_spectrum.shape
    held = 16 * groups + 16

    order = panel_order.reshape(strips, LANES)
    members = devices // HALVES
    block_charges, sent, spots = pl.pallas_call(
        project_kernel,
        out_shape=(
            struct((blocks, LANES), jnp.bfloat16),
            struct((members, held, LANES), jnp.bfloat16),
            struct((blocks, LANES), jnp.int32),
        ),
        in_specs=[pl.BlockSpec(memory_space=pltpu.HBM)] * 4,
        scratch_shapes=[
            pltpu.VMEM((strips, LANES), jnp.bfloat16),
            pltpu.VMEM((strips, LANES), jnp.int32),
            pltpu.VMEM(project.shape, jnp.bfloat16),
            pltpu.VMEM(patch_anchor.shape, jnp.int32),
            pltpu.VMEM((strips, LANES), jnp.float32),
            pltpu.VMEM((blocks, LANES), jnp.float32),
            pltpu.SemaphoreType.DMA((4,)),
        ],
        compiler_params=params(58),
        name="project",
    )(
        charges.reshape(strips, LANES),
        order,
        project,
        patch_anchor,
    )
    cores = [
        [r * cols + c for r in range(rows) for c in range(core, cols, HALVES)]
        for core in range(HALVES)
    ]

    def swap_members(array):
        return lax.all_to_all(
            array, axes, split_axis=0, concat_axis=0, axis_index_groups=cores, tiled=True
        )

    mine = swap_members(sent)
    theirs = lax.ppermute(mine, "col", mates)
    inverse = pl.pallas_call(
        inverse_kernel,
        out_shape=struct((2 * strips, LANES), jnp.int32),
        compiler_params=params(32),
        name="inverse",
    )(order)

    mine, inverse = lax.optimization_barrier((mine, inverse))
    anchors = jnp.stack([part[:, 17 * groups : 17 * groups + 3] for part in (mine, theirs)])
    anchors = anchors.astype(jnp.int32)
    lane = 4 * (jnp.arange(blocks, dtype=jnp.int32) % GROUP)
    forth = ((anchors[:, :, 0] - lane) & (LANES - 1)).reshape(devices * blocks)
    back = ((lane - anchors[:, :, 0]) & (LANES - 1)).reshape(devices * blocks)
    group = anchors[:, :, 2] // QUAD
    inner = PAD + QUAD * anchors[:, :, 1] + anchors[:, :, 2] % QUAD
    side = jnp.arange(HALVES, dtype=jnp.int32)[:, None] ^ half
    col = jnp.arange(members, dtype=jnp.int32) % (cols // HALVES) * HALVES + side
    piece = (col * SLABS // cols * PIECE)[:, :, None]
    slab_at = (group * SLAB + inner - QUAD * piece).reshape(devices * blocks)
    cell_at = (group * CELLS + inner).reshape(devices * blocks)
    place = jnp.stack([half, row_at, col_at]).astype(jnp.int32)
    cas = jnp.asarray(CAS)

    smem = pl.BlockSpec(memory_space=pltpu.SMEM)
    steps = gs // LINES
    lines_type = struct((gs, fs, LANES), jnp.bfloat16)
    late = pl.BlockSpec((LINES, fs, LANES), lambda n: (jnp.maximum(n - 1, 0), 0, 0))
    own, other = pl.pallas_call(
        functools.partial(scatter_kernel, cols, gs, fs),
        grid=(1 + steps,),
        in_specs=[smem] * 3 + [whole(mine.shape)] * 2 + [whole(cas.shape)],
        out_specs=(late, late),
        out_shape=(lines_type, lines_type),
        scratch_shapes=[
            pltpu.VMEM((devices, 16 * groups, LANES), jnp.bfloat16),
            pltpu.VMEM((devices, 16, LANES), jnp.bfloat16),
            pltpu.VMEM((gs * STRIDE, LANES), jnp.float32),
        ]
        + [pltpu.VMEM(((G // QUAD + 1) * SLAB, LANES), jnp.float32)] * SLABS,
        compiler_params=params(53),
        name="scatter",
    )(place, forth, slab_at, mine, theirs, cas)
    other = lax.ppermute(other, "col", mates)
    own, block_charges = lax.optimization_barrier((own, block_charges))
    around = beside(block_charges[None, None], "row", 0)
    other, around = lax.optimization_barrier((other, around))

    part = lambda shape: pl.BlockSpec((BATCH,) + shape, lambda n: (n, 0, 0))
    own, other = pl.pallas_call(
        spectrum_kernel,
        grid=(gs // BATCH,),
        in_specs=[
            smem,
            part((fs, LANES)),
            part((fs, LANES)),
            part((fs, P_SIZE)),
            whole(cas.shape),
        ],
        out_specs=(part((fs, LANES)), part((fs, LANES))),
        out_shape=(lines_type, lines_type),
        compiler_params=params(40),
        name="spectrum",
    )(place, own, other, kernel_spectrum, cas)
    other = lax.ppermute(other, "col", mates)
    own, around = lax.optimization_barrier((own, around))
    around = beside(around, "col", 1).reshape(9, blocks, LANES)
    other, around = lax.optimization_barrier((other, around))

    early = pl.BlockSpec((LINES, fs, LANES), lambda n: (n, 0, 0))
    values = pl.pallas_call(
        functools.partial(sample_kernel, cols),
        grid=(steps,),
        in_specs=[smem] * 3 + [whole(mine.shape)] * 2 + [early, early, whole(cas.shape)],
        out_specs=whole((devices, 16 * groups, LANES)),
        out_shape=struct((devices, 16 * groups, LANES), jnp.bfloat16),
        scratch_shapes=[
            pltpu.VMEM((devices, 16, LANES), jnp.bfloat16),
            pltpu.VMEM((G, gs), jnp.bfloat16),
            pltpu.VMEM((G, 2 * fs), jnp.bfloat16),
            pltpu.VMEM((gs * STRIDE, LANES), jnp.float32),
            pltpu.VMEM(((G // QUAD + 1) * CELLS, LANES), jnp.float32),
        ],
        compiler_params=params(46),
        name="sample",
    )(place, back, cell_at, mine, theirs, own, other, cas)
    values = values.reshape(HALVES, members, 16 * groups, LANES)
    received = lax.ppermute(values[1], "col", mates).astype(jnp.float32)
    values = (values[0].astype(jnp.float32) + received).astype(jnp.bfloat16)
    values, around = lax.optimization_barrier((values, around))
    values = swap_members(values)

    source = near_pairs[1]
    source_device = source // blocks
    code = (source_device // cols - row_at + 1) * 3 + (source_device % cols - col_at + 1)
    wanted = code * blocks + source % blocks
    target = near_pairs[0] - (row_at * cols + col_at) * blocks
    pairs = near_blocks.shape[0]
    near = pl.pallas_call(
        near_kernel,
        grid=(pairs // blocks,),
        in_specs=[
            smem,
            pl.BlockSpec((blocks, BLK * BLK), lambda n: (n, 0)),
            pl.BlockSpec((1, blocks), lambda n: (0, n)),
            whole((9, blocks, LANES)),
        ],
        out_specs=whole((blocks, LANES)),
        out_shape=struct((blocks, LANES), jnp.float32),
        scratch_shapes=[
            pltpu.VMEM((9 * blocks, LANES), jnp.float32),
            pltpu.VMEM((blocks, LANES), jnp.float32),
        ],
        compiler_params=params(56),
        name="near",
    )(wanted, near_blocks, target.reshape(1, pairs), around)

    result = pl.pallas_call(
        finish_kernel,
        out_shape=struct((strips, LANES), jnp.float32),
        scratch_shapes=[pltpu.VMEM((blocks, LANES), jnp.float32)],
        compiler_params=params(32),
        name="finish",
    )(values, interpolate, near, inverse, spots)
    return result.reshape(panels)


def solution(mesh):
    placed = (
        P(("row", "col")),
        P(("row", "col")),
        P(None, ("row", "col")),
        P(("row", "col"), None),
        P(("row", "col"), None),
        P("row", "col", None),
        P(None, ("row", "col")),
        P(("row", "col"), None),
    )
    return jax.shard_map(
        body, mesh=mesh, in_specs=placed, out_specs=P(("row", "col")), check_vma=False
    )
```

```python
import functools

import jax
import jax.numpy as jnp
import ml_dtypes
import numpy as np
from jax import lax
from jax.experimental import pallas as pl
from jax.experimental.pallas import tpu as pltpu
from jax.sharding import PartitionSpec as P

G = 256
P_SIZE = 512
BLK = 64
PTS = 64
LANES = 128
GROUP = LANES // 4
HALVES = G // LANES
SLABS = 4
PIECE = G // SLABS
QUAD = 4
PAD = 8
SLAB = PAD + QUAD * PIECE + 32
CELLS = PAD + QUAD * G + 16
STRIDE = G + 1
BATCH = 8
LINES = 16
UNROLL = 32
UNROLL_PLANES = 16
MB = 1 << 20
NT = (((1,), (1,)), ((), ()))


def cas_table():
    index = np.arange(P_SIZE, dtype=np.int64)
    phase = (index[:, None] * index[None, :] % P_SIZE).astype(np.float64) * (2.0 * np.pi / P_SIZE)
    return ((np.cos(phase) + np.sin(phase)) / np.sqrt(P_SIZE)).astype(ml_dtypes.bfloat16)


CAS = cas_table()


def dot(a, b):
    return jnp.dot(a, b, preferred_element_type=jnp.float32)


def dot_nt(a, b):
    return lax.dot_general(a, b, NT, preferred_element_type=jnp.float32)


def iota(shape, dim):
    return lax.broadcasted_iota(jnp.int32, shape, dim)


def split(value):
    high = value.astype(jnp.bfloat16)
    return high, (value - high.astype(jnp.float32)).astype(jnp.bfloat16)


def lane_gather(table, index):
    return jnp.take_along_axis(table, index, axis=1, mode="promise_in_bounds")


def block_sums(mats, vecs):
    rows = vecs.shape[0]
    pair = jnp.concatenate([vecs, vecs], axis=1)
    total = jnp.zeros((2 * rows, LANES), jnp.float32)
    for t in range(mats.shape[1] // 256):
        high, low = split(mats[:, 256 * t : 256 * t + 256].astype(jnp.float32) * pair)
        owner = iota((256, LANES), 0) // BLK + 4 * t
        table = (owner == iota((256, LANES), 1) % BLK).astype(jnp.bfloat16)
        total = total + dot(jnp.concatenate([high, low], axis=0), table)
    return total[:rows] + total[rows:]


def patch_places(spots):
    blocks = spots.shape[0]
    spots = jnp.concatenate([spots] * (4 * blocks // LANES), axis=1)
    lane = iota(spots.shape, 1)
    lanes = [(lane == 4 * spots + i).astype(jnp.float32).astype(jnp.bfloat16) for i in range(4)]
    row = iota((16, LANES), 0)
    rows = [
        (iota((16, LANES), 1) % PTS == 16 * i + row).astype(jnp.float32).astype(jnp.bfloat16)
        for i in range(4)
    ]
    return rows, lanes


def block_spots(first):
    blocks = first.shape[1]
    shape = (blocks, blocks)
    crossing = ((first & (LANES - 1)) > LANES - 4).astype(jnp.float32)
    crossing = jnp.broadcast_to(crossing, (8, blocks))
    earlier = (iota(shape, 0) < iota(shape, 1)).astype(jnp.float32).astype(jnp.bfloat16)
    ahead = dot(crossing.astype(jnp.bfloat16), earlier)
    total = jnp.sum(crossing, axis=1, keepdims=True)
    block = iota((8, blocks), 1).astype(jnp.float32)
    spot = jnp.where(crossing > 0.0, ahead, total + block - ahead)
    spread = jnp.broadcast_to(spot[:1], (LANES, blocks)).astype(jnp.bfloat16)
    unit = (iota(shape, 0) == iota(shape, 1)).astype(jnp.float32).astype(jnp.bfloat16)
    return dot_nt(unit, spread).astype(jnp.int32)


def project_kernel(
    charges_in,
    order_in,
    project_in,
    anchors_in,
    sent_out,
    spot_out,
    charges,
    order,
    project,
    anchors,
    table,
    doubled,
    sems,
):
    blocks = spot_out.shape[0]
    groups = blocks // GROUP
    pairs = ((charges_in, charges), (order_in, order), (project_in, project), (anchors_in, anchors))
    copies = [pltpu.make_async_copy(a, b, sems.at[n]) for n, (a, b) in enumerate(pairs)]
    for copy in copies:
        copy.start()
    copies[0].wait()
    copies[1].wait()
    table[...] = charges[...].astype(jnp.float32)
    strips = table.shape[0]
    upper = order[...] // LANES
    lower = order[...] % LANES

    def step(u, acc):
        row = jnp.broadcast_to(table[pl.ds(u, 1), :], lower.shape)
        return jnp.where(upper == u, lane_gather(row, lower), acc)

    slots = lax.fori_loop(0, strips, step, jnp.zeros(lower.shape, jnp.float32), unroll=4)
    swapped = pltpu.roll(slots, BLK, 1)
    left = iota(slots.shape, 1) < BLK
    doubled[pl.ds(0, strips, stride=2), :] = jnp.where(left, slots, swapped)
    doubled[pl.ds(1, strips, stride=2), :] = jnp.where(left, swapped, slots)
    twice = doubled[...]
    copies[2].wait()
    copies[3].wait()
    patch = block_sums(project, twice)
    patch = jnp.where(iota(patch.shape, 1) < PTS, patch, 0.0).astype(jnp.bfloat16)
    spots = block_spots(anchors[:1, :])
    spot_out[...] = spots
    rows, lanes = patch_places(spots)
    moved = (iota(spots.shape, 1) == spots).astype(jnp.float32).astype(jnp.bfloat16)
    corner = anchors[...].astype(jnp.float32).astype(jnp.bfloat16)
    corner = dot(jnp.concatenate([corner] * 3, axis=0)[:8], moved)
    cells = (iota((8, 4 * blocks), 1) % 4).astype(jnp.float32)
    start = jnp.broadcast_to(anchors[:1, :].astype(jnp.float32), (8, blocks)).astype(jnp.bfloat16)
    for i in range(4):
        cells = cells + dot(start, lanes[i])
    spread = jnp.zeros((16, 4 * blocks), jnp.float32)
    for i in range(4):
        spread = spread + dot(dot_nt(rows[i], patch).astype(jnp.bfloat16), lanes[i])
    tiles = [slice(LANES * t, LANES * t + LANES) for t in range(groups)]
    sent = [spread[:, tile].astype(jnp.bfloat16) for tile in tiles]
    sent.append(slots.astype(jnp.bfloat16))
    extra = [cells[:1, tile] for tile in tiles] + [corner[:3]]
    extra.append(jnp.zeros((13 - groups, LANES), jnp.float32))
    sent.append(jnp.concatenate(extra, axis=0).astype(jnp.bfloat16))
    sent = jnp.concatenate(sent, axis=0)
    for n in range(sent_out.shape[0]):
        sent_out[n] = sent


def inverse_kernel(order, out):
    rows = order.shape[0]

    def step(r, acc):
        here = order[pl.ds(r, 1), :]
        upper = iota((rows, LANES), 0) == here // LANES
        lower = iota((LANES, LANES), 0) == here % LANES
        values = jnp.concatenate(
            [
                jnp.where(upper, r.astype(jnp.float32), 0.0),
                jnp.where(upper, iota((rows, LANES), 1).astype(jnp.float32), 0.0),
            ],
            axis=0,
        )
        return acc + dot_nt(
            values.astype(jnp.bfloat16), lower.astype(jnp.float32).astype(jnp.bfloat16)
        )

    out[...] = lax.fori_loop(
        0, rows, step, jnp.zeros((2 * rows, LANES), jnp.float32), unroll=4
    ).astype(jnp.int32)


def near_kernel(source, near_blocks, target, mine, theirs, out, table, picked):
    step = pl.program_id(0)
    pairs = picked.shape[0]
    blocks = out.shape[0]

    @pl.when(step == 0)
    def _():
        members, strips, _ = mine.shape
        left = iota((strips, LANES), 1) < BLK
        for side, part in enumerate((mine, theirs)):
            for n in range(members):
                at = (side * members + n) * blocks
                slots = part[n].astype(jnp.float32)
                swapped = pltpu.roll(slots, BLK, 1)
                table[pl.ds(at, strips, stride=2), :] = jnp.where(left, slots, swapped)
                table[pl.ds(at + 1, strips, stride=2), :] = jnp.where(left, swapped, slots)
        out[...] = jnp.zeros_like(out)

    def pick(p, carry):
        picked[pl.ds(p, 1), :] = table[pl.ds(source[step * pairs + p], 1), :]
        return carry

    lax.fori_loop(0, pairs, pick, 0, unroll=8)
    terms = block_sums(near_blocks, picked[...])
    owner = (iota((blocks, pairs), 0) == target[...]).astype(jnp.float32).astype(jnp.bfloat16)
    high, low = split(terms)
    out[...] += dot(owner, high) + dot(owner, low)


def table_rows(cas, numbers, count):
    parts = [cas[pl.ds(pl.multiple_of(n * count, 16), count), :G] for n in numbers]
    return jnp.concatenate(parts, axis=0) if len(parts) > 1 else parts[0]


def turned(rows):
    unit = (iota((G, G), 0) == iota((G, G), 1)).astype(jnp.float32).astype(jnp.bfloat16)
    return dot_nt(unit, rows).astype(jnp.bfloat16)


def tile_loop(half, rows, cols, groups, crosses, body):
    per_slab = cols // SLABS
    low = jnp.maximum(half * (rows // HALVES) - 1, 0)
    high = (half + 1) * (rows // HALVES)
    per_row = per_slab * groups

    def place(row, col):
        side = (col % HALVES) ^ half
        return side * (rows * cols // HALVES) + row * (cols // HALVES) + col // HALVES

    def step(n, carry):
        row = low + n // per_row
        left = n % per_row
        t = left % groups
        devices = [place(row, s * per_slab + left // groups) for s in range(SLABS)]
        found = [crosses((d * groups + t) * GROUP) for d in devices]
        inside = row >= half * (rows // HALVES)
        pl.when(functools.reduce(jnp.logical_or, found, inside))(lambda: body(devices, t))
        return carry

    lax.fori_loop(0, (high - low) * per_row, step, 0)


def lanes_inside(extra, d, t, half):
    extra = extra[d].astype(jnp.float32)
    picked = jnp.where(iota(extra.shape, 0) == t, extra, 0.0)
    cells = jnp.sum(picked, axis=0, keepdims=True) - (half * LANES).astype(jnp.float32)
    return jnp.broadcast_to((cells >= 0.0) & (cells < LANES), (16, LANES))


def scatter_kernel(
    cols,
    gs,
    fs,
    place,
    shift,
    start,
    mine,
    theirs,
    my_extra,
    their_extra,
    cas,
    own_out,
    other_out,
    patches,
    extra,
    lines,
    *slabs,
):
    half = place[0]
    step = pl.program_id(0)
    devices, held, _ = patches.shape
    groups = held // 16
    blocks = groups * GROUP
    owner = iota((16, LANES), 1) // 4
    plane = iota((16, LANES), 0) % QUAD

    @pl.when(step == 0)
    def _():
        def clear(n, carry):
            for slab in slabs:
                slab[pl.ds(pl.multiple_of(n * SLAB, 8), SLAB), :] = jnp.zeros(
                    (SLAB, LANES), jnp.float32
                )
            return carry

        lax.fori_loop(0, slabs[0].shape[0] // SLAB, clear, 0)
        for side, part in enumerate(((mine, my_extra), (theirs, their_extra))):
            at = slice(side * (devices // 2), (side + 1) * (devices // 2))
            patches[at] = part[0][...]
            extra[at] = part[1][...]

        def tile(numbers, t):
            values = []
            for d in numbers:
                part = patches[d, pl.ds(pl.multiple_of(16 * t, 16), 16), :].astype(jnp.float32)
                values.append(jnp.where(lanes_inside(extra, d, t, half), part, 0.0))

            def one(k, carry):
                spot = owner == k
                sums = []
                for s in range(SLABS):
                    b = numbers[s] * blocks + t * GROUP + k
                    at = start[b]
                    moved = pltpu.roll(jnp.where(spot, values[s], 0.0), shift[b], 1)
                    here = plane < QUAD - (at & (QUAD - 1))
                    near = slabs[s][pl.ds(at, 16), :] + jnp.where(here, moved, 0.0)
                    at_next = at + (SLAB - QUAD)
                    far = slabs[s][pl.ds(at_next, 16), :] + jnp.where(here, 0.0, moved)
                    sums.append((at, near, at_next, far))
                for s, (at, near, at_next, far) in enumerate(sums):
                    slabs[s][pl.ds(at, 16), :] = near
                    slabs[s][pl.ds(at_next, 16), :] = far
                return carry

            lax.fori_loop(0, GROUP, one, 0, unroll=UNROLL)

        def crosses(b):
            return shift[b] > LANES - 4

        tile_loop(half, devices // cols, cols, groups, crosses, tile)

        table = table_rows(cas, [place[1]], gs)

        def planes(n, carry):
            base = pl.multiple_of(n * SLAB, 8)
            sheets = []
            for q in range(QUAD):
                parts = []
                for s in range(SLABS):
                    part = slabs[s][pl.ds(base + (PAD + q), PIECE, stride=QUAD), :]
                    if s > 0:
                        at = base + (PAD + QUAD * PIECE + q)
                        over = slabs[s - 1][pl.ds(at, 8, stride=QUAD), :]
                        part = jnp.concatenate([part[:8] + over, part[8:]], axis=0)
                    parts.append(part.astype(jnp.bfloat16))
                sheets.append(jnp.concatenate(parts, axis=0))
            field = dot(table, jnp.concatenate(sheets, axis=1))
            for q in range(QUAD):
                part = field[:, LANES * q : LANES * q + LANES]
                lines[pl.ds(n * QUAD + q, gs, stride=STRIDE), :] = part
            return carry

        lax.fori_loop(0, G // QUAD, planes, 0, unroll=UNROLL_PLANES)

    @pl.when(step > 0)
    def _():
        third = table_rows(cas, [place[2], place[2] ^ 1], fs)
        for g in range(0, LINES, 2):
            pair = []
            for n in (g, g + 1):
                at = ((step - 1) * LINES + n) * STRIDE
                pair.append(lines[pl.ds(at, G), :].astype(jnp.bfloat16))
            field = dot(third, jnp.concatenate(pair, axis=1)).astype(jnp.bfloat16)
            for n in range(2):
                own_out[g + n] = field[:fs, LANES * n : LANES * n + LANES]
                other_out[g + n] = field[fs:, LANES * n : LANES * n + LANES]


def spectrum_kernel(place, own, other, weights, cas, own_out, other_out):
    tiles = [pl.ds(pl.multiple_of(h * LANES, LANES), LANES) for h in (place[0], 1 - place[0])]
    first = jnp.concatenate([cas[tile, :] for tile in tiles], axis=0)
    first_back = jnp.concatenate([cas[:, tile] for tile in tiles], axis=1)
    count, freqs, _ = weights.shape
    step = max(1, G // freqs)
    rows = step * freqs
    for g in range(0, count, step):
        part = slice(g, g + step)
        line = jnp.concatenate(
            [own[part].reshape(rows, LANES), other[part].reshape(rows, LANES)], axis=1
        )
        s = dot(line, first) * weights[part].reshape(rows, P_SIZE)
        line = dot(s.astype(jnp.bfloat16), first_back).astype(jnp.bfloat16)
        own_out[part] = line[:, :LANES].reshape(step, freqs, LANES)
        other_out[part] = line[:, LANES:].reshape(step, freqs, LANES)


def sample_kernel(
    cols,
    place,
    shift,
    start,
    my_extra,
    their_extra,
    own,
    other,
    cas,
    out,
    extra,
    second,
    third,
    lines,
    cells,
):
    half = place[0]
    step = pl.program_id(0)
    devices, held, _ = out.shape
    groups = held // 16
    blocks = groups * GROUP
    gs = second.shape[1]
    owner = iota((16, LANES), 1) // 4
    plane = iota((16, LANES), 0) % QUAD

    @pl.when(step == 0)
    def _():
        for side, part in enumerate((my_extra, their_extra)):
            extra[side * (devices // 2) : (side + 1) * (devices // 2)] = part[...]
        second[...] = turned(table_rows(cas, [place[1]], gs))
        third[...] = turned(table_rows(cas, [place[2], place[2] ^ 1], own.shape[1]))

    for g in range(0, LINES, 2):
        pair = [jnp.concatenate([own[n], other[n]], axis=0) for n in (g, g + 1)]
        field = dot(third[...], jnp.concatenate(pair, axis=1))
        for n in range(2):
            at = (step * LINES + g + n) * STRIDE
            lines[pl.ds(at, G), :] = field[:, LANES * n : LANES * n + LANES]

    @pl.when(step == pl.num_programs(0) - 1)
    def _():
        def planes(n, carry):
            sheets = [
                lines[pl.ds(n * QUAD + q, gs, stride=STRIDE), :].astype(jnp.bfloat16)
                for q in range(QUAD)
            ]
            field = dot(second[...], jnp.concatenate(sheets, axis=1))
            base = pl.multiple_of(n * CELLS, 8)
            for q in range(QUAD):
                part = field[:, LANES * q : LANES * q + LANES]
                cells[pl.ds(base + (PAD + q), G, stride=QUAD), :] = part
            return carry

        lax.fori_loop(0, G // QUAD, planes, 0, unroll=UNROLL_PLANES)
        out[...] = jnp.zeros_like(out)

        def tile(numbers, t):
            def one(k, sums):
                spot = owner == k
                new = []
                for s in range(SLABS):
                    b = numbers[s] * blocks + t * GROUP + k
                    at = start[b]
                    here = plane < QUAD - (at & (QUAD - 1))
                    near = cells[pl.ds(at, 16), :]
                    far = cells[pl.ds(at + (CELLS - QUAD), 16), :]
                    moved = pltpu.roll(jnp.where(here, near, far), shift[b], 1)
                    new.append(jnp.where(spot, moved, sums[s]))
                return tuple(new)

            zero = (jnp.zeros((16, LANES), jnp.float32),) * SLABS
            sums = lax.fori_loop(0, GROUP, one, zero, unroll=UNROLL)
            for s, d in enumerate(numbers):
                inside = lanes_inside(extra, d, t, half)
                out[d, pl.ds(pl.multiple_of(16 * t, 16), 16), :] = jnp.where(
                    inside, sums[s], 0.0
                ).astype(jnp.bfloat16)

        def crosses(b):
            return (shift[b] > 0) & (shift[b] < 4)

        tile_loop(half, devices // cols, cols, groups, crosses, tile)


def finish_kernel(values, interpolate, near, inverse, spots, out, total):
    blocks = near.shape[0]
    groups = values.shape[1] // 16
    rows, lanes = patch_places(spots[...])
    summed = values[0].astype(jnp.float32)
    for d in range(1, values.shape[0]):
        summed = summed + values[d].astype(jnp.float32)
    spread = jnp.concatenate([summed[16 * t : 16 * t + 16] for t in range(groups)], axis=1)
    parts = jnp.concatenate(split(spread), axis=0)
    patch = jnp.zeros((blocks, LANES), jnp.float32)
    for i in range(4):
        column = dot_nt(lanes[i], parts).astype(jnp.bfloat16)
        patch = patch + dot(column, jnp.concatenate([rows[i], rows[i]], axis=0))
    total[...] = block_sums(interpolate, patch) + near[...]
    count = out.shape[0]
    even = total[pl.ds(0, count, stride=2), :]
    odd = total[pl.ds(1, count, stride=2), :]
    total[:count] = jnp.where(iota(even.shape, 1) < BLK, even, odd)
    upper = inverse[:count]
    lower = inverse[count:]

    def step(u, acc):
        row = jnp.broadcast_to(total[pl.ds(u, 1), :], lower.shape)
        return jnp.where(upper == u, lane_gather(row, lower), acc)

    out[...] = lax.fori_loop(0, count, step, jnp.zeros(out.shape, jnp.float32), unroll=4)


def struct(shape, dtype):
    return jax.ShapeDtypeStruct(shape, dtype)


def whole(shape):
    return pl.BlockSpec(shape, lambda *_: (0,) * len(shape))


def params(mib):
    return pltpu.CompilerParams(vmem_limit_bytes=mib * MB)


def body(
    charges,
    panel_order,
    patch_anchor,
    project,
    interpolate,
    kernel_spectrum,
    near_pairs,
    near_blocks,
):
    axes = ("row", "col")
    rows = lax.axis_size("row")
    cols = lax.axis_size("col")
    devices = rows * cols
    row_at = lax.axis_index("row")
    col_at = lax.axis_index("col")
    half = col_at % HALVES
    mates = [(c, c ^ 1) for c in range(cols)]
    blocks = project.shape[0]
    groups = blocks // GROUP
    panels = charges.shape[0]
    strips = panels // LANES
    gs, fs, _ = kernel_spectrum.shape
    held = 16 * groups + strips + 16

    order = panel_order.reshape(strips, LANES)
    members = devices // HALVES
    sent, spots = pl.pallas_call(
        project_kernel,
        out_shape=(
            struct((members, held, LANES), jnp.bfloat16),
            struct((blocks, LANES), jnp.int32),
        ),
        in_specs=[pl.BlockSpec(memory_space=pltpu.HBM)] * 4,
        scratch_shapes=[
            pltpu.VMEM((strips, LANES), jnp.bfloat16),
            pltpu.VMEM((strips, LANES), jnp.int32),
            pltpu.VMEM(project.shape, jnp.bfloat16),
            pltpu.VMEM(patch_anchor.shape, jnp.int32),
            pltpu.VMEM((strips, LANES), jnp.float32),
            pltpu.VMEM((blocks, LANES), jnp.float32),
            pltpu.SemaphoreType.DMA((4,)),
        ],
        compiler_params=params(58),
        name="project",
    )(
        charges.reshape(strips, LANES),
        order,
        project,
        patch_anchor,
    )
    cores = [
        [r * cols + c for r in range(rows) for c in range(core, cols, HALVES)]
        for core in range(HALVES)
    ]

    def swap_members(array):
        return lax.all_to_all(
            array, axes, split_axis=0, concat_axis=0, axis_index_groups=cores, tiled=True
        )

    mine = swap_members(sent)
    theirs = lax.ppermute(mine, "col", mates)
    inverse = pl.pallas_call(
        inverse_kernel,
        out_shape=struct((2 * strips, LANES), jnp.int32),
        compiler_params=params(32),
        name="inverse",
    )(order)

    mine, inverse = lax.optimization_barrier((mine, inverse))
    at = held - 16 + groups
    anchors = jnp.stack([part[:, at : at + 3] for part in (mine, theirs)])
    anchors = anchors.astype(jnp.int32)
    lane = 4 * (jnp.arange(blocks, dtype=jnp.int32) % GROUP)
    forth = ((anchors[:, :, 0] - lane) & (LANES - 1)).reshape(devices * blocks)
    back = ((lane - anchors[:, :, 0]) & (LANES - 1)).reshape(devices * blocks)
    group = anchors[:, :, 2] // QUAD
    inner = PAD + QUAD * anchors[:, :, 1] + anchors[:, :, 2] % QUAD
    side = jnp.arange(HALVES, dtype=jnp.int32)[:, None] ^ half
    col = jnp.arange(members, dtype=jnp.int32) % (cols // HALVES) * HALVES + side
    piece = (col * SLABS // cols * PIECE)[:, :, None]
    slab_at = (group * SLAB + inner - QUAD * piece).reshape(devices * blocks)
    cell_at = (group * CELLS + inner).reshape(devices * blocks)
    place = jnp.stack([half, row_at, col_at]).astype(jnp.int32)
    cas = jnp.asarray(CAS)

    smem = pl.BlockSpec(memory_space=pltpu.SMEM)

    def rows_at(start, count):
        return pl.BlockSpec((members, count, LANES), lambda *_: (0, start // count, 0))

    patch_rows = rows_at(0, 16 * groups)
    charge_rows = rows_at(16 * groups, strips)
    extra_rows = rows_at(16 * groups + strips, 16)
    steps = gs // LINES
    lines_type = struct((gs, fs, LANES), jnp.bfloat16)
    late = pl.BlockSpec((LINES, fs, LANES), lambda n: (jnp.maximum(n - 1, 0), 0, 0))
    own, other = pl.pallas_call(
        functools.partial(scatter_kernel, cols, gs, fs),
        grid=(1 + steps,),
        in_specs=[smem] * 3 + [patch_rows] * 2 + [extra_rows] * 2 + [whole(cas.shape)],
        out_specs=(late, late),
        out_shape=(lines_type, lines_type),
        scratch_shapes=[
            pltpu.VMEM((devices, 16 * groups, LANES), jnp.bfloat16),
            pltpu.VMEM((devices, 16, LANES), jnp.bfloat16),
            pltpu.VMEM((gs * STRIDE, LANES), jnp.float32),
        ]
        + [pltpu.VMEM(((G // QUAD + 1) * SLAB, LANES), jnp.float32)] * SLABS,
        compiler_params=params(53),
        name="scatter",
    )(place, forth, slab_at, mine, theirs, mine, theirs, cas)
    other = lax.ppermute(other, "col", mates)

    part = lambda shape: pl.BlockSpec((BATCH,) + shape, lambda n: (n, 0, 0))
    own, other = pl.pallas_call(
        spectrum_kernel,
        grid=(gs // BATCH,),
        in_specs=[
            smem,
            part((fs, LANES)),
            part((fs, LANES)),
            part((fs, P_SIZE)),
            whole(cas.shape),
        ],
        out_specs=(part((fs, LANES)), part((fs, LANES))),
        out_shape=(lines_type, lines_type),
        compiler_params=params(40),
        name="spectrum",
    )(place, own, other, kernel_spectrum, cas)
    other = lax.ppermute(other, "col", mates)

    early = pl.BlockSpec((LINES, fs, LANES), lambda n: (n, 0, 0))
    values = pl.pallas_call(
        functools.partial(sample_kernel, cols),
        grid=(steps,),
        in_specs=[smem] * 3 + [extra_rows] * 2 + [early, early, whole(cas.shape)],
        out_specs=whole((devices, 16 * groups, LANES)),
        out_shape=struct((devices, 16 * groups, LANES), jnp.bfloat16),
        scratch_shapes=[
            pltpu.VMEM((devices, 16, LANES), jnp.bfloat16),
            pltpu.VMEM((G, gs), jnp.bfloat16),
            pltpu.VMEM((G, 2 * fs), jnp.bfloat16),
            pltpu.VMEM((gs * STRIDE, LANES), jnp.float32),
            pltpu.VMEM(((G // QUAD + 1) * CELLS, LANES), jnp.float32),
        ],
        compiler_params=params(46),
        name="sample",
    )(place, back, cell_at, mine, theirs, own, other, cas)
    values = values.reshape(HALVES, members, 16 * groups, LANES)
    received = lax.ppermute(values[1], "col", mates).astype(jnp.float32)
    values = (values[0].astype(jnp.float32) + received).astype(jnp.bfloat16)
    values, my_charges, their_charges = lax.optimization_barrier((values, mine, theirs))
    values = swap_members(values)

    source = near_pairs[1]
    source_row = source // blocks // cols
    source_col = source // blocks % cols
    wanted = (source_col % HALVES ^ half) * members + source_row * (cols // HALVES)
    wanted = (wanted + source_col // HALVES) * blocks + source % blocks
    target = near_pairs[0] - (row_at * cols + col_at) * blocks
    pairs = near_blocks.shape[0]
    near = pl.pallas_call(
        near_kernel,
        grid=(pairs // blocks,),
        in_specs=[
            smem,
            pl.BlockSpec((blocks, BLK * BLK), lambda n: (n, 0)),
            pl.BlockSpec((1, blocks), lambda n: (0, n)),
            charge_rows,
            charge_rows,
        ],
        out_specs=whole((blocks, LANES)),
        out_shape=struct((blocks, LANES), jnp.float32),
        scratch_shapes=[
            pltpu.VMEM((devices * blocks, LANES), jnp.float32),
            pltpu.VMEM((blocks, LANES), jnp.float32),
        ],
        compiler_params=params(56),
        name="near",
    )(wanted, near_blocks, target.reshape(1, pairs), my_charges, their_charges)

    result = pl.pallas_call(
        finish_kernel,
        out_shape=struct((strips, LANES), jnp.float32),
        scratch_shapes=[pltpu.VMEM((blocks, LANES), jnp.float32)],
        compiler_params=params(32),
        name="finish",
    )(values, interpolate, near, inverse, spots)
    return result.reshape(panels)


def solution(mesh):
    placed = (
        P(("row", "col")),
        P(("row", "col")),
        P(None, ("row", "col")),
        P(("row", "col"), None),
        P(("row", "col"), None),
        P("row", "col", None),
        P(None, ("row", "col")),
        P(("row", "col"), None),
    )
    return jax.shard_map(
        body, mesh=mesh, in_specs=placed, out_specs=P(("row", "col")), check_vma=False
    )
```

```python
import functools

import jax
import jax.numpy as jnp
import ml_dtypes
import numpy as np
from jax import lax
from jax.experimental import pallas as pl
from jax.experimental.pallas import tpu as pltpu
from jax.sharding import PartitionSpec as P

G = 256
P_SIZE = 512
BLK = 64
PTS = 64
LANES = 128
GROUP = LANES // 4
HALVES = G // LANES
SLABS = 4
PIECE = G // SLABS
QUAD = 4
PAD = 8
SLAB = PAD + QUAD * PIECE + 16
CELLS = PAD + QUAD * G + 16
STRIDE = G + 1
BATCH = 8
LINES = 16
UNROLL = 32
UNROLL_PLANES = 16
MB = 1 << 20
NT = (((1,), (1,)), ((), ()))


def cas_table():
    index = np.arange(P_SIZE, dtype=np.int64)
    phase = (index[:, None] * index[None, :] % P_SIZE).astype(np.float64) * (2.0 * np.pi / P_SIZE)
    return ((np.cos(phase) + np.sin(phase)) / np.sqrt(P_SIZE)).astype(ml_dtypes.bfloat16)


CAS = cas_table()


def dot(a, b):
    return jnp.dot(a, b, preferred_element_type=jnp.float32)


def dot_nt(a, b):
    return lax.dot_general(a, b, NT, preferred_element_type=jnp.float32)


def iota(shape, dim):
    return lax.broadcasted_iota(jnp.int32, shape, dim)


def split(value):
    high = value.astype(jnp.bfloat16)
    return high, (value - high.astype(jnp.float32)).astype(jnp.bfloat16)


def lane_gather(table, index):
    return jnp.take_along_axis(table, index, axis=1, mode="promise_in_bounds")


def block_sums(mats, vecs):
    rows = vecs.shape[0]
    pair = jnp.concatenate([vecs, vecs], axis=1)
    total = jnp.zeros((2 * rows, LANES), jnp.float32)
    for t in range(mats.shape[1] // 256):
        high, low = split(mats[:, 256 * t : 256 * t + 256].astype(jnp.float32) * pair)
        owner = iota((256, LANES), 0) // BLK + 4 * t
        table = (owner == iota((256, LANES), 1) % BLK).astype(jnp.bfloat16)
        total = total + dot(jnp.concatenate([high, low], axis=0), table)
    return total[:rows] + total[rows:]


def patch_places(spots):
    blocks = spots.shape[0]
    spots = jnp.concatenate([spots] * (4 * blocks // LANES), axis=1)
    lane = iota(spots.shape, 1)
    lanes = [(lane == 4 * spots + i).astype(jnp.float32).astype(jnp.bfloat16) for i in range(4)]
    row = iota((16, LANES), 0)
    rows = [
        (iota((16, LANES), 1) % PTS == 16 * i + row).astype(jnp.float32).astype(jnp.bfloat16)
        for i in range(4)
    ]
    return rows, lanes


def block_spots(first):
    blocks = first.shape[1]
    shape = (blocks, blocks)
    crossing = ((first & (LANES - 1)) > LANES - 4).astype(jnp.float32)
    crossing = jnp.broadcast_to(crossing, (8, blocks))
    earlier = (iota(shape, 0) < iota(shape, 1)).astype(jnp.float32).astype(jnp.bfloat16)
    ahead = dot(crossing.astype(jnp.bfloat16), earlier)
    total = jnp.sum(crossing, axis=1, keepdims=True)
    block = iota((8, blocks), 1).astype(jnp.float32)
    spot = jnp.where(crossing > 0.0, ahead, total + block - ahead)
    spread = jnp.broadcast_to(spot[:1], (LANES, blocks)).astype(jnp.bfloat16)
    unit = (iota(shape, 0) == iota(shape, 1)).astype(jnp.float32).astype(jnp.bfloat16)
    return dot_nt(unit, spread).astype(jnp.int32)


def project_kernel(
    charges_in,
    order_in,
    project_in,
    anchors_in,
    sent_out,
    spot_out,
    charges,
    order,
    project,
    anchors,
    table,
    doubled,
    sems,
):
    blocks = spot_out.shape[0]
    groups = blocks // GROUP
    pairs = ((charges_in, charges), (order_in, order), (project_in, project), (anchors_in, anchors))
    copies = [pltpu.make_async_copy(a, b, sems.at[n]) for n, (a, b) in enumerate(pairs)]
    for copy in copies:
        copy.start()
    copies[0].wait()
    copies[1].wait()
    table[...] = charges[...].astype(jnp.float32)
    strips = table.shape[0]
    upper = order[...] // LANES
    lower = order[...] % LANES

    def step(u, acc):
        row = jnp.broadcast_to(table[pl.ds(u, 1), :], lower.shape)
        return jnp.where(upper == u, lane_gather(row, lower), acc)

    slots = lax.fori_loop(0, strips, step, jnp.zeros(lower.shape, jnp.float32), unroll=16)
    swapped = pltpu.roll(slots, BLK, 1)
    left = iota(slots.shape, 1) < BLK
    doubled[pl.ds(0, strips, stride=2), :] = jnp.where(left, slots, swapped)
    doubled[pl.ds(1, strips, stride=2), :] = jnp.where(left, swapped, slots)
    twice = doubled[...]
    copies[2].wait()
    copies[3].wait()
    patch = block_sums(project, twice)
    patch = jnp.where(iota(patch.shape, 1) < PTS, patch, 0.0).astype(jnp.bfloat16)
    spots = block_spots(anchors[:1, :])
    spot_out[...] = spots
    rows, lanes = patch_places(spots)
    moved = (iota(spots.shape, 1) == spots).astype(jnp.float32).astype(jnp.bfloat16)
    corner = anchors[...].astype(jnp.float32).astype(jnp.bfloat16)
    corner = dot(jnp.concatenate([corner] * 3, axis=0)[:8], moved)
    cells = (iota((8, 4 * blocks), 1) % 4).astype(jnp.float32)
    start = jnp.broadcast_to(anchors[:1, :].astype(jnp.float32), (8, blocks)).astype(jnp.bfloat16)
    for i in range(4):
        cells = cells + dot(start, lanes[i])
    spread = jnp.zeros((16, 4 * blocks), jnp.float32)
    for i in range(4):
        spread = spread + dot(dot_nt(rows[i], patch).astype(jnp.bfloat16), lanes[i])
    tiles = [slice(LANES * t, LANES * t + LANES) for t in range(groups)]
    sent = [spread[:, tile].astype(jnp.bfloat16) for tile in tiles]
    sent.append(slots.astype(jnp.bfloat16))
    extra = [cells[:1, tile] for tile in tiles] + [corner[:3]]
    extra.append(jnp.zeros((13 - groups, LANES), jnp.float32))
    sent.append(jnp.concatenate(extra, axis=0).astype(jnp.bfloat16))
    sent = jnp.concatenate(sent, axis=0)
    for n in range(sent_out.shape[0]):
        sent_out[n] = sent


def inverse_kernel(order, out):
    rows = order.shape[0]

    def step(r, acc):
        here = order[pl.ds(r, 1), :]
        upper = iota((rows, LANES), 0) == here // LANES
        lower = iota((LANES, LANES), 0) == here % LANES
        values = jnp.concatenate(
            [
                jnp.where(upper, r.astype(jnp.float32), 0.0),
                jnp.where(upper, iota((rows, LANES), 1).astype(jnp.float32), 0.0),
            ],
            axis=0,
        )
        return acc + dot_nt(
            values.astype(jnp.bfloat16), lower.astype(jnp.float32).astype(jnp.bfloat16)
        )

    out[...] = lax.fori_loop(
        0, rows, step, jnp.zeros((2 * rows, LANES), jnp.float32), unroll=4
    ).astype(jnp.int32)


def near_kernel(source, near_blocks, target, mine, theirs, out, table, picked):
    step = pl.program_id(0)
    pairs = picked.shape[0]
    blocks = out.shape[0]

    @pl.when(step == 0)
    def _():
        members, strips, _ = mine.shape
        left = iota((strips, LANES), 1) < BLK
        for side, part in enumerate((mine, theirs)):
            for n in range(members):
                at = (side * members + n) * blocks
                slots = part[n].astype(jnp.float32)
                swapped = pltpu.roll(slots, BLK, 1)
                table[pl.ds(at, strips, stride=2), :] = jnp.where(left, slots, swapped)
                table[pl.ds(at + 1, strips, stride=2), :] = jnp.where(left, swapped, slots)
        out[...] = jnp.zeros_like(out)

    def pick(p, carry):
        picked[pl.ds(p, 1), :] = table[pl.ds(source[step * pairs + p], 1), :]
        return carry

    lax.fori_loop(0, pairs, pick, 0, unroll=8)
    terms = block_sums(near_blocks, picked[...])
    owner = (iota((blocks, pairs), 0) == target[...]).astype(jnp.float32).astype(jnp.bfloat16)
    high, low = split(terms)
    out[...] += dot(owner, high) + dot(owner, low)


def table_rows(cas, numbers, count):
    parts = [cas[pl.ds(pl.multiple_of(n * count, 16), count), :G] for n in numbers]
    return jnp.concatenate(parts, axis=0) if len(parts) > 1 else parts[0]


def turned(rows):
    unit = (iota((G, G), 0) == iota((G, G), 1)).astype(jnp.float32).astype(jnp.bfloat16)
    return dot_nt(unit, rows).astype(jnp.bfloat16)


def tile_loop(half, rows, cols, groups, crosses, body):
    per_slab = cols // SLABS
    low = jnp.maximum(half * (rows // HALVES) - 1, 0)
    high = (half + 1) * (rows // HALVES)
    per_row = per_slab * groups

    def place(row, col):
        side = (col % HALVES) ^ half
        return side * (rows * cols // HALVES) + row * (cols // HALVES) + col // HALVES

    def step(n, carry):
        row = low + n // per_row
        left = n % per_row
        t = left % groups
        devices = [place(row, s * per_slab + left // groups) for s in range(SLABS)]
        found = [crosses((d * groups + t) * GROUP) for d in devices]
        inside = row >= half * (rows // HALVES)
        pl.when(functools.reduce(jnp.logical_or, found, inside))(lambda: body(devices, t))
        return carry

    lax.fori_loop(0, (high - low) * per_row, step, 0)


def lanes_inside(extra, d, t, half):
    extra = extra[d].astype(jnp.float32)
    picked = jnp.where(iota(extra.shape, 0) == t, extra, 0.0)
    cells = jnp.sum(picked, axis=0, keepdims=True) - (half * LANES).astype(jnp.float32)
    return jnp.broadcast_to((cells >= 0.0) & (cells < LANES), (16, LANES))


def scatter_kernel(
    cols,
    gs,
    fs,
    place,
    shift,
    start,
    mine,
    theirs,
    my_extra,
    their_extra,
    cas,
    own_out,
    other_out,
    patches,
    extra,
    lines,
    *slabs,
):
    half = place[0]
    step = pl.program_id(0)
    devices, held, _ = patches.shape
    groups = held // 16
    blocks = groups * GROUP
    owner = iota((16, LANES), 1) // 4
    plane = iota((16, LANES), 0) % QUAD

    @pl.when(step == 0)
    def _():
        def clear(n, carry):
            for slab in slabs:
                at = pl.multiple_of(n * SLAB + PAD, 8)
                slab[pl.ds(at, SLAB - PAD), :] = jnp.zeros((SLAB - PAD, LANES), jnp.float32)
            return carry

        lax.fori_loop(0, G // QUAD, clear, 0)
        for side, part in enumerate(((mine, my_extra), (theirs, their_extra))):
            at = slice(side * (devices // 2), (side + 1) * (devices // 2))
            patches[at] = part[0][...]
            extra[at] = part[1][...]

        def tile(numbers, t):
            values = []
            for d in numbers:
                part = patches[d, pl.ds(pl.multiple_of(16 * t, 16), 16), :].astype(jnp.float32)
                values.append(jnp.where(lanes_inside(extra, d, t, half), part, 0.0))

            def one(k, carry):
                spot = owner == k
                sums = []
                for s in range(SLABS):
                    b = numbers[s] * blocks + t * GROUP + k
                    at = start[b]
                    moved = pltpu.roll(jnp.where(spot, values[s], 0.0), shift[b], 1)
                    here = plane < QUAD - (at & (QUAD - 1))
                    near = slabs[s][pl.ds(at, 16), :] + jnp.where(here, moved, 0.0)
                    at_next = at + (SLAB - QUAD)
                    far = slabs[s][pl.ds(at_next, 16), :] + jnp.where(here, 0.0, moved)
                    sums.append((at, near, at_next, far))
                for s, (at, near, at_next, far) in enumerate(sums):
                    slabs[s][pl.ds(at, 16), :] = near
                    slabs[s][pl.ds(at_next, 16), :] = far
                return carry

            lax.fori_loop(0, GROUP, one, 0, unroll=UNROLL)

        def crosses(b):
            return shift[b] > LANES - 4

        tile_loop(half, devices // cols, cols, groups, crosses, tile)

        table = table_rows(cas, [place[1]], gs)

        def planes(n, carry):
            base = pl.multiple_of(n * SLAB, 8)
            sheets = []
            for q in range(QUAD):
                parts = []
                for s in range(SLABS):
                    part = slabs[s][pl.ds(base + (PAD + q), PIECE, stride=QUAD), :]
                    if s > 0:
                        at = base + (PAD + QUAD * PIECE + q)
                        over = slabs[s - 1][pl.ds(at, 4, stride=QUAD), :]
                        over = jnp.concatenate([over, jnp.zeros_like(over)], axis=0)
                        part = jnp.concatenate([part[:8] + over, part[8:]], axis=0)
                    parts.append(part.astype(jnp.bfloat16))
                sheets.append(jnp.concatenate(parts, axis=0))
            field = dot(table, jnp.concatenate(sheets, axis=1))
            for q in range(QUAD):
                part = field[:, LANES * q : LANES * q + LANES]
                lines[pl.ds(n * QUAD + q, gs, stride=STRIDE), :] = part
            return carry

        lax.fori_loop(0, G // QUAD, planes, 0, unroll=UNROLL_PLANES)

    @pl.when(step > 0)
    def _():
        third = table_rows(cas, [place[2], place[2] ^ 1], fs)
        for g in range(0, LINES, 2):
            pair = []
            for n in (g, g + 1):
                at = ((step - 1) * LINES + n) * STRIDE
                pair.append(lines[pl.ds(at, G), :].astype(jnp.bfloat16))
            field = dot(third, jnp.concatenate(pair, axis=1)).astype(jnp.bfloat16)
            for n in range(2):
                own_out[g + n] = field[:fs, LANES * n : LANES * n + LANES]
                other_out[g + n] = field[fs:, LANES * n : LANES * n + LANES]


def spectrum_kernel(place, own, other, weights, cas, own_out, other_out):
    tiles = [pl.ds(pl.multiple_of(h * LANES, LANES), LANES) for h in (place[0], 1 - place[0])]
    first = jnp.concatenate([cas[tile, :] for tile in tiles], axis=0)
    first_back = jnp.concatenate([cas[:, tile] for tile in tiles], axis=1)
    count, freqs, _ = weights.shape
    step = min(count, max(1, 2 * G // freqs))
    rows = step * freqs
    for g in range(0, count, step):
        part = slice(g, g + step)
        line = jnp.concatenate(
            [own[part].reshape(rows, LANES), other[part].reshape(rows, LANES)], axis=1
        )
        s = dot(line, first) * weights[part].reshape(rows, P_SIZE)
        line = dot(s.astype(jnp.bfloat16), first_back).astype(jnp.bfloat16)
        own_out[part] = line[:, :LANES].reshape(step, freqs, LANES)
        other_out[part] = line[:, LANES:].reshape(step, freqs, LANES)


def sample_kernel(
    cols,
    place,
    shift,
    start,
    my_extra,
    their_extra,
    own,
    other,
    cas,
    out,
    extra,
    second,
    third,
    lines,
    cells,
):
    half = place[0]
    step = pl.program_id(0)
    devices, held, _ = out.shape
    groups = held // 16
    blocks = groups * GROUP
    gs = second.shape[1] // QUAD
    owner = iota((16, LANES), 1) // 4
    plane = iota((16, LANES), 0) % QUAD

    @pl.when(step == 0)
    def _():
        for side, part in enumerate((my_extra, their_extra)):
            extra[side * (devices // 2) : (side + 1) * (devices // 2)] = part[...]
        wide = (iota((gs, QUAD * gs), 1) % gs == iota((gs, QUAD * gs), 0)).astype(jnp.float32)
        back = turned(table_rows(cas, [place[1]], gs))
        back = dot(back, wide.astype(jnp.bfloat16)).astype(jnp.bfloat16)
        tall = (iota((QUAD * G, G), 0) // QUAD == iota((QUAD * G, G), 1)).astype(jnp.float32)
        back = dot(tall.astype(jnp.bfloat16), back)
        same = iota(back.shape, 0) % QUAD == iota(back.shape, 1) // gs
        second[...] = jnp.where(same, back, 0.0).astype(jnp.bfloat16)
        third[...] = turned(table_rows(cas, [place[2], place[2] ^ 1], own.shape[1]))

    for g in range(0, LINES, 2):
        pair = [jnp.concatenate([own[n], other[n]], axis=0) for n in (g, g + 1)]
        field = dot(third[...], jnp.concatenate(pair, axis=1))
        for n in range(2):
            at = (step * LINES + g + n) * STRIDE
            lines[pl.ds(at, G), :] = field[:, LANES * n : LANES * n + LANES]

    @pl.when(step == pl.num_programs(0) - 1)
    def _():
        def planes(n, carry):
            sheets = []
            for group in (2 * n, 2 * n + 1):
                rows = [
                    lines[pl.ds(group * QUAD + q, gs, stride=STRIDE), :].astype(jnp.bfloat16)
                    for q in range(QUAD)
                ]
                sheets.append(jnp.concatenate(rows, axis=0))
            field = dot(second[...], jnp.concatenate(sheets, axis=1))
            for m in range(2):
                at = pl.multiple_of((2 * n + m) * CELLS + PAD, 8)
                cells[pl.ds(at, QUAD * G), :] = field[:, LANES * m : LANES * m + LANES]
            return carry

        lax.fori_loop(0, G // QUAD // 2, planes, 0, unroll=4)
        out[...] = jnp.zeros_like(out)

        def tile(numbers, t):
            def one(k, sums):
                spot = owner == k
                new = []
                for s in range(SLABS):
                    b = numbers[s] * blocks + t * GROUP + k
                    at = start[b]
                    here = plane < QUAD - (at & (QUAD - 1))
                    near = cells[pl.ds(at, 16), :]
                    far = cells[pl.ds(at + (CELLS - QUAD), 16), :]
                    moved = pltpu.roll(jnp.where(here, near, far), shift[b], 1)
                    new.append(jnp.where(spot, moved, sums[s]))
                return tuple(new)

            zero = (jnp.zeros((16, LANES), jnp.float32),) * SLABS
            sums = lax.fori_loop(0, GROUP, one, zero, unroll=UNROLL)
            for s, d in enumerate(numbers):
                inside = lanes_inside(extra, d, t, half)
                out[d, pl.ds(pl.multiple_of(16 * t, 16), 16), :] = jnp.where(
                    inside, sums[s], 0.0
                ).astype(jnp.bfloat16)

        def crosses(b):
            return (shift[b] > 0) & (shift[b] < 4)

        tile_loop(half, devices // cols, cols, groups, crosses, tile)


def finish_kernel(values, interpolate, near, inverse, spots, out, total):
    blocks = near.shape[0]
    groups = values.shape[1] // 16
    rows, lanes = patch_places(spots[...])
    summed = values[0].astype(jnp.float32)
    for d in range(1, values.shape[0]):
        summed = summed + values[d].astype(jnp.float32)
    spread = jnp.concatenate([summed[16 * t : 16 * t + 16] for t in range(groups)], axis=1)
    parts = jnp.concatenate(split(spread), axis=0)
    patch = jnp.zeros((blocks, LANES), jnp.float32)
    for i in range(4):
        column = dot_nt(lanes[i], parts).astype(jnp.bfloat16)
        patch = patch + dot(column, jnp.concatenate([rows[i], rows[i]], axis=0))
    total[...] = block_sums(interpolate, patch) + near[...]
    count = out.shape[0]
    even = total[pl.ds(0, count, stride=2), :]
    odd = total[pl.ds(1, count, stride=2), :]
    total[:count] = jnp.where(iota(even.shape, 1) < BLK, even, odd)
    upper = inverse[:count]
    lower = inverse[count:]

    def step(u, acc):
        row = jnp.broadcast_to(total[pl.ds(u, 1), :], lower.shape)
        return jnp.where(upper == u, lane_gather(row, lower), acc)

    out[...] = lax.fori_loop(0, count, step, jnp.zeros(out.shape, jnp.float32), unroll=16)


def struct(shape, dtype):
    return jax.ShapeDtypeStruct(shape, dtype)


def whole(shape):
    return pl.BlockSpec(shape, lambda *_: (0,) * len(shape))


def params(mib):
    return pltpu.CompilerParams(vmem_limit_bytes=mib * MB)


def body(
    charges,
    panel_order,
    patch_anchor,
    project,
    interpolate,
    kernel_spectrum,
    near_pairs,
    near_blocks,
):
    axes = ("row", "col")
    rows = lax.axis_size("row")
    cols = lax.axis_size("col")
    devices = rows * cols
    row_at = lax.axis_index("row")
    col_at = lax.axis_index("col")
    half = col_at % HALVES
    mates = [(c, c ^ 1) for c in range(cols)]
    blocks = project.shape[0]
    groups = blocks // GROUP
    panels = charges.shape[0]
    strips = panels // LANES
    gs, fs, _ = kernel_spectrum.shape
    held = 16 * groups + strips + 16

    order = panel_order.reshape(strips, LANES)
    members = devices // HALVES
    sent, spots = pl.pallas_call(
        project_kernel,
        out_shape=(
            struct((members, held, LANES), jnp.bfloat16),
            struct((blocks, LANES), jnp.int32),
        ),
        in_specs=[pl.BlockSpec(memory_space=pltpu.HBM)] * 4,
        scratch_shapes=[
            pltpu.VMEM((strips, LANES), jnp.bfloat16),
            pltpu.VMEM((strips, LANES), jnp.int32),
            pltpu.VMEM(project.shape, jnp.bfloat16),
            pltpu.VMEM(patch_anchor.shape, jnp.int32),
            pltpu.VMEM((strips, LANES), jnp.float32),
            pltpu.VMEM((blocks, LANES), jnp.float32),
            pltpu.SemaphoreType.DMA((4,)),
        ],
        compiler_params=params(58),
        name="project",
    )(
        charges.reshape(strips, LANES),
        order,
        project,
        patch_anchor,
    )
    cores = [
        [r * cols + c for r in range(rows) for c in range(core, cols, HALVES)]
        for core in range(HALVES)
    ]

    def swap_members(array):
        return lax.all_to_all(
            array, axes, split_axis=0, concat_axis=0, axis_index_groups=cores, tiled=True
        )

    mine = swap_members(sent)
    theirs = lax.ppermute(mine, "col", mates)
    at = held - 16 + groups
    anchors = jnp.stack([part[:, at : at + 3] for part in (mine, theirs)])
    anchors = anchors.astype(jnp.int32)
    lane = 4 * (jnp.arange(blocks, dtype=jnp.int32) % GROUP)
    forth = ((anchors[:, :, 0] - lane) & (LANES - 1)).reshape(devices * blocks)
    back = ((lane - anchors[:, :, 0]) & (LANES - 1)).reshape(devices * blocks)
    group = anchors[:, :, 2] // QUAD
    inner = PAD + QUAD * anchors[:, :, 1] + anchors[:, :, 2] % QUAD
    side = jnp.arange(HALVES, dtype=jnp.int32)[:, None] ^ half
    col = jnp.arange(members, dtype=jnp.int32) % (cols // HALVES) * HALVES + side
    piece = (col * SLABS // cols * PIECE)[:, :, None]
    slab_at = (group * SLAB + inner - QUAD * piece).reshape(devices * blocks)
    cell_at = (group * CELLS + inner).reshape(devices * blocks)
    place = jnp.stack([half, row_at, col_at]).astype(jnp.int32)
    cas = jnp.asarray(CAS)

    smem = pl.BlockSpec(memory_space=pltpu.SMEM)

    def rows_at(start, count):
        return pl.BlockSpec((members, count, LANES), lambda *_: (0, start // count, 0))

    patch_rows = rows_at(0, 16 * groups)
    charge_rows = rows_at(16 * groups, strips)
    extra_rows = rows_at(16 * groups + strips, 16)
    steps = gs // LINES
    lines_type = struct((gs, fs, LANES), jnp.bfloat16)
    late = pl.BlockSpec((LINES, fs, LANES), lambda n: (jnp.maximum(n - 1, 0), 0, 0))
    own, other = pl.pallas_call(
        functools.partial(scatter_kernel, cols, gs, fs),
        grid=(1 + steps,),
        in_specs=[smem] * 3 + [patch_rows] * 2 + [extra_rows] * 2 + [whole(cas.shape)],
        out_specs=(late, late),
        out_shape=(lines_type, lines_type),
        scratch_shapes=[
            pltpu.VMEM((devices, 16 * groups, LANES), jnp.bfloat16),
            pltpu.VMEM((devices, 16, LANES), jnp.bfloat16),
            pltpu.VMEM((gs * STRIDE, LANES), jnp.float32),
        ]
        + [pltpu.VMEM(((G // QUAD + 1) * SLAB, LANES), jnp.float32)] * SLABS,
        compiler_params=params(53),
        name="scatter",
    )(place, forth, slab_at, mine, theirs, mine, theirs, cas)
    other = lax.ppermute(other, "col", mates)
    own, order = lax.optimization_barrier((own, order))
    inverse = pl.pallas_call(
        inverse_kernel,
        out_shape=struct((2 * strips, LANES), jnp.int32),
        compiler_params=params(32),
        name="inverse",
    )(order)

    other, inverse = lax.optimization_barrier((other, inverse))

    part = lambda shape: pl.BlockSpec((BATCH,) + shape, lambda n: (n, 0, 0))
    own, other = pl.pallas_call(
        spectrum_kernel,
        grid=(gs // BATCH,),
        in_specs=[
            smem,
            part((fs, LANES)),
            part((fs, LANES)),
            part((fs, P_SIZE)),
            whole(cas.shape),
        ],
        out_specs=(part((fs, LANES)), part((fs, LANES))),
        out_shape=(lines_type, lines_type),
        compiler_params=params(40),
        name="spectrum",
    )(place, own, other, kernel_spectrum, cas)
    other = lax.ppermute(other, "col", mates)

    early = pl.BlockSpec((LINES, fs, LANES), lambda n: (n, 0, 0))
    values = pl.pallas_call(
        functools.partial(sample_kernel, cols),
        grid=(steps,),
        in_specs=[smem] * 3 + [extra_rows] * 2 + [early, early, whole(cas.shape)],
        out_specs=whole((devices, 16 * groups, LANES)),
        out_shape=struct((devices, 16 * groups, LANES), jnp.bfloat16),
        scratch_shapes=[
            pltpu.VMEM((devices, 16, LANES), jnp.bfloat16),
            pltpu.VMEM((QUAD * G, QUAD * gs), jnp.bfloat16),
            pltpu.VMEM((G, 2 * fs), jnp.bfloat16),
            pltpu.VMEM((gs * STRIDE, LANES), jnp.float32),
            pltpu.VMEM(((G // QUAD + 1) * CELLS, LANES), jnp.float32),
        ],
        compiler_params=params(46),
        name="sample",
    )(place, back, cell_at, mine, theirs, own, other, cas)
    values = values.reshape(HALVES, members, 16 * groups, LANES)
    received = lax.ppermute(values[1], "col", mates).astype(jnp.float32)
    values = (values[0].astype(jnp.float32) + received).astype(jnp.bfloat16)
    values, my_charges, their_charges = lax.optimization_barrier((values, mine, theirs))
    values = swap_members(values)

    source = near_pairs[1]
    source_row = source // blocks // cols
    source_col = source // blocks % cols
    wanted = (source_col % HALVES ^ half) * members + source_row * (cols // HALVES)
    wanted = (wanted + source_col // HALVES) * blocks + source % blocks
    target = near_pairs[0] - (row_at * cols + col_at) * blocks
    pairs = near_blocks.shape[0]
    near = pl.pallas_call(
        near_kernel,
        grid=(pairs // blocks,),
        in_specs=[
            smem,
            pl.BlockSpec((blocks, BLK * BLK), lambda n: (n, 0)),
            pl.BlockSpec((1, blocks), lambda n: (0, n)),
            charge_rows,
            charge_rows,
        ],
        out_specs=whole((blocks, LANES)),
        out_shape=struct((blocks, LANES), jnp.float32),
        scratch_shapes=[
            pltpu.VMEM((devices * blocks, LANES), jnp.float32),
            pltpu.VMEM((blocks, LANES), jnp.float32),
        ],
        compiler_params=params(56),
        name="near",
    )(wanted, near_blocks, target.reshape(1, pairs), my_charges, their_charges)

    result = pl.pallas_call(
        finish_kernel,
        out_shape=struct((strips, LANES), jnp.float32),
        scratch_shapes=[pltpu.VMEM((blocks, LANES), jnp.float32)],
        compiler_params=params(32),
        name="finish",
    )(values, interpolate, near, inverse, spots)
    return result.reshape(panels)


def solution(mesh):
    placed = (
        P(("row", "col")),
        P(("row", "col")),
        P(None, ("row", "col")),
        P(("row", "col"), None),
        P(("row", "col"), None),
        P("row", "col", None),
        P(None, ("row", "col")),
        P(("row", "col"), None),
    )
    return jax.shard_map(
        body, mesh=mesh, in_specs=placed, out_specs=P(("row", "col")), check_vma=False
    )
```

```python
import functools

import jax
import jax.numpy as jnp
import ml_dtypes
import numpy as np
from jax import lax
from jax.experimental import pallas as pl
from jax.experimental.pallas import tpu as pltpu
from jax.sharding import PartitionSpec as P

G = 256
P_SIZE = 512
BLK = 64
PTS = 64
LANES = 128
GROUP = LANES // 4
HALVES = G // LANES
SLABS = 4
PIECE = G // SLABS
QUAD = 4
PAD = 8
SLAB = PAD + QUAD * PIECE + 16
CELLS = PAD + QUAD * G + 16
STRIDE = G + 1
BATCH = 8
WAYS = 4
LINES = 16
UNROLL = 32
UNROLL_PLANES = 16
MB = 1 << 20
NT = (((1,), (1,)), ((), ()))


def cas_table():
    index = np.arange(P_SIZE, dtype=np.int64)
    phase = (index[:, None] * index[None, :] % P_SIZE).astype(np.float64) * (2.0 * np.pi / P_SIZE)
    return ((np.cos(phase) + np.sin(phase)) / np.sqrt(P_SIZE)).astype(ml_dtypes.bfloat16)


CAS = cas_table()


def dot(a, b):
    return jnp.dot(a, b, preferred_element_type=jnp.float32)


def dot_nt(a, b):
    return lax.dot_general(a, b, NT, preferred_element_type=jnp.float32)


def iota(shape, dim):
    return lax.broadcasted_iota(jnp.int32, shape, dim)


def split(value):
    high = value.astype(jnp.bfloat16)
    return high, (value - high.astype(jnp.float32)).astype(jnp.bfloat16)


def lane_gather(table, index):
    return jnp.take_along_axis(table, index, axis=1, mode="promise_in_bounds")


def block_sums(mats, vecs):
    rows = vecs.shape[0]
    pair = jnp.concatenate([vecs, vecs], axis=1)
    total = jnp.zeros((2 * rows, LANES), jnp.float32)
    for t in range(mats.shape[1] // 256):
        high, low = split(mats[:, 256 * t : 256 * t + 256].astype(jnp.float32) * pair)
        owner = iota((256, LANES), 0) // BLK + 4 * t
        table = (owner == iota((256, LANES), 1) % BLK).astype(jnp.bfloat16)
        total = total + dot(jnp.concatenate([high, low], axis=0), table)
    return total[:rows] + total[rows:]


def patch_places(spots):
    blocks = spots.shape[0]
    spots = jnp.concatenate([spots] * (4 * blocks // LANES), axis=1)
    lane = iota(spots.shape, 1)
    lanes = [(lane == 4 * spots + i).astype(jnp.float32).astype(jnp.bfloat16) for i in range(4)]
    row = iota((16, LANES), 0)
    rows = [
        (iota((16, LANES), 1) % PTS == 16 * i + row).astype(jnp.float32).astype(jnp.bfloat16)
        for i in range(4)
    ]
    return rows, lanes


def block_spots(first):
    blocks = first.shape[1]
    shape = (blocks, blocks)
    crossing = ((first & (LANES - 1)) > LANES - 4).astype(jnp.float32)
    crossing = jnp.broadcast_to(crossing, (8, blocks))
    earlier = (iota(shape, 0) < iota(shape, 1)).astype(jnp.float32).astype(jnp.bfloat16)
    ahead = dot(crossing.astype(jnp.bfloat16), earlier)
    total = jnp.sum(crossing, axis=1, keepdims=True)
    block = iota((8, blocks), 1).astype(jnp.float32)
    spot = jnp.where(crossing > 0.0, ahead, total + block - ahead)
    spread = jnp.broadcast_to(spot[:1], (LANES, blocks)).astype(jnp.bfloat16)
    unit = (iota(shape, 0) == iota(shape, 1)).astype(jnp.float32).astype(jnp.bfloat16)
    return dot_nt(unit, spread).astype(jnp.int32)


def project_kernel(
    charges_in,
    order_in,
    project_in,
    anchors_in,
    sent_out,
    spot_out,
    charges,
    order,
    project,
    anchors,
    table,
    doubled,
    sems,
):
    blocks = spot_out.shape[0]
    groups = blocks // GROUP
    pairs = ((charges_in, charges), (order_in, order), (project_in, project), (anchors_in, anchors))
    copies = [pltpu.make_async_copy(a, b, sems.at[n]) for n, (a, b) in enumerate(pairs)]
    for copy in copies:
        copy.start()
    copies[0].wait()
    copies[1].wait()
    table[...] = charges[...].astype(jnp.float32)
    strips = table.shape[0]
    upper = order[...] // LANES
    lower = order[...] % LANES

    def step(u, acc):
        row = jnp.broadcast_to(table[pl.ds(u, 1), :], lower.shape)
        return jnp.where(upper == u, lane_gather(row, lower), acc)

    slots = lax.fori_loop(0, strips, step, jnp.zeros(lower.shape, jnp.float32), unroll=True)
    swapped = pltpu.roll(slots, BLK, 1)
    left = iota(slots.shape, 1) < BLK
    doubled[pl.ds(0, strips, stride=2), :] = jnp.where(left, slots, swapped)
    doubled[pl.ds(1, strips, stride=2), :] = jnp.where(left, swapped, slots)
    twice = doubled[...]
    copies[2].wait()
    copies[3].wait()
    patch = block_sums(project, twice)
    patch = jnp.where(iota(patch.shape, 1) < PTS, patch, 0.0).astype(jnp.bfloat16)
    spots = block_spots(anchors[:1, :])
    spot_out[...] = spots
    rows, lanes = patch_places(spots)
    moved = (iota(spots.shape, 1) == spots).astype(jnp.float32).astype(jnp.bfloat16)
    corner = anchors[...].astype(jnp.float32).astype(jnp.bfloat16)
    corner = dot(jnp.concatenate([corner] * 3, axis=0)[:8], moved)
    cells = (iota((8, 4 * blocks), 1) % 4).astype(jnp.float32)
    start = jnp.broadcast_to(anchors[:1, :].astype(jnp.float32), (8, blocks)).astype(jnp.bfloat16)
    for i in range(4):
        cells = cells + dot(start, lanes[i])
    spread = jnp.zeros((16, 4 * blocks), jnp.float32)
    for i in range(4):
        spread = spread + dot(dot_nt(rows[i], patch).astype(jnp.bfloat16), lanes[i])
    tiles = [slice(LANES * t, LANES * t + LANES) for t in range(groups)]
    sent = [spread[:, tile].astype(jnp.bfloat16) for tile in tiles]
    sent.append(slots.astype(jnp.bfloat16))
    extra = [cells[:1, tile] for tile in tiles] + [corner[:3]]
    extra.append(jnp.zeros((13 - groups, LANES), jnp.float32))
    sent.append(jnp.concatenate(extra, axis=0).astype(jnp.bfloat16))
    sent = jnp.concatenate(sent, axis=0)
    for n in range(sent_out.shape[0]):
        sent_out[n] = sent


def inverse_kernel(order, out):
    rows = order.shape[0]

    def step(r, acc):
        here = order[pl.ds(r, 1), :]
        upper = iota((rows, LANES), 0) == here // LANES
        lower = iota((LANES, LANES), 0) == here % LANES
        values = jnp.concatenate(
            [
                jnp.where(upper, r.astype(jnp.float32), 0.0),
                jnp.where(upper, iota((rows, LANES), 1).astype(jnp.float32), 0.0),
            ],
            axis=0,
        )
        return acc + dot_nt(
            values.astype(jnp.bfloat16), lower.astype(jnp.float32).astype(jnp.bfloat16)
        )

    out[...] = lax.fori_loop(
        0, rows, step, jnp.zeros((2 * rows, LANES), jnp.float32), unroll=4
    ).astype(jnp.int32)


def near_kernel(source, near_blocks, target, mine, theirs, out, table, picked):
    step = pl.program_id(0)
    pairs = picked.shape[0]
    blocks = out.shape[0]

    @pl.when(step == 0)
    def _():
        members, strips, _ = mine.shape
        left = iota((strips, LANES), 1) < BLK
        for side, part in enumerate((mine, theirs)):
            for n in range(members):
                at = (side * members + n) * blocks
                slots = part[n].astype(jnp.float32)
                swapped = pltpu.roll(slots, BLK, 1)
                table[pl.ds(at, strips, stride=2), :] = jnp.where(left, slots, swapped)
                table[pl.ds(at + 1, strips, stride=2), :] = jnp.where(left, swapped, slots)
        out[...] = jnp.zeros_like(out)

    def pick(p, carry):
        picked[pl.ds(p, 1), :] = table[pl.ds(source[step * pairs + p], 1), :]
        return carry

    lax.fori_loop(0, pairs, pick, 0, unroll=8)
    terms = block_sums(near_blocks, picked[...])
    owner = (iota((blocks, pairs), 0) == target[...]).astype(jnp.float32).astype(jnp.bfloat16)
    high, low = split(terms)
    out[...] += dot(owner, high) + dot(owner, low)


def table_rows(cas, numbers, count):
    parts = [cas[pl.ds(pl.multiple_of(n * count, 16), count), :G] for n in numbers]
    return jnp.concatenate(parts, axis=0) if len(parts) > 1 else parts[0]


def turned(rows):
    unit = (iota((G, G), 0) == iota((G, G), 1)).astype(jnp.float32).astype(jnp.bfloat16)
    return dot_nt(unit, rows).astype(jnp.bfloat16)


def tile_loop(half, rows, cols, groups, crosses, body):
    per_slab = cols // SLABS
    low = jnp.maximum(half * (rows // HALVES) - 1, 0)
    high = (half + 1) * (rows // HALVES)
    per_row = per_slab * groups

    def place(row, col):
        side = (col % HALVES) ^ half
        return side * (rows * cols // HALVES) + row * (cols // HALVES) + col // HALVES

    def step(n, carry):
        row = low + n // per_row
        left = n % per_row
        t = left % groups
        devices = [place(row, s * per_slab + left // groups) for s in range(SLABS)]
        found = [crosses((d * groups + t) * GROUP) for d in devices]
        inside = row >= half * (rows // HALVES)
        pl.when(functools.reduce(jnp.logical_or, found, inside))(lambda: body(devices, t))
        return carry

    lax.fori_loop(0, (high - low) * per_row, step, 0)


def lanes_inside(extra, d, t, half):
    extra = extra[d].astype(jnp.float32)
    picked = jnp.where(iota(extra.shape, 0) == t, extra, 0.0)
    cells = jnp.sum(picked, axis=0, keepdims=True) - (half * LANES).astype(jnp.float32)
    return jnp.broadcast_to((cells >= 0.0) & (cells < LANES), (16, LANES))


def scatter_kernel(
    cols,
    gs,
    fs,
    place,
    shift,
    start,
    mine,
    theirs,
    my_extra,
    their_extra,
    cas,
    own_out,
    other_out,
    patches,
    extra,
    lines,
    *slabs,
):
    half = place[0]
    step = pl.program_id(0)
    devices, held, _ = patches.shape
    groups = held // 16
    blocks = groups * GROUP
    owner = iota((16, LANES), 1) // 4
    plane = iota((16, LANES), 0) % QUAD

    @pl.when(step == 0)
    def _():
        def clear(n, carry):
            for slab in slabs:
                at = pl.multiple_of(n * SLAB + PAD, 8)
                slab[pl.ds(at, SLAB - PAD), :] = jnp.zeros((SLAB - PAD, LANES), jnp.float32)
            return carry

        lax.fori_loop(0, G // QUAD, clear, 0)
        for side, part in enumerate(((mine, my_extra), (theirs, their_extra))):
            at = slice(side * (devices // 2), (side + 1) * (devices // 2))
            patches[at] = part[0][...]
            extra[at] = part[1][...]

        def tile(numbers, t):
            values = []
            for d in numbers:
                part = patches[d, pl.ds(pl.multiple_of(16 * t, 16), 16), :].astype(jnp.float32)
                values.append(jnp.where(lanes_inside(extra, d, t, half), part, 0.0))

            def one(k, carry):
                spot = owner == k
                sums = []
                for s in range(SLABS):
                    b = numbers[s] * blocks + t * GROUP + k
                    at = start[b]
                    moved = pltpu.roll(jnp.where(spot, values[s], 0.0), shift[b], 1)
                    here = plane < QUAD - (at & (QUAD - 1))
                    near = slabs[s][pl.ds(at, 16), :] + jnp.where(here, moved, 0.0)
                    at_next = at + (SLAB - QUAD)
                    far = slabs[s][pl.ds(at_next, 16), :] + jnp.where(here, 0.0, moved)
                    sums.append((at, near, at_next, far))
                for s, (at, near, at_next, far) in enumerate(sums):
                    slabs[s][pl.ds(at, 16), :] = near
                    slabs[s][pl.ds(at_next, 16), :] = far
                return carry

            lax.fori_loop(0, GROUP, one, 0, unroll=UNROLL)

        def crosses(b):
            return shift[b] > LANES - 4

        tile_loop(half, devices // cols, cols, groups, crosses, tile)

        table = table_rows(cas, [place[1]], gs)

        def planes(n, carry):
            base = pl.multiple_of(n * SLAB, 8)
            sheets = []
            for q in range(QUAD):
                parts = []
                for s in range(SLABS):
                    part = slabs[s][pl.ds(base + (PAD + q), PIECE, stride=QUAD), :]
                    if s > 0:
                        at = base + (PAD + QUAD * PIECE + q)
                        over = slabs[s - 1][pl.ds(at, 4, stride=QUAD), :]
                        over = jnp.concatenate([over, jnp.zeros_like(over)], axis=0)
                        part = jnp.concatenate([part[:8] + over, part[8:]], axis=0)
                    parts.append(part.astype(jnp.bfloat16))
                sheets.append(jnp.concatenate(parts, axis=0))
            field = dot(table, jnp.concatenate(sheets, axis=1))
            for q in range(QUAD):
                part = field[:, LANES * q : LANES * q + LANES]
                lines[pl.ds(n * QUAD + q, gs, stride=STRIDE), :] = part
            return carry

        lax.fori_loop(0, G // QUAD, planes, 0, unroll=UNROLL_PLANES)

    @pl.when(step > 0)
    def _():
        third = table_rows(cas, [place[2], place[2] ^ 1], fs)
        for g in range(0, LINES, 2):
            pair = []
            for n in (g, g + 1):
                at = ((step - 1) * LINES + n) * STRIDE
                pair.append(lines[pl.ds(at, G), :].astype(jnp.bfloat16))
            field = dot(third, jnp.concatenate(pair, axis=1)).astype(jnp.bfloat16)
            for n in range(2):
                own_out[g + n] = field[:fs, LANES * n : LANES * n + LANES]
                other_out[g + n] = field[fs:, LANES * n : LANES * n + LANES]


def spectrum_kernel(place, own, other, *refs):
    weights, (cas, own_out, other_out) = refs[:WAYS], refs[WAYS:]
    tiles = [pl.ds(pl.multiple_of(h * LANES, LANES), LANES) for h in (place[0], 1 - place[0])]
    first = jnp.concatenate([cas[tile, :] for tile in tiles], axis=0)
    first_back = jnp.concatenate([cas[:, tile] for tile in tiles], axis=1)
    step, freqs, _ = weights[0].shape
    rows = step * freqs
    for n in range(WAYS):
        part = slice(n * step, (n + 1) * step)
        line = jnp.concatenate(
            [own[part].reshape(rows, LANES), other[part].reshape(rows, LANES)], axis=1
        )
        s = dot(line, first) * weights[n][...].reshape(rows, P_SIZE)
        line = dot(s.astype(jnp.bfloat16), first_back).astype(jnp.bfloat16)
        own_out[part] = line[:, :LANES].reshape(step, freqs, LANES)
        other_out[part] = line[:, LANES:].reshape(step, freqs, LANES)


def sample_kernel(
    cols,
    place,
    shift,
    start,
    my_extra,
    their_extra,
    own,
    other,
    cas,
    out,
    extra,
    second,
    third,
    lines,
    cells,
):
    half = place[0]
    step = pl.program_id(0)
    devices, held, _ = out.shape
    groups = held // 16
    blocks = groups * GROUP
    gs = second.shape[1]
    owner = iota((16, LANES), 1) // 4
    plane = iota((16, LANES), 0) % QUAD

    @pl.when(step == 0)
    def _():
        for side, part in enumerate((my_extra, their_extra)):
            extra[side * (devices // 2) : (side + 1) * (devices // 2)] = part[...]
        second[...] = turned(table_rows(cas, [place[1]], gs))
        third[...] = turned(table_rows(cas, [place[2], place[2] ^ 1], own.shape[1]))

    for g in range(0, LINES, 2):
        pair = [jnp.concatenate([own[n], other[n]], axis=0) for n in (g, g + 1)]
        field = dot(third[...], jnp.concatenate(pair, axis=1))
        for n in range(2):
            at = (step * LINES + g + n) * STRIDE
            lines[pl.ds(at, G), :] = field[:, LANES * n : LANES * n + LANES]

    @pl.when(step == pl.num_programs(0) - 1)
    def _():
        def planes(n, carry):
            sheets = [
                lines[pl.ds(n * QUAD + q, gs, stride=STRIDE), :].astype(jnp.bfloat16)
                for q in range(QUAD)
            ]
            field = dot(second[...], jnp.concatenate(sheets, axis=1))
            base = pl.multiple_of(n * CELLS, 8)
            for q in range(QUAD):
                part = field[:, LANES * q : LANES * q + LANES]
                cells[pl.ds(base + (PAD + q), G, stride=QUAD), :] = part
            return carry

        lax.fori_loop(0, G // QUAD, planes, 0, unroll=UNROLL_PLANES)
        out[...] = jnp.zeros_like(out)

        def tile(numbers, t):
            def one(k, sums):
                spot = owner == k
                new = []
                for s in range(SLABS):
                    b = numbers[s] * blocks + t * GROUP + k
                    at = start[b]
                    here = plane < QUAD - (at & (QUAD - 1))
                    near = cells[pl.ds(at, 16), :]
                    far = cells[pl.ds(at + (CELLS - QUAD), 16), :]
                    moved = pltpu.roll(jnp.where(here, near, far), shift[b], 1)
                    new.append(jnp.where(spot, moved, sums[s]))
                return tuple(new)

            zero = (jnp.zeros((16, LANES), jnp.float32),) * SLABS
            sums = lax.fori_loop(0, GROUP, one, zero, unroll=UNROLL)
            for s, d in enumerate(numbers):
                inside = lanes_inside(extra, d, t, half)
                out[d, pl.ds(pl.multiple_of(16 * t, 16), 16), :] = jnp.where(
                    inside, sums[s], 0.0
                ).astype(jnp.bfloat16)

        def crosses(b):
            return (shift[b] > 0) & (shift[b] < 4)

        tile_loop(half, devices // cols, cols, groups, crosses, tile)


def finish_kernel(values, interpolate, near, inverse, spots, out, total):
    blocks = near.shape[0]
    groups = values.shape[1] // 16
    rows, lanes = patch_places(spots[...])
    summed = values[0].astype(jnp.float32)
    for d in range(1, values.shape[0]):
        summed = summed + values[d].astype(jnp.float32)
    spread = jnp.concatenate([summed[16 * t : 16 * t + 16] for t in range(groups)], axis=1)
    parts = jnp.concatenate(split(spread), axis=0)
    patch = jnp.zeros((blocks, LANES), jnp.float32)
    for i in range(4):
        column = dot_nt(lanes[i], parts).astype(jnp.bfloat16)
        patch = patch + dot(column, jnp.concatenate([rows[i], rows[i]], axis=0))
    total[...] = block_sums(interpolate, patch) + near[...]
    count = out.shape[0]
    even = total[pl.ds(0, count, stride=2), :]
    odd = total[pl.ds(1, count, stride=2), :]
    total[:count] = jnp.where(iota(even.shape, 1) < BLK, even, odd)
    upper = inverse[:count]
    lower = inverse[count:]

    def step(u, acc):
        row = jnp.broadcast_to(total[pl.ds(u, 1), :], lower.shape)
        return jnp.where(upper == u, lane_gather(row, lower), acc)

    out[...] = lax.fori_loop(0, count, step, jnp.zeros(out.shape, jnp.float32), unroll=True)


def struct(shape, dtype):
    return jax.ShapeDtypeStruct(shape, dtype)


def whole(shape):
    return pl.BlockSpec(shape, lambda *_: (0,) * len(shape))


def params(mib):
    return pltpu.CompilerParams(vmem_limit_bytes=mib * MB)


def body(
    charges,
    panel_order,
    patch_anchor,
    project,
    interpolate,
    kernel_spectrum,
    near_pairs,
    near_blocks,
):
    axes = ("row", "col")
    rows = lax.axis_size("row")
    cols = lax.axis_size("col")
    devices = rows * cols
    row_at = lax.axis_index("row")
    col_at = lax.axis_index("col")
    half = col_at % HALVES
    mates = [(c, c ^ 1) for c in range(cols)]
    blocks = project.shape[0]
    groups = blocks // GROUP
    panels = charges.shape[0]
    strips = panels // LANES
    gs, fs, _ = kernel_spectrum.shape
    held = 16 * groups + strips + 16

    order = panel_order.reshape(strips, LANES)
    members = devices // HALVES
    sent, spots = pl.pallas_call(
        project_kernel,
        out_shape=(
            struct((members, held, LANES), jnp.bfloat16),
            struct((blocks, LANES), jnp.int32),
        ),
        in_specs=[pl.BlockSpec(memory_space=pltpu.HBM)] * 4,
        scratch_shapes=[
            pltpu.VMEM((strips, LANES), jnp.bfloat16),
            pltpu.VMEM((strips, LANES), jnp.int32),
            pltpu.VMEM(project.shape, jnp.bfloat16),
            pltpu.VMEM(patch_anchor.shape, jnp.int32),
            pltpu.VMEM((strips, LANES), jnp.float32),
            pltpu.VMEM((blocks, LANES), jnp.float32),
            pltpu.SemaphoreType.DMA((4,)),
        ],
        compiler_params=params(58),
        name="project",
    )(
        charges.reshape(strips, LANES),
        order,
        project,
        patch_anchor,
    )
    cores = [
        [r * cols + c for r in range(rows) for c in range(core, cols, HALVES)]
        for core in range(HALVES)
    ]

    def swap_members(array):
        return lax.all_to_all(
            array, axes, split_axis=0, concat_axis=0, axis_index_groups=cores, tiled=True
        )

    mine = swap_members(sent)
    theirs = lax.ppermute(mine, "col", mates)
    at = held - 16 + groups
    anchors = jnp.stack([part[:, at : at + 3] for part in (mine, theirs)])
    anchors = anchors.astype(jnp.int32)
    lane = 4 * (jnp.arange(blocks, dtype=jnp.int32) % GROUP)
    forth = ((anchors[:, :, 0] - lane) & (LANES - 1)).reshape(devices * blocks)
    back = ((lane - anchors[:, :, 0]) & (LANES - 1)).reshape(devices * blocks)
    group = anchors[:, :, 2] // QUAD
    inner = PAD + QUAD * anchors[:, :, 1] + anchors[:, :, 2] % QUAD
    side = jnp.arange(HALVES, dtype=jnp.int32)[:, None] ^ half
    col = jnp.arange(members, dtype=jnp.int32) % (cols // HALVES) * HALVES + side
    piece = (col * SLABS // cols * PIECE)[:, :, None]
    slab_at = (group * SLAB + inner - QUAD * piece).reshape(devices * blocks)
    cell_at = (group * CELLS + inner).reshape(devices * blocks)
    place = jnp.stack([half, row_at, col_at]).astype(jnp.int32)
    cas = jnp.asarray(CAS)

    smem = pl.BlockSpec(memory_space=pltpu.SMEM)

    def rows_at(start, count):
        return pl.BlockSpec((members, count, LANES), lambda *_: (0, start // count, 0))

    patch_rows = rows_at(0, 16 * groups)
    charge_rows = rows_at(16 * groups, strips)
    extra_rows = rows_at(16 * groups + strips, 16)
    steps = gs // LINES
    lines_type = struct((gs, fs, LANES), jnp.bfloat16)
    late = pl.BlockSpec((LINES, fs, LANES), lambda n: (jnp.maximum(n - 1, 0), 0, 0))
    own, other = pl.pallas_call(
        functools.partial(scatter_kernel, cols, gs, fs),
        grid=(1 + steps,),
        in_specs=[smem] * 3 + [patch_rows] * 2 + [extra_rows] * 2 + [whole(cas.shape)],
        out_specs=(late, late),
        out_shape=(lines_type, lines_type),
        scratch_shapes=[
            pltpu.VMEM((devices, 16 * groups, LANES), jnp.bfloat16),
            pltpu.VMEM((devices, 16, LANES), jnp.bfloat16),
            pltpu.VMEM((gs * STRIDE, LANES), jnp.float32),
        ]
        + [pltpu.VMEM(((G // QUAD + 1) * SLAB, LANES), jnp.float32)] * SLABS,
        compiler_params=params(53),
        name="scatter",
    )(place, forth, slab_at, mine, theirs, mine, theirs, cas)
    other = lax.ppermute(other, "col", mates)
    own, order = lax.optimization_barrier((own, order))
    inverse = pl.pallas_call(
        inverse_kernel,
        out_shape=struct((2 * strips, LANES), jnp.int32),
        compiler_params=params(32),
        name="inverse",
    )(order)

    other, inverse = lax.optimization_barrier((other, inverse))

    part = lambda shape: pl.BlockSpec((BATCH,) + shape, lambda n: (n, 0, 0))

    def weight_part(way):
        return pl.BlockSpec((BATCH // WAYS, fs, P_SIZE), lambda n: (n * WAYS + way, 0, 0))

    own, other = pl.pallas_call(
        spectrum_kernel,
        grid=(gs // BATCH,),
        in_specs=[
            smem,
            part((fs, LANES)),
            part((fs, LANES)),
            *[weight_part(n) for n in range(WAYS)],
            whole(cas.shape),
        ],
        out_specs=(part((fs, LANES)), part((fs, LANES))),
        out_shape=(lines_type, lines_type),
        compiler_params=params(40),
        name="spectrum",
    )(place, own, other, *[kernel_spectrum] * WAYS, cas)
    other = lax.ppermute(other, "col", mates)

    early = pl.BlockSpec((LINES, fs, LANES), lambda n: (n, 0, 0))
    values = pl.pallas_call(
        functools.partial(sample_kernel, cols),
        grid=(steps,),
        in_specs=[smem] * 3 + [extra_rows] * 2 + [early, early, whole(cas.shape)],
        out_specs=whole((devices, 16 * groups, LANES)),
        out_shape=struct((devices, 16 * groups, LANES), jnp.bfloat16),
        scratch_shapes=[
            pltpu.VMEM((devices, 16, LANES), jnp.bfloat16),
            pltpu.VMEM((G, gs), jnp.bfloat16),
            pltpu.VMEM((G, 2 * fs), jnp.bfloat16),
            pltpu.VMEM((gs * STRIDE, LANES), jnp.float32),
            pltpu.VMEM(((G // QUAD + 1) * CELLS, LANES), jnp.float32),
        ],
        compiler_params=params(46),
        name="sample",
    )(place, back, cell_at, mine, theirs, own, other, cas)
    values = values.reshape(HALVES, members, 16 * groups, LANES)
    received = lax.ppermute(values[1], "col", mates).astype(jnp.float32)
    values = (values[0].astype(jnp.float32) + received).astype(jnp.bfloat16)
    values, my_charges, their_charges = lax.optimization_barrier((values, mine, theirs))
    values = swap_members(values)

    source = near_pairs[1]
    source_row = source // blocks // cols
    source_col = source // blocks % cols
    wanted = (source_col % HALVES ^ half) * members + source_row * (cols // HALVES)
    wanted = (wanted + source_col // HALVES) * blocks + source % blocks
    target = near_pairs[0] - (row_at * cols + col_at) * blocks
    pairs = near_blocks.shape[0]
    near = pl.pallas_call(
        near_kernel,
        grid=(pairs // blocks,),
        in_specs=[
            smem,
            pl.BlockSpec((blocks, BLK * BLK), lambda n: (n, 0)),
            pl.BlockSpec((1, blocks), lambda n: (0, n)),
            charge_rows,
            charge_rows,
        ],
        out_specs=whole((blocks, LANES)),
        out_shape=struct((blocks, LANES), jnp.float32),
        scratch_shapes=[
            pltpu.VMEM((devices * blocks, LANES), jnp.float32),
            pltpu.VMEM((blocks, LANES), jnp.float32),
        ],
        compiler_params=params(56),
        name="near",
    )(wanted, near_blocks, target.reshape(1, pairs), my_charges, their_charges)

    result = pl.pallas_call(
        finish_kernel,
        out_shape=struct((strips, LANES), jnp.float32),
        scratch_shapes=[pltpu.VMEM((blocks, LANES), jnp.float32)],
        compiler_params=params(32),
        name="finish",
    )(values, interpolate, near, inverse, spots)
    return result.reshape(panels)


def solution(mesh):
    placed = (
        P(("row", "col")),
        P(("row", "col")),
        P(None, ("row", "col")),
        P(("row", "col"), None),
        P(("row", "col"), None),
        P("row", "col", None),
        P(None, ("row", "col")),
        P(("row", "col"), None),
    )
    return jax.shard_map(
        body, mesh=mesh, in_specs=placed, out_specs=P(("row", "col")), check_vma=False
    )
```

```python
import functools

import jax
import jax.numpy as jnp
import ml_dtypes
import numpy as np
from jax import lax
from jax.experimental import pallas as pl
from jax.experimental.pallas import tpu as pltpu
from jax.sharding import PartitionSpec as P

G = 256
P_SIZE = 512
BLK = 64
PTS = 64
LANES = 128
GROUP = LANES // 4
HALVES = G // LANES
SLABS = 4
PIECE = G // SLABS
QUAD = 4
PAD = 8
SLAB = PAD + QUAD * PIECE + 16
CELLS = PAD + QUAD * G + 16
STRIDE = G + 1
BATCH = 8
WAYS = 4
LINES = 16
UNROLL_PLANES = 16
MB = 1 << 20
NT = (((1,), (1,)), ((), ()))


def cas_table():
    index = np.arange(P_SIZE, dtype=np.int64)
    phase = (index[:, None] * index[None, :] % P_SIZE).astype(np.float64) * (2.0 * np.pi / P_SIZE)
    return ((np.cos(phase) + np.sin(phase)) / np.sqrt(P_SIZE)).astype(ml_dtypes.bfloat16)


CAS = cas_table()


def dot(a, b):
    return jnp.dot(a, b, preferred_element_type=jnp.float32)


def dot_nt(a, b):
    return lax.dot_general(a, b, NT, preferred_element_type=jnp.float32)


def iota(shape, dim):
    return lax.broadcasted_iota(jnp.int32, shape, dim)


def split(value):
    high = value.astype(jnp.bfloat16)
    return high, (value - high.astype(jnp.float32)).astype(jnp.bfloat16)


def lane_gather(table, index):
    return jnp.take_along_axis(table, index, axis=1, mode="promise_in_bounds")


def block_sums(mats, vecs):
    rows = vecs.shape[0]
    pair = jnp.concatenate([vecs, vecs], axis=1)
    total = jnp.zeros((2 * rows, LANES), jnp.float32)
    for t in range(mats.shape[1] // 256):
        high, low = split(mats[:, 256 * t : 256 * t + 256].astype(jnp.float32) * pair)
        owner = iota((256, LANES), 0) // BLK + 4 * t
        table = (owner == iota((256, LANES), 1) % BLK).astype(jnp.bfloat16)
        total = total + dot(jnp.concatenate([high, low], axis=0), table)
    return total[:rows] + total[rows:]


def patch_places(spots):
    blocks = spots.shape[0]
    spots = jnp.concatenate([spots] * (4 * blocks // LANES), axis=1)
    lane = iota(spots.shape, 1)
    lanes = [(lane == 4 * spots + i).astype(jnp.float32).astype(jnp.bfloat16) for i in range(4)]
    row = iota((16, LANES), 0)
    rows = [
        (iota((16, LANES), 1) % PTS == 16 * i + row).astype(jnp.float32).astype(jnp.bfloat16)
        for i in range(4)
    ]
    return rows, lanes


def block_spots(first):
    blocks = first.shape[1]
    shape = (blocks, blocks)
    crossing = ((first & (LANES - 1)) > LANES - 4).astype(jnp.float32)
    crossing = jnp.broadcast_to(crossing, (8, blocks))
    earlier = (iota(shape, 0) < iota(shape, 1)).astype(jnp.float32).astype(jnp.bfloat16)
    ahead = dot(crossing.astype(jnp.bfloat16), earlier)
    total = jnp.sum(crossing, axis=1, keepdims=True)
    block = iota((8, blocks), 1).astype(jnp.float32)
    spot = jnp.where(crossing > 0.0, ahead, total + block - ahead)
    spread = jnp.broadcast_to(spot[:1], (LANES, blocks)).astype(jnp.bfloat16)
    unit = (iota(shape, 0) == iota(shape, 1)).astype(jnp.float32).astype(jnp.bfloat16)
    return dot_nt(unit, spread).astype(jnp.int32)


def project_kernel(
    charges_in,
    order_in,
    project_in,
    anchors_in,
    sent_out,
    spot_out,
    charges,
    order,
    project,
    anchors,
    table,
    doubled,
    sems,
):
    blocks = spot_out.shape[0]
    groups = blocks // GROUP
    pairs = ((charges_in, charges), (order_in, order), (project_in, project), (anchors_in, anchors))
    copies = [pltpu.make_async_copy(a, b, sems.at[n]) for n, (a, b) in enumerate(pairs)]
    for copy in copies:
        copy.start()
    copies[0].wait()
    copies[1].wait()
    table[...] = charges[...].astype(jnp.float32)
    strips = table.shape[0]
    upper = order[...] // LANES
    lower = order[...] % LANES

    def step(u, acc):
        row = jnp.broadcast_to(table[pl.ds(u, 1), :], lower.shape)
        return jnp.where(upper == u, lane_gather(row, lower), acc)

    slots = lax.fori_loop(0, strips, step, jnp.zeros(lower.shape, jnp.float32), unroll=True)
    swapped = pltpu.roll(slots, BLK, 1)
    left = iota(slots.shape, 1) < BLK
    doubled[pl.ds(0, strips, stride=2), :] = jnp.where(left, slots, swapped)
    doubled[pl.ds(1, strips, stride=2), :] = jnp.where(left, swapped, slots)
    twice = doubled[...]
    copies[2].wait()
    copies[3].wait()
    patch = block_sums(project, twice)
    patch = jnp.where(iota(patch.shape, 1) < PTS, patch, 0.0).astype(jnp.bfloat16)
    spots = block_spots(anchors[:1, :])
    spot_out[...] = spots
    rows, lanes = patch_places(spots)
    moved = (iota(spots.shape, 1) == spots).astype(jnp.float32).astype(jnp.bfloat16)
    corner = anchors[...].astype(jnp.float32).astype(jnp.bfloat16)
    corner = dot(jnp.concatenate([corner] * 3, axis=0)[:8], moved)
    cells = (iota((8, 4 * blocks), 1) % 4).astype(jnp.float32)
    start = jnp.broadcast_to(anchors[:1, :].astype(jnp.float32), (8, blocks)).astype(jnp.bfloat16)
    for i in range(4):
        cells = cells + dot(start, lanes[i])
    spread = jnp.zeros((16, 4 * blocks), jnp.float32)
    for i in range(4):
        spread = spread + dot(dot_nt(rows[i], patch).astype(jnp.bfloat16), lanes[i])
    tiles = [slice(LANES * t, LANES * t + LANES) for t in range(groups)]
    sent = [spread[:, tile].astype(jnp.bfloat16) for tile in tiles]
    sent.append(slots.astype(jnp.bfloat16))
    extra = [cells[:1, tile] for tile in tiles] + [corner[:3]]
    extra.append(jnp.zeros((13 - groups, LANES), jnp.float32))
    sent.append(jnp.concatenate(extra, axis=0).astype(jnp.bfloat16))
    sent = jnp.concatenate(sent, axis=0)
    for n in range(sent_out.shape[0]):
        sent_out[n] = sent


def inverse_kernel(order, out):
    rows = order.shape[0]

    def step(r, acc):
        here = order[pl.ds(r, 1), :]
        upper = iota((rows, LANES), 0) == here // LANES
        lower = iota((LANES, LANES), 0) == here % LANES
        values = jnp.concatenate(
            [
                jnp.where(upper, r.astype(jnp.float32), 0.0),
                jnp.where(upper, iota((rows, LANES), 1).astype(jnp.float32), 0.0),
            ],
            axis=0,
        )
        return acc + dot_nt(
            values.astype(jnp.bfloat16), lower.astype(jnp.float32).astype(jnp.bfloat16)
        )

    out[...] = lax.fori_loop(
        0, rows, step, jnp.zeros((2 * rows, LANES), jnp.float32), unroll=4
    ).astype(jnp.int32)


def near_kernel(source, near_blocks, target, mine, theirs, out, table, picked):
    step = pl.program_id(0)
    pairs = picked.shape[0]
    blocks = out.shape[0]

    @pl.when(step == 0)
    def _():
        members, strips, _ = mine.shape
        left = iota((strips, LANES), 1) < BLK
        for side, part in enumerate((mine, theirs)):
            for n in range(members):
                at = (side * members + n) * blocks
                slots = part[n].astype(jnp.float32)
                swapped = pltpu.roll(slots, BLK, 1)
                table[pl.ds(at, strips, stride=2), :] = jnp.where(left, slots, swapped)
                table[pl.ds(at + 1, strips, stride=2), :] = jnp.where(left, swapped, slots)
        out[...] = jnp.zeros_like(out)

    def pick(p, carry):
        picked[pl.ds(p, 1), :] = table[pl.ds(source[step * pairs + p], 1), :]
        return carry

    lax.fori_loop(0, pairs, pick, 0, unroll=8)
    terms = block_sums(near_blocks, picked[...])
    owner = (iota((blocks, pairs), 0) == target[...]).astype(jnp.float32).astype(jnp.bfloat16)
    high, low = split(terms)
    out[...] += dot(owner, high) + dot(owner, low)


def table_rows(cas, numbers, count):
    parts = [cas[pl.ds(pl.multiple_of(n * count, 16), count), :G] for n in numbers]
    return jnp.concatenate(parts, axis=0) if len(parts) > 1 else parts[0]


def turned(rows):
    unit = (iota((G, G), 0) == iota((G, G), 1)).astype(jnp.float32).astype(jnp.bfloat16)
    return dot_nt(unit, rows).astype(jnp.bfloat16)


def tile_loop(half, rows, cols, groups, crosses, body):
    per_slab = cols // SLABS
    low = jnp.maximum(half * (rows // HALVES) - 1, 0)
    high = (half + 1) * (rows // HALVES)
    per_row = per_slab * groups

    def place(row, col):
        side = (col % HALVES) ^ half
        return side * (rows * cols // HALVES) + row * (cols // HALVES) + col // HALVES

    def step(n, carry):
        row = low + n // per_row
        left = n % per_row
        t = left % groups
        devices = [place(row, s * per_slab + left // groups) for s in range(SLABS)]
        found = [crosses((d * groups + t) * GROUP) for d in devices]
        inside = row >= half * (rows // HALVES)
        pl.when(functools.reduce(jnp.logical_or, found, inside))(lambda: body(devices, t))
        return carry

    lax.fori_loop(0, (high - low) * per_row, step, 0)


def lanes_inside(extra, d, t, half):
    extra = extra[d].astype(jnp.float32)
    picked = jnp.where(iota(extra.shape, 0) == t, extra, 0.0)
    cells = jnp.sum(picked, axis=0, keepdims=True) - (half * LANES).astype(jnp.float32)
    return jnp.broadcast_to((cells >= 0.0) & (cells < LANES), (16, LANES))


def scatter_kernel(
    cols,
    gs,
    fs,
    place,
    shift,
    start,
    mine,
    theirs,
    my_extra,
    their_extra,
    cas,
    own_out,
    other_out,
    patches,
    extra,
    lines,
    *slabs,
):
    half = place[0]
    step = pl.program_id(0)
    devices, held, _ = patches.shape
    groups = held // 16
    blocks = groups * GROUP
    owner = (iota((16, LANES), 1) // 4).astype(jnp.float32).astype(jnp.bfloat16)
    plane = iota((16, LANES), 0) % QUAD

    @pl.when(step == 0)
    def _():
        def clear(n, carry):
            for slab in slabs:
                at = pl.multiple_of(n * SLAB + PAD, 8)
                slab[pl.ds(at, SLAB - PAD), :] = jnp.zeros((SLAB - PAD, LANES), jnp.float32)
            return carry

        lax.fori_loop(0, G // QUAD, clear, 0)
        for side, part in enumerate(((mine, my_extra), (theirs, their_extra))):
            at = slice(side * (devices // 2), (side + 1) * (devices // 2))
            patches[at] = part[0][...]
            extra[at] = part[1][...]

        def tile(numbers, t):
            values = []
            for d in numbers:
                part = patches[d, pl.ds(pl.multiple_of(16 * t, 16), 16), :].astype(jnp.float32)
                part = jnp.where(lanes_inside(extra, d, t, half), part, 0.0)
                values.append(part.astype(jnp.bfloat16))

            for k in range(GROUP):
                sums = []
                for s in range(SLABS):
                    b = numbers[s] * blocks + t * GROUP + k
                    at = start[b]
                    moved = jnp.where(owner == k, values[s], jnp.zeros_like(values[s]))
                    moved = pltpu.roll(moved, shift[b], 1).astype(jnp.float32)
                    here = plane < QUAD - (at & (QUAD - 1))
                    near = slabs[s][pl.ds(at, 16), :] + jnp.where(here, moved, 0.0)
                    at_next = at + (SLAB - QUAD)
                    far = slabs[s][pl.ds(at_next, 16), :] + jnp.where(here, 0.0, moved)
                    sums.append((at, near, at_next, far))
                for s, (at, near, at_next, far) in enumerate(sums):
                    slabs[s][pl.ds(at, 16), :] = near
                    slabs[s][pl.ds(at_next, 16), :] = far

        def crosses(b):
            return shift[b] > LANES - 4

        tile_loop(half, devices // cols, cols, groups, crosses, tile)

        table = table_rows(cas, [place[1]], gs)

        def planes(n, carry):
            base = pl.multiple_of(n * SLAB, 8)
            sheets = []
            for q in range(QUAD):
                parts = []
                for s in range(SLABS):
                    part = slabs[s][pl.ds(base + (PAD + q), PIECE, stride=QUAD), :]
                    if s > 0:
                        at = base + (PAD + QUAD * PIECE + q)
                        over = slabs[s - 1][pl.ds(at, 4, stride=QUAD), :]
                        over = jnp.concatenate([over, jnp.zeros_like(over)], axis=0)
                        part = jnp.concatenate([part[:8] + over, part[8:]], axis=0)
                    parts.append(part.astype(jnp.bfloat16))
                sheets.append(jnp.concatenate(parts, axis=0))
            field = dot(table, jnp.concatenate(sheets, axis=1))
            for q in range(QUAD):
                part = field[:, LANES * q : LANES * q + LANES]
                lines[pl.ds(n * QUAD + q, gs, stride=STRIDE), :] = part
            return carry

        lax.fori_loop(0, G // QUAD, planes, 0, unroll=UNROLL_PLANES)

    @pl.when(step > 0)
    def _():
        third = table_rows(cas, [place[2], place[2] ^ 1], fs)
        for g in range(0, LINES, 2):
            pair = []
            for n in (g, g + 1):
                at = ((step - 1) * LINES + n) * STRIDE
                pair.append(lines[pl.ds(at, G), :].astype(jnp.bfloat16))
            field = dot(third, jnp.concatenate(pair, axis=1)).astype(jnp.bfloat16)
            for n in range(2):
                own_out[g + n] = field[:fs, LANES * n : LANES * n + LANES]
                other_out[g + n] = field[fs:, LANES * n : LANES * n + LANES]


def spectrum_kernel(place, own, other, *refs):
    weights, (cas, own_out, other_out) = refs[:WAYS], refs[WAYS:]
    tiles = [pl.ds(pl.multiple_of(h * LANES, LANES), LANES) for h in (place[0], 1 - place[0])]
    first = jnp.concatenate([cas[tile, :] for tile in tiles], axis=0)
    first_back = jnp.concatenate([cas[:, tile] for tile in tiles], axis=1)
    step, freqs, _ = weights[0].shape
    rows = step * freqs
    for n in range(WAYS):
        part = slice(n * step, (n + 1) * step)
        line = jnp.concatenate(
            [own[part].reshape(rows, LANES), other[part].reshape(rows, LANES)], axis=1
        )
        s = dot(line, first) * weights[n][...].reshape(rows, P_SIZE)
        line = dot(s.astype(jnp.bfloat16), first_back).astype(jnp.bfloat16)
        own_out[part] = line[:, :LANES].reshape(step, freqs, LANES)
        other_out[part] = line[:, LANES:].reshape(step, freqs, LANES)


def sample_kernel(
    cols,
    place,
    shift,
    start,
    my_extra,
    their_extra,
    own,
    other,
    cas,
    out,
    extra,
    second,
    third,
    lines,
    cells,
):
    half = place[0]
    step = pl.program_id(0)
    devices, held, _ = out.shape
    groups = held // 16
    blocks = groups * GROUP
    gs = second.shape[1]
    owner = (iota((16, LANES), 1) // 4).astype(jnp.float32).astype(jnp.bfloat16)
    plane = iota((16, LANES), 0) % QUAD

    @pl.when(step == 0)
    def _():
        for side, part in enumerate((my_extra, their_extra)):
            extra[side * (devices // 2) : (side + 1) * (devices // 2)] = part[...]
        second[...] = turned(table_rows(cas, [place[1]], gs))
        third[...] = turned(table_rows(cas, [place[2], place[2] ^ 1], own.shape[1]))

    for g in range(0, LINES, 2):
        pair = [jnp.concatenate([own[n], other[n]], axis=0) for n in (g, g + 1)]
        field = dot(third[...], jnp.concatenate(pair, axis=1))
        for n in range(2):
            at = (step * LINES + g + n) * STRIDE
            lines[pl.ds(at, G), :] = field[:, LANES * n : LANES * n + LANES]

    @pl.when(step == pl.num_programs(0) - 1)
    def _():
        def planes(n, carry):
            sheets = [
                lines[pl.ds(n * QUAD + q, gs, stride=STRIDE), :].astype(jnp.bfloat16)
                for q in range(QUAD)
            ]
            field = dot(second[...], jnp.concatenate(sheets, axis=1))
            base = pl.multiple_of(n * CELLS, 8)
            for q in range(QUAD):
                part = field[:, LANES * q : LANES * q + LANES]
                cells[pl.ds(base + (PAD + q), G, stride=QUAD), :] = part
            return carry

        lax.fori_loop(0, G // QUAD, planes, 0, unroll=UNROLL_PLANES)
        out[...] = jnp.zeros_like(out)

        def tile(numbers, t):
            sums = [jnp.zeros((16, LANES), jnp.bfloat16)] * SLABS
            for k in range(GROUP):
                for s in range(SLABS):
                    b = numbers[s] * blocks + t * GROUP + k
                    at = start[b]
                    here = plane < QUAD - (at & (QUAD - 1))
                    near = cells[pl.ds(at, 16), :]
                    far = cells[pl.ds(at + (CELLS - QUAD), 16), :]
                    moved = jnp.where(here, near, far).astype(jnp.bfloat16)
                    sums[s] = jnp.where(owner == k, pltpu.roll(moved, shift[b], 1), sums[s])
            for s, d in enumerate(numbers):
                inside = lanes_inside(extra, d, t, half)
                out[d, pl.ds(pl.multiple_of(16 * t, 16), 16), :] = jnp.where(
                    inside, sums[s].astype(jnp.float32), 0.0
                ).astype(jnp.bfloat16)

        def crosses(b):
            return (shift[b] > 0) & (shift[b] < 4)

        tile_loop(half, devices // cols, cols, groups, crosses, tile)


def finish_kernel(values, interpolate, near, inverse, spots, out, total):
    blocks = near.shape[0]
    groups = values.shape[1] // 16
    rows, lanes = patch_places(spots[...])
    summed = values[0].astype(jnp.float32)
    for d in range(1, values.shape[0]):
        summed = summed + values[d].astype(jnp.float32)
    spread = jnp.concatenate([summed[16 * t : 16 * t + 16] for t in range(groups)], axis=1)
    parts = jnp.concatenate(split(spread), axis=0)
    patch = jnp.zeros((blocks, LANES), jnp.float32)
    for i in range(4):
        column = dot_nt(lanes[i], parts).astype(jnp.bfloat16)
        patch = patch + dot(column, jnp.concatenate([rows[i], rows[i]], axis=0))
    total[...] = block_sums(interpolate, patch) + near[...]
    count = out.shape[0]
    even = total[pl.ds(0, count, stride=2), :]
    odd = total[pl.ds(1, count, stride=2), :]
    total[:count] = jnp.where(iota(even.shape, 1) < BLK, even, odd)
    upper = inverse[:count]
    lower = inverse[count:]

    def step(u, acc):
        row = jnp.broadcast_to(total[pl.ds(u, 1), :], lower.shape)
        return jnp.where(upper == u, lane_gather(row, lower), acc)

    out[...] = lax.fori_loop(0, count, step, jnp.zeros(out.shape, jnp.float32), unroll=True)


def struct(shape, dtype):
    return jax.ShapeDtypeStruct(shape, dtype)


def whole(shape):
    return pl.BlockSpec(shape, lambda *_: (0,) * len(shape))


def params(mib):
    return pltpu.CompilerParams(vmem_limit_bytes=mib * MB)


def body(
    charges,
    panel_order,
    patch_anchor,
    project,
    interpolate,
    kernel_spectrum,
    near_pairs,
    near_blocks,
):
    axes = ("row", "col")
    rows = lax.axis_size("row")
    cols = lax.axis_size("col")
    devices = rows * cols
    row_at = lax.axis_index("row")
    col_at = lax.axis_index("col")
    half = col_at % HALVES
    mates = [(c, c ^ 1) for c in range(cols)]
    blocks = project.shape[0]
    groups = blocks // GROUP
    panels = charges.shape[0]
    strips = panels // LANES
    gs, fs, _ = kernel_spectrum.shape
    held = 16 * groups + strips + 16

    order = panel_order.reshape(strips, LANES)
    members = devices // HALVES
    sent, spots = pl.pallas_call(
        project_kernel,
        out_shape=(
            struct((members, held, LANES), jnp.bfloat16),
            struct((blocks, LANES), jnp.int32),
        ),
        in_specs=[pl.BlockSpec(memory_space=pltpu.HBM)] * 4,
        scratch_shapes=[
            pltpu.VMEM((strips, LANES), jnp.bfloat16),
            pltpu.VMEM((strips, LANES), jnp.int32),
            pltpu.VMEM(project.shape, jnp.bfloat16),
            pltpu.VMEM(patch_anchor.shape, jnp.int32),
            pltpu.VMEM((strips, LANES), jnp.float32),
            pltpu.VMEM((blocks, LANES), jnp.float32),
            pltpu.SemaphoreType.DMA((4,)),
        ],
        compiler_params=params(58),
        name="project",
    )(
        charges.reshape(strips, LANES),
        order,
        project,
        patch_anchor,
    )
    cores = [
        [r * cols + c for r in range(rows) for c in range(core, cols, HALVES)]
        for core in range(HALVES)
    ]

    def swap_members(array):
        return lax.all_to_all(
            array, axes, split_axis=0, concat_axis=0, axis_index_groups=cores, tiled=True
        )

    mine = swap_members(sent)
    theirs = lax.ppermute(mine, "col", mates)
    at = held - 16 + groups
    anchors = jnp.stack([part[:, at : at + 3] for part in (mine, theirs)])
    anchors = anchors.astype(jnp.int32)
    lane = 4 * (jnp.arange(blocks, dtype=jnp.int32) % GROUP)
    forth = ((anchors[:, :, 0] - lane) & (LANES - 1)).reshape(devices * blocks)
    back = ((lane - anchors[:, :, 0]) & (LANES - 1)).reshape(devices * blocks)
    group = anchors[:, :, 2] // QUAD
    inner = PAD + QUAD * anchors[:, :, 1] + anchors[:, :, 2] % QUAD
    side = jnp.arange(HALVES, dtype=jnp.int32)[:, None] ^ half
    col = jnp.arange(members, dtype=jnp.int32) % (cols // HALVES) * HALVES + side
    piece = (col * SLABS // cols * PIECE)[:, :, None]
    slab_at = (group * SLAB + inner - QUAD * piece).reshape(devices * blocks)
    cell_at = (group * CELLS + inner).reshape(devices * blocks)
    place = jnp.stack([half, row_at, col_at]).astype(jnp.int32)
    cas = jnp.asarray(CAS)

    smem = pl.BlockSpec(memory_space=pltpu.SMEM)

    def rows_at(start, count):
        return pl.BlockSpec((members, count, LANES), lambda *_: (0, start // count, 0))

    patch_rows = rows_at(0, 16 * groups)
    charge_rows = rows_at(16 * groups, strips)
    extra_rows = rows_at(16 * groups + strips, 16)
    steps = gs // LINES
    lines_type = struct((gs, fs, LANES), jnp.bfloat16)
    late = pl.BlockSpec((LINES, fs, LANES), lambda n: (jnp.maximum(n - 1, 0), 0, 0))
    own, other = pl.pallas_call(
        functools.partial(scatter_kernel, cols, gs, fs),
        grid=(1 + steps,),
        in_specs=[smem] * 3 + [patch_rows] * 2 + [extra_rows] * 2 + [whole(cas.shape)],
        out_specs=(late, late),
        out_shape=(lines_type, lines_type),
        scratch_shapes=[
            pltpu.VMEM((devices, 16 * groups, LANES), jnp.bfloat16),
            pltpu.VMEM((devices, 16, LANES), jnp.bfloat16),
            pltpu.VMEM((gs * STRIDE, LANES), jnp.float32),
        ]
        + [pltpu.VMEM(((G // QUAD + 1) * SLAB, LANES), jnp.float32)] * SLABS,
        compiler_params=params(53),
        name="scatter",
    )(place, forth, slab_at, mine, theirs, mine, theirs, cas)
    other = lax.ppermute(other, "col", mates)
    own, order = lax.optimization_barrier((own, order))
    inverse = pl.pallas_call(
        inverse_kernel,
        out_shape=struct((2 * strips, LANES), jnp.int32),
        compiler_params=params(32),
        name="inverse",
    )(order)

    other, inverse = lax.optimization_barrier((other, inverse))

    part = lambda shape: pl.BlockSpec((BATCH,) + shape, lambda n: (n, 0, 0))

    def weight_part(way):
        return pl.BlockSpec((BATCH // WAYS, fs, P_SIZE), lambda n: (n * WAYS + way, 0, 0))

    own, other = pl.pallas_call(
        spectrum_kernel,
        grid=(gs // BATCH,),
        in_specs=[
            smem,
            part((fs, LANES)),
            part((fs, LANES)),
            *[weight_part(n) for n in range(WAYS)],
            whole(cas.shape),
        ],
        out_specs=(part((fs, LANES)), part((fs, LANES))),
        out_shape=(lines_type, lines_type),
        compiler_params=params(40),
        name="spectrum",
    )(place, own, other, *[kernel_spectrum] * WAYS, cas)
    other = lax.ppermute(other, "col", mates)

    early = pl.BlockSpec((LINES, fs, LANES), lambda n: (n, 0, 0))
    values = pl.pallas_call(
        functools.partial(sample_kernel, cols),
        grid=(steps,),
        in_specs=[smem] * 3 + [extra_rows] * 2 + [early, early, whole(cas.shape)],
        out_specs=whole((devices, 16 * groups, LANES)),
        out_shape=struct((devices, 16 * groups, LANES), jnp.bfloat16),
        scratch_shapes=[
            pltpu.VMEM((devices, 16, LANES), jnp.bfloat16),
            pltpu.VMEM((G, gs), jnp.bfloat16),
            pltpu.VMEM((G, 2 * fs), jnp.bfloat16),
            pltpu.VMEM((gs * STRIDE, LANES), jnp.float32),
            pltpu.VMEM(((G // QUAD + 1) * CELLS, LANES), jnp.float32),
        ],
        compiler_params=params(46),
        name="sample",
    )(place, back, cell_at, mine, theirs, own, other, cas)
    values = values.reshape(HALVES, members, 16 * groups, LANES)
    received = lax.ppermute(values[1], "col", mates).astype(jnp.float32)
    values = (values[0].astype(jnp.float32) + received).astype(jnp.bfloat16)
    values, my_charges, their_charges = lax.optimization_barrier((values, mine, theirs))
    values = swap_members(values)

    source = near_pairs[1]
    source_row = source // blocks // cols
    source_col = source // blocks % cols
    wanted = (source_col % HALVES ^ half) * members + source_row * (cols // HALVES)
    wanted = (wanted + source_col // HALVES) * blocks + source % blocks
    target = near_pairs[0] - (row_at * cols + col_at) * blocks
    pairs = near_blocks.shape[0]
    near = pl.pallas_call(
        near_kernel,
        grid=(pairs // blocks,),
        in_specs=[
            smem,
            pl.BlockSpec((blocks, BLK * BLK), lambda n: (n, 0)),
            pl.BlockSpec((1, blocks), lambda n: (0, n)),
            charge_rows,
            charge_rows,
        ],
        out_specs=whole((blocks, LANES)),
        out_shape=struct((blocks, LANES), jnp.float32),
        scratch_shapes=[
            pltpu.VMEM((devices * blocks, LANES), jnp.float32),
            pltpu.VMEM((blocks, LANES), jnp.float32),
        ],
        compiler_params=params(56),
        name="near",
    )(wanted, near_blocks, target.reshape(1, pairs), my_charges, their_charges)

    result = pl.pallas_call(
        finish_kernel,
        out_shape=struct((strips, LANES), jnp.float32),
        scratch_shapes=[pltpu.VMEM((blocks, LANES), jnp.float32)],
        compiler_params=params(32),
        name="finish",
    )(values, interpolate, near, inverse, spots)
    return result.reshape(panels)


def solution(mesh):
    placed = (
        P(("row", "col")),
        P(("row", "col")),
        P(None, ("row", "col")),
        P(("row", "col"), None),
        P(("row", "col"), None),
        P("row", "col", None),
        P(None, ("row", "col")),
        P(("row", "col"), None),
    )
    return jax.shard_map(
        body, mesh=mesh, in_specs=placed, out_specs=P(("row", "col")), check_vma=False
    )
```

```python
import functools

import jax
import jax.numpy as jnp
import ml_dtypes
import numpy as np
from jax import lax
from jax.experimental import pallas as pl
from jax.experimental.pallas import tpu as pltpu
from jax.sharding import PartitionSpec as P

G = 256
P_SIZE = 512
BLK = 64
PTS = 64
LANES = 128
GROUP = LANES // 4
HALVES = G // LANES
SLABS = 4
PIECE = G // SLABS
QUAD = 4
PAD = 8
SLAB = PAD + QUAD * PIECE + 16
CELLS = PAD + QUAD * G + 16
STRIDE = G + 1
BATCH = 8
WAYS = 4
LINES = 16
UNROLL_PLANES = 16
MB = 1 << 20
NT = (((1,), (1,)), ((), ()))


def cas_table():
    index = np.arange(P_SIZE, dtype=np.int64)
    phase = (index[:, None] * index[None, :] % P_SIZE).astype(np.float64) * (2.0 * np.pi / P_SIZE)
    return ((np.cos(phase) + np.sin(phase)) / np.sqrt(P_SIZE)).astype(ml_dtypes.bfloat16)


CAS = cas_table()


def dot(a, b):
    return jnp.dot(a, b, preferred_element_type=jnp.float32)


def dot_nt(a, b):
    return lax.dot_general(a, b, NT, preferred_element_type=jnp.float32)


def iota(shape, dim):
    return lax.broadcasted_iota(jnp.int32, shape, dim)


def split(value):
    high = value.astype(jnp.bfloat16)
    return high, (value - high.astype(jnp.float32)).astype(jnp.bfloat16)


def lane_gather(table, index):
    return jnp.take_along_axis(table, index, axis=1, mode="promise_in_bounds")


def block_sums(mats, vecs):
    rows = vecs.shape[0]
    pair = jnp.concatenate([vecs, vecs], axis=1)
    total = jnp.zeros((2 * rows, LANES), jnp.float32)
    for t in range(mats.shape[1] // 256):
        high, low = split(mats[:, 256 * t : 256 * t + 256].astype(jnp.float32) * pair)
        owner = iota((256, LANES), 0) // BLK + 4 * t
        table = (owner == iota((256, LANES), 1) % BLK).astype(jnp.bfloat16)
        total = total + dot(jnp.concatenate([high, low], axis=0), table)
    return total[:rows] + total[rows:]


def patch_places(spots):
    blocks = spots.shape[0]
    spots = jnp.concatenate([spots] * (4 * blocks // LANES), axis=1)
    lane = iota(spots.shape, 1)
    lanes = [(lane == 4 * spots + i).astype(jnp.float32).astype(jnp.bfloat16) for i in range(4)]
    row = iota((16, LANES), 0)
    rows = [
        (iota((16, LANES), 1) % PTS == 16 * i + row).astype(jnp.float32).astype(jnp.bfloat16)
        for i in range(4)
    ]
    return rows, lanes


def block_spots(first):
    blocks = first.shape[1]
    shape = (blocks, blocks)
    crossing = ((first & (LANES - 1)) > LANES - 4).astype(jnp.float32)
    crossing = jnp.broadcast_to(crossing, (8, blocks))
    earlier = (iota(shape, 0) < iota(shape, 1)).astype(jnp.float32).astype(jnp.bfloat16)
    ahead = dot(crossing.astype(jnp.bfloat16), earlier)
    total = jnp.sum(crossing, axis=1, keepdims=True)
    block = iota((8, blocks), 1).astype(jnp.float32)
    spot = jnp.where(crossing > 0.0, ahead, total + block - ahead)
    spread = jnp.broadcast_to(spot[:1], (LANES, blocks)).astype(jnp.bfloat16)
    unit = (iota(shape, 0) == iota(shape, 1)).astype(jnp.float32).astype(jnp.bfloat16)
    return dot_nt(unit, spread).astype(jnp.int32)


def project_kernel(
    charges_in,
    order_in,
    project_in,
    anchors_in,
    sent_out,
    spot_out,
    charges,
    order,
    project,
    anchors,
    table,
    doubled,
    sems,
):
    blocks = spot_out.shape[0]
    groups = blocks // GROUP
    pairs = ((charges_in, charges), (order_in, order), (project_in, project), (anchors_in, anchors))
    copies = [pltpu.make_async_copy(a, b, sems.at[n]) for n, (a, b) in enumerate(pairs)]
    for copy in copies:
        copy.start()
    copies[0].wait()
    copies[1].wait()
    table[...] = charges[...].astype(jnp.float32)
    strips = table.shape[0]
    upper = order[...] // LANES
    lower = order[...] % LANES

    def step(u, acc):
        row = jnp.broadcast_to(table[pl.ds(u, 1), :], lower.shape)
        return jnp.where(upper == u, lane_gather(row, lower), acc)

    slots = lax.fori_loop(0, strips, step, jnp.zeros(lower.shape, jnp.float32), unroll=True)
    swapped = pltpu.roll(slots, BLK, 1)
    left = iota(slots.shape, 1) < BLK
    doubled[pl.ds(0, strips, stride=2), :] = jnp.where(left, slots, swapped)
    doubled[pl.ds(1, strips, stride=2), :] = jnp.where(left, swapped, slots)
    twice = doubled[...]
    copies[2].wait()
    copies[3].wait()
    patch = block_sums(project, twice)
    patch = jnp.where(iota(patch.shape, 1) < PTS, patch, 0.0).astype(jnp.bfloat16)
    spots = block_spots(anchors[:1, :])
    spot_out[...] = spots
    rows, lanes = patch_places(spots)
    moved = (iota(spots.shape, 1) == spots).astype(jnp.float32).astype(jnp.bfloat16)
    corner = anchors[...].astype(jnp.float32).astype(jnp.bfloat16)
    corner = dot(jnp.concatenate([corner] * 3, axis=0)[:8], moved)
    cells = (iota((8, 4 * blocks), 1) % 4).astype(jnp.float32)
    start = jnp.broadcast_to(anchors[:1, :].astype(jnp.float32), (8, blocks)).astype(jnp.bfloat16)
    for i in range(4):
        cells = cells + dot(start, lanes[i])
    spread = jnp.zeros((16, 4 * blocks), jnp.float32)
    for i in range(4):
        spread = spread + dot(dot_nt(rows[i], patch).astype(jnp.bfloat16), lanes[i])
    tiles = [slice(LANES * t, LANES * t + LANES) for t in range(groups)]
    sent = [spread[:, tile].astype(jnp.bfloat16) for tile in tiles]
    sent.append(slots.astype(jnp.bfloat16))
    extra = [cells[:1, tile] for tile in tiles] + [corner[:3]]
    extra.append(jnp.zeros((13 - groups, LANES), jnp.float32))
    sent.append(jnp.concatenate(extra, axis=0).astype(jnp.bfloat16))
    sent = jnp.concatenate(sent, axis=0)
    for n in range(sent_out.shape[0]):
        sent_out[n] = sent


def inverse_kernel(order, out):
    rows = order.shape[0]

    def step(r, acc):
        here = order[pl.ds(r, 1), :]
        upper = iota((rows, LANES), 0) == here // LANES
        lower = iota((LANES, LANES), 0) == here % LANES
        values = jnp.concatenate(
            [
                jnp.where(upper, r.astype(jnp.float32), 0.0),
                jnp.where(upper, iota((rows, LANES), 1).astype(jnp.float32), 0.0),
            ],
            axis=0,
        )
        return acc + dot_nt(
            values.astype(jnp.bfloat16), lower.astype(jnp.float32).astype(jnp.bfloat16)
        )

    out[...] = lax.fori_loop(
        0, rows, step, jnp.zeros((2 * rows, LANES), jnp.float32), unroll=4
    ).astype(jnp.int32)


def near_kernel(source, near_blocks, target, mine, theirs, out, table, picked):
    step = pl.program_id(0)
    pairs = picked.shape[0]
    blocks = out.shape[0]

    @pl.when(step == 0)
    def _():
        members, strips, _ = mine.shape
        left = iota((strips, LANES), 1) < BLK
        for side, part in enumerate((mine, theirs)):
            for n in range(members):
                at = (side * members + n) * blocks
                slots = part[n].astype(jnp.float32)
                swapped = pltpu.roll(slots, BLK, 1)
                table[pl.ds(at, strips, stride=2), :] = jnp.where(left, slots, swapped)
                table[pl.ds(at + 1, strips, stride=2), :] = jnp.where(left, swapped, slots)
        out[...] = jnp.zeros_like(out)

    def pick(p, carry):
        picked[pl.ds(p, 1), :] = table[pl.ds(source[step * pairs + p], 1), :]
        return carry

    lax.fori_loop(0, pairs, pick, 0, unroll=8)
    terms = block_sums(near_blocks, picked[...])
    owner = (iota((blocks, pairs), 0) == target[...]).astype(jnp.float32).astype(jnp.bfloat16)
    high, low = split(terms)
    out[...] += dot(owner, high) + dot(owner, low)


def table_rows(cas, numbers, count):
    parts = [cas[pl.ds(pl.multiple_of(n * count, 16), count), :G] for n in numbers]
    return jnp.concatenate(parts, axis=0) if len(parts) > 1 else parts[0]


def turned(rows):
    unit = (iota((G, G), 0) == iota((G, G), 1)).astype(jnp.float32).astype(jnp.bfloat16)
    return dot_nt(unit, rows).astype(jnp.bfloat16)


def tile_loop(half, rows, cols, groups, crosses, body):
    per_slab = cols // SLABS
    low = jnp.maximum(half * (rows // HALVES) - 1, 0)
    high = (half + 1) * (rows // HALVES)
    per_row = per_slab * groups

    def place(row, col):
        side = (col % HALVES) ^ half
        return side * (rows * cols // HALVES) + row * (cols // HALVES) + col // HALVES

    def step(n, carry):
        row = low + n // per_row
        left = n % per_row
        t = left % groups
        devices = [place(row, s * per_slab + left // groups) for s in range(SLABS)]
        found = [crosses((d * groups + t) * GROUP) for d in devices]
        inside = row >= half * (rows // HALVES)
        pl.when(functools.reduce(jnp.logical_or, found, inside))(lambda: body(devices, t))
        return carry

    lax.fori_loop(0, (high - low) * per_row, step, 0)


def lanes_inside(extra, d, t, half):
    extra = extra[d].astype(jnp.float32)
    picked = jnp.where(iota(extra.shape, 0) == t, extra, 0.0)
    cells = jnp.sum(picked, axis=0, keepdims=True) - (half * LANES).astype(jnp.float32)
    return jnp.broadcast_to((cells >= 0.0) & (cells < LANES), (16, LANES))


def scatter_kernel(
    cols,
    gs,
    fs,
    place,
    shift,
    start,
    mine,
    theirs,
    my_extra,
    their_extra,
    cas,
    own_out,
    other_out,
    patches,
    extra,
    lines,
    *slabs,
):
    half = place[0]
    step = pl.program_id(0)
    devices, held, _ = patches.shape
    groups = held // 16
    blocks = groups * GROUP
    owner = (iota((16, LANES), 1) // 4).astype(jnp.float32).astype(jnp.bfloat16)
    plane = iota((16, LANES), 0) % QUAD

    @pl.when(step == 0)
    def _():
        def clear(n, carry):
            for slab in slabs:
                at = pl.multiple_of(n * SLAB + PAD, 8)
                slab[pl.ds(at, SLAB - PAD), :] = jnp.zeros((SLAB - PAD, LANES), jnp.float32)
            return carry

        lax.fori_loop(0, G // QUAD, clear, 0)
        for side, part in enumerate(((mine, my_extra), (theirs, their_extra))):
            at = slice(side * (devices // 2), (side + 1) * (devices // 2))
            patches[at] = part[0][...]
            extra[at] = part[1][...]

        def tile(numbers, t):
            values = []
            for d in numbers:
                part = patches[d, pl.ds(pl.multiple_of(16 * t, 16), 16), :].astype(jnp.float32)
                part = jnp.where(lanes_inside(extra, d, t, half), part, 0.0)
                values.append(part.astype(jnp.bfloat16))

            for k in range(GROUP):
                sums = []
                for s in range(SLABS):
                    b = numbers[s] * blocks + t * GROUP + k
                    at = start[b]
                    moved = jnp.where(owner == k, values[s], jnp.zeros_like(values[s]))
                    moved = pltpu.roll(moved, shift[b], 1).astype(jnp.float32)
                    here = plane < QUAD - (at & (QUAD - 1))
                    near = slabs[s][pl.ds(at, 16), :] + jnp.where(here, moved, 0.0)
                    at_next = at + (SLAB - QUAD)
                    far = slabs[s][pl.ds(at_next, 16), :] + jnp.where(here, 0.0, moved)
                    sums.append((at, near, at_next, far))
                for s, (at, near, at_next, far) in enumerate(sums):
                    slabs[s][pl.ds(at, 16), :] = near
                    slabs[s][pl.ds(at_next, 16), :] = far

        def crosses(b):
            return shift[b] > LANES - 4

        tile_loop(half, devices // cols, cols, groups, crosses, tile)

        table = table_rows(cas, [place[1]], gs)

        def planes(n, carry):
            base = pl.multiple_of(n * SLAB, 8)
            sheets = []
            for q in range(QUAD):
                parts = []
                for s in range(SLABS):
                    part = slabs[s][pl.ds(base + (PAD + q), PIECE, stride=QUAD), :]
                    if s > 0:
                        at = base + (PAD + QUAD * PIECE + q)
                        over = slabs[s - 1][pl.ds(at, 4, stride=QUAD), :]
                        over = jnp.concatenate([over, jnp.zeros_like(over)], axis=0)
                        part = jnp.concatenate([part[:8] + over, part[8:]], axis=0)
                    parts.append(part.astype(jnp.bfloat16))
                sheets.append(jnp.concatenate(parts, axis=0))
            field = dot(table, jnp.concatenate(sheets, axis=1))
            for q in range(QUAD):
                part = field[:, LANES * q : LANES * q + LANES]
                lines[pl.ds(n * QUAD + q, gs, stride=STRIDE), :] = part
            return carry

        lax.fori_loop(0, G // QUAD, planes, 0, unroll=UNROLL_PLANES)

    @pl.when(step > 0)
    def _():
        third = table_rows(cas, [place[2], place[2] ^ 1], fs)
        for g in range(0, LINES, 2):
            pair = []
            for n in (g, g + 1):
                at = ((step - 1) * LINES + n) * STRIDE
                pair.append(lines[pl.ds(at, G), :].astype(jnp.bfloat16))
            field = dot(third, jnp.concatenate(pair, axis=1)).astype(jnp.bfloat16)
            for n in range(2):
                own_out[g + n] = field[:fs, LANES * n : LANES * n + LANES]
                other_out[g + n] = field[fs:, LANES * n : LANES * n + LANES]


def spectrum_kernel(place, own, other, *refs):
    weights, (cas, own_out, other_out) = refs[:WAYS], refs[WAYS:]
    tiles = [pl.ds(pl.multiple_of(h * LANES, LANES), LANES) for h in (place[0], 1 - place[0])]
    first = jnp.concatenate([cas[tile, :] for tile in tiles], axis=0)
    first_back = jnp.concatenate([cas[:, tile] for tile in tiles], axis=1)
    step, freqs, _ = weights[0].shape
    rows = step * freqs
    for n in range(WAYS):
        part = slice(n * step, (n + 1) * step)
        line = jnp.concatenate(
            [own[part].reshape(rows, LANES), other[part].reshape(rows, LANES)], axis=1
        )
        total = jnp.zeros((rows, G), jnp.float32)
        for f in (slice(0, G), slice(G, P_SIZE)):
            s = dot(line, first[:, f]) * weights[n][:, :, f].reshape(rows, G)
            total = total + dot(s.astype(jnp.bfloat16), first_back[f])
        line = total.astype(jnp.bfloat16)
        own_out[part] = line[:, :LANES].reshape(step, freqs, LANES)
        other_out[part] = line[:, LANES:].reshape(step, freqs, LANES)


def sample_kernel(
    cols,
    place,
    shift,
    start,
    my_extra,
    their_extra,
    own,
    other,
    cas,
    out,
    extra,
    second,
    third,
    lines,
    cells,
):
    half = place[0]
    step = pl.program_id(0)
    devices, held, _ = out.shape
    groups = held // 16
    blocks = groups * GROUP
    gs = second.shape[1]
    owner = (iota((16, LANES), 1) // 4).astype(jnp.float32).astype(jnp.bfloat16)
    plane = iota((16, LANES), 0) % QUAD

    @pl.when(step == 0)
    def _():
        for side, part in enumerate((my_extra, their_extra)):
            extra[side * (devices // 2) : (side + 1) * (devices // 2)] = part[...]
        second[...] = turned(table_rows(cas, [place[1]], gs))
        third[...] = turned(table_rows(cas, [place[2], place[2] ^ 1], own.shape[1]))

    for g in range(0, LINES, 2):
        pair = [jnp.concatenate([own[n], other[n]], axis=0) for n in (g, g + 1)]
        field = dot(third[...], jnp.concatenate(pair, axis=1))
        for n in range(2):
            at = (step * LINES + g + n) * STRIDE
            lines[pl.ds(at, G), :] = field[:, LANES * n : LANES * n + LANES]

    @pl.when(step == pl.num_programs(0) - 1)
    def _():
        def planes(n, carry):
            sheets = [
                lines[pl.ds(n * QUAD + q, gs, stride=STRIDE), :].astype(jnp.bfloat16)
                for q in range(QUAD)
            ]
            field = dot(second[...], jnp.concatenate(sheets, axis=1))
            base = pl.multiple_of(n * CELLS, 8)
            for q in range(QUAD):
                part = field[:, LANES * q : LANES * q + LANES]
                cells[pl.ds(base + (PAD + q), G, stride=QUAD), :] = part
            return carry

        lax.fori_loop(0, G // QUAD, planes, 0, unroll=UNROLL_PLANES)
        out[...] = jnp.zeros_like(out)

        def tile(numbers, t):
            sums = [jnp.zeros((16, LANES), jnp.bfloat16)] * SLABS
            for k in range(GROUP):
                for s in range(SLABS):
                    b = numbers[s] * blocks + t * GROUP + k
                    at = start[b]
                    here = plane < QUAD - (at & (QUAD - 1))
                    near = cells[pl.ds(at, 16), :]
                    far = cells[pl.ds(at + (CELLS - QUAD), 16), :]
                    moved = jnp.where(here, near, far).astype(jnp.bfloat16)
                    sums[s] = jnp.where(owner == k, pltpu.roll(moved, shift[b], 1), sums[s])
            for s, d in enumerate(numbers):
                inside = lanes_inside(extra, d, t, half)
                out[d, pl.ds(pl.multiple_of(16 * t, 16), 16), :] = jnp.where(
                    inside, sums[s].astype(jnp.float32), 0.0
                ).astype(jnp.bfloat16)

        def crosses(b):
            return (shift[b] > 0) & (shift[b] < 4)

        tile_loop(half, devices // cols, cols, groups, crosses, tile)


def finish_kernel(values, interpolate, near, inverse, spots, out, total):
    blocks = near.shape[0]
    groups = values.shape[1] // 16
    rows, lanes = patch_places(spots[...])
    summed = values[0].astype(jnp.float32)
    for d in range(1, values.shape[0]):
        summed = summed + values[d].astype(jnp.float32)
    spread = jnp.concatenate([summed[16 * t : 16 * t + 16] for t in range(groups)], axis=1)
    parts = jnp.concatenate(split(spread), axis=0)
    patch = jnp.zeros((blocks, LANES), jnp.float32)
    for i in range(4):
        column = dot_nt(lanes[i], parts).astype(jnp.bfloat16)
        patch = patch + dot(column, jnp.concatenate([rows[i], rows[i]], axis=0))
    total[...] = block_sums(interpolate, patch) + near[...]
    count = out.shape[0]
    even = total[pl.ds(0, count, stride=2), :]
    odd = total[pl.ds(1, count, stride=2), :]
    total[:count] = jnp.where(iota(even.shape, 1) < BLK, even, odd)
    upper = inverse[:count]
    lower = inverse[count:]

    def step(u, acc):
        row = jnp.broadcast_to(total[pl.ds(u, 1), :], lower.shape)
        return jnp.where(upper == u, lane_gather(row, lower), acc)

    out[...] = lax.fori_loop(0, count, step, jnp.zeros(out.shape, jnp.float32), unroll=True)


def struct(shape, dtype):
    return jax.ShapeDtypeStruct(shape, dtype)


def whole(shape):
    return pl.BlockSpec(shape, lambda *_: (0,) * len(shape))


def params(mib):
    return pltpu.CompilerParams(vmem_limit_bytes=mib * MB)


def body(
    charges,
    panel_order,
    patch_anchor,
    project,
    interpolate,
    kernel_spectrum,
    near_pairs,
    near_blocks,
):
    axes = ("row", "col")
    rows = lax.axis_size("row")
    cols = lax.axis_size("col")
    devices = rows * cols
    row_at = lax.axis_index("row")
    col_at = lax.axis_index("col")
    half = col_at % HALVES
    mates = [(c, c ^ 1) for c in range(cols)]
    blocks = project.shape[0]
    groups = blocks // GROUP
    panels = charges.shape[0]
    strips = panels // LANES
    gs, fs, _ = kernel_spectrum.shape
    held = 16 * groups + strips + 16

    order = panel_order.reshape(strips, LANES)
    members = devices // HALVES
    sent, spots = pl.pallas_call(
        project_kernel,
        out_shape=(
            struct((members, held, LANES), jnp.bfloat16),
            struct((blocks, LANES), jnp.int32),
        ),
        in_specs=[pl.BlockSpec(memory_space=pltpu.HBM)] * 4,
        scratch_shapes=[
            pltpu.VMEM((strips, LANES), jnp.bfloat16),
            pltpu.VMEM((strips, LANES), jnp.int32),
            pltpu.VMEM(project.shape, jnp.bfloat16),
            pltpu.VMEM(patch_anchor.shape, jnp.int32),
            pltpu.VMEM((strips, LANES), jnp.float32),
            pltpu.VMEM((blocks, LANES), jnp.float32),
            pltpu.SemaphoreType.DMA((4,)),
        ],
        compiler_params=params(58),
        name="project",
    )(
        charges.reshape(strips, LANES),
        order,
        project,
        patch_anchor,
    )
    cores = [
        [r * cols + c for r in range(rows) for c in range(core, cols, HALVES)]
        for core in range(HALVES)
    ]

    def swap_members(array):
        return lax.all_to_all(
            array, axes, split_axis=0, concat_axis=0, axis_index_groups=cores, tiled=True
        )

    mine = swap_members(sent)
    theirs = lax.ppermute(mine, "col", mates)
    at = held - 16 + groups
    anchors = jnp.stack([part[:, at : at + 3] for part in (mine, theirs)])
    anchors = anchors.astype(jnp.int32)
    lane = 4 * (jnp.arange(blocks, dtype=jnp.int32) % GROUP)
    forth = ((anchors[:, :, 0] - lane) & (LANES - 1)).reshape(devices * blocks)
    back = ((lane - anchors[:, :, 0]) & (LANES - 1)).reshape(devices * blocks)
    group = anchors[:, :, 2] // QUAD
    inner = PAD + QUAD * anchors[:, :, 1] + anchors[:, :, 2] % QUAD
    side = jnp.arange(HALVES, dtype=jnp.int32)[:, None] ^ half
    col = jnp.arange(members, dtype=jnp.int32) % (cols // HALVES) * HALVES + side
    piece = (col * SLABS // cols * PIECE)[:, :, None]
    slab_at = (group * SLAB + inner - QUAD * piece).reshape(devices * blocks)
    cell_at = (group * CELLS + inner).reshape(devices * blocks)
    place = jnp.stack([half, row_at, col_at]).astype(jnp.int32)
    cas = jnp.asarray(CAS)

    smem = pl.BlockSpec(memory_space=pltpu.SMEM)

    def rows_at(start, count):
        return pl.BlockSpec((members, count, LANES), lambda *_: (0, start // count, 0))

    patch_rows = rows_at(0, 16 * groups)
    charge_rows = rows_at(16 * groups, strips)
    extra_rows = rows_at(16 * groups + strips, 16)
    steps = gs // LINES
    lines_type = struct((gs, fs, LANES), jnp.bfloat16)
    late = pl.BlockSpec((LINES, fs, LANES), lambda n: (jnp.maximum(n - 1, 0), 0, 0))
    own, other = pl.pallas_call(
        functools.partial(scatter_kernel, cols, gs, fs),
        grid=(1 + steps,),
        in_specs=[smem] * 3 + [patch_rows] * 2 + [extra_rows] * 2 + [whole(cas.shape)],
        out_specs=(late, late),
        out_shape=(lines_type, lines_type),
        scratch_shapes=[
            pltpu.VMEM((devices, 16 * groups, LANES), jnp.bfloat16),
            pltpu.VMEM((devices, 16, LANES), jnp.bfloat16),
            pltpu.VMEM((gs * STRIDE, LANES), jnp.float32),
        ]
        + [pltpu.VMEM(((G // QUAD + 1) * SLAB, LANES), jnp.float32)] * SLABS,
        compiler_params=params(50),
        name="scatter",
    )(place, forth, slab_at, mine, theirs, mine, theirs, cas)
    other = lax.ppermute(other, "col", mates)
    own, order = lax.optimization_barrier((own, order))
    inverse = pl.pallas_call(
        inverse_kernel,
        out_shape=struct((2 * strips, LANES), jnp.int32),
        compiler_params=params(32),
        name="inverse",
    )(order)

    other, inverse = lax.optimization_barrier((other, inverse))

    part = lambda shape: pl.BlockSpec((BATCH,) + shape, lambda n: (n, 0, 0))

    def weight_part(way):
        return pl.BlockSpec((BATCH // WAYS, fs, P_SIZE), lambda n: (n * WAYS + way, 0, 0))

    own, other = pl.pallas_call(
        spectrum_kernel,
        grid=(gs // BATCH,),
        in_specs=[
            smem,
            part((fs, LANES)),
            part((fs, LANES)),
            *[weight_part(n) for n in range(WAYS)],
            whole(cas.shape),
        ],
        out_specs=(part((fs, LANES)), part((fs, LANES))),
        out_shape=(lines_type, lines_type),
        compiler_params=params(40),
        name="spectrum",
    )(place, own, other, *[kernel_spectrum] * WAYS, cas)
    other = lax.ppermute(other, "col", mates)

    early = pl.BlockSpec((LINES, fs, LANES), lambda n: (n, 0, 0))
    values = pl.pallas_call(
        functools.partial(sample_kernel, cols),
        grid=(steps,),
        in_specs=[smem] * 3 + [extra_rows] * 2 + [early, early, whole(cas.shape)],
        out_specs=whole((devices, 16 * groups, LANES)),
        out_shape=struct((devices, 16 * groups, LANES), jnp.bfloat16),
        scratch_shapes=[
            pltpu.VMEM((devices, 16, LANES), jnp.bfloat16),
            pltpu.VMEM((G, gs), jnp.bfloat16),
            pltpu.VMEM((G, 2 * fs), jnp.bfloat16),
            pltpu.VMEM((gs * STRIDE, LANES), jnp.float32),
            pltpu.VMEM(((G // QUAD + 1) * CELLS, LANES), jnp.float32),
        ],
        compiler_params=params(46),
        name="sample",
    )(place, back, cell_at, mine, theirs, own, other, cas)
    values = values.reshape(HALVES, members, 16 * groups, LANES)
    received = lax.ppermute(values[1], "col", mates).astype(jnp.float32)
    values = (values[0].astype(jnp.float32) + received).astype(jnp.bfloat16)
    values, my_charges, their_charges = lax.optimization_barrier((values, mine, theirs))
    values = swap_members(values)

    source = near_pairs[1]
    source_row = source // blocks // cols
    source_col = source // blocks % cols
    wanted = (source_col % HALVES ^ half) * members + source_row * (cols // HALVES)
    wanted = (wanted + source_col // HALVES) * blocks + source % blocks
    target = near_pairs[0] - (row_at * cols + col_at) * blocks
    pairs = near_blocks.shape[0]
    near = pl.pallas_call(
        near_kernel,
        grid=(pairs // blocks,),
        in_specs=[
            smem,
            pl.BlockSpec((blocks, BLK * BLK), lambda n: (n, 0)),
            pl.BlockSpec((1, blocks), lambda n: (0, n)),
            charge_rows,
            charge_rows,
        ],
        out_specs=whole((blocks, LANES)),
        out_shape=struct((blocks, LANES), jnp.float32),
        scratch_shapes=[
            pltpu.VMEM((devices * blocks, LANES), jnp.float32),
            pltpu.VMEM((blocks, LANES), jnp.float32),
        ],
        compiler_params=params(40),
        name="near",
    )(wanted, near_blocks, target.reshape(1, pairs), my_charges, their_charges)

    result = pl.pallas_call(
        finish_kernel,
        out_shape=struct((strips, LANES), jnp.float32),
        scratch_shapes=[pltpu.VMEM((blocks, LANES), jnp.float32)],
        compiler_params=params(32),
        name="finish",
    )(values, interpolate, near, inverse, spots)
    return result.reshape(panels)


def solution(mesh):
    placed = (
        P(("row", "col")),
        P(("row", "col")),
        P(None, ("row", "col")),
        P(("row", "col"), None),
        P(("row", "col"), None),
        P("row", "col", None),
        P(None, ("row", "col")),
        P(("row", "col"), None),
    )
    return jax.shard_map(
        body, mesh=mesh, in_specs=placed, out_specs=P(("row", "col")), check_vma=False
    )
```

```python
import functools

import jax
import jax.numpy as jnp
import ml_dtypes
import numpy as np
from jax import lax
from jax.experimental import pallas as pl
from jax.experimental.pallas import tpu as pltpu
from jax.sharding import PartitionSpec as P

G = 256
P_SIZE = 512
BLK = 64
PTS = 64
LANES = 128
GROUP = LANES // 4
HALVES = G // LANES
SLABS = 4
PIECE = G // SLABS
QUAD = 4
PAD = 8
SLAB = PAD + QUAD * PIECE + 16
CELLS = PAD + QUAD * G + 16
STRIDE = G + 1
BATCH = 16
WAYS = 4
LINES = 16
UNROLL_PLANES = 8
MB = 1 << 20
NT = (((1,), (1,)), ((), ()))


def cas_table():
    index = np.arange(P_SIZE, dtype=np.int64)
    phase = (index[:, None] * index[None, :] % P_SIZE).astype(np.float64) * (2.0 * np.pi / P_SIZE)
    return ((np.cos(phase) + np.sin(phase)) / np.sqrt(P_SIZE)).astype(ml_dtypes.bfloat16)


CAS = cas_table()


def dot(a, b):
    return jnp.dot(a, b, preferred_element_type=jnp.float32)


def dot_nt(a, b):
    return lax.dot_general(a, b, NT, preferred_element_type=jnp.float32)


def iota(shape, dim):
    return lax.broadcasted_iota(jnp.int32, shape, dim)


def split(value):
    high = value.astype(jnp.bfloat16)
    return high, (value - high.astype(jnp.float32)).astype(jnp.bfloat16)


def lane_gather(table, index):
    return jnp.take_along_axis(table, index, axis=1, mode="promise_in_bounds")


def block_sums(mats, vecs):
    rows = vecs.shape[0]
    pair = jnp.concatenate([vecs, vecs], axis=1)
    total = jnp.zeros((2 * rows, LANES), jnp.float32)
    for t in range(mats.shape[1] // 256):
        high, low = split(mats[:, 256 * t : 256 * t + 256].astype(jnp.float32) * pair)
        owner = iota((256, LANES), 0) // BLK + 4 * t
        table = (owner == iota((256, LANES), 1) % BLK).astype(jnp.bfloat16)
        total = total + dot(jnp.concatenate([high, low], axis=0), table)
    return total[:rows] + total[rows:]


def patch_rows():
    row = iota((16, LANES), 0)
    return [
        (iota((16, LANES), 1) % PTS == 16 * i + row).astype(jnp.float32).astype(jnp.bfloat16)
        for i in range(4)
    ]


def patch_places(spots):
    blocks = spots.shape[0]
    spots = jnp.concatenate([spots] * (4 * blocks // LANES), axis=1)
    lane = iota(spots.shape, 1)
    lanes = [(lane == 4 * spots + i).astype(jnp.float32).astype(jnp.bfloat16) for i in range(4)]
    return patch_rows(), lanes


def block_spots(first):
    blocks = first.shape[1]
    shape = (blocks, blocks)
    crossing = ((first & (LANES - 1)) > LANES - 4).astype(jnp.float32)
    crossing = jnp.broadcast_to(crossing, (8, blocks))
    earlier = (iota(shape, 0) < iota(shape, 1)).astype(jnp.float32).astype(jnp.bfloat16)
    ahead = dot(crossing.astype(jnp.bfloat16), earlier)
    total = jnp.sum(crossing, axis=1, keepdims=True)
    block = iota((8, blocks), 1).astype(jnp.float32)
    spot = jnp.where(crossing > 0.0, ahead, total + block - ahead)
    spread = jnp.broadcast_to(spot[:1], (LANES, blocks)).astype(jnp.bfloat16)
    unit = (iota(shape, 0) == iota(shape, 1)).astype(jnp.float32).astype(jnp.bfloat16)
    return dot_nt(unit, spread).astype(jnp.int32)


def project_kernel(
    charges_in,
    order_in,
    project_in,
    anchors_in,
    sent_out,
    spot_out,
    charges,
    order,
    project,
    anchors,
    table,
    doubled,
    sems,
):
    blocks = spot_out.shape[0]
    groups = blocks // GROUP
    pairs = ((charges_in, charges), (order_in, order), (project_in, project), (anchors_in, anchors))
    copies = [pltpu.make_async_copy(a, b, sems.at[n]) for n, (a, b) in enumerate(pairs)]
    for copy in copies:
        copy.start()
    copies[0].wait()
    copies[1].wait()
    table[...] = charges[...].astype(jnp.float32)
    strips = table.shape[0]
    upper = order[...] // LANES
    lower = order[...] % LANES

    def step(u, acc):
        row = jnp.broadcast_to(table[pl.ds(u, 1), :], lower.shape)
        return jnp.where(upper == u, lane_gather(row, lower), acc)

    slots = lax.fori_loop(0, strips, step, jnp.zeros(lower.shape, jnp.float32), unroll=True)
    swapped = pltpu.roll(slots, BLK, 1)
    left = iota(slots.shape, 1) < BLK
    doubled[pl.ds(0, strips, stride=2), :] = jnp.where(left, slots, swapped)
    doubled[pl.ds(1, strips, stride=2), :] = jnp.where(left, swapped, slots)
    twice = doubled[...]
    copies[2].wait()
    copies[3].wait()
    patch = block_sums(project, twice)
    patch = jnp.where(iota(patch.shape, 1) < PTS, patch, 0.0).astype(jnp.bfloat16)
    spots = block_spots(anchors[:1, :])
    spot_out[...] = spots
    rows, lanes = patch_places(spots)
    moved = (iota(spots.shape, 1) == spots).astype(jnp.float32).astype(jnp.bfloat16)
    corner = anchors[...].astype(jnp.float32).astype(jnp.bfloat16)
    corner = dot(jnp.concatenate([corner] * 3, axis=0)[:8], moved)
    cells = (iota((8, 4 * blocks), 1) % 4).astype(jnp.float32)
    start = jnp.broadcast_to(anchors[:1, :].astype(jnp.float32), (8, blocks)).astype(jnp.bfloat16)
    for i in range(4):
        cells = cells + dot(start, lanes[i])
    spread = jnp.zeros((16, 4 * blocks), jnp.float32)
    for i in range(4):
        spread = spread + dot(dot_nt(rows[i], patch).astype(jnp.bfloat16), lanes[i])
    tiles = [slice(LANES * t, LANES * t + LANES) for t in range(groups)]
    sent = [spread[:, tile].astype(jnp.bfloat16) for tile in tiles]
    sent.append(slots.astype(jnp.bfloat16))
    extra = [cells[:1, tile] for tile in tiles] + [corner[:3]]
    extra.append(jnp.zeros((13 - groups, LANES), jnp.float32))
    sent.append(jnp.concatenate(extra, axis=0).astype(jnp.bfloat16))
    sent = jnp.concatenate(sent, axis=0)
    for n in range(sent_out.shape[0]):
        sent_out[n] = sent


def inverse_kernel(order, out):
    rows = order.shape[0]

    def step(r, acc):
        here = order[pl.ds(r, 1), :]
        upper = iota((rows, LANES), 0) == here // LANES
        lower = iota((LANES, LANES), 0) == here % LANES
        values = jnp.concatenate(
            [
                jnp.where(upper, r.astype(jnp.float32), 0.0),
                jnp.where(upper, iota((rows, LANES), 1).astype(jnp.float32), 0.0),
            ],
            axis=0,
        )
        return acc + dot_nt(
            values.astype(jnp.bfloat16), lower.astype(jnp.float32).astype(jnp.bfloat16)
        )

    out[...] = lax.fori_loop(
        0, rows, step, jnp.zeros((2 * rows, LANES), jnp.float32), unroll=4
    ).astype(jnp.int32)


def near_kernel(source, near_blocks, target, mine, theirs, spots, out, lanes_out, table, picked):
    step = pl.program_id(0)
    pairs = picked.shape[0]
    blocks = out.shape[0]

    @pl.when(step == 0)
    def _():
        members, strips, _ = mine.shape
        left = iota((strips, LANES), 1) < BLK
        for side, part in enumerate((mine, theirs)):
            for n in range(members):
                at = (side * members + n) * blocks
                slots = part[n].astype(jnp.float32)
                swapped = pltpu.roll(slots, BLK, 1)
                table[pl.ds(at, strips, stride=2), :] = jnp.where(left, slots, swapped)
                table[pl.ds(at + 1, strips, stride=2), :] = jnp.where(left, swapped, slots)
        out[...] = jnp.zeros_like(out)
        for i, lanes in enumerate(patch_places(spots[...])[1]):
            lanes_out[i] = lanes

    def pick(p, carry):
        picked[pl.ds(p, 1), :] = table[pl.ds(source[step * pairs + p], 1), :]
        return carry

    lax.fori_loop(0, pairs, pick, 0, unroll=8)
    terms = block_sums(near_blocks, picked[...])
    owner = (iota((blocks, pairs), 0) == target[...]).astype(jnp.float32).astype(jnp.bfloat16)
    high, low = split(terms)
    out[...] += dot(owner, high) + dot(owner, low)


def table_rows(cas, numbers, count):
    parts = [cas[pl.ds(pl.multiple_of(n * count, 16), count), :G] for n in numbers]
    return jnp.concatenate(parts, axis=0) if len(parts) > 1 else parts[0]


def turned(rows):
    unit = (iota((G, G), 0) == iota((G, G), 1)).astype(jnp.float32).astype(jnp.bfloat16)
    return dot_nt(unit, rows).astype(jnp.bfloat16)


def tile_loop(half, rows, cols, groups, crosses, body):
    per_slab = cols // SLABS
    low = jnp.maximum(half * (rows // HALVES) - 1, 0)
    high = (half + 1) * (rows // HALVES)
    per_row = per_slab * groups

    def place(row, col):
        side = (col % HALVES) ^ half
        return side * (rows * cols // HALVES) + row * (cols // HALVES) + col // HALVES

    def step(n, carry):
        row = low + n // per_row
        left = n % per_row
        t = left % groups
        devices = [place(row, s * per_slab + left // groups) for s in range(SLABS)]
        found = [crosses((d * groups + t) * GROUP) for d in devices]
        inside = row >= half * (rows // HALVES)
        pl.when(functools.reduce(jnp.logical_or, found, inside))(lambda: body(devices, t))
        return carry

    lax.fori_loop(0, (high - low) * per_row, step, 0)


def lanes_inside(extra, d, t, half):
    extra = extra[d].astype(jnp.float32)
    picked = jnp.where(iota(extra.shape, 0) == t, extra, 0.0)
    cells = jnp.sum(picked, axis=0, keepdims=True) - (half * LANES).astype(jnp.float32)
    return jnp.broadcast_to((cells >= 0.0) & (cells < LANES), (16, LANES))


def scatter_kernel(
    cols,
    gs,
    fs,
    place,
    shift,
    start,
    mine,
    theirs,
    my_extra,
    their_extra,
    cas,
    own_out,
    other_out,
    patches,
    extra,
    lines,
    *slabs,
):
    half = place[0]
    step = pl.program_id(0)
    devices, held, _ = patches.shape
    groups = held // 16
    blocks = groups * GROUP
    owner = (iota((16, LANES), 1) // 4).astype(jnp.float32).astype(jnp.bfloat16)
    plane = iota((16, LANES), 0) % QUAD

    @pl.when(step == 0)
    def _():
        def clear(n, carry):
            for slab in slabs:
                at = pl.multiple_of(n * SLAB + PAD, 8)
                slab[pl.ds(at, SLAB - PAD), :] = jnp.zeros((SLAB - PAD, LANES), jnp.float32)
            return carry

        lax.fori_loop(0, G // QUAD, clear, 0)
        for side, part in enumerate(((mine, my_extra), (theirs, their_extra))):
            at = slice(side * (devices // 2), (side + 1) * (devices // 2))
            patches[at] = part[0][...]
            extra[at] = part[1][...]

        def tile(numbers, t):
            values = []
            for d in numbers:
                part = patches[d, pl.ds(pl.multiple_of(16 * t, 16), 16), :].astype(jnp.float32)
                part = jnp.where(lanes_inside(extra, d, t, half), part, 0.0)
                values.append(part.astype(jnp.bfloat16))

            for k in range(GROUP):
                sums = []
                for s in range(SLABS):
                    b = numbers[s] * blocks + t * GROUP + k
                    at = start[b]
                    moved = jnp.where(owner == k, values[s], jnp.zeros_like(values[s]))
                    moved = pltpu.roll(moved, shift[b], 1).astype(jnp.float32)
                    here = plane < QUAD - (at & (QUAD - 1))
                    near = slabs[s][pl.ds(at, 16), :] + jnp.where(here, moved, 0.0)
                    at_next = at + (SLAB - QUAD)
                    far = slabs[s][pl.ds(at_next, 16), :] + jnp.where(here, 0.0, moved)
                    sums.append((at, near, at_next, far))
                for s, (at, near, at_next, far) in enumerate(sums):
                    slabs[s][pl.ds(at, 16), :] = near
                    slabs[s][pl.ds(at_next, 16), :] = far

        def crosses(b):
            return shift[b] > LANES - 4

        tile_loop(half, devices // cols, cols, groups, crosses, tile)

        table = table_rows(cas, [place[1]], gs)

        def planes(n, carry):
            base = pl.multiple_of(n * SLAB, 8)
            sheets = []
            for q in range(QUAD):
                parts = []
                for s in range(SLABS):
                    part = slabs[s][pl.ds(base + (PAD + q), PIECE, stride=QUAD), :]
                    if s > 0:
                        at = base + (PAD + QUAD * PIECE + q)
                        over = slabs[s - 1][pl.ds(at, 4, stride=QUAD), :]
                        over = jnp.concatenate([over, jnp.zeros_like(over)], axis=0)
                        part = jnp.concatenate([part[:8] + over, part[8:]], axis=0)
                    parts.append(part.astype(jnp.bfloat16))
                sheets.append(jnp.concatenate(parts, axis=0))
            field = dot(table, jnp.concatenate(sheets, axis=1))
            for q in range(QUAD):
                part = field[:, LANES * q : LANES * q + LANES]
                lines[pl.ds(n * QUAD + q, gs, stride=STRIDE), :] = part
            return carry

        lax.fori_loop(0, G // QUAD, planes, 0, unroll=UNROLL_PLANES)

    @pl.when(step > 0)
    def _():
        third = table_rows(cas, [place[2], place[2] ^ 1], fs)
        for g in range(0, LINES, 2):
            pair = []
            for n in (g, g + 1):
                at = ((step - 1) * LINES + n) * STRIDE
                pair.append(lines[pl.ds(at, G), :].astype(jnp.bfloat16))
            field = dot(third, jnp.concatenate(pair, axis=1)).astype(jnp.bfloat16)
            for n in range(2):
                own_out[g + n] = field[:fs, LANES * n : LANES * n + LANES]
                other_out[g + n] = field[fs:, LANES * n : LANES * n + LANES]


def spectrum_kernel(place, own, other, *refs):
    weights, (cas, own_out, other_out) = refs[:WAYS], refs[WAYS:]
    tiles = [pl.ds(pl.multiple_of(h * LANES, LANES), LANES) for h in (place[0], 1 - place[0])]
    first = jnp.concatenate([cas[tile, :] for tile in tiles], axis=0)
    first_back = jnp.concatenate([cas[:, tile] for tile in tiles], axis=1)
    step, freqs, _ = weights[0].shape
    rows = step * freqs
    for n in range(WAYS):
        part = slice(n * step, (n + 1) * step)
        line = jnp.concatenate(
            [own[part].reshape(rows, LANES), other[part].reshape(rows, LANES)], axis=1
        )
        s = dot(line, first) * weights[n][...].reshape(rows, P_SIZE)
        line = dot(s.astype(jnp.bfloat16), first_back).astype(jnp.bfloat16)
        own_out[part] = line[:, :LANES].reshape(step, freqs, LANES)
        other_out[part] = line[:, LANES:].reshape(step, freqs, LANES)


def sample_kernel(
    cols,
    place,
    shift,
    start,
    my_extra,
    their_extra,
    own,
    other,
    cas,
    out,
    extra,
    second,
    third,
    lines,
    cells,
):
    half = place[0]
    step = pl.program_id(0)
    devices, held, _ = out.shape
    groups = held // 16
    blocks = groups * GROUP
    gs = second.shape[1]
    owner = (iota((16, LANES), 1) // 4).astype(jnp.float32).astype(jnp.bfloat16)
    plane = iota((16, LANES), 0) % QUAD

    @pl.when(step == 0)
    def _():
        for side, part in enumerate((my_extra, their_extra)):
            extra[side * (devices // 2) : (side + 1) * (devices // 2)] = part[...]
        second[...] = turned(table_rows(cas, [place[1]], gs))
        third[...] = turned(table_rows(cas, [place[2], place[2] ^ 1], own.shape[1]))

    for g in range(0, LINES, 2):
        pair = [jnp.concatenate([own[n], other[n]], axis=0) for n in (g, g + 1)]
        field = dot(third[...], jnp.concatenate(pair, axis=1))
        for n in range(2):
            at = (step * LINES + g + n) * STRIDE
            lines[pl.ds(at, G), :] = field[:, LANES * n : LANES * n + LANES]

    @pl.when(step == pl.num_programs(0) - 1)
    def _():
        def planes(n, carry):
            sheets = [
                lines[pl.ds(n * QUAD + q, gs, stride=STRIDE), :].astype(jnp.bfloat16)
                for q in range(QUAD)
            ]
            field = dot(second[...], jnp.concatenate(sheets, axis=1))
            base = pl.multiple_of(n * CELLS, 8)
            for q in range(QUAD):
                part = field[:, LANES * q : LANES * q + LANES]
                cells[pl.ds(base + (PAD + q), G, stride=QUAD), :] = part
            return carry

        lax.fori_loop(0, G // QUAD, planes, 0, unroll=UNROLL_PLANES)
        out[...] = jnp.zeros_like(out)

        def tile(numbers, t):
            sums = [jnp.zeros((16, LANES), jnp.bfloat16)] * SLABS
            for k in range(GROUP):
                for s in range(SLABS):
                    b = numbers[s] * blocks + t * GROUP + k
                    at = start[b]
                    here = plane < QUAD - (at & (QUAD - 1))
                    near = cells[pl.ds(at, 16), :]
                    far = cells[pl.ds(at + (CELLS - QUAD), 16), :]
                    moved = jnp.where(here, near, far).astype(jnp.bfloat16)
                    sums[s] = jnp.where(owner == k, pltpu.roll(moved, shift[b], 1), sums[s])
            for s, d in enumerate(numbers):
                inside = lanes_inside(extra, d, t, half)
                out[d, pl.ds(pl.multiple_of(16 * t, 16), 16), :] = jnp.where(
                    inside, sums[s].astype(jnp.float32), 0.0
                ).astype(jnp.bfloat16)

        def crosses(b):
            return (shift[b] > 0) & (shift[b] < 4)

        tile_loop(half, devices // cols, cols, groups, crosses, tile)


def finish_kernel(values, interpolate, near, inverse, lanes, out, total):
    blocks = near.shape[0]
    groups = values.shape[1] // 16
    rows = patch_rows()
    summed = values[0].astype(jnp.float32)
    for d in range(1, values.shape[0]):
        summed = summed + values[d].astype(jnp.float32)
    spread = jnp.concatenate([summed[16 * t : 16 * t + 16] for t in range(groups)], axis=1)
    parts = jnp.concatenate(split(spread), axis=0)
    patch = jnp.zeros((blocks, LANES), jnp.float32)
    for i in range(4):
        column = dot_nt(lanes[i], parts).astype(jnp.bfloat16)
        patch = patch + dot(column, jnp.concatenate([rows[i], rows[i]], axis=0))
    total[...] = block_sums(interpolate, patch) + near[...]
    count = out.shape[0]
    even = total[pl.ds(0, count, stride=2), :]
    odd = total[pl.ds(1, count, stride=2), :]
    total[:count] = jnp.where(iota(even.shape, 1) < BLK, even, odd)
    upper = inverse[:count]
    lower = inverse[count:]

    def step(u, acc):
        row = jnp.broadcast_to(total[pl.ds(u, 1), :], lower.shape)
        return jnp.where(upper == u, lane_gather(row, lower), acc)

    out[...] = lax.fori_loop(0, count, step, jnp.zeros(out.shape, jnp.float32), unroll=True)


def struct(shape, dtype):
    return jax.ShapeDtypeStruct(shape, dtype)


def whole(shape):
    return pl.BlockSpec(shape, lambda *_: (0,) * len(shape))


def params(mib):
    return pltpu.CompilerParams(vmem_limit_bytes=mib * MB)


def body(
    charges,
    panel_order,
    patch_anchor,
    project,
    interpolate,
    kernel_spectrum,
    near_pairs,
    near_blocks,
):
    axes = ("row", "col")
    rows = lax.axis_size("row")
    cols = lax.axis_size("col")
    devices = rows * cols
    row_at = lax.axis_index("row")
    col_at = lax.axis_index("col")
    half = col_at % HALVES
    mates = [(c, c ^ 1) for c in range(cols)]
    blocks = project.shape[0]
    groups = blocks // GROUP
    panels = charges.shape[0]
    strips = panels // LANES
    gs, fs, _ = kernel_spectrum.shape
    held = 16 * groups + strips + 16

    order = panel_order.reshape(strips, LANES)
    members = devices // HALVES
    sent, spots = pl.pallas_call(
        project_kernel,
        out_shape=(
            struct((members, held, LANES), jnp.bfloat16),
            struct((blocks, LANES), jnp.int32),
        ),
        in_specs=[pl.BlockSpec(memory_space=pltpu.HBM)] * 4,
        scratch_shapes=[
            pltpu.VMEM((strips, LANES), jnp.bfloat16),
            pltpu.VMEM((strips, LANES), jnp.int32),
            pltpu.VMEM(project.shape, jnp.bfloat16),
            pltpu.VMEM(patch_anchor.shape, jnp.int32),
            pltpu.VMEM((strips, LANES), jnp.float32),
            pltpu.VMEM((blocks, LANES), jnp.float32),
            pltpu.SemaphoreType.DMA((4,)),
        ],
        compiler_params=params(58),
        name="project",
    )(
        charges.reshape(strips, LANES),
        order,
        project,
        patch_anchor,
    )
    cores = [
        [r * cols + c for r in range(rows) for c in range(core, cols, HALVES)]
        for core in range(HALVES)
    ]

    def swap_members(array):
        return lax.all_to_all(
            array, axes, split_axis=0, concat_axis=0, axis_index_groups=cores, tiled=True
        )

    mine = swap_members(sent)
    theirs = lax.ppermute(mine, "col", mates)
    at = held - 16 + groups
    anchors = jnp.stack([part[:, at : at + 3] for part in (mine, theirs)])
    anchors = anchors.astype(jnp.int32)
    lane = 4 * (jnp.arange(blocks, dtype=jnp.int32) % GROUP)
    forth = ((anchors[:, :, 0] - lane) & (LANES - 1)).reshape(devices * blocks)
    back = ((lane - anchors[:, :, 0]) & (LANES - 1)).reshape(devices * blocks)
    group = anchors[:, :, 2] // QUAD
    inner = PAD + QUAD * anchors[:, :, 1] + anchors[:, :, 2] % QUAD
    side = jnp.arange(HALVES, dtype=jnp.int32)[:, None] ^ half
    col = jnp.arange(members, dtype=jnp.int32) % (cols // HALVES) * HALVES + side
    piece = (col * SLABS // cols * PIECE)[:, :, None]
    slab_at = (group * SLAB + inner - QUAD * piece).reshape(devices * blocks)
    cell_at = (group * CELLS + inner).reshape(devices * blocks)
    place = jnp.stack([half, row_at, col_at]).astype(jnp.int32)
    cas = jnp.asarray(CAS)

    smem = pl.BlockSpec(memory_space=pltpu.SMEM)

    def rows_at(start, count):
        return pl.BlockSpec((members, count, LANES), lambda *_: (0, start // count, 0))

    patch_rows = rows_at(0, 16 * groups)
    charge_rows = rows_at(16 * groups, strips)
    extra_rows = rows_at(16 * groups + strips, 16)
    steps = gs // LINES
    lines_type = struct((gs, fs, LANES), jnp.bfloat16)
    late = pl.BlockSpec((LINES, fs, LANES), lambda n: (jnp.maximum(n - 1, 0), 0, 0))
    own, other = pl.pallas_call(
        functools.partial(scatter_kernel, cols, gs, fs),
        grid=(1 + steps,),
        in_specs=[smem] * 3 + [patch_rows] * 2 + [extra_rows] * 2 + [whole(cas.shape)],
        out_specs=(late, late),
        out_shape=(lines_type, lines_type),
        scratch_shapes=[
            pltpu.VMEM((devices, 16 * groups, LANES), jnp.bfloat16),
            pltpu.VMEM((devices, 16, LANES), jnp.bfloat16),
            pltpu.VMEM((gs * STRIDE, LANES), jnp.float32),
        ]
        + [pltpu.VMEM(((G // QUAD + 1) * SLAB, LANES), jnp.float32)] * SLABS,
        compiler_params=params(50),
        name="scatter",
    )(place, forth, slab_at, mine, theirs, mine, theirs, cas)
    other = lax.ppermute(other, "col", mates)
    own, order = lax.optimization_barrier((own, order))
    inverse = pl.pallas_call(
        inverse_kernel,
        out_shape=struct((2 * strips, LANES), jnp.int32),
        compiler_params=params(32),
        name="inverse",
    )(order)

    other, inverse = lax.optimization_barrier((other, inverse))

    part = lambda shape: pl.BlockSpec((BATCH,) + shape, lambda n: (n, 0, 0))

    def weight_part(way):
        return pl.BlockSpec((BATCH // WAYS, fs, P_SIZE), lambda n: (n * WAYS + way, 0, 0))

    own, other = pl.pallas_call(
        spectrum_kernel,
        grid=(gs // BATCH,),
        in_specs=[
            smem,
            part((fs, LANES)),
            part((fs, LANES)),
            *[weight_part(n) for n in range(WAYS)],
            whole(cas.shape),
        ],
        out_specs=(part((fs, LANES)), part((fs, LANES))),
        out_shape=(lines_type, lines_type),
        compiler_params=params(40),
        name="spectrum",
    )(place, own, other, *[kernel_spectrum] * WAYS, cas)
    other = lax.ppermute(other, "col", mates)

    early = pl.BlockSpec((LINES, fs, LANES), lambda n: (n, 0, 0))
    values = pl.pallas_call(
        functools.partial(sample_kernel, cols),
        grid=(steps,),
        in_specs=[smem] * 3 + [extra_rows] * 2 + [early, early, whole(cas.shape)],
        out_specs=whole((devices, 16 * groups, LANES)),
        out_shape=struct((devices, 16 * groups, LANES), jnp.bfloat16),
        scratch_shapes=[
            pltpu.VMEM((devices, 16, LANES), jnp.bfloat16),
            pltpu.VMEM((G, gs), jnp.bfloat16),
            pltpu.VMEM((G, 2 * fs), jnp.bfloat16),
            pltpu.VMEM((gs * STRIDE, LANES), jnp.float32),
            pltpu.VMEM(((G // QUAD + 1) * CELLS, LANES), jnp.float32),
        ],
        compiler_params=params(46),
        name="sample",
    )(place, back, cell_at, mine, theirs, own, other, cas)
    values = values.reshape(HALVES, members, 16 * groups, LANES)
    received = lax.ppermute(values[1], "col", mates).astype(jnp.float32)
    values = (values[0].astype(jnp.float32) + received).astype(jnp.bfloat16)
    values, my_charges, their_charges = lax.optimization_barrier((values, mine, theirs))
    values = swap_members(values)

    source = near_pairs[1]
    source_row = source // blocks // cols
    source_col = source // blocks % cols
    wanted = (source_col % HALVES ^ half) * members + source_row * (cols // HALVES)
    wanted = (wanted + source_col // HALVES) * blocks + source % blocks
    target = near_pairs[0] - (row_at * cols + col_at) * blocks
    pairs = near_blocks.shape[0]
    near, lanes = pl.pallas_call(
        near_kernel,
        grid=(pairs // blocks,),
        in_specs=[
            smem,
            pl.BlockSpec((blocks, BLK * BLK), lambda n: (n, 0)),
            pl.BlockSpec((1, blocks), lambda n: (0, n)),
            charge_rows,
            charge_rows,
            whole((blocks, LANES)),
        ],
        out_specs=(whole((blocks, LANES)), whole((4, blocks, 4 * blocks))),
        out_shape=(
            struct((blocks, LANES), jnp.float32),
            struct((4, blocks, 4 * blocks), jnp.bfloat16),
        ),
        scratch_shapes=[
            pltpu.VMEM((devices * blocks, LANES), jnp.float32),
            pltpu.VMEM((blocks, LANES), jnp.float32),
        ],
        compiler_params=params(40),
        name="near",
    )(wanted, near_blocks, target.reshape(1, pairs), my_charges, their_charges, spots)

    result = pl.pallas_call(
        finish_kernel,
        out_shape=struct((strips, LANES), jnp.float32),
        scratch_shapes=[pltpu.VMEM((blocks, LANES), jnp.float32)],
        compiler_params=params(32),
        name="finish",
    )(values, interpolate, near, inverse, lanes)
    return result.reshape(panels)


def solution(mesh):
    placed = (
        P(("row", "col")),
        P(("row", "col")),
        P(None, ("row", "col")),
        P(("row", "col"), None),
        P(("row", "col"), None),
        P("row", "col", None),
        P(None, ("row", "col")),
        P(("row", "col"), None),
    )
    return jax.shard_map(
        body, mesh=mesh, in_specs=placed, out_specs=P(("row", "col")), check_vma=False
    )
```

```python
import functools

import jax
import jax.numpy as jnp
import ml_dtypes
import numpy as np
from jax import lax
from jax.experimental import pallas as pl
from jax.experimental.pallas import tpu as pltpu
from jax.sharding import PartitionSpec as P

G = 256
P_SIZE = 512
BLK = 64
PTS = 64
LANES = 128
GROUP = LANES // 4
HALVES = G // LANES
SLABS = 4
PIECE = G // SLABS
QUAD = 4
PAD = 8
SLAB = PAD + QUAD * PIECE + 16
CELLS = PAD + QUAD * G + 16
STRIDE = G + 1
BATCH = 16
WAYS = 4
LINES = 32
UNROLL_PLANES = 32
MB = 1 << 20
NT = (((1,), (1,)), ((), ()))


def cas_table():
    index = np.arange(P_SIZE, dtype=np.int64)
    phase = (index[:, None] * index[None, :] % P_SIZE).astype(np.float64) * (2.0 * np.pi / P_SIZE)
    return ((np.cos(phase) + np.sin(phase)) / np.sqrt(P_SIZE)).astype(ml_dtypes.bfloat16)


CAS = cas_table()


def dot(a, b):
    return jnp.dot(a, b, preferred_element_type=jnp.float32)


def dot_nt(a, b):
    return lax.dot_general(a, b, NT, preferred_element_type=jnp.float32)


def iota(shape, dim):
    return lax.broadcasted_iota(jnp.int32, shape, dim)


def split(value):
    high = value.astype(jnp.bfloat16)
    return high, (value - high.astype(jnp.float32)).astype(jnp.bfloat16)


def lane_gather(table, index):
    return jnp.take_along_axis(table, index, axis=1, mode="promise_in_bounds")


def block_sums(mats, vecs):
    rows = vecs.shape[0]
    pair = jnp.concatenate([vecs, vecs], axis=1)
    total = jnp.zeros((2 * rows, LANES), jnp.float32)
    for t in range(mats.shape[1] // 256):
        high, low = split(mats[:, 256 * t : 256 * t + 256].astype(jnp.float32) * pair)
        owner = iota((256, LANES), 0) // BLK + 4 * t
        table = (owner == iota((256, LANES), 1) % BLK).astype(jnp.bfloat16)
        total = total + dot(jnp.concatenate([high, low], axis=0), table)
    return total[:rows] + total[rows:]


def patch_rows():
    row = iota((16, LANES), 0)
    return [
        (iota((16, LANES), 1) % PTS == 16 * i + row).astype(jnp.float32).astype(jnp.bfloat16)
        for i in range(4)
    ]


def patch_places(spots):
    blocks = spots.shape[0]
    spots = jnp.concatenate([spots] * (4 * blocks // LANES), axis=1)
    lane = iota(spots.shape, 1)
    lanes = [(lane == 4 * spots + i).astype(jnp.float32).astype(jnp.bfloat16) for i in range(4)]
    return patch_rows(), lanes


def block_spots(first):
    blocks = first.shape[1]
    shape = (blocks, blocks)
    crossing = ((first & (LANES - 1)) > LANES - 4).astype(jnp.float32)
    crossing = jnp.broadcast_to(crossing, (8, blocks))
    earlier = (iota(shape, 0) < iota(shape, 1)).astype(jnp.float32).astype(jnp.bfloat16)
    ahead = dot(crossing.astype(jnp.bfloat16), earlier)
    total = jnp.sum(crossing, axis=1, keepdims=True)
    block = iota((8, blocks), 1).astype(jnp.float32)
    spot = jnp.where(crossing > 0.0, ahead, total + block - ahead)
    spread = jnp.broadcast_to(spot[:1], (LANES, blocks)).astype(jnp.bfloat16)
    unit = (iota(shape, 0) == iota(shape, 1)).astype(jnp.float32).astype(jnp.bfloat16)
    return dot_nt(unit, spread).astype(jnp.int32)


def project_kernel(
    charges_in,
    order_in,
    project_in,
    anchors_in,
    sent_out,
    spot_out,
    charges,
    order,
    project,
    anchors,
    table,
    doubled,
    sems,
):
    blocks = spot_out.shape[0]
    groups = blocks // GROUP
    pairs = ((charges_in, charges), (order_in, order), (project_in, project), (anchors_in, anchors))
    copies = [pltpu.make_async_copy(a, b, sems.at[n]) for n, (a, b) in enumerate(pairs)]
    for copy in copies:
        copy.start()
    copies[0].wait()
    copies[1].wait()
    table[...] = charges[...].astype(jnp.float32)
    strips = table.shape[0]
    upper = order[...] // LANES
    lower = order[...] % LANES

    def step(u, acc):
        row = jnp.broadcast_to(table[pl.ds(u, 1), :], lower.shape)
        return jnp.where(upper == u, lane_gather(row, lower), acc)

    slots = lax.fori_loop(0, strips, step, jnp.zeros(lower.shape, jnp.float32), unroll=True)
    swapped = pltpu.roll(slots, BLK, 1)
    left = iota(slots.shape, 1) < BLK
    doubled[pl.ds(0, strips, stride=2), :] = jnp.where(left, slots, swapped)
    doubled[pl.ds(1, strips, stride=2), :] = jnp.where(left, swapped, slots)
    twice = doubled[...]
    copies[2].wait()
    copies[3].wait()
    patch = block_sums(project, twice)
    patch = jnp.where(iota(patch.shape, 1) < PTS, patch, 0.0).astype(jnp.bfloat16)
    spots = block_spots(anchors[:1, :])
    spot_out[...] = spots
    rows, lanes = patch_places(spots)
    moved = (iota(spots.shape, 1) == spots).astype(jnp.float32).astype(jnp.bfloat16)
    corner = anchors[...].astype(jnp.float32).astype(jnp.bfloat16)
    corner = dot(jnp.concatenate([corner] * 3, axis=0)[:8], moved)
    cells = (iota((8, 4 * blocks), 1) % 4).astype(jnp.float32)
    start = jnp.broadcast_to(anchors[:1, :].astype(jnp.float32), (8, blocks)).astype(jnp.bfloat16)
    for i in range(4):
        cells = cells + dot(start, lanes[i])
    spread = jnp.zeros((16, 4 * blocks), jnp.float32)
    for i in range(4):
        spread = spread + dot(dot_nt(rows[i], patch).astype(jnp.bfloat16), lanes[i])
    tiles = [slice(LANES * t, LANES * t + LANES) for t in range(groups)]
    sent = [spread[:, tile].astype(jnp.bfloat16) for tile in tiles]
    sent.append(slots.astype(jnp.bfloat16))
    extra = [cells[:1, tile] for tile in tiles] + [corner[:3]]
    extra.append(jnp.zeros((13 - groups, LANES), jnp.float32))
    sent.append(jnp.concatenate(extra, axis=0).astype(jnp.bfloat16))
    sent = jnp.concatenate(sent, axis=0)
    for n in range(sent_out.shape[0]):
        sent_out[n] = sent


def inverse_kernel(order, out):
    rows = order.shape[0]

    def step(r, acc):
        here = order[pl.ds(r, 1), :]
        upper = iota((rows, LANES), 0) == here // LANES
        lower = iota((LANES, LANES), 0) == here % LANES
        values = jnp.concatenate(
            [
                jnp.where(upper, r.astype(jnp.float32), 0.0),
                jnp.where(upper, iota((rows, LANES), 1).astype(jnp.float32), 0.0),
            ],
            axis=0,
        )
        return acc + dot_nt(
            values.astype(jnp.bfloat16), lower.astype(jnp.float32).astype(jnp.bfloat16)
        )

    out[...] = lax.fori_loop(
        0, rows, step, jnp.zeros((2 * rows, LANES), jnp.float32), unroll=4
    ).astype(jnp.int32)


def near_kernel(source, near_blocks, target, mine, theirs, spots, out, lanes_out, table, picked):
    step = pl.program_id(0)
    pairs = picked.shape[0]
    blocks = out.shape[0]

    @pl.when(step == 0)
    def _():
        members, strips, _ = mine.shape
        left = iota((strips, LANES), 1) < BLK
        for side, part in enumerate((mine, theirs)):
            for n in range(members):
                at = (side * members + n) * blocks
                slots = part[n].astype(jnp.float32)
                swapped = pltpu.roll(slots, BLK, 1)
                table[pl.ds(at, strips, stride=2), :] = jnp.where(left, slots, swapped)
                table[pl.ds(at + 1, strips, stride=2), :] = jnp.where(left, swapped, slots)
        out[...] = jnp.zeros_like(out)
        for i, lanes in enumerate(patch_places(spots[...])[1]):
            lanes_out[i] = lanes

    def pick(p, carry):
        picked[pl.ds(p, 1), :] = table[pl.ds(source[step * pairs + p], 1), :]
        return carry

    lax.fori_loop(0, pairs, pick, 0, unroll=8)
    terms = block_sums(near_blocks, picked[...])
    owner = (iota((blocks, pairs), 0) == target[...]).astype(jnp.float32).astype(jnp.bfloat16)
    high, low = split(terms)
    out[...] += dot(owner, high) + dot(owner, low)


def table_rows(cas, numbers, count):
    parts = [cas[pl.ds(pl.multiple_of(n * count, 16), count), :G] for n in numbers]
    return jnp.concatenate(parts, axis=0) if len(parts) > 1 else parts[0]


def turned(rows):
    unit = (iota((G, G), 0) == iota((G, G), 1)).astype(jnp.float32).astype(jnp.bfloat16)
    return dot_nt(unit, rows).astype(jnp.bfloat16)


def tile_loop(half, rows, cols, groups, crosses, body):
    per_slab = cols // SLABS
    low = jnp.maximum(half * (rows // HALVES) - 1, 0)
    high = (half + 1) * (rows // HALVES)
    per_row = per_slab * groups

    def place(row, col):
        side = (col % HALVES) ^ half
        return side * (rows * cols // HALVES) + row * (cols // HALVES) + col // HALVES

    def step(n, carry):
        row = low + n // per_row
        left = n % per_row
        t = left % groups
        devices = [place(row, s * per_slab + left // groups) for s in range(SLABS)]
        found = [crosses((d * groups + t) * GROUP) for d in devices]
        inside = row >= half * (rows // HALVES)
        pl.when(functools.reduce(jnp.logical_or, found, inside))(lambda: body(devices, t))
        return carry

    lax.fori_loop(0, (high - low) * per_row, step, 0)


def lanes_inside(extra, d, t, half):
    extra = extra[d].astype(jnp.float32)
    picked = jnp.where(iota(extra.shape, 0) == t, extra, 0.0)
    cells = jnp.sum(picked, axis=0, keepdims=True) - (half * LANES).astype(jnp.float32)
    return jnp.broadcast_to((cells >= 0.0) & (cells < LANES), (16, LANES))


def scatter_kernel(
    cols,
    gs,
    fs,
    place,
    shift,
    start,
    mine,
    theirs,
    my_extra,
    their_extra,
    cas,
    own_out,
    other_out,
    patches,
    extra,
    lines,
    *slabs,
):
    half = place[0]
    step = pl.program_id(0)
    devices, held, _ = patches.shape
    groups = held // 16
    blocks = groups * GROUP
    owner = (iota((16, LANES), 1) // 4).astype(jnp.float32).astype(jnp.bfloat16)
    plane = iota((16, LANES), 0) % QUAD

    @pl.when(step == 0)
    def _():
        def clear(n, carry):
            for slab in slabs:
                at = pl.multiple_of(n * SLAB + PAD, 8)
                slab[pl.ds(at, SLAB - PAD), :] = jnp.zeros((SLAB - PAD, LANES), jnp.float32)
            return carry

        lax.fori_loop(0, G // QUAD, clear, 0)
        for side, part in enumerate(((mine, my_extra), (theirs, their_extra))):
            at = slice(side * (devices // 2), (side + 1) * (devices // 2))
            patches[at] = part[0][...]
            extra[at] = part[1][...]

        def tile(numbers, t):
            values = []
            for d in numbers:
                part = patches[d, pl.ds(pl.multiple_of(16 * t, 16), 16), :].astype(jnp.float32)
                part = jnp.where(lanes_inside(extra, d, t, half), part, 0.0)
                values.append(part.astype(jnp.bfloat16))

            for k in range(GROUP):
                sums = []
                for s in range(SLABS):
                    b = numbers[s] * blocks + t * GROUP + k
                    at = start[b]
                    moved = jnp.where(owner == k, values[s], jnp.zeros_like(values[s]))
                    moved = pltpu.roll(moved, shift[b], 1).astype(jnp.float32)
                    here = plane < QUAD - (at & (QUAD - 1))
                    near = slabs[s][pl.ds(at, 16), :] + jnp.where(here, moved, 0.0)
                    at_next = at + (SLAB - QUAD)
                    far = slabs[s][pl.ds(at_next, 16), :] + jnp.where(here, 0.0, moved)
                    sums.append((at, near, at_next, far))
                for s, (at, near, at_next, far) in enumerate(sums):
                    slabs[s][pl.ds(at, 16), :] = near
                    slabs[s][pl.ds(at_next, 16), :] = far

        def crosses(b):
            return shift[b] > LANES - 4

        tile_loop(half, devices // cols, cols, groups, crosses, tile)

        table = table_rows(cas, [place[1]], gs)

        def planes(n, carry):
            base = pl.multiple_of(n * SLAB, 8)
            sheets = []
            for q in range(QUAD):
                parts = []
                for s in range(SLABS):
                    part = slabs[s][pl.ds(base + (PAD + q), PIECE, stride=QUAD), :]
                    if s > 0:
                        at = base + (PAD + QUAD * PIECE + q)
                        over = slabs[s - 1][pl.ds(at, 4, stride=QUAD), :]
                        over = jnp.concatenate([over, jnp.zeros_like(over)], axis=0)
                        part = jnp.concatenate([part[:8] + over, part[8:]], axis=0)
                    parts.append(part.astype(jnp.bfloat16))
                sheets.append(jnp.concatenate(parts, axis=0))
            field = dot(table, jnp.concatenate(sheets, axis=1))
            for q in range(QUAD):
                part = field[:, LANES * q : LANES * q + LANES]
                lines[pl.ds(n * QUAD + q, gs, stride=STRIDE), :] = part
            return carry

        lax.fori_loop(0, G // QUAD, planes, 0, unroll=UNROLL_PLANES)

    @pl.when(step > 0)
    def _():
        third = table_rows(cas, [place[2], place[2] ^ 1], fs)
        for g in range(0, LINES, 2):
            pair = []
            for n in (g, g + 1):
                at = ((step - 1) * LINES + n) * STRIDE
                pair.append(lines[pl.ds(at, G), :].astype(jnp.bfloat16))
            field = dot(third, jnp.concatenate(pair, axis=1)).astype(jnp.bfloat16)
            for n in range(2):
                own_out[g + n] = field[:fs, LANES * n : LANES * n + LANES]
                other_out[g + n] = field[fs:, LANES * n : LANES * n + LANES]


def spectrum_kernel(place, own, other, *refs):
    weights, (cas, own_out, other_out) = refs[:WAYS], refs[WAYS:]
    tiles = [pl.ds(pl.multiple_of(h * LANES, LANES), LANES) for h in (place[0], 1 - place[0])]
    first = jnp.concatenate([cas[tile, :] for tile in tiles], axis=0)
    first_back = jnp.concatenate([cas[:, tile] for tile in tiles], axis=1)
    step, freqs, _ = weights[0].shape
    rows = step * freqs
    for n in range(WAYS):
        part = slice(n * step, (n + 1) * step)
        line = jnp.concatenate(
            [own[part].reshape(rows, LANES), other[part].reshape(rows, LANES)], axis=1
        )
        s = dot(line, first) * weights[n][...].reshape(rows, P_SIZE)
        line = dot(s.astype(jnp.bfloat16), first_back).astype(jnp.bfloat16)
        own_out[part] = line[:, :LANES].reshape(step, freqs, LANES)
        other_out[part] = line[:, LANES:].reshape(step, freqs, LANES)


def sample_kernel(
    cols,
    place,
    shift,
    start,
    my_extra,
    their_extra,
    own,
    other,
    cas,
    out,
    extra,
    second,
    third,
    lines,
    cells,
):
    half = place[0]
    step = pl.program_id(0)
    devices, held, _ = out.shape
    groups = held // 16
    blocks = groups * GROUP
    gs = second.shape[1]
    owner = (iota((16, LANES), 1) // 4).astype(jnp.float32).astype(jnp.bfloat16)
    plane = iota((16, LANES), 0) % QUAD

    @pl.when(step == 0)
    def _():
        for side, part in enumerate((my_extra, their_extra)):
            extra[side * (devices // 2) : (side + 1) * (devices // 2)] = part[...]
        second[...] = turned(table_rows(cas, [place[1]], gs))
        third[...] = turned(table_rows(cas, [place[2], place[2] ^ 1], own.shape[1]))

    for g in range(0, LINES, 2):
        pair = [jnp.concatenate([own[n], other[n]], axis=0) for n in (g, g + 1)]
        field = dot(third[...], jnp.concatenate(pair, axis=1))
        for n in range(2):
            at = (step * LINES + g + n) * STRIDE
            lines[pl.ds(at, G), :] = field[:, LANES * n : LANES * n + LANES]

    @pl.when(step == pl.num_programs(0) - 1)
    def _():
        def planes(n, carry):
            sheets = [
                lines[pl.ds(n * QUAD + q, gs, stride=STRIDE), :].astype(jnp.bfloat16)
                for q in range(QUAD)
            ]
            field = dot(second[...], jnp.concatenate(sheets, axis=1))
            base = pl.multiple_of(n * CELLS, 8)
            for q in range(QUAD):
                part = field[:, LANES * q : LANES * q + LANES]
                cells[pl.ds(base + (PAD + q), G, stride=QUAD), :] = part
            return carry

        lax.fori_loop(0, G // QUAD, planes, 0, unroll=UNROLL_PLANES)
        out[...] = jnp.zeros_like(out)

        def tile(numbers, t):
            sums = [jnp.zeros((16, LANES), jnp.bfloat16)] * SLABS
            for k in range(GROUP):
                for s in range(SLABS):
                    b = numbers[s] * blocks + t * GROUP + k
                    at = start[b]
                    here = plane < QUAD - (at & (QUAD - 1))
                    near = cells[pl.ds(at, 16), :]
                    far = cells[pl.ds(at + (CELLS - QUAD), 16), :]
                    moved = jnp.where(here, near, far).astype(jnp.bfloat16)
                    sums[s] = jnp.where(owner == k, pltpu.roll(moved, shift[b], 1), sums[s])
            for s, d in enumerate(numbers):
                inside = lanes_inside(extra, d, t, half)
                out[d, pl.ds(pl.multiple_of(16 * t, 16), 16), :] = jnp.where(
                    inside, sums[s].astype(jnp.float32), 0.0
                ).astype(jnp.bfloat16)

        def crosses(b):
            return (shift[b] > 0) & (shift[b] < 4)

        tile_loop(half, devices // cols, cols, groups, crosses, tile)


def finish_kernel(values, interpolate, near, inverse, lanes, out, total):
    blocks = near.shape[0]
    groups = values.shape[1] // 16
    rows = patch_rows()
    summed = values[0].astype(jnp.float32)
    for d in range(1, values.shape[0]):
        summed = summed + values[d].astype(jnp.float32)
    spread = jnp.concatenate([summed[16 * t : 16 * t + 16] for t in range(groups)], axis=1)
    parts = jnp.concatenate(split(spread), axis=0)
    patch = jnp.zeros((blocks, LANES), jnp.float32)
    for i in range(4):
        column = dot_nt(lanes[i], parts).astype(jnp.bfloat16)
        patch = patch + dot(column, jnp.concatenate([rows[i], rows[i]], axis=0))
    total[...] = block_sums(interpolate, patch) + near[...]
    count = out.shape[0]
    even = total[pl.ds(0, count, stride=2), :]
    odd = total[pl.ds(1, count, stride=2), :]
    total[:count] = jnp.where(iota(even.shape, 1) < BLK, even, odd)
    upper = inverse[:count]
    lower = inverse[count:]

    def step(u, acc):
        row = jnp.broadcast_to(total[pl.ds(u, 1), :], lower.shape)
        return jnp.where(upper == u, lane_gather(row, lower), acc)

    out[...] = lax.fori_loop(0, count, step, jnp.zeros(out.shape, jnp.float32), unroll=True)


def struct(shape, dtype):
    return jax.ShapeDtypeStruct(shape, dtype)


def whole(shape):
    return pl.BlockSpec(shape, lambda *_: (0,) * len(shape))


def params(mib):
    return pltpu.CompilerParams(vmem_limit_bytes=mib * MB)


def body(
    charges,
    panel_order,
    patch_anchor,
    project,
    interpolate,
    kernel_spectrum,
    near_pairs,
    near_blocks,
):
    axes = ("row", "col")
    rows = lax.axis_size("row")
    cols = lax.axis_size("col")
    devices = rows * cols
    row_at = lax.axis_index("row")
    col_at = lax.axis_index("col")
    half = col_at % HALVES
    mates = [(c, c ^ 1) for c in range(cols)]
    blocks = project.shape[0]
    groups = blocks // GROUP
    panels = charges.shape[0]
    strips = panels // LANES
    gs, fs, _ = kernel_spectrum.shape
    held = 16 * groups + strips + 16

    order = panel_order.reshape(strips, LANES)
    members = devices // HALVES
    sent, spots = pl.pallas_call(
        project_kernel,
        out_shape=(
            struct((members, held, LANES), jnp.bfloat16),
            struct((blocks, LANES), jnp.int32),
        ),
        in_specs=[pl.BlockSpec(memory_space=pltpu.HBM)] * 4,
        scratch_shapes=[
            pltpu.VMEM((strips, LANES), jnp.bfloat16),
            pltpu.VMEM((strips, LANES), jnp.int32),
            pltpu.VMEM(project.shape, jnp.bfloat16),
            pltpu.VMEM(patch_anchor.shape, jnp.int32),
            pltpu.VMEM((strips, LANES), jnp.float32),
            pltpu.VMEM((blocks, LANES), jnp.float32),
            pltpu.SemaphoreType.DMA((4,)),
        ],
        compiler_params=params(58),
        name="project",
    )(
        charges.reshape(strips, LANES),
        order,
        project,
        patch_anchor,
    )
    cores = [
        [r * cols + c for r in range(rows) for c in range(core, cols, HALVES)]
        for core in range(HALVES)
    ]

    def swap_members(array):
        return lax.all_to_all(
            array, axes, split_axis=0, concat_axis=0, axis_index_groups=cores, tiled=True
        )

    mine = swap_members(sent)
    theirs = lax.ppermute(mine, "col", mates)
    at = held - 16 + groups
    anchors = jnp.stack([part[:, at : at + 3] for part in (mine, theirs)])
    anchors = anchors.astype(jnp.int32)
    lane = 4 * (jnp.arange(blocks, dtype=jnp.int32) % GROUP)
    forth = ((anchors[:, :, 0] - lane) & (LANES - 1)).reshape(devices * blocks)
    back = ((lane - anchors[:, :, 0]) & (LANES - 1)).reshape(devices * blocks)
    group = anchors[:, :, 2] // QUAD
    inner = PAD + QUAD * anchors[:, :, 1] + anchors[:, :, 2] % QUAD
    side = jnp.arange(HALVES, dtype=jnp.int32)[:, None] ^ half
    col = jnp.arange(members, dtype=jnp.int32) % (cols // HALVES) * HALVES + side
    piece = (col * SLABS // cols * PIECE)[:, :, None]
    slab_at = (group * SLAB + inner - QUAD * piece).reshape(devices * blocks)
    cell_at = (group * CELLS + inner).reshape(devices * blocks)
    place = jnp.stack([half, row_at, col_at]).astype(jnp.int32)
    cas = jnp.asarray(CAS)

    smem = pl.BlockSpec(memory_space=pltpu.SMEM)

    def rows_at(start, count):
        return pl.BlockSpec((members, count, LANES), lambda *_: (0, start // count, 0))

    patch_rows = rows_at(0, 16 * groups)
    charge_rows = rows_at(16 * groups, strips)
    extra_rows = rows_at(16 * groups + strips, 16)
    steps = gs // LINES
    lines_type = struct((gs, fs, LANES), jnp.bfloat16)
    late = pl.BlockSpec((LINES, fs, LANES), lambda n: (jnp.maximum(n - 1, 0), 0, 0))
    own, other = pl.pallas_call(
        functools.partial(scatter_kernel, cols, gs, fs),
        grid=(1 + steps,),
        in_specs=[smem] * 3 + [patch_rows] * 2 + [extra_rows] * 2 + [whole(cas.shape)],
        out_specs=(late, late),
        out_shape=(lines_type, lines_type),
        scratch_shapes=[
            pltpu.VMEM((devices, 16 * groups, LANES), jnp.bfloat16),
            pltpu.VMEM((devices, 16, LANES), jnp.bfloat16),
            pltpu.VMEM((gs * STRIDE, LANES), jnp.float32),
        ]
        + [pltpu.VMEM(((G // QUAD + 1) * SLAB, LANES), jnp.float32)] * SLABS,
        compiler_params=params(50),
        name="scatter",
    )(place, forth, slab_at, mine, theirs, mine, theirs, cas)
    other = lax.ppermute(other, "col", mates)
    own, order = lax.optimization_barrier((own, order))
    inverse = pl.pallas_call(
        inverse_kernel,
        out_shape=struct((2 * strips, LANES), jnp.int32),
        compiler_params=params(32),
        name="inverse",
    )(order)

    other, inverse = lax.optimization_barrier((other, inverse))

    part = lambda shape: pl.BlockSpec((BATCH,) + shape, lambda n: (n, 0, 0))

    def weight_part(way):
        return pl.BlockSpec((BATCH // WAYS, fs, P_SIZE), lambda n: (n * WAYS + way, 0, 0))

    own, other = pl.pallas_call(
        spectrum_kernel,
        grid=(gs // BATCH,),
        in_specs=[
            smem,
            part((fs, LANES)),
            part((fs, LANES)),
            *[weight_part(n) for n in range(WAYS)],
            whole(cas.shape),
        ],
        out_specs=(part((fs, LANES)), part((fs, LANES))),
        out_shape=(lines_type, lines_type),
        compiler_params=params(40),
        name="spectrum",
    )(place, own, other, *[kernel_spectrum] * WAYS, cas)
    other = lax.ppermute(other, "col", mates)

    early = pl.BlockSpec((LINES, fs, LANES), lambda n: (n, 0, 0))
    values = pl.pallas_call(
        functools.partial(sample_kernel, cols),
        grid=(steps,),
        in_specs=[smem] * 3 + [extra_rows] * 2 + [early, early, whole(cas.shape)],
        out_specs=whole((devices, 16 * groups, LANES)),
        out_shape=struct((devices, 16 * groups, LANES), jnp.bfloat16),
        scratch_shapes=[
            pltpu.VMEM((devices, 16, LANES), jnp.bfloat16),
            pltpu.VMEM((G, gs), jnp.bfloat16),
            pltpu.VMEM((G, 2 * fs), jnp.bfloat16),
            pltpu.VMEM((gs * STRIDE, LANES), jnp.float32),
            pltpu.VMEM(((G // QUAD + 1) * CELLS, LANES), jnp.float32),
        ],
        compiler_params=params(46),
        name="sample",
    )(place, back, cell_at, mine, theirs, own, other, cas)
    values = values.reshape(HALVES, members, 16 * groups, LANES)
    received = lax.ppermute(values[1], "col", mates).astype(jnp.float32)
    values = (values[0].astype(jnp.float32) + received).astype(jnp.bfloat16)
    values, my_charges, their_charges = lax.optimization_barrier((values, mine, theirs))
    values = swap_members(values)

    source = near_pairs[1]
    source_row = source // blocks // cols
    source_col = source // blocks % cols
    wanted = (source_col % HALVES ^ half) * members + source_row * (cols // HALVES)
    wanted = (wanted + source_col // HALVES) * blocks + source % blocks
    target = near_pairs[0] - (row_at * cols + col_at) * blocks
    pairs = near_blocks.shape[0]
    near, lanes = pl.pallas_call(
        near_kernel,
        grid=(pairs // blocks,),
        in_specs=[
            smem,
            pl.BlockSpec((blocks, BLK * BLK), lambda n: (n, 0)),
            pl.BlockSpec((1, blocks), lambda n: (0, n)),
            charge_rows,
            charge_rows,
            whole((blocks, LANES)),
        ],
        out_specs=(whole((blocks, LANES)), whole((4, blocks, 4 * blocks))),
        out_shape=(
            struct((blocks, LANES), jnp.float32),
            struct((4, blocks, 4 * blocks), jnp.bfloat16),
        ),
        scratch_shapes=[
            pltpu.VMEM((devices * blocks, LANES), jnp.float32),
            pltpu.VMEM((blocks, LANES), jnp.float32),
        ],
        compiler_params=params(40),
        name="near",
    )(wanted, near_blocks, target.reshape(1, pairs), my_charges, their_charges, spots)

    result = pl.pallas_call(
        finish_kernel,
        out_shape=struct((strips, LANES), jnp.float32),
        scratch_shapes=[pltpu.VMEM((blocks, LANES), jnp.float32)],
        compiler_params=params(32),
        name="finish",
    )(values, interpolate, near, inverse, lanes)
    return result.reshape(panels)


def solution(mesh):
    placed = (
        P(("row", "col")),
        P(("row", "col")),
        P(None, ("row", "col")),
        P(("row", "col"), None),
        P(("row", "col"), None),
        P("row", "col", None),
        P(None, ("row", "col")),
        P(("row", "col"), None),
    )
    return jax.shard_map(
        body, mesh=mesh, in_specs=placed, out_specs=P(("row", "col")), check_vma=False
    )
```

```python
import functools

import jax
import jax.numpy as jnp
import ml_dtypes
import numpy as np
from jax import lax
from jax.experimental import pallas as pl
from jax.experimental.pallas import tpu as pltpu
from jax.sharding import PartitionSpec as P

G = 256
P_SIZE = 512
BLK = 64
PTS = 64
LANES = 128
GROUP = LANES // 4
HALVES = G // LANES
SLABS = 4
PIECE = G // SLABS
QUAD = 4
PAD = 8
SLAB = PAD + QUAD * PIECE + 16
CELLS = PAD + QUAD * G + 16
STRIDE = G + 1
BATCH = 16
WAYS = 8
LINES = 32
UNROLL_PLANES = 64
MB = 1 << 20
NT = (((1,), (1,)), ((), ()))


def cas_table():
    index = np.arange(P_SIZE, dtype=np.int64)
    phase = (index[:, None] * index[None, :] % P_SIZE).astype(np.float64) * (2.0 * np.pi / P_SIZE)
    return ((np.cos(phase) + np.sin(phase)) / np.sqrt(P_SIZE)).astype(ml_dtypes.bfloat16)


CAS = cas_table()


def dot(a, b):
    return jnp.dot(a, b, preferred_element_type=jnp.float32)


def dot_nt(a, b):
    return lax.dot_general(a, b, NT, preferred_element_type=jnp.float32)


def iota(shape, dim):
    return lax.broadcasted_iota(jnp.int32, shape, dim)


def split(value):
    high = value.astype(jnp.bfloat16)
    return high, (value - high.astype(jnp.float32)).astype(jnp.bfloat16)


def lane_gather(table, index):
    return jnp.take_along_axis(table, index, axis=1, mode="promise_in_bounds")


def block_sums(mats, vecs):
    rows = vecs.shape[0]
    pair = jnp.concatenate([vecs, vecs], axis=1)
    total = jnp.zeros((2 * rows, LANES), jnp.float32)
    for t in range(mats.shape[1] // 256):
        high, low = split(mats[:, 256 * t : 256 * t + 256].astype(jnp.float32) * pair)
        owner = iota((256, LANES), 0) // BLK + 4 * t
        table = (owner == iota((256, LANES), 1) % BLK).astype(jnp.bfloat16)
        total = total + dot(jnp.concatenate([high, low], axis=0), table)
    return total[:rows] + total[rows:]


def patch_rows():
    row = iota((16, LANES), 0)
    return [
        (iota((16, LANES), 1) % PTS == 16 * i + row).astype(jnp.float32).astype(jnp.bfloat16)
        for i in range(4)
    ]


def patch_places(spots):
    blocks = spots.shape[0]
    spots = jnp.concatenate([spots] * (4 * blocks // LANES), axis=1)
    lane = iota(spots.shape, 1)
    lanes = [(lane == 4 * spots + i).astype(jnp.float32).astype(jnp.bfloat16) for i in range(4)]
    return patch_rows(), lanes


def block_spots(first):
    blocks = first.shape[1]
    shape = (blocks, blocks)
    crossing = ((first & (LANES - 1)) > LANES - 4).astype(jnp.float32)
    crossing = jnp.broadcast_to(crossing, (8, blocks))
    earlier = (iota(shape, 0) < iota(shape, 1)).astype(jnp.float32).astype(jnp.bfloat16)
    ahead = dot(crossing.astype(jnp.bfloat16), earlier)
    total = jnp.sum(crossing, axis=1, keepdims=True)
    block = iota((8, blocks), 1).astype(jnp.float32)
    spot = jnp.where(crossing > 0.0, ahead, total + block - ahead)
    spread = jnp.broadcast_to(spot[:1], (LANES, blocks)).astype(jnp.bfloat16)
    unit = (iota(shape, 0) == iota(shape, 1)).astype(jnp.float32).astype(jnp.bfloat16)
    return dot_nt(unit, spread).astype(jnp.int32)


def project_kernel(
    charges_in,
    order_in,
    project_in,
    anchors_in,
    sent_out,
    spot_out,
    charges,
    order,
    project,
    anchors,
    table,
    doubled,
    sems,
):
    blocks = spot_out.shape[0]
    groups = blocks // GROUP
    pairs = ((charges_in, charges), (order_in, order), (project_in, project), (anchors_in, anchors))
    copies = [pltpu.make_async_copy(a, b, sems.at[n]) for n, (a, b) in enumerate(pairs)]
    for copy in copies:
        copy.start()
    copies[0].wait()
    copies[1].wait()
    table[...] = charges[...].astype(jnp.float32)
    strips = table.shape[0]
    upper = order[...] // LANES
    lower = order[...] % LANES

    def step(u, acc):
        row = jnp.broadcast_to(table[pl.ds(u, 1), :], lower.shape)
        return jnp.where(upper == u, lane_gather(row, lower), acc)

    slots = lax.fori_loop(0, strips, step, jnp.zeros(lower.shape, jnp.float32), unroll=True)
    swapped = pltpu.roll(slots, BLK, 1)
    left = iota(slots.shape, 1) < BLK
    doubled[pl.ds(0, strips, stride=2), :] = jnp.where(left, slots, swapped)
    doubled[pl.ds(1, strips, stride=2), :] = jnp.where(left, swapped, slots)
    twice = doubled[...]
    copies[2].wait()
    copies[3].wait()
    patch = block_sums(project, twice)
    patch = jnp.where(iota(patch.shape, 1) < PTS, patch, 0.0).astype(jnp.bfloat16)
    spots = block_spots(anchors[:1, :])
    spot_out[...] = spots
    rows, lanes = patch_places(spots)
    moved = (iota(spots.shape, 1) == spots).astype(jnp.float32).astype(jnp.bfloat16)
    corner = anchors[...].astype(jnp.float32).astype(jnp.bfloat16)
    corner = dot(jnp.concatenate([corner] * 3, axis=0)[:8], moved)
    cells = (iota((8, 4 * blocks), 1) % 4).astype(jnp.float32)
    start = jnp.broadcast_to(anchors[:1, :].astype(jnp.float32), (8, blocks)).astype(jnp.bfloat16)
    for i in range(4):
        cells = cells + dot(start, lanes[i])
    spread = jnp.zeros((16, 4 * blocks), jnp.float32)
    for i in range(4):
        spread = spread + dot(dot_nt(rows[i], patch).astype(jnp.bfloat16), lanes[i])
    tiles = [slice(LANES * t, LANES * t + LANES) for t in range(groups)]
    sent = [spread[:, tile].astype(jnp.bfloat16) for tile in tiles]
    sent.append(slots.astype(jnp.bfloat16))
    extra = [cells[:1, tile] for tile in tiles] + [corner[:3]]
    extra.append(jnp.zeros((13 - groups, LANES), jnp.float32))
    sent.append(jnp.concatenate(extra, axis=0).astype(jnp.bfloat16))
    sent = jnp.concatenate(sent, axis=0)
    for n in range(sent_out.shape[0]):
        sent_out[n] = sent


def inverse_kernel(order, out):
    rows = order.shape[0]

    def step(r, acc):
        here = order[pl.ds(r, 1), :]
        upper = iota((rows, LANES), 0) == here // LANES
        lower = iota((LANES, LANES), 0) == here % LANES
        values = jnp.concatenate(
            [
                jnp.where(upper, r.astype(jnp.float32), 0.0),
                jnp.where(upper, iota((rows, LANES), 1).astype(jnp.float32), 0.0),
            ],
            axis=0,
        )
        return acc + dot_nt(
            values.astype(jnp.bfloat16), lower.astype(jnp.float32).astype(jnp.bfloat16)
        )

    out[...] = lax.fori_loop(
        0, rows, step, jnp.zeros((2 * rows, LANES), jnp.float32), unroll=4
    ).astype(jnp.int32)


def near_kernel(source, near_blocks, target, mine, theirs, spots, out, lanes_out, table, picked):
    step = pl.program_id(0)
    pairs = picked.shape[0]
    blocks = out.shape[0]

    @pl.when(step == 0)
    def _():
        members, strips, _ = mine.shape
        left = iota((strips, LANES), 1) < BLK
        for side, part in enumerate((mine, theirs)):
            for n in range(members):
                at = (side * members + n) * blocks
                slots = part[n].astype(jnp.float32)
                swapped = pltpu.roll(slots, BLK, 1)
                table[pl.ds(at, strips, stride=2), :] = jnp.where(left, slots, swapped)
                table[pl.ds(at + 1, strips, stride=2), :] = jnp.where(left, swapped, slots)
        out[...] = jnp.zeros_like(out)
        for i, lanes in enumerate(patch_places(spots[...])[1]):
            lanes_out[i] = lanes

    def pick(p, carry):
        picked[pl.ds(p, 1), :] = table[pl.ds(source[step * pairs + p], 1), :]
        return carry

    lax.fori_loop(0, pairs, pick, 0, unroll=8)
    terms = block_sums(near_blocks, picked[...])
    owner = (iota((blocks, pairs), 0) == target[...]).astype(jnp.float32).astype(jnp.bfloat16)
    high, low = split(terms)
    out[...] += dot(owner, high) + dot(owner, low)


def table_rows(cas, numbers, count):
    parts = [cas[pl.ds(pl.multiple_of(n * count, 16), count), :G] for n in numbers]
    return jnp.concatenate(parts, axis=0) if len(parts) > 1 else parts[0]


def turned(rows):
    unit = (iota((G, G), 0) == iota((G, G), 1)).astype(jnp.float32).astype(jnp.bfloat16)
    return dot_nt(unit, rows).astype(jnp.bfloat16)


def tile_loop(half, rows, cols, groups, crosses, body):
    per_slab = cols // SLABS
    low = jnp.maximum(half * (rows // HALVES) - 1, 0)
    high = (half + 1) * (rows // HALVES)
    per_row = per_slab * groups

    def place(row, col):
        side = (col % HALVES) ^ half
        return side * (rows * cols // HALVES) + row * (cols // HALVES) + col // HALVES

    def step(n, carry):
        row = low + n // per_row
        left = n % per_row
        t = left % groups
        devices = [place(row, s * per_slab + left // groups) for s in range(SLABS)]
        found = [crosses((d * groups + t) * GROUP) for d in devices]
        inside = row >= half * (rows // HALVES)
        pl.when(functools.reduce(jnp.logical_or, found, inside))(lambda: body(devices, t))
        return carry

    lax.fori_loop(0, (high - low) * per_row, step, 0)


def lanes_inside(extra, d, t, half):
    extra = extra[d].astype(jnp.float32)
    picked = jnp.where(iota(extra.shape, 0) == t, extra, 0.0)
    cells = jnp.sum(picked, axis=0, keepdims=True) - (half * LANES).astype(jnp.float32)
    return jnp.broadcast_to((cells >= 0.0) & (cells < LANES), (16, LANES))


def scatter_kernel(
    cols,
    gs,
    fs,
    place,
    shift,
    start,
    mine,
    theirs,
    my_extra,
    their_extra,
    cas,
    own_out,
    other_out,
    patches,
    extra,
    lines,
    *slabs,
):
    half = place[0]
    step = pl.program_id(0)
    devices, held, _ = patches.shape
    groups = held // 16
    blocks = groups * GROUP
    owner = (iota((16, LANES), 1) // 4).astype(jnp.float32).astype(jnp.bfloat16)
    plane = iota((16, LANES), 0) % QUAD

    @pl.when(step == 0)
    def _():
        def clear(n, carry):
            for slab in slabs:
                at = pl.multiple_of(n * SLAB + PAD, 8)
                slab[pl.ds(at, SLAB - PAD), :] = jnp.zeros((SLAB - PAD, LANES), jnp.float32)
            return carry

        lax.fori_loop(0, G // QUAD, clear, 0)
        for side, part in enumerate(((mine, my_extra), (theirs, their_extra))):
            at = slice(side * (devices // 2), (side + 1) * (devices // 2))
            patches[at] = part[0][...]
            extra[at] = part[1][...]

        def tile(numbers, t):
            values = []
            for d in numbers:
                part = patches[d, pl.ds(pl.multiple_of(16 * t, 16), 16), :].astype(jnp.float32)
                part = jnp.where(lanes_inside(extra, d, t, half), part, 0.0)
                values.append(part.astype(jnp.bfloat16))

            for k in range(GROUP):
                sums = []
                for s in range(SLABS):
                    b = numbers[s] * blocks + t * GROUP + k
                    at = start[b]
                    moved = jnp.where(owner == k, values[s], jnp.zeros_like(values[s]))
                    moved = pltpu.roll(moved, shift[b], 1).astype(jnp.float32)
                    here = plane < QUAD - (at & (QUAD - 1))
                    near = slabs[s][pl.ds(at, 16), :] + jnp.where(here, moved, 0.0)
                    at_next = at + (SLAB - QUAD)
                    far = slabs[s][pl.ds(at_next, 16), :] + jnp.where(here, 0.0, moved)
                    sums.append((at, near, at_next, far))
                for s, (at, near, at_next, far) in enumerate(sums):
                    slabs[s][pl.ds(at, 16), :] = near
                    slabs[s][pl.ds(at_next, 16), :] = far

        def crosses(b):
            return shift[b] > LANES - 4

        tile_loop(half, devices // cols, cols, groups, crosses, tile)

        table = table_rows(cas, [place[1]], gs)

        def planes(n, carry):
            base = pl.multiple_of(n * SLAB, 8)
            sheets = []
            for q in range(QUAD):
                parts = []
                for s in range(SLABS):
                    part = slabs[s][pl.ds(base + (PAD + q), PIECE, stride=QUAD), :]
                    if s > 0:
                        at = base + (PAD + QUAD * PIECE + q)
                        over = slabs[s - 1][pl.ds(at, 4, stride=QUAD), :]
                        over = jnp.concatenate([over, jnp.zeros_like(over)], axis=0)
                        part = jnp.concatenate([part[:8] + over, part[8:]], axis=0)
                    parts.append(part.astype(jnp.bfloat16))
                sheets.append(jnp.concatenate(parts, axis=0))
            field = dot(table, jnp.concatenate(sheets, axis=1))
            for q in range(QUAD):
                part = field[:, LANES * q : LANES * q + LANES]
                lines[pl.ds(n * QUAD + q, gs, stride=STRIDE), :] = part
            return carry

        lax.fori_loop(0, G // QUAD, planes, 0, unroll=UNROLL_PLANES)

    @pl.when(step > 0)
    def _():
        third = table_rows(cas, [place[2], place[2] ^ 1], fs)
        for g in range(0, LINES, 2):
            pair = []
            for n in (g, g + 1):
                at = ((step - 1) * LINES + n) * STRIDE
                pair.append(lines[pl.ds(at, G), :].astype(jnp.bfloat16))
            field = dot(third, jnp.concatenate(pair, axis=1)).astype(jnp.bfloat16)
            for n in range(2):
                own_out[g + n] = field[:fs, LANES * n : LANES * n + LANES]
                other_out[g + n] = field[fs:, LANES * n : LANES * n + LANES]


def spectrum_kernel(place, own, other, *refs):
    weights, (cas, own_out, other_out) = refs[:WAYS], refs[WAYS:]
    tiles = [pl.ds(pl.multiple_of(h * LANES, LANES), LANES) for h in (place[0], 1 - place[0])]
    first = jnp.concatenate([cas[tile, :] for tile in tiles], axis=0)
    first_back = jnp.concatenate([cas[:, tile] for tile in tiles], axis=1)
    step, freqs, _ = weights[0].shape
    rows = step * freqs
    for n in range(WAYS):
        part = slice(n * step, (n + 1) * step)
        line = jnp.concatenate(
            [own[part].reshape(rows, LANES), other[part].reshape(rows, LANES)], axis=1
        )
        s = dot(line, first) * weights[n][...].reshape(rows, P_SIZE)
        line = dot(s.astype(jnp.bfloat16), first_back).astype(jnp.bfloat16)
        own_out[part] = line[:, :LANES].reshape(step, freqs, LANES)
        other_out[part] = line[:, LANES:].reshape(step, freqs, LANES)


def sample_kernel(
    cols,
    place,
    shift,
    start,
    my_extra,
    their_extra,
    own,
    other,
    cas,
    out,
    extra,
    second,
    third,
    lines,
    cells,
):
    half = place[0]
    step = pl.program_id(0)
    devices, held, _ = out.shape
    groups = held // 16
    blocks = groups * GROUP
    gs = second.shape[1]
    owner = (iota((16, LANES), 1) // 4).astype(jnp.float32).astype(jnp.bfloat16)
    plane = iota((16, LANES), 0) % QUAD

    @pl.when(step == 0)
    def _():
        for side, part in enumerate((my_extra, their_extra)):
            extra[side * (devices // 2) : (side + 1) * (devices // 2)] = part[...]
        second[...] = turned(table_rows(cas, [place[1]], gs))
        third[...] = turned(table_rows(cas, [place[2], place[2] ^ 1], own.shape[1]))

    for g in range(0, LINES, 2):
        pair = [jnp.concatenate([own[n], other[n]], axis=0) for n in (g, g + 1)]
        field = dot(third[...], jnp.concatenate(pair, axis=1))
        for n in range(2):
            at = (step * LINES + g + n) * STRIDE
            lines[pl.ds(at, G), :] = field[:, LANES * n : LANES * n + LANES]

    @pl.when(step == pl.num_programs(0) - 1)
    def _():
        def planes(n, carry):
            sheets = [
                lines[pl.ds(n * QUAD + q, gs, stride=STRIDE), :].astype(jnp.bfloat16)
                for q in range(QUAD)
            ]
            field = dot(second[...], jnp.concatenate(sheets, axis=1))
            base = pl.multiple_of(n * CELLS, 8)
            for q in range(QUAD):
                part = field[:, LANES * q : LANES * q + LANES]
                cells[pl.ds(base + (PAD + q), G, stride=QUAD), :] = part
            return carry

        lax.fori_loop(0, G // QUAD, planes, 0, unroll=UNROLL_PLANES)
        out[...] = jnp.zeros_like(out)

        def tile(numbers, t):
            sums = [jnp.zeros((16, LANES), jnp.bfloat16)] * SLABS
            for k in range(GROUP):
                for s in range(SLABS):
                    b = numbers[s] * blocks + t * GROUP + k
                    at = start[b]
                    here = plane < QUAD - (at & (QUAD - 1))
                    near = cells[pl.ds(at, 16), :]
                    far = cells[pl.ds(at + (CELLS - QUAD), 16), :]
                    moved = jnp.where(here, near, far).astype(jnp.bfloat16)
                    sums[s] = jnp.where(owner == k, pltpu.roll(moved, shift[b], 1), sums[s])
            for s, d in enumerate(numbers):
                inside = lanes_inside(extra, d, t, half)
                out[d, pl.ds(pl.multiple_of(16 * t, 16), 16), :] = jnp.where(
                    inside, sums[s].astype(jnp.float32), 0.0
                ).astype(jnp.bfloat16)

        def crosses(b):
            return (shift[b] > 0) & (shift[b] < 4)

        tile_loop(half, devices // cols, cols, groups, crosses, tile)


def finish_kernel(values, interpolate, near, inverse, lanes, out, total):
    blocks = near.shape[0]
    groups = values.shape[1] // 16
    rows = patch_rows()
    summed = values[0].astype(jnp.float32)
    for d in range(1, values.shape[0]):
        summed = summed + values[d].astype(jnp.float32)
    spread = jnp.concatenate([summed[16 * t : 16 * t + 16] for t in range(groups)], axis=1)
    parts = jnp.concatenate(split(spread), axis=0)
    patch = jnp.zeros((blocks, LANES), jnp.float32)
    for i in range(4):
        column = dot_nt(lanes[i], parts).astype(jnp.bfloat16)
        patch = patch + dot(column, jnp.concatenate([rows[i], rows[i]], axis=0))
    total[...] = block_sums(interpolate, patch) + near[...]
    count = out.shape[0]
    even = total[pl.ds(0, count, stride=2), :]
    odd = total[pl.ds(1, count, stride=2), :]
    total[:count] = jnp.where(iota(even.shape, 1) < BLK, even, odd)
    upper = inverse[:count]
    lower = inverse[count:]

    def step(u, acc):
        row = jnp.broadcast_to(total[pl.ds(u, 1), :], lower.shape)
        return jnp.where(upper == u, lane_gather(row, lower), acc)

    out[...] = lax.fori_loop(0, count, step, jnp.zeros(out.shape, jnp.float32), unroll=True)


def struct(shape, dtype):
    return jax.ShapeDtypeStruct(shape, dtype)


def whole(shape):
    return pl.BlockSpec(shape, lambda *_: (0,) * len(shape))


def params(mib):
    return pltpu.CompilerParams(vmem_limit_bytes=mib * MB)


def body(
    charges,
    panel_order,
    patch_anchor,
    project,
    interpolate,
    kernel_spectrum,
    near_pairs,
    near_blocks,
):
    axes = ("row", "col")
    rows = lax.axis_size("row")
    cols = lax.axis_size("col")
    devices = rows * cols
    row_at = lax.axis_index("row")
    col_at = lax.axis_index("col")
    half = col_at % HALVES
    mates = [(c, c ^ 1) for c in range(cols)]
    blocks = project.shape[0]
    groups = blocks // GROUP
    panels = charges.shape[0]
    strips = panels // LANES
    gs, fs, _ = kernel_spectrum.shape
    held = 16 * groups + strips + 16

    order = panel_order.reshape(strips, LANES)
    members = devices // HALVES
    sent, spots = pl.pallas_call(
        project_kernel,
        out_shape=(
            struct((members, held, LANES), jnp.bfloat16),
            struct((blocks, LANES), jnp.int32),
        ),
        in_specs=[pl.BlockSpec(memory_space=pltpu.HBM)] * 4,
        scratch_shapes=[
            pltpu.VMEM((strips, LANES), jnp.bfloat16),
            pltpu.VMEM((strips, LANES), jnp.int32),
            pltpu.VMEM(project.shape, jnp.bfloat16),
            pltpu.VMEM(patch_anchor.shape, jnp.int32),
            pltpu.VMEM((strips, LANES), jnp.float32),
            pltpu.VMEM((blocks, LANES), jnp.float32),
            pltpu.SemaphoreType.DMA((4,)),
        ],
        compiler_params=params(58),
        name="project",
    )(
        charges.reshape(strips, LANES),
        order,
        project,
        patch_anchor,
    )
    cores = [
        [r * cols + c for r in range(rows) for c in range(core, cols, HALVES)]
        for core in range(HALVES)
    ]

    def swap_members(array):
        return lax.all_to_all(
            array, axes, split_axis=0, concat_axis=0, axis_index_groups=cores, tiled=True
        )

    mine = swap_members(sent)
    theirs = lax.ppermute(mine, "col", mates)
    at = held - 16 + groups
    anchors = jnp.stack([part[:, at : at + 3] for part in (mine, theirs)])
    anchors = anchors.astype(jnp.int32)
    lane = 4 * (jnp.arange(blocks, dtype=jnp.int32) % GROUP)
    forth = ((anchors[:, :, 0] - lane) & (LANES - 1)).reshape(devices * blocks)
    back = ((lane - anchors[:, :, 0]) & (LANES - 1)).reshape(devices * blocks)
    group = anchors[:, :, 2] // QUAD
    inner = PAD + QUAD * anchors[:, :, 1] + anchors[:, :, 2] % QUAD
    side = jnp.arange(HALVES, dtype=jnp.int32)[:, None] ^ half
    col = jnp.arange(members, dtype=jnp.int32) % (cols // HALVES) * HALVES + side
    piece = (col * SLABS // cols * PIECE)[:, :, None]
    slab_at = (group * SLAB + inner - QUAD * piece).reshape(devices * blocks)
    cell_at = (group * CELLS + inner).reshape(devices * blocks)
    place = jnp.stack([half, row_at, col_at]).astype(jnp.int32)
    cas = jnp.asarray(CAS)

    smem = pl.BlockSpec(memory_space=pltpu.SMEM)

    def rows_at(start, count):
        return pl.BlockSpec((members, count, LANES), lambda *_: (0, start // count, 0))

    patch_rows = rows_at(0, 16 * groups)
    charge_rows = rows_at(16 * groups, strips)
    extra_rows = rows_at(16 * groups + strips, 16)
    steps = gs // LINES
    lines_type = struct((gs, fs, LANES), jnp.bfloat16)
    late = pl.BlockSpec((LINES, fs, LANES), lambda n: (jnp.maximum(n - 1, 0), 0, 0))
    own, other = pl.pallas_call(
        functools.partial(scatter_kernel, cols, gs, fs),
        grid=(1 + steps,),
        in_specs=[smem] * 3 + [patch_rows] * 2 + [extra_rows] * 2 + [whole(cas.shape)],
        out_specs=(late, late),
        out_shape=(lines_type, lines_type),
        scratch_shapes=[
            pltpu.VMEM((devices, 16 * groups, LANES), jnp.bfloat16),
            pltpu.VMEM((devices, 16, LANES), jnp.bfloat16),
            pltpu.VMEM((gs * STRIDE, LANES), jnp.float32),
        ]
        + [pltpu.VMEM(((G // QUAD + 1) * SLAB, LANES), jnp.float32)] * SLABS,
        compiler_params=params(50),
        name="scatter",
    )(place, forth, slab_at, mine, theirs, mine, theirs, cas)
    other = lax.ppermute(other, "col", mates)
    own, order = lax.optimization_barrier((own, order))
    inverse = pl.pallas_call(
        inverse_kernel,
        out_shape=struct((2 * strips, LANES), jnp.int32),
        compiler_params=params(32),
        name="inverse",
    )(order)

    other, inverse = lax.optimization_barrier((other, inverse))

    part = lambda shape: pl.BlockSpec((BATCH,) + shape, lambda n: (n, 0, 0))

    def weight_part(way):
        return pl.BlockSpec((BATCH // WAYS, fs, P_SIZE), lambda n: (n * WAYS + way, 0, 0))

    own, other = pl.pallas_call(
        spectrum_kernel,
        grid=(gs // BATCH,),
        in_specs=[
            smem,
            part((fs, LANES)),
            part((fs, LANES)),
            *[weight_part(n) for n in range(WAYS)],
            whole(cas.shape),
        ],
        out_specs=(part((fs, LANES)), part((fs, LANES))),
        out_shape=(lines_type, lines_type),
        compiler_params=params(40),
        name="spectrum",
    )(place, own, other, *[kernel_spectrum] * WAYS, cas)
    other = lax.ppermute(other, "col", mates)

    early = pl.BlockSpec((LINES, fs, LANES), lambda n: (n, 0, 0))
    values = pl.pallas_call(
        functools.partial(sample_kernel, cols),
        grid=(steps,),
        in_specs=[smem] * 3 + [extra_rows] * 2 + [early, early, whole(cas.shape)],
        out_specs=whole((devices, 16 * groups, LANES)),
        out_shape=struct((devices, 16 * groups, LANES), jnp.bfloat16),
        scratch_shapes=[
            pltpu.VMEM((devices, 16, LANES), jnp.bfloat16),
            pltpu.VMEM((G, gs), jnp.bfloat16),
            pltpu.VMEM((G, 2 * fs), jnp.bfloat16),
            pltpu.VMEM((gs * STRIDE, LANES), jnp.float32),
            pltpu.VMEM(((G // QUAD + 1) * CELLS, LANES), jnp.float32),
        ],
        compiler_params=params(46),
        name="sample",
    )(place, back, cell_at, mine, theirs, own, other, cas)
    values = values.reshape(HALVES, members, 16 * groups, LANES)
    received = lax.ppermute(values[1], "col", mates).astype(jnp.float32)
    values = (values[0].astype(jnp.float32) + received).astype(jnp.bfloat16)
    values, my_charges, their_charges = lax.optimization_barrier((values, mine, theirs))
    values = swap_members(values)

    source = near_pairs[1]
    source_row = source // blocks // cols
    source_col = source // blocks % cols
    wanted = (source_col % HALVES ^ half) * members + source_row * (cols // HALVES)
    wanted = (wanted + source_col // HALVES) * blocks + source % blocks
    target = near_pairs[0] - (row_at * cols + col_at) * blocks
    pairs = near_blocks.shape[0]
    near, lanes = pl.pallas_call(
        near_kernel,
        grid=(pairs // blocks,),
        in_specs=[
            smem,
            pl.BlockSpec((blocks, BLK * BLK), lambda n: (n, 0)),
            pl.BlockSpec((1, blocks), lambda n: (0, n)),
            charge_rows,
            charge_rows,
            whole((blocks, LANES)),
        ],
        out_specs=(whole((blocks, LANES)), whole((4, blocks, 4 * blocks))),
        out_shape=(
            struct((blocks, LANES), jnp.float32),
            struct((4, blocks, 4 * blocks), jnp.bfloat16),
        ),
        scratch_shapes=[
            pltpu.VMEM((devices * blocks, LANES), jnp.float32),
            pltpu.VMEM((blocks, LANES), jnp.float32),
        ],
        compiler_params=params(40),
        name="near",
    )(wanted, near_blocks, target.reshape(1, pairs), my_charges, their_charges, spots)

    result = pl.pallas_call(
        finish_kernel,
        out_shape=struct((strips, LANES), jnp.float32),
        scratch_shapes=[pltpu.VMEM((blocks, LANES), jnp.float32)],
        compiler_params=params(32),
        name="finish",
    )(values, interpolate, near, inverse, lanes)
    return result.reshape(panels)


def solution(mesh):
    placed = (
        P(("row", "col")),
        P(("row", "col")),
        P(None, ("row", "col")),
        P(("row", "col"), None),
        P(("row", "col"), None),
        P("row", "col", None),
        P(None, ("row", "col")),
        P(("row", "col"), None),
    )
    return jax.shard_map(
        body, mesh=mesh, in_specs=placed, out_specs=P(("row", "col")), check_vma=False
    )
```
